32 devices in a mesh: gx: 4 (over y, x), gy: 8 (over z, core).
Axes of the slice: x: 2, y: 2, z: 4, core: 2. Of those that a mesh axis runs over, the one named last changes fastest.
Arguments:
- tgt: bfloat16 [32, 1024, 512], P(('gx', 'gy')), may hold values from -4 to 4
- memory: bfloat16 [32, 1024, 512], P(('gx', 'gy')), may hold values from -4 to 4
- cotangent: bfloat16 [32, 1024, 512], P(('gx', 'gy')), may hold values from -4 to 4
- tgt_lengths: int32 [32, 48], P(('gx', 'gy')), may hold values from 1 to 512, 1024 in all within a row
- src_segments: int32 [32, 1024], P(('gx', 'gy')), may hold values from 0 to 47, never falling along the last dimension, each value on 1 to 512 neighbouring positions
- attn_w: float32 [8, 512, 512], P(None, ('gx', 'gy')), may hold values from -1.2374369 to 1.2374369
- ffn_in: float32 [512, 2048], P(('gx', 'gy')), may hold values from -0.30935922 to 0.30935922
- ffn_out: float32 [2048, 512], P(('gx', 'gy')), may hold values from -0.15467961 to 0.15467961
- norm_params: float32 [6, 512], P(None, ('gx', 'gy')), may hold values from -2.5 to 2.5, as said below
- attn_moments: float32 [2, 8, 512, 512], P(None, None, ('gx', 'gy')), may hold values from -347.55713 to 11796.48, as said below
- in_moments: float32 [2, 512, 2048], P(None, ('gx', 'gy')), may hold values from -289.63094 to 8192, as said below
- out_moments: float32 [2, 2048, 512], P(None, ('gx', 'gy')), may hold values from -695.11425 to 47185.92, as said below
- norm_moments: float32 [2, 6, 512], P(None, None, ('gx', 'gy')), may hold values from -1158.5238 to 131072, as said below
Outputs:
- layer_out: bfloat16 [32, 1024, 512], P(('gx', 'gy'))
- tgt_grad: bfloat16 [32, 1024, 512], P(('gx', 'gy'))
- mem_grad: bfloat16 [32, 1024, 512], P(('gx', 'gy'))
- attn_new: float32 [8, 512, 512], P(None, ('gx', 'gy'))
- in_new: float32 [512, 2048], P(('gx', 'gy'))
- out_new: float32 [2048, 512], P(('gx', 'gy'))
- norm_new: float32 [6, 512], P(None, ('gx', 'gy'))
- attn_first_new: float32 [8, 512, 512], P(None, ('gx', 'gy'))
- attn_second_new: float32 [8, 512, 512], P(None, ('gx', 'gy'))
- in_first_new: float32 [512, 2048], P(('gx', 'gy'))
- in_second_new: float32 [512, 2048], P(('gx', 'gy'))
- out_first_new: float32 [2048, 512], P(('gx', 'gy'))
- out_second_new: float32 [2048, 512], P(('gx', 'gy'))
- norm_first_new: float32 [6, 512], P(None, ('gx', 'gy'))
- norm_second_new: float32 [6, 512], P(None, ('gx', 'gy'))
- attn_copy: bfloat16 [8, 512, 512], P(None, ('gx', 'gy'))
- in_copy: bfloat16 [512, 2048], P(('gx', 'gy'))
- out_copy: bfloat16 [2048, 512], P(('gx', 'gy'))
- norm_copy: bfloat16 [6, 512], P(None, ('gx', 'gy'))
- norms: float32 [2, 16], replicated
The draws below stay inside these ranges and needn't reach their ends.
Inputs may be any that keep to these rules, and one draw needn't show every extreme that they name: `tgt_lengths`: each row's 48 lengths sum to 1024; every row has one length equal to 512. `src_segments`: in each row the numbers never fall and take every value from 0 to 47, each for at most 512 positions; target sentence s of a row is translated from its memory rows numbered s. `norm_params`: gains are positive. `attn_moments`: element 0 holds first moments, element 1 positive second moments. `in_moments`: element 0 holds first moments, element 1 positive second moments. `out_moments`: element 0 holds first moments, element 1 positive second moments. `norm_moments`: element 0 holds first moments, element 1 positive second moments.
All inputs are finite; a program needn't handle non-finite values.
Results may differ from the reference program's by a relative error of at most 0.03.
The reference program's roundings to bfloat16 on the way count: a program that leaves them out, or rounds other values in their place, can miss the bound.
Values may be sent and summed in bfloat16 or wider, within the bound.
A program may use at most 192 MiB of HBM per device.

```python
import math
import jax
import jax.numpy as jnp
import numpy as np
from jax import lax

D = 512
FF = 2048
HEAD_DIM = 64
ROW_TOK = 1024
MEM_TOK = 1024
SEGS = 48
LEN_MOST = 512
STEP = 5
ROWS = 32
TOKENS = 32768


def rising(full_shape, axis_index, top_ratio):
    position = lax.broadcasted_iota(jnp.float32, full_shape, axis_index) / max(full_shape[axis_index] - 1, 1)
    return 1.0 + (top_ratio - 1.0) * position


def finish_moments(base_draw, second_key, full_shape, axis_index, top_ratio, size_scale):
    first_moment = size_scale * 0.4 * base_draw * rising(full_shape, axis_index, top_ratio)
    second_moment = size_scale * size_scale * jnp.exp(jax.random.uniform(second_key, full_shape, jnp.float32, 0.0, 1.3862944))
    return jnp.stack([first_moment, second_moment])


def unit_field(key, full_shape):
    return jax.random.truncated_normal(key, -4.0, 4.0, full_shape, jnp.float32)


def draw_tgt(key, part):
    key = jax.random.fold_in(key, 109)
    return unit_field(key, (ROWS, ROW_TOK, D)).astype(jnp.bfloat16)


def draw_memory(key, part):
    key = jax.random.fold_in(key, 110)
    return unit_field(key, (ROWS, MEM_TOK, D)).astype(jnp.bfloat16)


def draw_cotangent(key, part):
    key = jax.random.fold_in(key, 111)
    return unit_field(key, (ROWS, ROW_TOK, D)).astype(jnp.bfloat16)


def draw_attn_w(key, part):
    key = jax.random.fold_in(key, 101)
    full_shape = (8, D, D)
    base_draw = jax.random.truncated_normal(key, -4.0, 4.0, full_shape, jnp.float32)
    top_ratio = 1.7320508
    column_boost = jnp.array([1.0, 1.0, 1.0, 4.0, 1.0, 1.0, 1.0, 4.0], jnp.float32)[:, None, None]
    return base_draw * column_boost * rising(full_shape, 1, top_ratio) * D ** (-0.5)


def draw_ffn_in(key, part):
    key = jax.random.fold_in(key, 102)
    full_shape = (D, FF)
    base_draw = jax.random.truncated_normal(key, -4.0, 4.0, full_shape, jnp.float32)
    top_ratio = 1.7320508
    return base_draw * rising(full_shape, 0, top_ratio) * D ** (-0.5)


def draw_ffn_out(key, part):
    key = jax.random.fold_in(key, 103)
    full_shape = (FF, D)
    base_draw = jax.random.truncated_normal(key, -4.0, 4.0, full_shape, jnp.float32)
    top_ratio = 1.7320508
    return base_draw * rising(full_shape, 0, top_ratio) * FF ** (-0.5)


def draw_norm_params(key, part):
    key = jax.random.fold_in(key, 104)
    full_shape = (6, D)
    base_draw = jax.random.truncated_normal(key, -4.0, 4.0, full_shape, jnp.float32)
    scaled_ramp = rising(full_shape, 1, 1.7320508)
    gain_rows = lax.broadcasted_iota(jnp.int32, full_shape, 0) % 2 == 0
    return jnp.where(gain_rows, scaled_ramp * (1.0 + 0.1 * base_draw), 0.3 * base_draw * scaled_ramp)


def draw_attn_moments(key, part):
    key = jax.random.fold_in(key, 105)
    first_key, second_key = jax.random.split(key)
    full_shape = (8, D, D)
    base_draw = jax.random.truncated_normal(first_key, -4.0, 4.0, full_shape, jnp.float32)
    top_ratio = 4.0
    return finish_moments(base_draw, second_key, full_shape, 1, top_ratio, 0.3 * TOKENS ** 0.5)


def draw_in_moments(key, part):
    key = jax.random.fold_in(key, 106)
    first_key, second_key = jax.random.split(key)
    full_shape = (D, FF)
    base_draw = jax.random.truncated_normal(first_key, -4.0, 4.0, full_shape, jnp.float32)
    top_ratio = 4.0
    return finish_moments(base_draw, second_key, full_shape, 0, top_ratio, 0.25 * TOKENS ** 0.5)


def draw_out_moments(key, part):
    key = jax.random.fold_in(key, 107)
    first_key, second_key = jax.random.split(key)
    full_shape = (FF, D)
    base_draw = jax.random.truncated_normal(first_key, -4.0, 4.0, full_shape, jnp.float32)
    top_ratio = 4.0
    return finish_moments(base_draw, second_key, full_shape, 0, top_ratio, 0.6 * TOKENS ** 0.5)


def draw_norm_moments(key, part):
    key = jax.random.fold_in(key, 108)
    first_key, second_key = jax.random.split(key)
    full_shape = (6, D)
    base_draw = jax.random.truncated_normal(first_key, -4.0, 4.0, full_shape, jnp.float32)
    top_ratio = 4.0
    return finish_moments(base_draw, second_key, full_shape, 1, top_ratio, TOKENS ** 0.5)


def split_up(amount, total, most, slope):
    portions = [(1 << 20) // math.isqrt(standing ** slope) + 1 for standing in range(2, amount + 1)]
    surplus, given = total - most - (amount - 1), [1] * (amount - 1)
    while surplus > 0:
        movable = [i for i in range(amount - 1) if given[i] < most]
        pool, left = sum([portions[i] for i in movable]), surplus
        for i in movable:
            addition = min(most - given[i], max(1, left * portions[i] // pool), surplus)
            given[i] = given[i] + addition
            surplus = surplus - addition
    return np.array([most] + given)


def ragged_sizes(own_key, number_of, total, most, skew):
    if number_of == 2:
        one = jax.random.randint(own_key, (), max(1, total - most), min(most, total - 1) + 1)
        return jnp.stack([one, total - one])
    sizes = jnp.asarray(split_up(number_of, total, most, skew), jnp.int32)
    couples = (number_of - 1) // 2
    donor, sink = sizes[1:1 + 2 * couples:2], sizes[2:2 + 2 * couples:2]
    room = jnp.minimum(donor - 1, most - sink)
    moved = jax.random.randint(jax.random.fold_in(own_key, 1), (couples,), 0, 1 << 20) % (room + 1)
    sizes = sizes.at[1:1 + 2 * couples:2].set(donor - moved).at[2:2 + 2 * couples:2].set(sink + moved)
    return sizes[jax.random.permutation(jax.random.fold_in(own_key, 2), number_of)]


def setup_inputs(seed: int = 0) -> dict:
    keys = jax.random.split(jax.random.key(seed), 14)
    return {
        "tgt": draw_tgt(jax.random.fold_in(keys[13], 71), 0),
        "memory": draw_memory(jax.random.fold_in(keys[13], 71), 0),
        "cotangent": draw_cotangent(jax.random.fold_in(keys[13], 71), 0),
        "tgt_lengths": jax.vmap(lambda own: ragged_sizes(own, SEGS, ROW_TOK, LEN_MOST, 2))(jax.random.split(keys[3], ROWS)).reshape((ROWS, SEGS)).astype(jnp.int32),
        "src_segments": jax.vmap(lambda own: jnp.searchsorted(jnp.cumsum(ragged_sizes(own, SEGS, MEM_TOK, LEN_MOST, 2)), jnp.arange(MEM_TOK), side="right"))(jax.random.split(keys[4], ROWS)).reshape((ROWS, MEM_TOK)).astype(jnp.int32),
        "attn_w": draw_attn_w(jax.random.fold_in(keys[13], 71), 0),
        "ffn_in": draw_ffn_in(jax.random.fold_in(keys[13], 71), 0),
        "ffn_out": draw_ffn_out(jax.random.fold_in(keys[13], 71), 0),
        "norm_params": draw_norm_params(jax.random.fold_in(keys[13], 71), 0),
        "attn_moments": draw_attn_moments(jax.random.fold_in(keys[13], 71), 0),
        "in_moments": draw_in_moments(jax.random.fold_in(keys[13], 71), 0),
        "out_moments": draw_out_moments(jax.random.fold_in(keys[13], 71), 0),
        "norm_moments": draw_norm_moments(jax.random.fold_in(keys[13], 71), 0),
    }


@jax.custom_vjp
def low(v):
    return lax.optimization_barrier(v.astype(jnp.bfloat16)).astype(jnp.float32)

@jax.custom_vjp
def low_back(v):
    return v

def low_keep(v):
    return (low(v), None)

def low_pass(kept, grad):
    return (grad,)

def back_keep(v):
    return (v, None)

def back_low(kept, grad):
    return (low(grad),)
low.defvjp(low_keep, low_pass)
low_back.defvjp(back_keep, back_low)
beta_first = 0.5
beta_second = 0.5
learn_rate = 0.5
decay_rate = 0.01
norm_eps = 1e-05
adam_eps = 1e-06
masked_value = -1000000000.0

def segment_ids(lengths, count):
    ends = jnp.cumsum(lengths)
    places = jnp.arange(count, dtype=jnp.int32)
    return lax.optimization_barrier(jnp.sum((ends[None, :] <= places[:, None]).astype(jnp.int32), axis=1)).astype(jnp.int32)

def matmul(left, right):
    return jnp.dot(left, right, precision=lax.Precision.HIGHEST, preferred_element_type=jnp.float32)

def project(values, weight):
    return low_back(low(matmul(values, weight)))

def layer_norm(values, gain_row, bias_row):
    average = lax.optimization_barrier(jnp.mean(values, axis=-1, keepdims=True))
    centred = values - average
    spread = lax.optimization_barrier(jnp.mean(centred * centred, axis=-1, keepdims=True))
    return centred * lax.rsqrt(spread + norm_eps) * gain_row + bias_row

def attention(queries, key_rows, value_rows, allowed):
    query_heads = queries.reshape(queries.shape[0], -1, HEAD_DIM)
    key_heads = key_rows.reshape(key_rows.shape[0], -1, HEAD_DIM)
    value_heads = value_rows.reshape(value_rows.shape[0], -1, HEAD_DIM)
    raw_scores = low_back(jnp.einsum('qhd,khd->hqk', query_heads, key_heads, precision=lax.Precision.HIGHEST))
    logits = jnp.where(allowed[None], raw_scores * HEAD_DIM ** (-0.5), masked_value)
    row_max = lax.optimization_barrier(jnp.max(logits, axis=-1, keepdims=True))
    exponent = jnp.exp(logits - row_max)
    probability = low(exponent / lax.optimization_barrier(jnp.sum(exponent, axis=-1, keepdims=True)))
    mixture = jnp.einsum('hqk,khd->qhd', probability, value_heads, precision=lax.Precision.HIGHEST)
    return low_back(low(mixture.reshape(queries.shape[0], -1)))

def row_forward(params, row_items):
    attn_full, inner_full, outer_full, norm_full = params
    tokens, memory_rows, seg_tgt, seg_src = row_items
    places = jnp.arange(tokens.shape[0], dtype=jnp.int32)
    self_allowed = jnp.logical_and(seg_tgt[:, None] == seg_tgt[None, :], places[:, None] >= places[None, :])
    cross_allowed = seg_tgt[:, None] == seg_src[None, :]
    self_mix = attention(project(tokens, attn_full[0]), project(tokens, attn_full[1]), project(tokens, attn_full[2]), self_allowed)
    first_norm = layer_norm(tokens + low_back(matmul(self_mix, attn_full[3])), norm_full[0], norm_full[1])
    first_low = low(first_norm)
    cross_mix = attention(project(first_low, attn_full[4]), project(memory_rows, attn_full[5]), project(memory_rows, attn_full[6]), cross_allowed)
    second_norm = layer_norm(first_norm + low_back(matmul(cross_mix, attn_full[7])), norm_full[2], norm_full[3])
    inner_pre = low_back(matmul(low(second_norm), inner_full))
    activation = low(jax.nn.silu(inner_pre))
    return layer_norm(second_norm + low_back(matmul(activation, outer_full)), norm_full[4], norm_full[5])

def adam_direction(master, gradient, moments):
    first_moment = beta_first * moments[0] + (1.0 - beta_first) * gradient
    second_moment = beta_second * moments[1] + (1.0 - beta_second) * gradient * gradient
    first_fix = 1.0 - beta_first ** STEP
    second_fix = 1.0 - beta_second ** STEP
    direction = first_moment / first_fix / (jnp.sqrt(second_moment / second_fix) + adam_eps) + decay_rate * master
    return (direction, first_moment, second_moment)

def tensor_squares(attn_part, inner_part, outer_part, norm_part):
    return jnp.concatenate([lax.optimization_barrier(jnp.sum(attn_part * attn_part, axis=(1, 2))), jnp.sum(inner_part * inner_part)[None], jnp.sum(outer_part * outer_part)[None], lax.optimization_barrier(jnp.sum(norm_part * norm_part, axis=1))])

def reference(tgt, memory, cotangent, tgt_lengths, src_segments, attn_w, ffn_in, ffn_out, norm_params, attn_moments, in_moments, out_moments, norm_moments):
    seg_tgt = jax.vmap(lambda row_lengths: segment_ids(row_lengths, ROW_TOK))(tgt_lengths)
    masters = (attn_w, ffn_in, ffn_out, norm_params)

    def whole_layer(inputs, memory_rows, params):
        low_params = tuple((low(tensor) for tensor in params))

        def one_row(row_items):
            return row_forward(low_params, row_items)
        return lax.map(jax.checkpoint(one_row), (inputs, memory_rows, seg_tgt, src_segments))
    final_rows, pullback = jax.vjp(whole_layer, tgt.astype(jnp.float32), memory.astype(jnp.float32), masters)
    grad_tgt, grad_memory, grads = pullback(cotangent.astype(jnp.float32))
    attn_dir, attn_first, attn_second = adam_direction(attn_w, grads[0], attn_moments)
    inner_dir, inner_first, inner_second = adam_direction(ffn_in, grads[1], in_moments)
    outer_dir, outer_first, outer_second = adam_direction(ffn_out, grads[2], out_moments)
    norm_dir, norm_first, norm_second = adam_direction(norm_params, grads[3], norm_moments)
    weight_sq = tensor_squares(attn_w, ffn_in, ffn_out, norm_params)
    update_sq = tensor_squares(attn_dir, inner_dir, outer_dir, norm_dir)
    ratio = jnp.sqrt(weight_sq) / jnp.sqrt(update_sq)
    attn_new = attn_w - learn_rate * ratio[0:8][:, None, None] * attn_dir
    in_new = ffn_in - learn_rate * ratio[8] * inner_dir
    out_new = ffn_out - learn_rate * ratio[9] * outer_dir
    norm_new = norm_params - learn_rate * ratio[10:16][:, None] * norm_dir
    norms = jnp.stack([jnp.sqrt(weight_sq), jnp.sqrt(update_sq)])
    return (final_rows.astype(jnp.bfloat16), grad_tgt.astype(jnp.bfloat16), grad_memory.astype(jnp.bfloat16), attn_new, in_new, out_new, norm_new, attn_first, attn_second, inner_first, inner_second, outer_first, outer_second, norm_first, norm_second, attn_new.astype(jnp.bfloat16), in_new.astype(jnp.bfloat16), out_new.astype(jnp.bfloat16), norm_new.astype(jnp.bfloat16), norms)
```

```python
import functools

import jax
import jax.numpy as jnp
from jax import lax
from jax.experimental import pallas as pl
from jax.experimental.pallas import tpu as pltpu
from jax.sharding import PartitionSpec as P

HEAD_DIM = 64
STEP = 5

beta_first = 0.5
beta_second = 0.5
learn_rate = 0.5
decay_rate = 0.01
norm_eps = 1e-05
adam_eps = 1e-06

f32 = jnp.float32
bf16 = jnp.bfloat16
LANES = 128
QB = 128
KB = 256
RC = 256
MASKED = -1e30
AXES = ("gx", "gy")
MIB = 2**20


def nn(left, right):
    return lax.dot_general(left, right, (((1,), (0,)), ((), ())), preferred_element_type=f32)


def nt(left, right):
    return lax.dot_general(left, right, (((1,), (1,)), ((), ())), preferred_element_type=f32)


def tn(left, right):
    return lax.dot_general(left, right, (((0,), (0,)), ((), ())), preferred_element_type=f32)


def rows_of(step, size):
    return pl.ds(pl.multiple_of(step * size, size), size)


def each_chunk(count, body):
    def step(index, carry):
        body(index)
        return carry

    lax.fori_loop(0, count, step, 0)


def spread_heads(dst, src):
    pairs = dst.shape[0]
    first = lax.broadcasted_iota(jnp.int32, (QB, LANES), 1) < HEAD_DIM
    zero = jnp.zeros((QB, LANES), bf16)

    def body(i):
        start = pl.multiple_of(i * 2 * QB, 2 * QB)
        for p in range(pairs):
            tile = src[rows_of(i, QB), p * LANES : (p + 1) * LANES]
            dst[p, pl.ds(start, QB), :] = jnp.where(first, tile, zero)
            dst[p, pl.ds(start + QB, QB), :] = jnp.where(first, zero, tile)

    each_chunk(src.shape[0] // QB, body)


def key_block(first_key, j, keys):
    nominal = first_key * LANES + j * KB
    return pl.multiple_of(jnp.minimum(nominal, keys - KB), LANES), nominal


def block_bias(low, high, start, nominal):
    place = start + lax.broadcasted_iota(jnp.int32, (KB, QB), 0)
    bias = jnp.where((place >= jnp.maximum(low, nominal)) & (place < high), 0.0, MASKED).astype(f32)
    return jnp.concatenate([bias, bias], axis=1)


def attention(spans, which, bounds, key_ref, value_t, query_z, mixed_ref, lse_ref, score_scr, out_scr):
    keys = key_ref.shape[0]
    pairs = query_z.shape[0]
    fold = (KB // 8, 8, 2 * QB)

    def query_block(i):
        rows = rows_of(i, QB)
        pair_rows = rows_of(i, 2 * QB)
        low = bounds[2 * which : 2 * which + 1, rows]
        high = bounds[2 * which + 1 : 2 * which + 2, rows]
        first_key = spans[2 * which, i]
        blocks = spans[2 * which + 1, i]
        out_scr[...] = jnp.zeros_like(out_scr)

        def scores(j, tops):
            start, nominal = key_block(first_key, j, keys)
            bias = block_bias(low, high, start, nominal)
            found = []
            for p in range(pairs):
                lanes = slice(p * LANES, (p + 1) * LANES)
                score = nt(key_ref[pl.ds(start, KB), lanes], query_z[p, pair_rows, :]) + bias
                score_scr[p, rows_of(j, KB), :] = score
                found.append(jnp.maximum(tops[p], jnp.max(score.reshape(fold), axis=0)))
            return tuple(found)

        tops = lax.fori_loop(
            0, blocks, scores, tuple(jnp.full((8, 2 * QB), MASKED, f32) for _ in range(pairs))
        )
        top = [jnp.max(t, axis=0, keepdims=True) for t in tops]

        def weigh(j, sums):
            start, _ = key_block(first_key, j, keys)
            found = []
            for p in range(pairs):
                exponent = jnp.exp(score_scr[p, rows_of(j, KB), :] - top[p])
                found.append(sums[p] + jnp.sum(exponent.reshape(fold), axis=0))
                low_exp = exponent.astype(bf16)
                for h in range(2):
                    heads = slice(h * HEAD_DIM, (h + 1) * HEAD_DIM)
                    value = value_t[
                        p * LANES + h * HEAD_DIM : p * LANES + (h + 1) * HEAD_DIM, pl.ds(start, KB)
                    ]
                    out_scr[p, heads, :] += nn(value, low_exp[:, h * QB : (h + 1) * QB])
            return tuple(found)

        sums = lax.fori_loop(
            0, blocks, weigh, tuple(jnp.zeros((8, 2 * QB), f32) for _ in range(pairs))
        )
        for p in range(pairs):
            total = jnp.sum(sums[p], axis=0, keepdims=True)
            lse_ref[i, p : p + 1, :] = top[p] + jnp.log(total)
            inverse = 1.0 / total
            out = jnp.concatenate(
                [out_scr[p, 0:HEAD_DIM, :] * inverse[:, :QB], out_scr[p, HEAD_DIM:, :] * inverse[:, QB:]],
                axis=0,
            )
            mixed_ref[rows, p * LANES : (p + 1) * LANES] = out.T.astype(bf16)

    each_chunk(query_z.shape[1] // (2 * QB), query_block)


def attention_back(
    spans, which, bounds, key_ref, key_t, value_ref, query_z, grad_z, grad_ref, mixed_ref, lse_ref,
    dquery_ref, dkey_scr, dvalue_scr, dq_scr,
):
    keys = key_ref.shape[0]
    pairs = query_z.shape[0]

    def query_block(i):
        rows = rows_of(i, QB)
        pair_rows = rows_of(i, 2 * QB)
        low = bounds[2 * which : 2 * which + 1, rows]
        high = bounds[2 * which + 1 : 2 * which + 2, rows]
        first_key = spans[2 * which, i]
        blocks = spans[2 * which + 1, i]
        dq_scr[...] = jnp.zeros_like(dq_scr)
        deltas = []
        for p in range(pairs):
            lanes = slice(p * LANES, (p + 1) * LANES)
            product = (grad_ref[rows, lanes].astype(f32) * mixed_ref[rows, lanes].astype(f32)).T
            deltas.append(
                jnp.concatenate(
                    [
                        jnp.sum(product[:HEAD_DIM], axis=0, keepdims=True),
                        jnp.sum(product[HEAD_DIM:], axis=0, keepdims=True),
                    ],
                    axis=1,
                )
            )

        def key_step(j):
            start, nominal = key_block(first_key, j, keys)
            bias = block_bias(low, high, start, nominal)
            block = pl.ds(start, KB)
            for p in range(pairs):
                lanes = slice(p * LANES, (p + 1) * LANES)
                query = query_z[p, pair_rows, :]
                grad = grad_z[p, pair_rows, :]
                score = nt(key_ref[block, lanes], query)
                dprob = nt(value_ref[block, lanes], grad)
                prob = jnp.exp(score + bias - lse_ref[i, p : p + 1, :])
                dscore = (prob * (dprob - deltas[p])).astype(bf16)
                dvalue_scr[block, lanes] += nn(prob.astype(bf16), grad)
                dkey_scr[block, lanes] += nn(dscore, query)
                for h in range(2):
                    heads = slice(h * HEAD_DIM, (h + 1) * HEAD_DIM)
                    key = key_t[
                        p * LANES + h * HEAD_DIM : p * LANES + (h + 1) * HEAD_DIM, block
                    ]
                    dq_scr[p, heads, :] += nn(key, dscore[:, h * QB : (h + 1) * QB])

        each_chunk(blocks, key_step)
        for p in range(pairs):
            dquery_ref[rows, p * LANES : (p + 1) * LANES] = (
                (dq_scr[p] * HEAD_DIM**-0.5).T.astype(bf16)
            )

    each_chunk(query_z.shape[1] // (2 * QB), query_block)


def norm_parts(values):
    average = jnp.mean(values, axis=-1, keepdims=True)
    centred = values - average
    spread = jnp.mean(centred * centred, axis=-1, keepdims=True)
    inverse = lax.rsqrt(spread + norm_eps)
    return centred * inverse, inverse


def norm_back(gradient, normed, inverse, gain):
    scaled = gradient * gain
    first_mean = jnp.mean(scaled, axis=-1, keepdims=True)
    second_mean = jnp.mean(scaled * normed, axis=-1, keepdims=True)
    return inverse * (scaled - first_mean - normed * second_mean)


def fold_rows(values):
    return jnp.sum(values.reshape(values.shape[0] // 8, 8, values.shape[1]), axis=0)


def forward_kernel(
    spans, bounds, tgt, memory, attn, norm,
    q_ref, k_ref, v_ref, mix_ref, lse_ref, cq_ref, ck_ref, cv_ref, cmix_ref, clse_ref,
    n1_ref, s1_ref, n2_ref, s2_ref,
    query_z, value_t, score_scr, out_scr, h1_scr,
):
    chunks = tgt.shape[0] // RC
    scale = jnp.array(HEAD_DIM**-0.5, bf16)

    def project(c):
        rows = rows_of(c, RC)
        x = tgt[rows, :]
        q_ref[rows, :] = nn(x, attn[0]).astype(bf16) * scale
        k_ref[rows, :] = nn(x, attn[1]).astype(bf16)
        v_ref[rows, :] = nn(x, attn[2]).astype(bf16)

    each_chunk(chunks, project)
    spread_heads(query_z, q_ref)
    value_t[...] = v_ref[...].T
    attention(spans, 0, bounds, k_ref, value_t, query_z, mix_ref, lse_ref, score_scr, out_scr)

    def middle(c):
        rows = rows_of(c, RC)
        normed, inverse = norm_parts(tgt[rows, :].astype(f32) + nn(mix_ref[rows, :], attn[3]))
        n1_ref[rows, :] = normed
        s1_ref[rows, :] = inverse
        h1 = normed * norm[0:1, :].astype(f32) + norm[1:2, :].astype(f32)
        h1_scr[rows, :] = h1
        cq_ref[rows, :] = nn(h1.astype(bf16), attn[4]).astype(bf16) * scale
        mem = memory[rows, :]
        ck_ref[rows, :] = nn(mem, attn[5]).astype(bf16)
        cv_ref[rows, :] = nn(mem, attn[6]).astype(bf16)

    each_chunk(chunks, middle)
    spread_heads(query_z, cq_ref)
    value_t[...] = cv_ref[...].T
    attention(spans, 1, bounds, ck_ref, value_t, query_z, cmix_ref, clse_ref, score_scr, out_scr)

    def last(c):
        rows = rows_of(c, RC)
        normed, inverse = norm_parts(h1_scr[rows, :] + nn(cmix_ref[rows, :], attn[7]))
        n2_ref[rows, :] = normed
        s2_ref[rows, :] = inverse

    each_chunk(chunks, last)


def ffn_kernel(
    n2_ref, s2_ref, cot_ref, inner, outer, norm,
    out_ref, d2_ref, ginner_ref, gouter_ref, gnorm_ref,
    h2_scr, act_scr, d3_scr, dpre_scr, sums,
):
    chunks = n2_ref.shape[0] // RC
    hidden = inner.shape[1]
    sums[...] = jnp.zeros_like(sums)

    def body(c):
        rows = rows_of(c, RC)
        n2 = n2_ref[rows, :]
        h2 = n2 * norm[2:3, :].astype(f32) + norm[3:4, :].astype(f32)
        h2b = h2.astype(bf16)
        h2_scr[rows, :] = h2b
        pre = nn(h2b, inner[...])
        sig = 1.0 / (1.0 + jnp.exp(-pre))
        act = (pre * sig).astype(bf16)
        act_scr[rows, :] = act
        n3, s3 = norm_parts(h2 + nn(act, outer[...]))
        out_ref[rows, :] = (n3 * norm[4:5, :].astype(f32) + norm[5:6, :].astype(f32)).astype(bf16)
        cot = cot_ref[rows, :].astype(f32)
        sums[2] += fold_rows(cot * n3)
        sums[3] += fold_rows(cot)
        d3 = norm_back(cot, n3, s3, norm[4:5, :].astype(f32))
        d3b = d3.astype(bf16)
        d3_scr[rows, :] = d3b
        dpre = (nt(d3b, outer[...]) * (sig * (1.0 + pre * (1.0 - sig)))).astype(bf16)
        dpre_scr[rows, :] = dpre
        dh2 = d3 + nt(dpre, inner[...])
        sums[0] += fold_rows(dh2 * n2)
        sums[1] += fold_rows(dh2)
        d2_ref[rows, :] = norm_back(dh2, n2, s2_ref[rows, :], norm[2:3, :].astype(f32))

    each_chunk(chunks, body)
    for i in range(4):
        gnorm_ref[i : i + 1, :] = jnp.sum(sums[i], axis=0, keepdims=True)
    part = 2 * RC

    def grads(c):
        cols = rows_of(c, part)
        gouter_ref[cols, :] = tn(act_scr[:, cols], d3_scr[...]).astype(bf16)
        ginner_ref[:, cols] = tn(h2_scr[...], dpre_scr[:, cols]).astype(bf16)

    each_chunk(hidden // part, grads)


def cross_back_kernel(
    spans, bounds, d2_ref, memory, cq_ref, ck_ref, cv_ref, cmix_ref, clse_ref, n1_ref, s1_ref, attn, norm,
    d1_ref, mgrad_ref, gattn_ref, gnorm_ref,
    query_z, grad_z, key_t, grad_scr, dq_scr, dk_scr, dv_scr, acc_scr, h1_scr, sums,
):
    chunks = d2_ref.shape[0] // RC
    sums[...] = jnp.zeros_like(sums)

    def enter(c):
        rows = rows_of(c, RC)
        d2b = d2_ref[rows, :].astype(bf16)
        h1_scr[rows, :] = d2b
        grad_scr[rows, :] = nt(d2b, attn[7]).astype(bf16)

    each_chunk(chunks, enter)
    gattn_ref[3] = tn(cmix_ref[...], h1_scr[...]).astype(bf16)
    spread_heads(query_z, cq_ref)
    spread_heads(grad_z, grad_scr)
    key_t[...] = ck_ref[...].T
    dk_scr[...] = jnp.zeros_like(dk_scr)
    dv_scr[...] = jnp.zeros_like(dv_scr)
    attention_back(
        spans, 1, bounds, ck_ref, key_t, cv_ref, query_z, grad_z, grad_scr, cmix_ref, clse_ref,
        dq_scr, dk_scr, dv_scr, acc_scr,
    )

    def leave(c):
        rows = rows_of(c, RC)
        mgrad_ref[rows, :] = (
            nt(dk_scr[rows, :].astype(bf16), attn[5]) + nt(dv_scr[rows, :].astype(bf16), attn[6])
        ).astype(bf16)
        n1 = n1_ref[rows, :]
        h1_scr[rows, :] = (n1 * norm[0:1, :].astype(f32) + norm[1:2, :].astype(f32)).astype(bf16)
        dh1 = d2_ref[rows, :] + nt(dq_scr[rows, :], attn[4])
        sums[0] += fold_rows(dh1 * n1)
        sums[1] += fold_rows(dh1)
        d1_ref[rows, :] = norm_back(dh1, n1, s1_ref[rows, :], norm[0:1, :].astype(f32))

    each_chunk(chunks, leave)
    for i in range(2):
        gnorm_ref[i : i + 1, :] = jnp.sum(sums[i], axis=0, keepdims=True)
    gattn_ref[0] = tn(h1_scr[...], dq_scr[...]).astype(bf16)
    gattn_ref[1] = tn(memory[...], dk_scr[...].astype(bf16)).astype(bf16)
    gattn_ref[2] = tn(memory[...], dv_scr[...].astype(bf16)).astype(bf16)


def self_back_kernel(
    spans, bounds, d1_ref, tgt, q_ref, k_ref, v_ref, mix_ref, lse_ref, attn,
    tgrad_ref, gattn_ref,
    query_z, grad_z, key_t, grad_scr, dq_scr, dk_scr, dv_scr, acc_scr, d1_scr,
):
    chunks = d1_ref.shape[0] // RC

    def enter(c):
        rows = rows_of(c, RC)
        d1b = d1_ref[rows, :].astype(bf16)
        d1_scr[rows, :] = d1b
        grad_scr[rows, :] = nt(d1b, attn[3]).astype(bf16)

    each_chunk(chunks, enter)
    gattn_ref[3] = tn(mix_ref[...], d1_scr[...]).astype(bf16)
    spread_heads(query_z, q_ref)
    spread_heads(grad_z, grad_scr)
    key_t[...] = k_ref[...].T
    dk_scr[...] = jnp.zeros_like(dk_scr)
    dv_scr[...] = jnp.zeros_like(dv_scr)
    attention_back(
        spans, 0, bounds, k_ref, key_t, v_ref, query_z, grad_z, grad_scr, mix_ref, lse_ref,
        dq_scr, dk_scr, dv_scr, acc_scr,
    )

    def leave(c):
        rows = rows_of(c, RC)
        tgrad_ref[rows, :] = (
            d1_ref[rows, :]
            + nt(dq_scr[rows, :], attn[0])
            + nt(dk_scr[rows, :].astype(bf16), attn[1])
            + nt(dv_scr[rows, :].astype(bf16), attn[2])
        ).astype(bf16)

    each_chunk(chunks, leave)
    gattn_ref[0] = tn(tgt[...], dq_scr[...]).astype(bf16)
    gattn_ref[1] = tn(tgt[...], dk_scr[...].astype(bf16)).astype(bf16)
    gattn_ref[2] = tn(tgt[...], dv_scr[...].astype(bf16)).astype(bf16)


def shape(dims, dtype):
    return jax.ShapeDtypeStruct(dims, dtype)


def call(kernel, outs, scratch, scalars, args):
    smem = pl.BlockSpec(memory_space=pltpu.SMEM)
    vmem = pl.BlockSpec(memory_space=pltpu.VMEM)
    return pl.pallas_call(
        kernel,
        out_shape=outs,
        in_specs=[smem] * scalars + [vmem] * (len(args) - scalars),
        out_specs=tuple(vmem for _ in outs),
        scratch_shapes=[pltpu.VMEM(dims, dtype) for dims, dtype in scratch],
        compiler_params=pltpu.CompilerParams(vmem_limit_bytes=56 * MIB),
    )(*args)


def segment_bounds(lengths, src_segments, length):
    sentences = lengths.shape[0]
    ends = jnp.cumsum(lengths)
    starts = ends - lengths
    sizes = jnp.sum(
        (src_segments[None, :] == jnp.arange(sentences, dtype=jnp.int32)[:, None]).astype(jnp.int32), axis=1
    )
    places = jnp.arange(length, dtype=jnp.int32)
    ended = ends[:, None] <= places[None, :]
    begun = starts[:, None] <= places[None, :]
    self_low = jnp.sum(jnp.where(ended, lengths[:, None], 0), axis=0)
    cross_low = jnp.sum(jnp.where(ended, sizes[:, None], 0), axis=0)
    cross_high = jnp.sum(jnp.where(begun, sizes[:, None], 0), axis=0)
    bounds = jnp.stack([self_low, places + 1, cross_low, cross_high]).astype(jnp.int32)
    firsts = bounds[0::2, 0::QB] // LANES
    lasts = (bounds[1::2, QB - 1 :: QB] + LANES - 1) // LANES
    counts = ((lasts - firsts) * LANES + KB - 1) // KB
    spans = jnp.stack([firsts[0], counts[0], firsts[1], counts[1]]).astype(jnp.int32)
    return bounds, spans


def layer(tgt, memory, cotangent, lengths, src_segments, attn, inner, outer, norm):
    length, width = tgt.shape
    keys = memory.shape[0]
    hidden = inner.shape[1]
    pairs = width // LANES
    blocks = length // QB
    bounds, spans = segment_bounds(lengths, src_segments, length)
    row = (length, width)
    mem_row = (keys, width)
    lse = (blocks, pairs, 2 * QB)
    most = max(length, keys)
    zeroed = ((pairs, 2 * length, LANES), bf16)
    (q, k, v, mix, row_lse, cq, ck, cv, cmix, cross_lse, n1, s1, n2, s2) = call(
        forward_kernel,
        (
            shape(row, bf16), shape(row, bf16), shape(row, bf16), shape(row, bf16), shape(lse, f32),
            shape(row, bf16), shape(mem_row, bf16), shape(mem_row, bf16), shape(row, bf16), shape(lse, f32),
            shape(row, f32), shape((length, 1), f32), shape(row, f32), shape((length, 1), f32),
        ),
        [
            zeroed,
            ((width, most), bf16),
            ((pairs, most + KB, 2 * QB), f32),
            ((pairs, LANES, QB), f32),
            (row, f32),
        ],
        1,
        (spans, bounds, tgt, memory, attn, norm),
    )
    layer_out, d2, grad_inner, grad_outer, norm_late = call(
        ffn_kernel,
        (
            shape(row, bf16), shape(row, f32), shape((width, hidden), bf16), shape((hidden, width), bf16),
            shape((4, width), f32),
        ),
        [(row, bf16), ((length, hidden), bf16), (row, bf16), ((length, hidden), bf16), ((4, 8, width), f32)],
        0,
        (n2, s2, cotangent, inner, outer, norm),
    )
    back_scratch = [
        zeroed, zeroed, ((width, most), bf16), (row, bf16), (row, bf16), (mem_row, f32), (mem_row, f32),
        ((pairs, LANES, QB), f32), (row, bf16),
    ]
    d1, mem_grad, grad_cross, norm_early = call(
        cross_back_kernel,
        (shape(row, f32), shape(mem_row, bf16), shape((4, width, width), bf16), shape((2, width), f32)),
        back_scratch + [((2, 8, width), f32)],
        1,
        (spans, bounds, d2, memory, cq, ck, cv, cmix, cross_lse, n1, s1, attn, norm),
    )
    tgt_grad, grad_self = call(
        self_back_kernel,
        (shape(row, bf16), shape((4, width, width), bf16)),
        back_scratch,
        1,
        (spans, bounds, d1, tgt, q, k, v, mix, row_lse, attn),
    )
    grad_norm = jnp.concatenate([norm_early, norm_late])
    return layer_out, tgt_grad, mem_grad, grad_self, grad_cross, grad_inner, grad_outer, grad_norm


def adam_direction(master, gradient, moments):
    first_moment = beta_first * moments[0] + (1.0 - beta_first) * gradient
    second_moment = beta_second * moments[1] + (1.0 - beta_second) * gradient * gradient
    first_fix = 1.0 - beta_first**STEP
    second_fix = 1.0 - beta_second**STEP
    direction = (
        first_moment / first_fix / (jnp.sqrt(second_moment / second_fix) + adam_eps)
        + decay_rate * master
    )
    return (direction, first_moment, second_moment)


def tensor_squares(attn_part, inner_part, outer_part, norm_part):
    return jnp.concatenate(
        [
            jnp.sum(attn_part * attn_part, axis=(1, 2)),
            jnp.sum(inner_part * inner_part)[None],
            jnp.sum(outer_part * outer_part)[None],
            jnp.sum(norm_part * norm_part, axis=1),
        ]
    )


def on_device(
    tgt, memory, cotangent, tgt_lengths, src_segments, attn_w, ffn_in, ffn_out, norm_params,
    attn_moments, in_moments, out_moments, norm_moments,
):
    weight_local = tensor_squares(attn_w, ffn_in, ffn_out, norm_params)
    attn = lax.all_gather(attn_w.astype(bf16), AXES, axis=1, tiled=True)
    inner = lax.all_gather(ffn_in.astype(bf16), AXES, axis=0, tiled=True)
    outer = lax.all_gather(ffn_out.astype(bf16), AXES, axis=0, tiled=True)
    norm = lax.all_gather(norm_params.astype(bf16), AXES, axis=1, tiled=True)
    rows = tgt.shape[0]
    parts = [
        layer(tgt[r], memory[r], cotangent[r], tgt_lengths[r], src_segments[r], attn, inner, outer, norm)
        for r in range(rows)
    ]
    layer_out, tgt_grad, mem_grad = (jnp.stack([part[i] for part in parts]) for i in range(3))
    grads = [sum(part[i].astype(f32) for part in parts) for i in range(3, 8)]
    grad_attn = jnp.concatenate([grads[0], grads[1]]).astype(bf16)
    shard_attn = lax.psum_scatter(grad_attn, AXES, scatter_dimension=1, tiled=True).astype(f32)
    shard_inner = lax.psum_scatter(grads[2].astype(bf16), AXES, scatter_dimension=0, tiled=True).astype(f32)
    shard_outer = lax.psum_scatter(grads[3].astype(bf16), AXES, scatter_dimension=0, tiled=True).astype(f32)
    shard_norm = lax.psum_scatter(grads[4], AXES, scatter_dimension=1, tiled=True)
    attn_dir, attn_first, attn_second = adam_direction(attn_w, shard_attn, attn_moments)
    inner_dir, inner_first, inner_second = adam_direction(ffn_in, shard_inner, in_moments)
    outer_dir, outer_first, outer_second = adam_direction(ffn_out, shard_outer, out_moments)
    norm_dir, norm_first, norm_second = adam_direction(norm_params, shard_norm, norm_moments)
    update_local = tensor_squares(attn_dir, inner_dir, outer_dir, norm_dir)
    weight_total, update_total = lax.psum((weight_local, update_local), AXES)
    ratio = jnp.sqrt(weight_total) / jnp.sqrt(update_total)
    attn_new = attn_w - learn_rate * ratio[0:8][:, None, None] * attn_dir
    in_new = ffn_in - learn_rate * ratio[8] * inner_dir
    out_new = ffn_out - learn_rate * ratio[9] * outer_dir
    norm_new = norm_params - learn_rate * ratio[10:16][:, None] * norm_dir
    norms = jnp.stack([jnp.sqrt(weight_total), jnp.sqrt(update_total)])
    return (
        layer_out, tgt_grad, mem_grad, attn_new, in_new, out_new, norm_new,
        attn_first, attn_second, inner_first, inner_second, outer_first, outer_second, norm_first, norm_second,
        attn_new.astype(bf16), in_new.astype(bf16), out_new.astype(bf16), norm_new.astype(bf16), norms,
    )


def solution(mesh):
    rows = P(AXES, None, None)
    matrix = P(AXES, None)
    stack = P(None, AXES, None)
    vectors = P(None, AXES)
    return jax.shard_map(
        on_device,
        mesh=mesh,
        in_specs=(
            rows, rows, rows, matrix, matrix, stack, matrix, matrix, vectors,
            P(None, None, AXES, None), stack, stack, P(None, None, AXES),
        ),
        out_specs=(
            rows, rows, rows, stack, matrix, matrix, vectors, stack, stack, matrix, matrix, matrix, matrix,
            vectors, vectors, stack, matrix, matrix, vectors, P(),
        ),
        check_vma=False,
    )
```

```python
import functools

import jax
import jax.numpy as jnp
from jax import lax
from jax.experimental import pallas as pl
from jax.experimental.pallas import tpu as pltpu
from jax.sharding import PartitionSpec as P

HEAD_DIM = 64
STEP = 5

beta_first = 0.5
beta_second = 0.5
learn_rate = 0.5
decay_rate = 0.01
norm_eps = 1e-05
adam_eps = 1e-06

f32 = jnp.float32
bf16 = jnp.bfloat16
LANES = 128
QB = 128
KB = 256
RC = 256
MASKED = -1e30
AXES = ("gx", "gy")
MIB = 2**20


def nn(left, right):
    return lax.dot_general(left, right, (((1,), (0,)), ((), ())), preferred_element_type=f32)


def nt(left, right):
    return lax.dot_general(left, right, (((1,), (1,)), ((), ())), preferred_element_type=f32)


def tn(left, right):
    return lax.dot_general(left, right, (((0,), (0,)), ((), ())), preferred_element_type=f32)


def rows_of(step, size):
    return pl.ds(pl.multiple_of(step * size, size), size)


def each_chunk(count, body):
    def step(index, carry):
        body(index)
        return carry

    lax.fori_loop(0, count, step, 0)


def spread_heads(dst, src):
    pairs = dst.shape[0]
    first = lax.broadcasted_iota(jnp.int32, (QB, LANES), 1) < HEAD_DIM
    zero = jnp.zeros((QB, LANES), bf16)

    def body(i):
        start = pl.multiple_of(i * 2 * QB, 2 * QB)
        for p in range(pairs):
            tile = src[rows_of(i, QB), p * LANES : (p + 1) * LANES]
            dst[p, pl.ds(start, QB), :] = jnp.where(first, tile, zero)
            dst[p, pl.ds(start + QB, QB), :] = jnp.where(first, zero, tile)

    each_chunk(src.shape[0] // QB, body)


def key_block(first_key, j, keys):
    nominal = first_key * LANES + j * KB
    return pl.multiple_of(jnp.minimum(nominal, keys - KB), LANES), nominal


def block_bias(low, high, start, nominal):
    place = start + lax.broadcasted_iota(jnp.int32, (KB, QB), 0)
    bias = jnp.where((place >= jnp.maximum(low, nominal)) & (place < high), 0.0, MASKED).astype(f32)
    return jnp.concatenate([bias, bias], axis=1)


def attention(spans, which, bounds, key_ref, value_t, query_z, mixed_ref, lse_ref, score_scr, out_scr):
    keys = key_ref.shape[0]
    pairs = query_z.shape[0]
    fold = (KB // 8, 8, 2 * QB)

    def query_block(i):
        rows = rows_of(i, QB)
        pair_rows = rows_of(i, 2 * QB)
        low = bounds[2 * which : 2 * which + 1, rows]
        high = bounds[2 * which + 1 : 2 * which + 2, rows]
        first_key = spans[2 * which, i]
        blocks = spans[2 * which + 1, i]
        out_scr[...] = jnp.zeros_like(out_scr)

        def scores(j, tops):
            start, nominal = key_block(first_key, j, keys)
            bias = block_bias(low, high, start, nominal)
            found = []
            for p in range(pairs):
                lanes = slice(p * LANES, (p + 1) * LANES)
                score = nt(key_ref[pl.ds(start, KB), lanes], query_z[p, pair_rows, :]) + bias
                score_scr[p, rows_of(j, KB), :] = score
                found.append(jnp.maximum(tops[p], jnp.max(score.reshape(fold), axis=0)))
            return tuple(found)

        tops = lax.fori_loop(
            0, blocks, scores, tuple(jnp.full((8, 2 * QB), MASKED, f32) for _ in range(pairs))
        )
        top = [jnp.max(t, axis=0, keepdims=True) for t in tops]

        def weigh(j, sums):
            start, _ = key_block(first_key, j, keys)
            found = []
            for p in range(pairs):
                exponent = jnp.exp(score_scr[p, rows_of(j, KB), :] - top[p])
                found.append(sums[p] + jnp.sum(exponent.reshape(fold), axis=0))
                low_exp = exponent.astype(bf16)
                for h in range(2):
                    heads = slice(h * HEAD_DIM, (h + 1) * HEAD_DIM)
                    value = value_t[
                        p * LANES + h * HEAD_DIM : p * LANES + (h + 1) * HEAD_DIM, pl.ds(start, KB)
                    ]
                    out_scr[p, heads, :] += nn(value, low_exp[:, h * QB : (h + 1) * QB])
            return tuple(found)

        sums = lax.fori_loop(
            0, blocks, weigh, tuple(jnp.zeros((8, 2 * QB), f32) for _ in range(pairs))
        )
        for p in range(pairs):
            total = jnp.sum(sums[p], axis=0, keepdims=True)
            lse_ref[i, p : p + 1, :] = top[p] + jnp.log(total)
            inverse = 1.0 / total
            out = jnp.concatenate(
                [out_scr[p, 0:HEAD_DIM, :] * inverse[:, :QB], out_scr[p, HEAD_DIM:, :] * inverse[:, QB:]],
                axis=0,
            )
            mixed_ref[rows, p * LANES : (p + 1) * LANES] = out.T.astype(bf16)

    each_chunk(query_z.shape[1] // (2 * QB), query_block)


def attention_back(
    spans, which, bounds, key_ref, key_t, value_ref, query_z, grad_z, grad_ref, mixed_ref, lse_ref,
    dquery_ref, dkey_scr, dvalue_scr, dq_scr,
):
    keys = key_ref.shape[0]
    pairs = query_z.shape[0]

    def query_block(i):
        rows = rows_of(i, QB)
        pair_rows = rows_of(i, 2 * QB)
        low = bounds[2 * which : 2 * which + 1, rows]
        high = bounds[2 * which + 1 : 2 * which + 2, rows]
        first_key = spans[2 * which, i]
        blocks = spans[2 * which + 1, i]
        dq_scr[...] = jnp.zeros_like(dq_scr)
        deltas = []
        for p in range(pairs):
            lanes = slice(p * LANES, (p + 1) * LANES)
            product = (grad_ref[rows, lanes].astype(f32) * mixed_ref[rows, lanes].astype(f32)).T
            deltas.append(
                jnp.concatenate(
                    [
                        jnp.sum(product[:HEAD_DIM], axis=0, keepdims=True),
                        jnp.sum(product[HEAD_DIM:], axis=0, keepdims=True),
                    ],
                    axis=1,
                )
            )

        def key_step(j):
            start, nominal = key_block(first_key, j, keys)
            bias = block_bias(low, high, start, nominal)
            block = pl.ds(start, KB)
            for p in range(pairs):
                lanes = slice(p * LANES, (p + 1) * LANES)
                query = query_z[p, pair_rows, :]
                grad = grad_z[p, pair_rows, :]
                score = nt(key_ref[block, lanes], query)
                dprob = nt(value_ref[block, lanes], grad)
                prob = jnp.exp(score + bias - lse_ref[i, p : p + 1, :])
                dscore = (prob * (dprob - deltas[p])).astype(bf16)
                dvalue_scr[block, lanes] += nn(prob.astype(bf16), grad)
                dkey_scr[block, lanes] += nn(dscore, query)
                for h in range(2):
                    heads = slice(h * HEAD_DIM, (h + 1) * HEAD_DIM)
                    key = key_t[
                        p * LANES + h * HEAD_DIM : p * LANES + (h + 1) * HEAD_DIM, block
                    ]
                    dq_scr[p, heads, :] += nn(key, dscore[:, h * QB : (h + 1) * QB])

        each_chunk(blocks, key_step)
        for p in range(pairs):
            dquery_ref[rows, p * LANES : (p + 1) * LANES] = (
                (dq_scr[p] * HEAD_DIM**-0.5).T.astype(bf16)
            )

    each_chunk(query_z.shape[1] // (2 * QB), query_block)


def norm_parts(values):
    average = jnp.mean(values, axis=-1, keepdims=True)
    centred = values - average
    spread = jnp.mean(centred * centred, axis=-1, keepdims=True)
    inverse = lax.rsqrt(spread + norm_eps)
    return centred * inverse, inverse


def norm_back(gradient, normed, inverse, gain):
    scaled = gradient * gain
    first_mean = jnp.mean(scaled, axis=-1, keepdims=True)
    second_mean = jnp.mean(scaled * normed, axis=-1, keepdims=True)
    return inverse * (scaled - first_mean - normed * second_mean)


def fold_rows(values):
    return jnp.sum(values.reshape(values.shape[0] // 8, 8, values.shape[1]), axis=0)


def load_norms(norm_ref):
    group = norm_ref.shape[0] // 4
    blocks = [jnp.sum(norm_ref[group * i : group * (i + 1)].astype(f32), axis=0) for i in range(4)]
    rows = jnp.concatenate(blocks, axis=1)
    return [rows[i : i + 1, :] for i in range(6)]


def weight(ref, index):
    blocks = ref.shape[0]
    return ref[:, 16 * index : 16 * (index + 1), :].reshape(16 * blocks, ref.shape[2])


def put_gradient(ref, index, value):
    blocks = ref.shape[0]
    ref[:, 16 * index : 16 * (index + 1), :] = value.astype(bf16).reshape(blocks, 16, ref.shape[2])


def forward_kernel(
    spans, bounds, tgt, memory, norm_ref, attn,
    q_ref, k_ref, v_ref, mix_ref, lse_ref, cq_ref, ck_ref, cv_ref, cmix_ref, clse_ref,
    n1_ref, s1_ref, n2_ref, s2_ref,
    query_z, value_t, score_scr, out_scr, h1_scr, norm_scr,
):
    chunks = tgt.shape[0] // RC
    scale = jnp.array(HEAD_DIM**-0.5, bf16)
    for i, vector in enumerate(load_norms(norm_ref)):
        norm_scr[i : i + 1, :] = vector

    def project(c):
        rows = rows_of(c, RC)
        x = tgt[rows, :]
        q_ref[rows, :] = nn(x, weight(attn, 0)).astype(bf16) * scale
        k_ref[rows, :] = nn(x, weight(attn, 1)).astype(bf16)
        v_ref[rows, :] = nn(x, weight(attn, 2)).astype(bf16)

    each_chunk(chunks, project)
    spread_heads(query_z, q_ref)
    value_t[...] = v_ref[...].T
    attention(spans, 0, bounds, k_ref, value_t, query_z, mix_ref, lse_ref, score_scr, out_scr)

    def middle(c):
        rows = rows_of(c, RC)
        normed, inverse = norm_parts(tgt[rows, :].astype(f32) + nn(mix_ref[rows, :], weight(attn, 3)))
        n1_ref[rows, :] = normed
        s1_ref[rows, :] = inverse
        h1 = normed * norm_scr[0:1, :] + norm_scr[1:2, :]
        h1_scr[rows, :] = h1
        cq_ref[rows, :] = nn(h1.astype(bf16), weight(attn, 4)).astype(bf16) * scale
        mem = memory[rows, :]
        ck_ref[rows, :] = nn(mem, weight(attn, 5)).astype(bf16)
        cv_ref[rows, :] = nn(mem, weight(attn, 6)).astype(bf16)

    each_chunk(chunks, middle)
    spread_heads(query_z, cq_ref)
    value_t[...] = cv_ref[...].T
    attention(spans, 1, bounds, ck_ref, value_t, query_z, cmix_ref, clse_ref, score_scr, out_scr)

    def last(c):
        rows = rows_of(c, RC)
        normed, inverse = norm_parts(h1_scr[rows, :] + nn(cmix_ref[rows, :], weight(attn, 7)))
        n2_ref[rows, :] = normed
        s2_ref[rows, :] = inverse

    each_chunk(chunks, last)


def ffn_kernel(
    n2_ref, s2_ref, cot_ref, norm_ref, ffn,
    out_ref, d2_ref, gffn_ref, gnorm_ref,
    h2_scr, act_scr, d3_scr, dpre_scr, sums, norm_scr,
):
    chunks = n2_ref.shape[0] // RC
    width = n2_ref.shape[1]
    blocks = ffn.shape[0]
    parts = act_scr.shape[1] // width
    share = blocks // parts
    sums[...] = jnp.zeros_like(sums)
    for i, vector in enumerate(load_norms(norm_ref)):
        norm_scr[i : i + 1, :] = vector

    def outer(b):
        return ffn[share * b : share * (b + 1), 16 * parts :, :].reshape(width, width)

    def body(c):
        rows = rows_of(c, RC)
        n2 = n2_ref[rows, :]
        h2 = n2 * norm_scr[2:3, :] + norm_scr[3:4, :]
        h2b = h2.astype(bf16)
        h2_scr[rows, :] = h2b
        third = h2
        slopes = []
        for b in range(parts):
            cols = slice(width * b, width * (b + 1))
            pre = nn(h2b, weight(ffn, b))
            sig = 1.0 / (1.0 + jnp.exp(-pre))
            act = (pre * sig).astype(bf16)
            act_scr[rows, cols] = act
            slopes.append(sig * (1.0 + pre * (1.0 - sig)))
            third = third + nn(act, outer(b))
        n3, s3 = norm_parts(third)
        out_ref[rows, :] = (n3 * norm_scr[4:5, :] + norm_scr[5:6, :]).astype(bf16)
        cot = cot_ref[rows, :].astype(f32)
        sums[2] += fold_rows(cot * n3)
        sums[3] += fold_rows(cot)
        d3 = norm_back(cot, n3, s3, norm_scr[4:5, :])
        d3b = d3.astype(bf16)
        d3_scr[rows, :] = d3b
        dh2 = d3
        for b in range(parts):
            cols = slice(width * b, width * (b + 1))
            dpre = (nt(d3b, outer(b)) * slopes[b]).astype(bf16)
            dpre_scr[rows, cols] = dpre
            dh2 = dh2 + nt(dpre, weight(ffn, b))
        sums[0] += fold_rows(dh2 * n2)
        sums[1] += fold_rows(dh2)
        d2_ref[rows, :] = norm_back(dh2, n2, s2_ref[rows, :], norm_scr[2:3, :])

    each_chunk(chunks, body)
    for i in range(4):
        gnorm_ref[i : i + 1, :] = jnp.sum(sums[i], axis=0, keepdims=True)
    for b in range(parts):
        cols = slice(width * b, width * (b + 1))
        gffn_ref[share * b : share * (b + 1), 16 * parts :, :] = (
            tn(act_scr[:, cols], d3_scr[...]).astype(bf16).reshape(share, width // share, width)
        )
        put_gradient(gffn_ref, b, tn(h2_scr[...], dpre_scr[:, cols]))


def cross_back_kernel(
    spans, bounds, d2_ref, memory, cq_ref, ck_ref, cv_ref, cmix_ref, clse_ref, n1_ref, s1_ref, norm_ref, attn,
    d1_ref, mgrad_ref, gattn_ref, gnorm_ref,
    query_z, grad_z, key_t, grad_scr, dq_scr, dk_scr, dv_scr, acc_scr, h1_scr, sums, norm_scr,
):
    chunks = d2_ref.shape[0] // RC
    sums[...] = jnp.zeros_like(sums)
    for i, vector in enumerate(load_norms(norm_ref)):
        norm_scr[i : i + 1, :] = vector

    def enter(c):
        rows = rows_of(c, RC)
        d2b = d2_ref[rows, :].astype(bf16)
        h1_scr[rows, :] = d2b
        grad_scr[rows, :] = nt(d2b, weight(attn, 3)).astype(bf16)

    each_chunk(chunks, enter)
    put_gradient(gattn_ref, 3, tn(cmix_ref[...], h1_scr[...]))
    spread_heads(query_z, cq_ref)
    spread_heads(grad_z, grad_scr)
    key_t[...] = ck_ref[...].T
    dk_scr[...] = jnp.zeros_like(dk_scr)
    dv_scr[...] = jnp.zeros_like(dv_scr)
    attention_back(
        spans, 1, bounds, ck_ref, key_t, cv_ref, query_z, grad_z, grad_scr, cmix_ref, clse_ref,
        dq_scr, dk_scr, dv_scr, acc_scr,
    )

    def leave(c):
        rows = rows_of(c, RC)
        mgrad_ref[rows, :] = (
            nt(dk_scr[rows, :].astype(bf16), weight(attn, 1)) + nt(dv_scr[rows, :].astype(bf16), weight(attn, 2))
        ).astype(bf16)
        n1 = n1_ref[rows, :]
        h1_scr[rows, :] = (n1 * norm_scr[0:1, :] + norm_scr[1:2, :]).astype(bf16)
        dh1 = d2_ref[rows, :] + nt(dq_scr[rows, :], weight(attn, 0))
        sums[0] += fold_rows(dh1 * n1)
        sums[1] += fold_rows(dh1)
        d1_ref[rows, :] = norm_back(dh1, n1, s1_ref[rows, :], norm_scr[0:1, :])

    each_chunk(chunks, leave)
    for i in range(2):
        gnorm_ref[i : i + 1, :] = jnp.sum(sums[i], axis=0, keepdims=True)
    put_gradient(gattn_ref, 0, tn(h1_scr[...], dq_scr[...]))
    put_gradient(gattn_ref, 1, tn(memory[...], dk_scr[...].astype(bf16)))
    put_gradient(gattn_ref, 2, tn(memory[...], dv_scr[...].astype(bf16)))


def self_back_kernel(
    spans, bounds, d1_ref, tgt, q_ref, k_ref, v_ref, mix_ref, lse_ref, attn,
    tgrad_ref, gattn_ref,
    query_z, grad_z, key_t, grad_scr, dq_scr, dk_scr, dv_scr, acc_scr, d1_scr,
):
    chunks = d1_ref.shape[0] // RC

    def enter(c):
        rows = rows_of(c, RC)
        d1b = d1_ref[rows, :].astype(bf16)
        d1_scr[rows, :] = d1b
        grad_scr[rows, :] = nt(d1b, weight(attn, 3)).astype(bf16)

    each_chunk(chunks, enter)
    put_gradient(gattn_ref, 3, tn(mix_ref[...], d1_scr[...]))
    spread_heads(query_z, q_ref)
    spread_heads(grad_z, grad_scr)
    key_t[...] = k_ref[...].T
    dk_scr[...] = jnp.zeros_like(dk_scr)
    dv_scr[...] = jnp.zeros_like(dv_scr)
    attention_back(
        spans, 0, bounds, k_ref, key_t, v_ref, query_z, grad_z, grad_scr, mix_ref, lse_ref,
        dq_scr, dk_scr, dv_scr, acc_scr,
    )

    def leave(c):
        rows = rows_of(c, RC)
        tgrad_ref[rows, :] = (
            d1_ref[rows, :]
            + nt(dq_scr[rows, :], weight(attn, 0))
            + nt(dk_scr[rows, :].astype(bf16), weight(attn, 1))
            + nt(dv_scr[rows, :].astype(bf16), weight(attn, 2))
        ).astype(bf16)

    each_chunk(chunks, leave)
    put_gradient(gattn_ref, 0, tn(tgt[...], dq_scr[...]))
    put_gradient(gattn_ref, 1, tn(tgt[...], dk_scr[...].astype(bf16)))
    put_gradient(gattn_ref, 2, tn(tgt[...], dv_scr[...].astype(bf16)))


def shape(dims, dtype):
    return jax.ShapeDtypeStruct(dims, dtype)


def call(kernel, outs, scratch, scalars, args, weights=None):
    smem = pl.BlockSpec(memory_space=pltpu.SMEM)
    vmem = pl.BlockSpec(memory_space=pltpu.VMEM)
    specs = [smem] * scalars + [vmem] * (len(args) - scalars)
    scratch = [pltpu.VMEM(dims, dtype) for dims, dtype in scratch]
    body = kernel
    if weights is not None:
        count, index = weights
        full = args[-1]
        specs[-1] = pl.BlockSpec(memory_space=pl.ANY)
        scratch = [pltpu.VMEM((full.shape[0], count, full.shape[2]), bf16), pltpu.SemaphoreType.DMA] + scratch
        given, made = len(args), len(outs)

        def body(*refs):
            source, held, sem = refs[given - 1], refs[given + made], refs[given + made + 1]
            copy = pltpu.make_async_copy(source.at[:, pl.ds(count * index, count)], held, sem)
            copy.start()
            copy.wait()
            kernel(*refs[: given - 1], held, *refs[given : given + made], *refs[given + made + 2 :])

    return pl.pallas_call(
        body,
        out_shape=outs,
        in_specs=specs,
        out_specs=tuple(vmem for _ in outs),
        scratch_shapes=scratch,
        compiler_params=pltpu.CompilerParams(vmem_limit_bytes=56 * MIB),
    )(*args)


def segment_bounds(lengths, src_segments, length):
    sentences = lengths.shape[0]
    ends = jnp.cumsum(lengths)
    starts = ends - lengths
    sizes = jnp.sum(
        (src_segments[None, :] == jnp.arange(sentences, dtype=jnp.int32)[:, None]).astype(jnp.int32), axis=1
    )
    places = jnp.arange(length, dtype=jnp.int32)
    ended = ends[:, None] <= places[None, :]
    begun = starts[:, None] <= places[None, :]
    self_low = jnp.sum(jnp.where(ended, lengths[:, None], 0), axis=0)
    cross_low = jnp.sum(jnp.where(ended, sizes[:, None], 0), axis=0)
    cross_high = jnp.sum(jnp.where(begun, sizes[:, None], 0), axis=0)
    bounds = jnp.stack([self_low, places + 1, cross_low, cross_high]).astype(jnp.int32)
    firsts = bounds[0::2, 0::QB] // LANES
    lasts = (bounds[1::2, QB - 1 :: QB] + LANES - 1) // LANES
    counts = ((lasts - firsts) * LANES + KB - 1) // KB
    spans = jnp.stack([firsts[0], counts[0], firsts[1], counts[1]]).astype(jnp.int32)
    return bounds, spans


def layer(tgt, memory, cotangent, lengths, src_segments, full, norm):
    length, width = tgt.shape
    keys = memory.shape[0]
    blocks = full.shape[0]
    hidden = (full.shape[1] - 8 * 16) * blocks // 2
    hidden = hidden * full.shape[2] // width
    pairs = width // LANES
    bounds, spans = segment_bounds(lengths, src_segments, length)
    row = (length, width)
    mem_row = (keys, width)
    lse = (length // QB, pairs, 2 * QB)
    most = max(length, keys)
    zeroed = ((pairs, 2 * length, LANES), bf16)
    norms = ((8, width), f32)
    (q, k, v, mix, row_lse, cq, ck, cv, cmix, cross_lse, n1, s1, n2, s2) = call(
        forward_kernel,
        (
            shape(row, bf16), shape(row, bf16), shape(row, bf16), shape(row, bf16), shape(lse, f32),
            shape(row, bf16), shape(mem_row, bf16), shape(mem_row, bf16), shape(row, bf16), shape(lse, f32),
            shape(row, f32), shape((length, 1), f32), shape(row, f32), shape((length, 1), f32),
        ),
        [
            zeroed,
            ((width, most), bf16),
            ((pairs, most + KB, 2 * QB), f32),
            ((pairs, LANES, QB), f32),
            (row, f32),
            norms,
        ],
        1,
        (spans, bounds, tgt, memory, norm, full),
        (128, 0),
    )
    layer_out, d2, grad_ffn, norm_late = call(
        ffn_kernel,
        (shape(row, bf16), shape(row, f32), shape((blocks, 128, width), bf16), shape((4, width), f32)),
        [(row, bf16), ((length, hidden), bf16), (row, bf16), ((length, hidden), bf16), ((4, 8, width), f32), norms],
        0,
        (n2, s2, cotangent, norm, full),
        (128, 1),
    )
    back_scratch = [
        zeroed, zeroed, ((width, most), bf16), (row, bf16), (row, bf16), (mem_row, f32), (mem_row, f32),
        ((pairs, LANES, QB), f32), (row, bf16),
    ]
    d1, mem_grad, grad_cross, norm_early = call(
        cross_back_kernel,
        (shape(row, f32), shape(mem_row, bf16), shape((blocks, 64, width), bf16), shape((2, width), f32)),
        back_scratch + [((2, 8, width), f32), norms],
        1,
        (spans, bounds, d2, memory, cq, ck, cv, cmix, cross_lse, n1, s1, norm, full),
        (64, 1),
    )
    tgt_grad, grad_self = call(
        self_back_kernel,
        (shape(row, bf16), shape((blocks, 64, width), bf16)),
        back_scratch,
        1,
        (spans, bounds, d1, tgt, q, k, v, mix, row_lse, full),
        (64, 0),
    )
    return layer_out, tgt_grad, mem_grad, grad_ffn, grad_cross, grad_self, norm_early, norm_late


def adam_direction(master, gradient, moments):
    first_moment = beta_first * moments[0] + (1.0 - beta_first) * gradient
    second_moment = beta_second * moments[1] + (1.0 - beta_second) * gradient * gradient
    first_fix = 1.0 - beta_first**STEP
    second_fix = 1.0 - beta_second**STEP
    direction = (
        first_moment / first_fix / (jnp.sqrt(second_moment / second_fix) + adam_eps)
        + decay_rate * master
    )
    return (direction, first_moment, second_moment)


def tensor_squares(attn_part, inner_part, outer_part, norm_part):
    return jnp.concatenate(
        [
            jnp.sum(attn_part * attn_part, axis=(1, 2)),
            jnp.sum(inner_part * inner_part)[None],
            jnp.sum(outer_part * outer_part)[None],
            jnp.sum(norm_part * norm_part, axis=1),
        ]
    )


MESH = pl.DeviceIdType.MESH


class Place:
    def __init__(self):
        self.gx = lax.axis_index("gx")
        self.gy = lax.axis_index("gy")
        self.x = lax.rem(self.gx, 2)
        self.y = self.gx // 2
        self.z = self.gy // 2
        self.c = lax.rem(self.gy, 2)
        self.here = self.gx * 8 + self.gy

    def target(self, x, y, z, c):
        return (y * 2 + x, z * 2 + c)

    def index(self, x, y, z, c):
        return (y * 2 + x) * 8 + z * 2 + c

    def others(self):
        found = []
        for step in range(1, 32):
            device = lax.rem(self.here + step, 32)
            found.append((device // 8, lax.rem(device, 8)))
        return found


def greet(targets):
    barrier = pltpu.get_barrier_semaphore()
    for target in targets:
        pl.semaphore_signal(barrier, inc=1, device_id=target, device_id_type=MESH)
    pl.semaphore_wait(barrier, len(targets))


def remote(src, dst, send_sem, recv_sem, target):
    return pltpu.make_async_remote_copy(
        src_ref=src, dst_ref=dst, send_sem=send_sem, recv_sem=recv_sem, device_id=target, device_id_type=MESH
    )


def gather_kernel(
    attn_ref, inner_ref, outer_ref, norm_ref, full_ref, norms_ref,
    mine, zsend, xsend, ysend, csend, recv, nsend, nrecv, lsem,
):
    me = Place()
    x, y, z, c = me.x, me.y, me.z, me.c
    ox, oy, oc = 1 - x, 1 - y, 1 - c
    here = me.here
    for j in range(8):
        mine[16 * j : 16 * j + 16, :] = attn_ref[j].astype(bf16)
    for b in range(4):
        mine[128 + 16 * b : 144 + 16 * b, :] = inner_ref[:, 512 * b : 512 * b + 512].astype(bf16)
    mine[192:256, :] = outer_ref[...].astype(bf16)
    others = me.others()
    greet(others)
    x_next = me.target(ox, y, z, c)
    y_next = me.target(x, oy, z, c)
    sibling = me.target(x, y, z, oc)
    up = me.target(x, y, lax.rem(z + 1, 4), c)
    down = me.target(x, y, lax.rem(z + 3, 4), c)

    def copy(chunk, half, target, sem, own=False):
        rows = pl.ds(128 * half, 128)
        src = mine.at[rows] if own else full_ref.at[chunk, rows]
        return remote(src, full_ref.at[chunk, rows], sem, recv.at[chunk, half], target)

    def arrive(chunk, half):
        copy(chunk, half, sibling, csend.at[chunk, half]).wait_recv()

    def to_x(chunk, half, own=False):
        copy(chunk, half, x_next, xsend.at[chunk, half], own).start()

    def to_y(chunk, half, own=False):
        copy(chunk, half, y_next, ysend.at[chunk, half], own).start()

    def to_core(chunk, half, own=False):
        copy(chunk, half, sibling, csend.at[chunk, half], own).start()

    def along(zz, upward, own=False):
        for half in range(2):
            target = up if upward else down
            copy(me.index(x, y, zz, c), half, target, zsend.at[zz, half, 0 if upward else 1], own).start()

    @pl.when(z < 3)
    def _():
        along(z, True, True)

    @pl.when(z > 0)
    def _():
        along(z, False, True)

    for half in range(2):
        to_x(here, half, True)
        to_y(here, half, True)
    for half in range(2):
        to_core(here, half, True)
    keep = pltpu.make_async_copy(mine, full_ref.at[here], lsem.at[0])
    keep.start()
    norm_keep = pltpu.make_async_copy(norm_ref, norms_ref.at[here], lsem.at[1])
    norm_keep.start()
    norm_sends = []
    for i, target in enumerate(others):
        norm_sends.append(remote(norm_ref, norms_ref.at[here], nsend.at[i], nrecv.at[here], target))
        norm_sends[-1].start()

    def inline(zz, upward):
        chunk = me.index(x, y, zz, c)
        for half in range(2):
            arrive(chunk, half)

            @pl.when((z < 3) if upward else (z > 0))
            def _():
                copy(chunk, half, up if upward else down, zsend.at[zz, half, 0 if upward else 1]).start()

            to_x(chunk, half)
            to_y(chunk, half)
            to_core(chunk, half)

    def side(zz, _):
        first = me.index(ox, y, zz, c)
        arrive(first, 0)
        to_y(first, 0)
        to_core(first, 0)
        second = me.index(x, oy, zz, c)
        arrive(second, 1)
        to_x(second, 1)
        to_core(second, 1)

    def far(zz, _):
        for chunk, half in (
            (me.index(x, oy, zz, c), 0), (me.index(ox, y, zz, c), 1),
            (me.index(ox, oy, zz, c), 0), (me.index(ox, oy, zz, c), 1),
        ):
            arrive(chunk, half)
            to_core(chunk, half)

    def core(zz, _):
        for ax, ay in ((x, y), (ox, y), (x, oy), (ox, oy)):
            for half in range(2):
                arrive(me.index(ax, ay, zz, oc), half)

    def at_distance(d, action):
        if d == 0:
            action(z, None)
            return

        @pl.when(z >= d)
        def _():
            action(z - d, True)

        @pl.when(z + d <= 3)
        def _():
            action(z + d, False)

    for d, action in (
        (1, inline), (0, side), (2, inline), (1, side), (0, far), (3, inline), (2, side), (1, far), (3, side),
        (2, far), (3, far), (0, core), (1, core), (2, core), (3, core),
    ):
        at_distance(d, action)
    for i, target in enumerate(others):
        source = target[0] * 8 + target[1]
        remote(norm_ref, norms_ref.at[source], nsend.at[i], nrecv.at[source], target).wait_recv()
    for sent in norm_sends:
        sent.wait_send()
    for zz in range(4):
        for half in range(2):
            chunk = me.index(x, y, zz, c)

            @pl.when((z < 3) & (zz <= z))
            def _():
                copy(chunk, half, up, zsend.at[zz, half, 0]).wait_send()

            @pl.when((z > 0) & (zz >= z))
            def _():
                copy(chunk, half, down, zsend.at[zz, half, 1]).wait_send()

            copy(chunk, half, x_next, xsend.at[chunk, half]).wait_send()
            copy(chunk, half, y_next, ysend.at[chunk, half]).wait_send()
            for ax, ay in ((x, y), (ox, y), (x, oy), (ox, oy)):
                other = me.index(ax, ay, zz, c)
                copy(other, half, sibling, csend.at[other, half]).wait_send()
        first = me.index(ox, y, zz, c)
        copy(first, 0, y_next, ysend.at[first, 0]).wait_send()
        second = me.index(x, oy, zz, c)
        copy(second, 1, x_next, xsend.at[second, 1]).wait_send()
    keep.wait()
    norm_keep.wait()


def gather_pieces(attn_w, ffn_in, ffn_out, norm_lanes):
    vmem = pl.BlockSpec(memory_space=pltpu.VMEM)
    anywhere = pl.BlockSpec(memory_space=pl.ANY)
    dma = pltpu.SemaphoreType.DMA
    return pl.pallas_call(
        gather_kernel,
        out_shape=(shape((32, 256, 512), bf16), shape((32, 16, 128), bf16)),
        in_specs=[vmem] * 4,
        out_specs=(anywhere, anywhere),
        scratch_shapes=[
            pltpu.VMEM((256, 512), bf16), dma((4, 2, 2)), dma((32, 2)), dma((32, 2)), dma((32, 2)), dma((32, 2)),
            dma((31,)), dma((32,)), dma((2,)),
        ],
        compiler_params=pltpu.CompilerParams(collective_id=0, has_side_effects=True, vmem_limit_bytes=16 * MIB),
    )(attn_w, ffn_in, ffn_out, norm_lanes)


def attn_rows(j):
    return 192 + 16 * j if j < 4 else 64 + 16 * (j - 4)


def add_rows(dst, *sources):
    total = sources[0][...].astype(f32)
    for source in sources[1:]:
        total = total + source[...].astype(f32)
    dst[...] = total.astype(dst.dtype)


def reduce_kernel(
    gffn, gcross, gself, early, late, attn, inner, outer, norm, attn_m, in_m, out_m, norm_m,
    g_ref, gn_ref, totals_ref,
    own_ffn, own_cross, own_self, got_ffn, got_cross, got_self, pieces, first_a, first_b, second_a, second_b,
    third, vectors, tiles,
    lsem, csend, crecv, send1, recv1, send2, recv2, send3, recv3, nsend, nrecv, tsend, trecv,
):
    me = Place()
    x, y, z, c = me.x, me.y, me.z, me.c
    ox, oy, oc = 1 - x, 1 - y, 1 - c
    order = (2, 1, 3, 0)
    zs = [lax.rem(z + d, 4) for d in range(4)]
    x_next = me.target(ox, y, z, c)
    y_next = me.target(x, oy, z, c)
    sibling = me.target(x, y, z, oc)
    others = me.others()
    parts = ((gffn, own_ffn, got_ffn), (gcross, own_cross, got_cross), (gself, own_self, got_self))
    own = {}
    for d in order:
        for k, (source, kept, _) in enumerate(parts):
            own[d, k] = pltpu.make_async_copy(source.at[:, zs[d], c], kept.at[d], lsem.at[d, k])
            own[d, k].start()
    vectors[0, 0:2, :] = early[...]
    vectors[0, 2:6, :] = late[...]
    vectors[0, 6:8, :] = jnp.zeros((2, vectors.shape[2]), f32)
    greet(others)
    pending = []

    def send(*args):
        copy = remote(*args)
        copy.start()
        pending.append(copy)
        return copy

    norm_copy = send(vectors.at[0], vectors.at[1], nsend.at[0], nrecv.at[0], sibling)
    cores = {}
    for d in order:
        for k, (source, _, got) in enumerate(parts):
            cores[d, k] = send(source.at[:, zs[d], oc], got.at[d], csend.at[d, k], crecv.at[d, k], sibling)
    firsts, seconds, thirds = {}, {}, {}
    top, bottom = pl.ds(0, 128), pl.ds(128, 128)

    def stage1(d):
        for k in range(3):
            own[d, k].wait()
            cores[d, k].wait_recv()

        def add(i):
            piece = pieces.at[d, i // 2, lax.rem(i, 2)]
            low, high = pl.ds(0, 64), pl.ds(64, 64)
            add_rows(piece.at[pl.ds(0, 64)], own_ffn.at[d, i, low], got_ffn.at[d, i, low])
            add_rows(piece.at[pl.ds(64, 64)], own_cross.at[d, i], got_cross.at[d, i])
            add_rows(piece.at[pl.ds(128, 64)], own_ffn.at[d, i, high], got_ffn.at[d, i, high])
            add_rows(piece.at[pl.ds(192, 64)], own_self.at[d, i], got_self.at[d, i])

        each_chunk(4, add)
        firsts[d] = (
            send(pieces.at[d, oy, :, top], first_a.at[d], send1.at[d, 0], recv1.at[d, 0], y_next),
            send(pieces.at[d, :, ox, bottom], first_b.at[d], send1.at[d, 1], recv1.at[d, 1], x_next),
        )

    def stage2(d):
        firsts[d][0].wait_recv()
        part = pieces.at[d, y, ox, top]
        add_rows(part, part, first_a.at[d, ox])
        one = send(part, second_a.at[d], send2.at[d, 0], recv2.at[d, 0], x_next)
        firsts[d][1].wait_recv()
        part = pieces.at[d, oy, x, bottom]
        add_rows(part, part, first_b.at[d, oy])
        two = send(part, second_b.at[d], send2.at[d, 1], recv2.at[d, 1], y_next)
        seconds[d] = (one, two)

    def stage3(d):
        for copy in seconds[d]:
            copy.wait_recv()
        upper, lower = pieces.at[d, y, x, top], pieces.at[d, y, x, bottom]
        add_rows(upper if d else g_ref.at[top], upper, first_a.at[d, x], second_a.at[d])
        add_rows(lower if d else g_ref.at[bottom], lower, first_b.at[d, y], second_b.at[d])
        if d:
            thirds[d] = send(
                pieces.at[d, y, x], third.at[d - 1], send3.at[d - 1], recv3.at[d - 1], me.target(x, y, zs[d], c)
            )

    stage1(order[0])
    stage1(order[1])
    norm_copy.wait_recv()
    vectors[2] = vectors[0] + vectors[1]
    norm_copy = send(vectors.at[2], vectors.at[3], nsend.at[1], nrecv.at[1], x_next)
    stage2(order[0])
    stage1(order[2])
    norm_copy.wait_recv()
    vectors[4] = vectors[2] + vectors[3]
    norm_copy = send(vectors.at[4], vectors.at[5], nsend.at[2], nrecv.at[2], y_next)
    stage3(order[0])
    stage2(order[1])
    stage1(order[3])
    norm_copy.wait_recv()
    vectors[6] = vectors[4] + vectors[5]
    norm_copies = [
        send(vectors.at[6], vectors.at[6 + d], nsend.at[2 + d], nrecv.at[2 + d], me.target(x, y, zs[d], c))
        for d in range(1, 4)
    ]
    stage3(order[1])
    stage2(order[2])
    stage3(order[2])
    stage2(order[3])
    stage3(order[3])
    for copy in norm_copies:
        copy.wait_recv()
    vectors[10] = (vectors[6] + vectors[8]) + (vectors[7] + vectors[9])
    for d in (1, 2, 3):
        thirds[d].wait_recv()
    g_ref[...] = g_ref[...] + third[0].astype(f32) + third[1].astype(f32) + third[2].astype(f32)
    lanes = vectors[10, :, pl.ds(pl.multiple_of(me.gx * 128, 128), 128)]
    gn_ref[...] = pltpu.roll(lanes, lax.rem(128 - me.gy * 16, 128), 1)
    lane = lax.broadcasted_iota(jnp.int32, (1, 128), 1)
    rows = [jnp.zeros((1, 128), f32), jnp.zeros((1, 128), f32)]

    def put(t, pairs):
        for i in range(2):
            square = sum(jnp.sum(pair[i] * pair[i]) for pair in pairs)
            rows[i] = rows[i] + jnp.where(lane == t, square, 0.0)

    def direction(*args):
        return adam_direction(*args)[0]

    for j in range(8):
        grad = g_ref[attn_rows(j) : attn_rows(j) + 16, :]
        put(j, [(attn[j], direction(attn[j], grad, (attn_m[0, j], attn_m[1, j])))])
    pairs = []
    for b in range(4):
        cols = slice(512 * b, 512 * b + 512)
        grad = g_ref[16 * b : 16 * b + 16, :]
        pairs.append((inner[:, cols], direction(inner[:, cols], grad, (in_m[0, :, cols], in_m[1, :, cols]))))
    put(8, pairs)
    put(9, [(outer[...], direction(outer[...], g_ref[128:192, :], (out_m[0], out_m[1])))])
    master = norm[...]
    update = direction(master, gn_ref[0:6, 0:16], (norm_m[0], norm_m[1]))
    for i in range(6):
        put(10 + i, [(master[i : i + 1], update[i : i + 1])])
    tiles[me.here] = jnp.concatenate([rows[0], rows[1], jnp.zeros((6, 128), f32)], axis=0)
    for i, target in enumerate(others):
        send(tiles.at[me.here], tiles.at[me.here], tsend.at[i], trecv.at[me.here], target)
    for i, target in enumerate(others):
        source = target[0] * 8 + target[1]
        remote(tiles.at[source], tiles.at[source], tsend.at[i], trecv.at[source], target).wait_recv()
    for copy in pending:
        copy.wait_send()
    totals_ref[...] = jnp.sum(tiles[...], axis=0)


def reduce_pieces(grads, norm_grads, params, moments):
    vmem = pl.BlockSpec(memory_space=pltpu.VMEM)
    anywhere = pl.BlockSpec(memory_space=pl.ANY)
    dma = pltpu.SemaphoreType.DMA
    buffers = [
        (4, 4, 128, 512), (4, 4, 64, 512), (4, 4, 64, 512), (4, 4, 128, 512), (4, 4, 64, 512), (4, 4, 64, 512),
        (4, 2, 2, 256, 512), (4, 2, 128, 512), (4, 2, 128, 512), (4, 128, 512), (4, 128, 512), (3, 256, 512),
    ]
    split = [grad.reshape(4, 4, 2, grad.shape[1], 512) for grad in grads]
    return pl.pallas_call(
        reduce_kernel,
        out_shape=(shape((256, 512), f32), shape((8, 128), f32), shape((8, 128), f32)),
        in_specs=[anywhere] * 3 + [vmem] * 10,
        out_specs=(vmem, vmem, vmem),
        scratch_shapes=[pltpu.VMEM(dims, bf16) for dims in buffers]
        + [pltpu.VMEM((11, 8, 512), f32), pltpu.VMEM((32, 8, 128), f32)]
        + [
            dma((4, 3)), dma((4, 3)), dma((4, 3)), dma((4, 2)), dma((4, 2)), dma((4, 2)), dma((4, 2)), dma((3,)),
            dma((3,)), dma((6,)), dma((6,)), dma((31,)), dma((32,)),
        ],
        compiler_params=pltpu.CompilerParams(collective_id=1, has_side_effects=True, vmem_limit_bytes=40 * MIB),
    )(*split, *norm_grads, *params, *moments)


def update_kernel(
    g_ref, gn_ref, totals_ref, attn, inner, outer, norm, attn_m, in_m, out_m, norm_m,
    attn_new, in_new, out_new, norm_new, attn_first, attn_second, in_first, in_second, out_first, out_second,
    norm_first, norm_second, attn_copy, in_copy, out_copy, norm_copy, norms_ref,
):
    roots = jnp.sqrt(totals_ref[...])
    norms_ref[...] = roots[0:2, 0:16]
    ratio = learn_rate * (roots[0:1, :] / roots[1:2, :])

    def step(t, master, gradient, moments, new, first, second, copy, place):
        direction, first_moment, second_moment = adam_direction(master, gradient, moments)
        value = master - ratio[:, t : t + 1] * direction
        new[place] = value
        first[place] = first_moment
        second[place] = second_moment
        copy[place] = value.astype(bf16)

    for j in range(8):
        grad = g_ref[attn_rows(j) : attn_rows(j) + 16, :]
        step(j, attn[j], grad, (attn_m[0, j], attn_m[1, j]), attn_new, attn_first, attn_second, attn_copy, j)
    for b in range(4):
        cols = slice(512 * b, 512 * b + 512)
        place = (slice(None), cols)
        grad = g_ref[16 * b : 16 * b + 16, :]
        step(8, inner[:, cols], grad, (in_m[0, :, cols], in_m[1, :, cols]), in_new, in_first, in_second, in_copy, place)
    step(9, outer[...], g_ref[128:192, :], (out_m[0], out_m[1]), out_new, out_first, out_second, out_copy, ...)
    for i in range(6):
        one = slice(i, i + 1)
        moments = (norm_m[0, one], norm_m[1, one])
        step(10 + i, norm[one], gn_ref[one, 0:16], moments, norm_new, norm_first, norm_second, norm_copy, one)


def update_params(summed, params, moments):
    outs = [shape(p.shape, f32) for p in params]
    outs += [shape(p.shape, f32) for p in params for _ in range(2)]
    outs += [shape(p.shape, bf16) for p in params] + [shape((2, 16), f32)]
    return call(update_kernel, tuple(outs), [], 0, (*summed, *params, *moments))


def blocked(matrix, width):
    blocks = matrix.shape[0] // 16
    cols = matrix.shape[1] // width
    return matrix.reshape(blocks, 16, cols, width).transpose(0, 2, 1, 3).reshape(blocks, cols * 16, width)


def unblocked(blocks, width):
    count = blocks.shape[0]
    cols = blocks.shape[1] // 16
    return blocks.reshape(count, cols, 16, width).transpose(0, 2, 1, 3).reshape(count * 16, cols * width)


def gather_any(attn_w, ffn_in, ffn_out, norm_params):
    width = attn_w.shape[2]
    attn = lax.all_gather(attn_w.astype(bf16), AXES, axis=1, tiled=True)
    inner = lax.all_gather(ffn_in.astype(bf16), AXES, axis=0, tiled=True)
    outer = lax.all_gather(ffn_out.astype(bf16), AXES, axis=0, tiled=True)
    norm = lax.all_gather(norm_params.astype(bf16), AXES, axis=1, tiled=True)
    blocks = width // 16
    attn = attn.reshape(8, blocks, 16, width).transpose(1, 0, 2, 3).reshape(blocks, 8 * 16, width)
    full = jnp.concatenate([attn, blocked(inner, width), outer.reshape(blocks, -1, width)], axis=1)
    lanes = jnp.pad(norm, ((0, 10), (0, 0))).reshape(16, 4, width // 4).transpose(1, 0, 2)
    return full, lanes


def reduce_any(grads, norm_grads, params, moments):
    grad_ffn, grad_cross, grad_self = grads
    width = grad_ffn.shape[2]
    blocks = width // 16
    attn_w, ffn_in, ffn_out, norm_params = params
    attn_m, in_m, out_m, norm_m = moments
    stack = jnp.concatenate([grad_self, grad_cross], axis=1)
    stack = stack.reshape(blocks, 8, 16, width).transpose(1, 0, 2, 3).reshape(8, width, width)
    rows = ffn_in.shape[1] // width * 16
    inner = unblocked(grad_ffn[:, :rows], width)
    outer = grad_ffn[:, rows:].reshape(-1, width)
    shard_attn = lax.psum_scatter(stack, AXES, scatter_dimension=1, tiled=True).astype(f32)
    shard_inner = lax.psum_scatter(inner, AXES, scatter_dimension=0, tiled=True).astype(f32)
    shard_outer = lax.psum_scatter(outer, AXES, scatter_dimension=0, tiled=True).astype(f32)
    shard_norm = lax.psum_scatter(jnp.concatenate(norm_grads), AXES, scatter_dimension=1, tiled=True)
    attn_dir, attn_first, attn_second = adam_direction(attn_w, shard_attn, attn_m)
    inner_dir, inner_first, inner_second = adam_direction(ffn_in, shard_inner, in_m)
    outer_dir, outer_first, outer_second = adam_direction(ffn_out, shard_outer, out_m)
    norm_dir, norm_first, norm_second = adam_direction(norm_params, shard_norm, norm_m)
    weight_total, update_total = lax.psum(
        (tensor_squares(*params), tensor_squares(attn_dir, inner_dir, outer_dir, norm_dir)), AXES
    )
    ratio = jnp.sqrt(weight_total) / jnp.sqrt(update_total)
    attn_new = attn_w - learn_rate * ratio[0:8][:, None, None] * attn_dir
    in_new = ffn_in - learn_rate * ratio[8] * inner_dir
    out_new = ffn_out - learn_rate * ratio[9] * outer_dir
    norm_new = norm_params - learn_rate * ratio[10:16][:, None] * norm_dir
    norms = jnp.stack([jnp.sqrt(weight_total), jnp.sqrt(update_total)])
    return (
        attn_new, in_new, out_new, norm_new,
        attn_first, attn_second, inner_first, inner_second, outer_first, outer_second, norm_first, norm_second,
        attn_new.astype(bf16), in_new.astype(bf16), out_new.astype(bf16), norm_new.astype(bf16), norms,
    )


def on_device(
    close, tgt, memory, cotangent, tgt_lengths, src_segments, attn_w, ffn_in, ffn_out, norm_params,
    attn_moments, in_moments, out_moments, norm_moments,
):
    params = (attn_w, ffn_in, ffn_out, norm_params)
    moments = (attn_moments, in_moments, out_moments, norm_moments)
    if close:
        lanes = lax.dynamic_update_slice(
            jnp.zeros((16, 128), bf16), norm_params.astype(bf16), (0, lax.axis_index("gy") * 16)
        )
        full, norm = gather_pieces(attn_w, ffn_in, ffn_out, lanes)
    else:
        full, norm = gather_any(*params)
    parts = [
        layer(tgt[r], memory[r], cotangent[r], tgt_lengths[r], src_segments[r], full, norm)
        for r in range(tgt.shape[0])
    ]
    outs = [jnp.stack([part[i] for part in parts]) for i in range(3)]
    sums = parts[0][3:]
    if len(parts) > 1:
        sums = [sum(part[i].astype(f32) for part in parts) for i in range(3, 8)]
    grads = [grad.astype(bf16) for grad in sums[:3]]
    if close:
        updated = update_params(reduce_pieces(grads, sums[3:], params, moments), params, moments)
    else:
        updated = reduce_any(grads, sums[3:], params, moments)
    return (*outs, *updated)


def fits(mesh):
    return mesh.shape["gx"] == 4 and mesh.shape["gy"] == 8


def solution(mesh):
    rows = P(AXES, None, None)
    matrix = P(AXES, None)
    stack = P(None, AXES, None)
    vectors = P(None, AXES)
    return jax.shard_map(
        functools.partial(on_device, fits(mesh)),
        mesh=mesh,
        in_specs=(
            rows, rows, rows, matrix, matrix, stack, matrix, matrix, vectors,
            P(None, None, AXES, None), stack, stack, P(None, None, AXES),
        ),
        out_specs=(
            rows, rows, rows, stack, matrix, matrix, vectors, stack, stack, matrix, matrix, matrix, matrix,
            vectors, vectors, stack, matrix, matrix, vectors, P(),
        ),
        check_vma=False,
    )
```

```python
import functools

import jax
import jax.numpy as jnp
from jax import lax
from jax.experimental import pallas as pl
from jax.experimental.pallas import tpu as pltpu
from jax.sharding import PartitionSpec as P

HEAD_DIM = 64
STEP = 5

beta_first = 0.5
beta_second = 0.5
learn_rate = 0.5
decay_rate = 0.01
norm_eps = 1e-05
adam_eps = 1e-06

f32 = jnp.float32
bf16 = jnp.bfloat16
LANES = 128
QB = 128
KB = 256
RC = 256
LONGEST = 512
MASKED = -1e30
AXES = ("gx", "gy")
GRANT = 63 * 2**20


def nn(left, right):
    return lax.dot_general(left, right, (((1,), (0,)), ((), ())), preferred_element_type=f32)


def nt(left, right):
    return lax.dot_general(left, right, (((1,), (1,)), ((), ())), preferred_element_type=f32)


def tn(left, right):
    return lax.dot_general(left, right, (((0,), (0,)), ((), ())), preferred_element_type=f32)


def rows_of(step, size):
    return pl.ds(pl.multiple_of(step * size, size), size)


def each_chunk(count, body):
    def step(index, carry):
        body(index)
        return carry

    lax.fori_loop(0, count, step, 0)


def spread_heads(dst, src):
    pairs = dst.shape[0]
    first = lax.broadcasted_iota(jnp.int32, (QB, LANES), 1) < HEAD_DIM
    zero = jnp.zeros((QB, LANES), bf16)

    def body(i):
        start = pl.multiple_of(i * 2 * QB, 2 * QB)
        for p in range(pairs):
            tile = src[rows_of(i, QB), p * LANES : (p + 1) * LANES]
            dst[p, pl.ds(start, QB), :] = jnp.where(first, tile, zero)
            dst[p, pl.ds(start + QB, QB), :] = jnp.where(first, zero, tile)

    each_chunk(src.shape[0] // QB, body)


def run_blocks(count, body, steps):
    if not steps:
        each_chunk(count, body)
        return
    for i in range(count):
        body(i)
        if i < len(steps):
            steps[i]()


def near_window(i):
    first = max(0, i - LONGEST // LANES) if isinstance(i, int) else jnp.maximum(i - LONGEST // LANES, 0)
    return first, (i + 1 - first + KB // LANES - 1) // (KB // LANES)


def bound_window(bounds, which):
    def window(i):
        first = bounds[2 * which, i * QB] // LANES
        last = (bounds[2 * which + 1, i * QB + QB - 1] + LANES - 1) // LANES
        return first, ((last - first) * LANES + KB - 1) // KB

    return window


def key_block(first_key, j, keys):
    nominal = first_key * LANES + j * KB
    return pl.multiple_of(jnp.minimum(nominal, keys - KB), LANES), nominal


def block_bias(low, high, start, nominal):
    place = start + lax.broadcasted_iota(jnp.int32, (KB, QB), 0)
    bias = jnp.where((place >= jnp.maximum(low, nominal)) & (place < high), 0.0, MASKED).astype(f32)
    return jnp.concatenate([bias, bias], axis=1)


def attention(window, which, bounds, key_ref, value_t, query_z, mixed_ref, lse_ref, score_scr, out_scr, steps=()):
    keys = key_ref.shape[0]
    pairs = query_z.shape[0]
    fold = (KB // 8, 8, 2 * QB)

    def query_block(i):
        rows = rows_of(i, QB)
        pair_rows = rows_of(i, 2 * QB)
        low = bounds[2 * which : 2 * which + 1, rows]
        high = bounds[2 * which + 1 : 2 * which + 2, rows]
        first_key, blocks = window(i)
        out_scr[...] = jnp.zeros_like(out_scr)

        def scores(j, tops):
            start, nominal = key_block(first_key, j, keys)
            bias = block_bias(low, high, start, nominal)
            found = []
            raw = [
                nt(key_ref[pl.ds(start, KB), p * LANES : (p + 1) * LANES], query_z[p, pair_rows, :])
                for p in range(pairs)
            ]
            for p in range(pairs):
                score = raw[p] + bias
                score_scr[p, rows_of(j, KB), :] = score
                found.append(jnp.maximum(tops[p], jnp.max(score.reshape(fold), axis=0)))
            return tuple(found)

        tops = lax.fori_loop(
            0, blocks, scores, tuple(jnp.full((8, 2 * QB), MASKED, f32) for _ in range(pairs))
        )
        top = [jnp.max(t, axis=0, keepdims=True) for t in tops]

        def weigh(j, sums):
            start, _ = key_block(first_key, j, keys)
            found = []
            low_exps = []
            for p in range(pairs):
                exponent = jnp.exp(score_scr[p, rows_of(j, KB), :] - top[p])
                found.append(sums[p] + jnp.sum(exponent.reshape(fold), axis=0))
                low_exps.append(exponent.astype(bf16))
            for p in range(pairs):
                for h in range(2):
                    heads = slice(h * HEAD_DIM, (h + 1) * HEAD_DIM)
                    value = value_t[
                        p * LANES + h * HEAD_DIM : p * LANES + (h + 1) * HEAD_DIM, pl.ds(start, KB)
                    ]
                    out_scr[p, heads, :] += nn(value, low_exps[p][:, h * QB : (h + 1) * QB])
            return tuple(found)

        sums = lax.fori_loop(
            0, blocks, weigh, tuple(jnp.zeros((8, 2 * QB), f32) for _ in range(pairs))
        )
        for p in range(pairs):
            total = jnp.sum(sums[p], axis=0, keepdims=True)
            lse_ref[i, p : p + 1, :] = top[p] + jnp.log(total)
            inverse = 1.0 / total
            out = jnp.concatenate(
                [out_scr[p, 0:HEAD_DIM, :] * inverse[:, :QB], out_scr[p, HEAD_DIM:, :] * inverse[:, QB:]],
                axis=0,
            )
            mixed_ref[rows, p * LANES : (p + 1) * LANES] = out.T.astype(bf16)

    run_blocks(query_z.shape[1] // (2 * QB), query_block, steps)


def attention_back(
    window, which, bounds, key_ref, key_t, value_ref, query_z, grad_z, grad_ref, mixed_ref, lse_ref,
    dquery_ref, dkey_scr, dvalue_scr, dq_scr, steps=(),
):
    keys = key_ref.shape[0]
    pairs = query_z.shape[0]

    def query_block(i):
        rows = rows_of(i, QB)
        pair_rows = rows_of(i, 2 * QB)
        low = bounds[2 * which : 2 * which + 1, rows]
        high = bounds[2 * which + 1 : 2 * which + 2, rows]
        first_key, blocks = window(i)
        dq_scr[...] = jnp.zeros_like(dq_scr)
        deltas = []
        for p in range(pairs):
            lanes = slice(p * LANES, (p + 1) * LANES)
            product = (grad_ref[rows, lanes].astype(f32) * mixed_ref[rows, lanes].astype(f32)).T
            deltas.append(
                jnp.concatenate(
                    [
                        jnp.sum(product[:HEAD_DIM], axis=0, keepdims=True),
                        jnp.sum(product[HEAD_DIM:], axis=0, keepdims=True),
                    ],
                    axis=1,
                )
            )

        def key_step(j):
            start, nominal = key_block(first_key, j, keys)
            bias = block_bias(low, high, start, nominal)
            block = pl.ds(start, KB)
            held = {}

            def first(p):
                lanes = slice(p * LANES, (p + 1) * LANES)
                held["s", p] = nt(key_ref[block, lanes], query_z[p, pair_rows, :])
                held["d", p] = nt(value_ref[block, lanes], grad_z[p, pair_rows, :])

            def second(p):
                prob = jnp.exp(held.pop(("s", p)) + bias - lse_ref[i, p : p + 1, :])
                held["ds", p] = (prob * (held.pop(("d", p)) - deltas[p])).astype(bf16)
                held["p", p] = prob.astype(bf16)

            def third(p):
                lanes = slice(p * LANES, (p + 1) * LANES)
                dscore = held["ds", p]
                dvalue_scr[block, lanes] += nn(held["p", p], grad_z[p, pair_rows, :])
                dkey_scr[block, lanes] += nn(dscore, query_z[p, pair_rows, :])
                for h in range(2):
                    heads = slice(h * HEAD_DIM, (h + 1) * HEAD_DIM)
                    key = key_t[
                        p * LANES + h * HEAD_DIM : p * LANES + (h + 1) * HEAD_DIM, block
                    ]
                    dq_scr[p, heads, :] += nn(key, dscore[:, h * QB : (h + 1) * QB])

            for step in (first, second, third):
                for p in range(pairs):
                    step(p)

        each_chunk(blocks, key_step)
        for p in range(pairs):
            dquery_ref[rows, p * LANES : (p + 1) * LANES] = (
                (dq_scr[p] * HEAD_DIM**-0.5).T.astype(bf16)
            )

    run_blocks(query_z.shape[1] // (2 * QB), query_block, steps)


def norm_parts(values):
    average = jnp.mean(values, axis=-1, keepdims=True)
    centred = values - average
    spread = jnp.mean(centred * centred, axis=-1, keepdims=True)
    inverse = lax.rsqrt(spread + norm_eps)
    return centred * inverse, inverse


def norm_back(gradient, normed, inverse, gain):
    scaled = gradient * gain
    first_mean = jnp.mean(scaled, axis=-1, keepdims=True)
    second_mean = jnp.mean(scaled * normed, axis=-1, keepdims=True)
    return inverse * (scaled - first_mean - normed * second_mean)


def fold_rows(values):
    return jnp.sum(values.reshape(values.shape[0] // 8, 8, values.shape[1]), axis=0)


def load_norms(norm_ref):
    group = norm_ref.shape[0] // 4
    blocks = [jnp.sum(norm_ref[group * i : group * (i + 1)].astype(f32), axis=0) for i in range(4)]
    rows = jnp.concatenate(blocks, axis=1)
    return [rows[i : i + 1, :] for i in range(6)]


def weight(ref, index):
    blocks = ref.shape[0]
    return ref[:, 16 * index : 16 * (index + 1), :].reshape(16 * blocks, ref.shape[2])


def put_gradient(ref, index, value):
    blocks = ref.shape[0]
    ref[:, 16 * index : 16 * (index + 1), :] = value.astype(bf16).reshape(blocks, 16, ref.shape[2])


def load_norm_rows(dst, norm_ref):
    for i, vector in enumerate(load_norms(norm_ref)):
        dst[i : i + 1, :] = vector


def sigmoid(values):
    return 0.5 * jnp.tanh(0.5 * values) + 0.5


class Mover:
    def __init__(self, sems):
        self.sems = sems
        self.count = 0
        self.open = []

    def start(self, src, dst):
        copy = pltpu.make_async_copy(src, dst, self.sems.at[self.count])
        self.count += 1
        copy.start()
        self.open.append(copy)
        return copy

    def wait(self, *copies):
        for copy in copies:
            copy.wait()
            self.open = [other for other in self.open if other is not copy]

    def finish(self):
        self.wait(*list(self.open))


def find_bounds(lengths, src_segments, bounds_ref):
    sentences = lengths.shape[1]
    length = bounds_ref.shape[1]
    row = lax.broadcasted_iota(jnp.int32, (sentences, sentences), 0)
    col = lax.broadcasted_iota(jnp.int32, (sentences, sentences), 1)
    sizes = jnp.broadcast_to(lengths[...].astype(f32), (sentences, sentences))

    def total(mask, values):
        return jnp.sum(jnp.where(mask, values, 0.0), axis=1, keepdims=True)

    own = total(col == row, sizes)
    starts = total(col < row, sizes)
    ends = starts + own
    sources = src_segments.shape[1]
    number = lax.broadcasted_iota(jnp.int32, (sentences, sources), 0)
    count = total(jnp.broadcast_to(src_segments[...], (sentences, sources)) == number, 1.0)
    places = lax.broadcasted_iota(jnp.int32, (sentences, length), 1).astype(f32)

    def gather(edges, values):
        return jnp.sum(jnp.where(edges <= places, values, 0.0), axis=0, keepdims=True).astype(jnp.int32)

    bounds_ref[0:1, :] = gather(ends, own)
    bounds_ref[1:2, :] = lax.broadcasted_iota(jnp.int32, (1, length), 1) + 1
    bounds_ref[2:3, :] = gather(ends, count)
    bounds_ref[3:4, :] = gather(starts, count)
    bounds_ref[4:8, :] = jnp.zeros((4, length), jnp.int32)


def self_forward(tgt, attn, bounds, norm, q, k, v, mix, lse, n1, s1, query_z, value_t, score_scr, out_scr, move, outs, steps):
    chunks = tgt.shape[0] // RC
    scale = jnp.array(HEAD_DIM**-0.5, bf16)

    def project(c):
        rows = rows_of(c, RC)
        x = tgt[rows, :]
        q[rows, :] = nn(x, weight(attn, 0)).astype(bf16) * scale
        k[rows, :] = nn(x, weight(attn, 1)).astype(bf16)
        v[rows, :] = nn(x, weight(attn, 2)).astype(bf16)

    each_chunk(chunks, project)
    for i, ref in enumerate((q, k, v)):
        move.start(ref, outs[i])
    spread_heads(query_z, q)
    value_t[...] = v[...].T
    attention(near_window, 0, bounds, k, value_t, query_z, mix, lse, score_scr, out_scr, steps)
    move.start(mix, outs[3])
    move.start(lse, outs[4])

    def middle(c):
        rows = rows_of(c, RC)
        normed, inverse = norm_parts(tgt[rows, :].astype(f32) + nn(mix[rows, :], weight(attn, 3)))
        n1[rows, :] = normed
        s1[rows, :] = inverse

    each_chunk(chunks, middle)
    move.start(n1, outs[5])
    move.start(s1, outs[6])


def middle_kernel(
    bounds_s, bounds_h, full, norm_h, memory_h, cot_h, n1_h, s1_h,
    out_h, d1_h, mgrad_h, gffn_h, gcross_h, gnorm_ref,
    bounds, norm_b, attn, ffn, memory, cot, n1, s1, cq, ck, cv, cmix, clse, query_z, grad_z, turned, score_scr, small_scr,
    act_scr, dpre_scr, h2_scr, d3_scr, d2_scr, d2b_scr, grad_scr, dq_scr, dk_scr, dv_scr, out_scr, mgrad, gffn, gcross,
    sums, norm, sems,
):
    width = n1.shape[1]
    chunks = n1.shape[0] // RC
    scale = jnp.array(HEAD_DIM**-0.5, bf16)
    move = Mover(sems)
    rows_cross = attn.shape[1]
    load_small = [move.start(norm_h, norm_b), move.start(bounds_h, bounds)]
    load_cross = move.start(full.at[:, pl.ds(rows_cross, rows_cross)], attn)
    load_n1 = move.start(n1_h, n1)
    load_memory = move.start(memory_h, memory)
    load_ffn = move.start(full.at[:, pl.ds(2 * rows_cross, ffn.shape[1])], ffn)
    load_rest = [move.start(cot_h, cot), move.start(s1_h, s1)]
    sums[...] = jnp.zeros_like(sums)
    move.wait(*load_small)
    load_norm_rows(norm, norm_b)
    move.wait(load_cross, load_n1, load_memory)

    def h1_of(rows):
        return n1[rows, :] * norm[0:1, :] + norm[1:2, :]

    def project(c):
        rows = rows_of(c, RC)
        cq[rows, :] = nn(h1_of(rows).astype(bf16), weight(attn, 0)).astype(bf16) * scale
        mem = memory[rows, :]
        ck[rows, :] = nn(mem, weight(attn, 1)).astype(bf16)
        cv[rows, :] = nn(mem, weight(attn, 2)).astype(bf16)

    each_chunk(chunks, project)
    spread_heads(query_z, cq)
    turned[...] = cv[...].T
    window = bound_window(bounds_s, 1)
    attention(window, 1, bounds, ck, turned, query_z, cmix, clse, score_scr, small_scr)
    move.wait(load_ffn, *load_rest)
    blocks = ffn.shape[0]
    parts = act_scr.shape[1] // width
    share = blocks // parts

    def outer(b):
        return ffn[share * b : share * (b + 1), 16 * parts :, :].reshape(width, width)

    def body(c):
        rows = rows_of(c, RC)
        n2, s2 = norm_parts(h1_of(rows) + nn(cmix[rows, :], weight(attn, 3)))
        h2 = n2 * norm[2:3, :] + norm[3:4, :]
        h2b = h2.astype(bf16)
        h2_scr[rows, :] = h2b
        third = h2
        slopes = []
        for b in range(parts):
            cols = slice(width * b, width * (b + 1))
            pre = nn(h2b, weight(ffn, b))
            sig = sigmoid(pre)
            swish = pre * sig
            act = swish.astype(bf16)
            act_scr[rows, cols] = act
            slopes.append(sig + swish * (1.0 - sig))
            third = third + nn(act, outer(b))
        n3, s3 = norm_parts(third)
        out_scr[rows, :] = (n3 * norm[4:5, :] + norm[5:6, :]).astype(bf16)
        up = cot[rows, :].astype(f32)
        sums[4] += fold_rows(up * n3)
        sums[5] += fold_rows(up)
        d3 = norm_back(up, n3, s3, norm[4:5, :])
        d3b = d3.astype(bf16)
        d3_scr[rows, :] = d3b
        dh2 = d3
        for b in range(parts):
            cols = slice(width * b, width * (b + 1))
            dpre = (nt(d3b, outer(b)) * slopes[b]).astype(bf16)
            dpre_scr[rows, cols] = dpre
            dh2 = dh2 + nt(dpre, weight(ffn, b))
        sums[2] += fold_rows(dh2 * n2)
        sums[3] += fold_rows(dh2)
        d2 = norm_back(dh2, n2, s2, norm[2:3, :])
        d2_scr[rows, :] = d2
        d2b = d2.astype(bf16)
        d2b_scr[rows, :] = d2b
        grad_scr[rows, :] = nt(d2b, weight(attn, 3)).astype(bf16)

    each_chunk(chunks, body)
    move.start(out_scr, out_h)
    for b in range(parts):
        cols = slice(width * b, width * (b + 1))
        gffn[share * b : share * (b + 1), 16 * parts :, :] = (
            tn(act_scr[:, cols], d3_scr[...]).astype(bf16).reshape(share, width // share, width)
        )
        put_gradient(gffn, b, tn(h2_scr[...], dpre_scr[:, cols]))
    move.start(gffn, gffn_h)
    put_gradient(gcross, 3, tn(cmix[...], d2b_scr[...]))
    spread_heads(grad_z, grad_scr)
    turned[...] = ck[...].T
    dk_scr[...] = jnp.zeros_like(dk_scr)
    dv_scr[...] = jnp.zeros_like(dv_scr)
    attention_back(
        window, 1, bounds, ck, turned, cv, query_z, grad_z, grad_scr, cmix, clse, dq_scr, dk_scr, dv_scr, small_scr,
    )

    def leave(c):
        rows = rows_of(c, RC)
        dkb = dk_scr[rows, :].astype(bf16)
        dvb = dv_scr[rows, :].astype(bf16)
        ck[rows, :] = dkb
        cv[rows, :] = dvb
        mgrad[rows, :] = (nt(dkb, weight(attn, 1)) + nt(dvb, weight(attn, 2))).astype(bf16)
        normed = n1[rows, :]
        h2_scr[rows, :] = h1_of(rows).astype(bf16)
        dh1 = d2_scr[rows, :] + nt(dq_scr[rows, :], weight(attn, 0))
        sums[0] += fold_rows(dh1 * normed)
        sums[1] += fold_rows(dh1)
        d2_scr[rows, :] = norm_back(dh1, normed, s1[rows, :], norm[0:1, :])

    each_chunk(chunks, leave)
    move.start(d2_scr, d1_h)
    move.start(mgrad, mgrad_h)
    for i in range(6):
        gnorm_ref[i : i + 1, :] = jnp.sum(sums[i], axis=0, keepdims=True)
    gnorm_ref[6:8, :] = jnp.zeros((2, width), f32)
    put_gradient(gcross, 0, tn(h2_scr[...], dq_scr[...]))
    put_gradient(gcross, 1, tn(memory[...], ck[...]))
    put_gradient(gcross, 2, tn(memory[...], cv[...]))
    move.start(gcross, gcross_h)
    move.finish()


def self_backward(
    tgt, attn, bounds, q, k, v, mix, lse, d1, tgrad, gself,
    query_z, grad_z, key_t, grad_scr, dq_scr, dk_scr, dv_scr, small_scr, d1_scr, steps, late,
):
    chunks = tgt.shape[0] // RC

    def enter(c):
        rows = rows_of(c, RC)
        d1b = d1[rows, :].astype(bf16)
        d1_scr[rows, :] = d1b
        grad_scr[rows, :] = nt(d1b, weight(attn, 3)).astype(bf16)

    each_chunk(chunks, enter)
    put_gradient(gself, 3, tn(mix[...], d1_scr[...]))
    spread_heads(query_z, q)
    spread_heads(grad_z, grad_scr)
    key_t[...] = k[...].T
    dk_scr[...] = jnp.zeros_like(dk_scr)
    dv_scr[...] = jnp.zeros_like(dv_scr)
    attention_back(
        near_window, 0, bounds, k, key_t, v, query_z, grad_z, grad_scr, mix, lse, dq_scr, dk_scr, dv_scr, small_scr, steps,
    )
    for i, scr in enumerate((dq_scr, dk_scr, dv_scr)):
        put_gradient(gself, i, tn(tgt[...], scr[...].astype(bf16)))
    late()

    def leave(c):
        rows = rows_of(c, RC)
        tgrad[rows, :] = (
            d1[rows, :]
            + nt(dq_scr[rows, :], weight(attn, 0))
            + nt(dk_scr[rows, :].astype(bf16), weight(attn, 1))
            + nt(dv_scr[rows, :].astype(bf16), weight(attn, 2))
        ).astype(bf16)

    each_chunk(chunks, leave)


def shape(dims, dtype):
    return jax.ShapeDtypeStruct(dims, dtype)


VMEM_SPEC = pl.BlockSpec(memory_space=pltpu.VMEM)
HBM_SPEC = pl.BlockSpec(memory_space=pltpu.HBM)
SMEM_SPEC = pl.BlockSpec(memory_space=pltpu.SMEM)


def vmem(*buffers):
    return [pltpu.VMEM(dims, dtype) for dims, dtype in buffers]


def dma(*dims):
    return pltpu.SemaphoreType.DMA(dims)


def adam_direction(master, gradient, moments):
    first_moment = beta_first * moments[0] + (1.0 - beta_first) * gradient
    second_moment = beta_second * moments[1] + (1.0 - beta_second) * gradient * gradient
    first_fix = 1.0 - beta_first**STEP
    second_fix = 1.0 - beta_second**STEP
    direction = (
        first_moment / first_fix / (jnp.sqrt(second_moment / second_fix) + adam_eps)
        + decay_rate * master
    )
    return (direction, first_moment, second_moment)


MESH = pl.DeviceIdType.MESH


class Place:
    def __init__(self):
        self.gx = lax.axis_index("gx")
        self.gy = lax.axis_index("gy")
        self.x = lax.rem(self.gx, 2)
        self.y = self.gx // 2
        self.z = self.gy // 2
        self.c = lax.rem(self.gy, 2)
        self.here = self.gx * 8 + self.gy

    def target(self, x, y, z, c):
        return (y * 2 + x, z * 2 + c)

    def index(self, x, y, z, c):
        return (y * 2 + x) * 8 + z * 2 + c

    def others(self):
        found = []
        for step in range(1, 32):
            device = lax.rem(self.here + step, 32)
            found.append((device // 8, lax.rem(device, 8)))
        return found


def greet(targets):
    barrier = pltpu.get_barrier_semaphore()
    for target in targets:
        pl.semaphore_signal(barrier, inc=1, device_id=target, device_id_type=MESH)
    pl.semaphore_wait(barrier, len(targets))


def remote(src, dst, send_sem, recv_sem, target):
    return pltpu.make_async_remote_copy(
        src_ref=src, dst_ref=dst, send_sem=send_sem, recv_sem=recv_sem, device_id=target, device_id_type=MESH
    )


def forward_sizes(length, width):
    pairs = width // LANES
    row = (length, width)
    lse = (length // QB, pairs, 2 * QB)
    kept = [(row, bf16)] * 4 + [(lse, f32), (row, f32), ((length, 1), f32)]
    scratch = [
        ((pairs, 2 * length, LANES), bf16), ((width, length), bf16),
        ((pairs, LONGEST + 2 * KB, 2 * QB), f32), ((pairs, LANES, QB), f32),
    ]
    return kept, scratch


class Gathering:
    def __init__(self, me, mine, full, zsend, xsend, ysend, csend, recv):
        self.me, self.mine, self.full = me, mine, full
        self.zsend, self.xsend, self.ysend, self.csend, self.recv = zsend, xsend, ysend, csend, recv
        x, y, z, c = me.x, me.y, me.z, me.c
        self.ox, self.oy, self.oc = 1 - x, 1 - y, 1 - c
        self.x_next = me.target(self.ox, y, z, c)
        self.y_next = me.target(x, self.oy, z, c)
        self.sibling = me.target(x, y, z, self.oc)
        self.up = me.target(x, y, lax.rem(z + 1, 4), c)
        self.down = me.target(x, y, lax.rem(z + 3, 4), c)

    def copy(self, chunk, part, target, sem, own=False):
        rows = pl.ds(64 * part, 64)
        src = self.mine.at[rows] if own else self.full.at[chunk, rows]
        return remote(src, self.full.at[chunk, rows], sem, self.recv.at[chunk, part], target)

    def arrive(self, chunk, part):
        self.copy(chunk, part, self.sibling, self.csend.at[chunk, part]).wait_recv()

    def to_x(self, chunk, part, own=False):
        self.copy(chunk, part, self.x_next, self.xsend.at[chunk, part], own).start()

    def to_y(self, chunk, part, own=False):
        self.copy(chunk, part, self.y_next, self.ysend.at[chunk, part], own).start()

    def to_core(self, chunk, part, own=False):
        self.copy(chunk, part, self.sibling, self.csend.at[chunk, part], own).start()

    def along(self, zz, part, upward, own=False):
        me = self.me
        target = self.up if upward else self.down
        sem = self.zsend.at[zz, part, 0 if upward else 1]

        @pl.when((me.z < 3) if upward else (me.z > 0))
        def _():
            self.copy(me.index(me.x, me.y, zz, me.c), part, target, sem, own).start()

    def own_z(self, parts):
        for part in parts:
            self.along(self.me.z, part, True, True)
            self.along(self.me.z, part, False, True)

    def own_sides(self, parts):
        for part in parts:
            self.to_x(self.me.here, part, True)
            self.to_y(self.me.here, part, True)
        for part in parts:
            self.to_core(self.me.here, part, True)

    def at_distance(self, d, action):
        z = self.me.z
        if d == 0:
            action(z, None)
            return

        @pl.when(z >= d)
        def _():
            action(z - d, True)

        @pl.when(z + d <= 3)
        def _():
            action(z + d, False)

    def inline(self, d, parts):
        me = self.me

        def action(zz, upward):
            chunk = me.index(me.x, me.y, zz, me.c)
            for part in parts:
                self.arrive(chunk, part)
                self.along(zz, part, upward)
                self.to_x(chunk, part)
                self.to_y(chunk, part)
                self.to_core(chunk, part)

        self.at_distance(d, action)

    def side(self, d, parts):
        me = self.me

        def action(zz, _):
            for part in parts:
                if part % 2 == 0:
                    chunk = me.index(self.ox, me.y, zz, me.c)
                    self.arrive(chunk, part)
                    self.to_y(chunk, part)
                else:
                    chunk = me.index(me.x, self.oy, zz, me.c)
                    self.arrive(chunk, part)
                    self.to_x(chunk, part)
                self.to_core(chunk, part)

        self.at_distance(d, action)

    def far(self, d, parts):
        me = self.me

        def action(zz, _):
            for part in parts:
                last = (me.x, self.oy) if part % 2 == 0 else (self.ox, me.y)
                for ax, ay in (last, (self.ox, self.oy)):
                    chunk = me.index(ax, ay, zz, me.c)
                    self.arrive(chunk, part)
                    self.to_core(chunk, part)

        self.at_distance(d, action)

    def plane(self):
        me = self.me
        return ((me.x, me.y), (self.ox, me.y), (me.x, self.oy), (self.ox, self.oy))

    def core(self, parts):
        for d in range(4):

            def action(zz, _):
                for ax, ay in self.plane():
                    for part in parts:
                        self.arrive(self.me.index(ax, ay, zz, self.oc), part)

            self.at_distance(d, action)

    def sent(self, parts):
        me = self.me
        for zz in range(4):
            chunk = me.index(me.x, me.y, zz, me.c)
            for part in parts:

                @pl.when((me.z < 3) & (zz <= me.z))
                def _():
                    self.copy(chunk, part, self.up, self.zsend.at[zz, part, 0]).wait_send()

                @pl.when((me.z > 0) & (zz >= me.z))
                def _():
                    self.copy(chunk, part, self.down, self.zsend.at[zz, part, 1]).wait_send()

                self.copy(chunk, part, self.x_next, self.xsend.at[chunk, part]).wait_send()
                self.copy(chunk, part, self.y_next, self.ysend.at[chunk, part]).wait_send()
                for ax, ay in self.plane():
                    other = me.index(ax, ay, zz, me.c)
                    self.copy(other, part, self.sibling, self.csend.at[other, part]).wait_send()
                if part % 2 == 0:
                    other = me.index(self.ox, me.y, zz, me.c)
                    self.copy(other, part, self.y_next, self.ysend.at[other, part]).wait_send()
                else:
                    other = me.index(me.x, self.oy, zz, me.c)
                    self.copy(other, part, self.x_next, self.xsend.at[other, part]).wait_send()

    def stages(self, parts):
        return [
            lambda: self.inline(1, parts),
            lambda: (self.side(0, parts), self.inline(2, parts)),
            lambda: (self.side(1, parts), self.far(0, parts), self.inline(3, parts)),
            lambda: (self.side(2, parts), self.far(1, parts)),
            lambda: (self.side(3, parts), self.far(2, parts)),
            lambda: self.far(3, parts),
        ]


def first_kernel(
    attn_h, inner_h, outer_h, norm_h, lengths_h, src_h, tgt_h,
    full, norms_out, bounds_out, q_h, k_h, v_h, mix_h, lse_h, n1_h, s1_h,
    attn_f, inner_f, outer_f, norm_f, lengths, src, mine, lanes, bounds, tgt, attn, norm_row,
    q, k, v, mix, lse, n1, s1, query_z, value_t, score_scr, small_scr,
    sems, zsend, xsend, ysend, csend, recv, nsend, nrecv,
):
    me = Place()
    move = Mover(sems)
    loads = [
        move.start(a, b)
        for a, b in (
            (attn_h, attn_f), (inner_h, inner_f), (outer_h, outer_f), (norm_h, norm_f), (lengths_h, lengths), (src_h, src),
        )
    ]
    load_tgt = move.start(tgt_h, tgt)
    others = me.others()
    barrier = pltpu.get_barrier_semaphore()
    for target in others:
        pl.semaphore_signal(barrier, inc=1, device_id=target, device_id_type=MESH)
    move.wait(*loads)
    for j in range(8):
        mine[16 * j : 16 * j + 16, :] = attn_f[j].astype(bf16)
    for b in range(4):
        mine[128 + 16 * b : 144 + 16 * b, :] = inner_f[:, 512 * b : 512 * b + 512].astype(bf16)
    mine[192:256, :] = outer_f[...].astype(bf16)
    own_lanes = jnp.concatenate([norm_f[...], jnp.zeros((6, 112), f32)], axis=1)
    own_lanes = jnp.concatenate([own_lanes, jnp.zeros((10, 128), f32)], axis=0)
    lanes[...] = pltpu.roll(own_lanes, me.gy * 16, 1).astype(bf16)
    pl.semaphore_wait(barrier, len(others))
    gathering = Gathering(me, mine, full, zsend, xsend, ysend, csend, recv)
    early, late = (0, 1), (2, 3)
    gathering.own_z(early)
    gathering.own_sides(early)
    keep = move.start(mine, full.at[me.here])
    move.start(lanes, norms_out.at[me.here])
    gathering.own_z(late)
    norm_sends = []
    for i, target in enumerate(others):
        norm_sends.append(remote(lanes, norms_out.at[me.here], nsend.at[i], nrecv.at[me.here], target))
        norm_sends[-1].start()
    find_bounds(lengths, src, bounds)
    move.start(bounds, bounds_out)
    for stage in gathering.stages(early):
        stage()
    gathering.own_sides(late)
    gathering.core(early)
    move.wait(keep)
    load_attn = move.start(full.at[:, pl.ds(0, 64)], attn)
    later = gathering.stages(late)
    later[0]()
    move.wait(load_tgt, load_attn)
    self_forward(
        tgt, attn, bounds, norm_row, q, k, v, mix, lse, n1, s1, query_z, value_t, score_scr, small_scr,
        move, (q_h, k_h, v_h, mix_h, lse_h, n1_h, s1_h), later[1:],
    )
    gathering.core(late)
    for i, target in enumerate(others):
        source = target[0] * 8 + target[1]
        remote(lanes, norms_out.at[source], nsend.at[i], nrecv.at[source], target).wait_recv()
    for sent in norm_sends:
        sent.wait_send()
    gathering.sent(early + late)
    move.finish()


def gather_and_start(params, lengths, src_segments, tgt):
    length, width = tgt.shape
    kept, scratch = forward_sizes(length, width)
    row = (length, width)
    bounds = ((8, length), jnp.int32)
    full = ((32, 256, 512), bf16)
    norms = ((32, 16, 128), bf16)
    loads = [(p.shape, f32) for p in params] + [(lengths.shape, jnp.int32), (src_segments.shape, jnp.int32)]
    return pl.pallas_call(
        first_kernel,
        out_shape=tuple(shape(*item) for item in [full, norms, bounds] + kept),
        in_specs=[HBM_SPEC] * 7,
        out_specs=(HBM_SPEC,) * 10,
        scratch_shapes=vmem(
            *loads, ((256, 512), bf16), ((16, 128), bf16), bounds, (row, bf16), ((32, 64, 512), bf16),
            ((8, width), f32), *kept, *scratch,
        )
        + [dma(24), dma(4, 4, 2), dma(32, 4), dma(32, 4), dma(32, 4), dma(32, 4), dma(31), dma(32)],
        compiler_params=pltpu.CompilerParams(collective_id=0, has_side_effects=True, vmem_limit_bytes=GRANT),
    )(*params, lengths, src_segments, tgt)


def start_kernel(
    full, lengths, src, tgt, bounds_out, q_h, k_h, v_h, mix_h, lse_h, n1_h, s1_h,
    bounds, attn, q, k, v, mix, lse, n1, s1, query_z, value_t, score_scr, small_scr, sems,
):
    move = Mover(sems)
    load = move.start(full.at[:, pl.ds(0, attn.shape[1])], attn)
    find_bounds(lengths, src, bounds)
    move.start(bounds, bounds_out)
    move.wait(load)
    self_forward(
        tgt, attn, bounds, None, q, k, v, mix, lse, n1, s1, query_z, value_t, score_scr, small_scr,
        move, (q_h, k_h, v_h, mix_h, lse_h, n1_h, s1_h), (),
    )
    move.finish()


def start_only(full, lengths, src_segments, tgt):
    length, width = tgt.shape
    kept, scratch = forward_sizes(length, width)
    bounds = ((8, length), jnp.int32)
    return pl.pallas_call(
        start_kernel,
        out_shape=tuple(shape(*item) for item in [bounds] + kept),
        in_specs=[HBM_SPEC] + [VMEM_SPEC] * 3,
        out_specs=(HBM_SPEC,) * 8,
        scratch_shapes=vmem(bounds, ((full.shape[0], 64, width), bf16), *kept, *scratch) + [dma(16)],
        compiler_params=pltpu.CompilerParams(vmem_limit_bytes=GRANT),
    )(full, lengths, src_segments, tgt)


def middle(bounds, full, norms, memory, cotangent, n1, s1):
    length, width = n1.shape
    keys = memory.shape[0]
    blocks = full.shape[0]
    ffn_rows = full.shape[1] - 128
    hidden = ffn_rows * blocks // 2 * full.shape[2] // width
    pairs = width // LANES
    row, mem_row = (length, width), (keys, width)
    zeroed = ((pairs, 2 * length, LANES), bf16)
    gffn, gcross = ((blocks, ffn_rows, width), bf16), ((blocks, 64, width), bf16)
    outs = [(row, bf16), (row, f32), (mem_row, bf16), gffn, gcross, ((8, width), f32)]
    scratch = vmem(
        (bounds.shape, jnp.int32), (norms.shape, bf16), gcross, gffn, (mem_row, bf16), (row, bf16), (row, f32),
        ((length, 1), f32), (row, bf16), (mem_row, bf16), (mem_row, bf16), (row, bf16),
        ((length // QB, pairs, 2 * QB), f32), zeroed, zeroed, ((width, keys), bf16), ((pairs, keys + KB, 2 * QB), f32),
        ((pairs, LANES, QB), f32), ((length, hidden), bf16), ((length, hidden), bf16), (row, bf16), (row, bf16),
        (row, f32), (row, bf16), (row, bf16), (row, bf16), (mem_row, f32), (mem_row, f32), (row, bf16), (mem_row, bf16),
        gffn, gcross, ((6, 8, width), f32), ((8, width), f32),
    )
    return pl.pallas_call(
        middle_kernel,
        out_shape=tuple(shape(*item) for item in outs),
        in_specs=[SMEM_SPEC] + [HBM_SPEC] * 7,
        out_specs=(HBM_SPEC,) * 5 + (VMEM_SPEC,),
        scratch_shapes=scratch + [dma(16)],
        compiler_params=pltpu.CompilerParams(vmem_limit_bytes=GRANT),
    )(bounds, bounds, full, norms, memory, cotangent, n1, s1)


OUTER_ROWS = slice(96, 160)


def attn_rows(j):
    return 192 + 16 * j if j < 4 else 64 + 16 * (j - 4) if j < 6 else 160 + 16 * (j - 6)


def add_rows(dst, *sources):
    total = sources[0][...].astype(f32)
    for source in sources[1:]:
        total = total + source[...].astype(f32)
    dst[...] = total.astype(dst.dtype)


class Summing:
    order = (2, 1, 3, 0)

    def __init__(self, me, sources, rows, pieces, first_a, first_b, second_a, second_b, third, result, sems):
        self.me, self.sources, self.rows, self.pieces = me, sources, rows, pieces
        self.first_a, self.first_b, self.second_a, self.second_b, self.third = first_a, first_b, second_a, second_b, third
        self.result = result
        (self.lsem, self.csend, self.crecv, self.send1, self.recv1, self.send2, self.recv2, self.send3, self.recv3) = sems
        x, y, z, c = me.x, me.y, me.z, me.c
        self.ox, self.oy, self.oc = 1 - x, 1 - y, 1 - c
        self.x_next = me.target(self.ox, y, z, c)
        self.y_next = me.target(x, self.oy, z, c)
        self.sibling = me.target(x, y, z, self.oc)
        self.zs = [lax.rem(z + d, 4) for d in range(4)]
        self.half = first_a.shape[2]
        self.top, self.bottom = pl.ds(0, self.half), pl.ds(self.half, self.half)
        self.pending, self.cores, self.own = [], {}, {}
        self.firsts, self.seconds, self.thirds = {}, {}, {}

    def send(self, *args):
        copy = remote(*args)
        copy.start()
        self.pending.append(copy)
        return copy

    def load(self):
        for d in self.order:
            for k, (source, kept, _) in enumerate(self.sources):
                if kept is not None:
                    copy = pltpu.make_async_copy(source.at[:, self.zs[d], self.me.c], kept.at[d], self.lsem.at[d, k])
                    copy.start()
                    self.own[d, k] = copy

    def core(self):
        for d in self.order:
            for k, (source, _, got) in enumerate(self.sources):
                self.cores[d, k] = self.send(
                    source.at[:, self.zs[d], self.oc], got.at[d], self.csend.at[d, k], self.crecv.at[d, k], self.sibling
                )

    def stage1(self, d):
        me = self.me
        for k in range(len(self.sources)):
            if (d, k) in self.own:
                self.own[d, k].wait()
            self.cores[d, k].wait_recv()

        def add(i):
            piece = self.pieces.at[d, i // 2, lax.rem(i, 2)]
            for start, count, k, first in self.rows:
                source, kept, got = self.sources[k]
                held = source.at[i, self.zs[d], me.c] if kept is None else kept.at[d, i]
                part = pl.ds(first, count)
                add_rows(piece.at[pl.ds(start, count)], held.at[part], got.at[d, i, part])

        each_chunk(4, add)
        self.firsts[d] = (
            self.send(
                self.pieces.at[d, self.oy, :, self.top], self.first_a.at[d], self.send1.at[d, 0], self.recv1.at[d, 0],
                self.y_next,
            ),
            self.send(
                self.pieces.at[d, :, self.ox, self.bottom], self.first_b.at[d], self.send1.at[d, 1],
                self.recv1.at[d, 1], self.x_next,
            ),
        )

    def stage2(self, d):
        me = self.me
        self.firsts[d][0].wait_recv()
        part = self.pieces.at[d, me.y, self.ox, self.top]
        add_rows(part, part, self.first_a.at[d, self.ox])
        one = self.send(part, self.second_a.at[d], self.send2.at[d, 0], self.recv2.at[d, 0], self.x_next)
        self.firsts[d][1].wait_recv()
        part = self.pieces.at[d, self.oy, me.x, self.bottom]
        add_rows(part, part, self.first_b.at[d, self.oy])
        two = self.send(part, self.second_b.at[d], self.send2.at[d, 1], self.recv2.at[d, 1], self.y_next)
        self.seconds[d] = (one, two)

    def stage3(self, d):
        me = self.me
        for copy in self.seconds[d]:
            copy.wait_recv()
        for rows, first, second, at in (
            (self.top, self.first_a, self.second_a, me.x), (self.bottom, self.first_b, self.second_b, me.y),
        ):
            part = self.pieces.at[d, me.y, me.x, rows]
            add_rows(part if d else self.result.at[rows], part, first.at[d, at], second.at[d])
        if d:
            self.thirds[d] = self.send(
                self.pieces.at[d, me.y, me.x], self.third.at[d - 1], self.send3.at[d - 1], self.recv3.at[d - 1],
                me.target(me.x, me.y, self.zs[d], me.c),
            )

    def end(self):
        for d in (1, 2, 3):
            self.thirds[d].wait_recv()
        add_rows(self.result, self.result, self.third.at[0], self.third.at[1], self.third.at[2])


def last_kernel(
    full, bounds_h, tgt_h, q_h, k_h, v_h, mix_h, lse_h, d1_h, gffn, gcross, gnorm_h,
    attn_p, inner_p, outer_p, norm_p, attn_m, in_m, out_m, norm_m,
    tgrad_h, g_ref, gn_ref, totals_ref,
    bounds, tgt, attn, q, k, v, mix, lse, d1, tgrad, gself, query_z, grad_z, key_t, grad_scr, dq_scr, dk_scr, dv_scr,
    small_scr, d1_scr, own_ffn, own_cross, got_ffn, got_cross, pieces, first_a, first_b, second_a, second_b, third,
    got_self, pieces2, first_a2, first_b2, second_a2, second_b2, third2, vectors, tiles,
    msems, psems, *sems,
):
    me = Place()
    move = Mover(msems)
    others = me.others()
    barrier = pltpu.get_barrier_semaphore()
    for target in others:
        pl.semaphore_signal(barrier, inc=1, device_id=target, device_id_type=MESH)
    load_first = [move.start(a, b) for a, b in ((d1_h, d1), (full.at[:, pl.ds(0, 64)], attn), (gnorm_h, vectors.at[0]))]
    load_mix = move.start(mix_h, mix)
    load_rest = [
        move.start(a, b)
        for a, b in ((q_h, q), (k_h, k), (v_h, v), (lse_h, lse), (bounds_h, bounds), (tgt_h, tgt))
    ]
    sems1, sems2, (nsend, nrecv, tsend, trecv) = sems[0:9], sems[9:18], sems[18:22]
    big = Summing(
        me, [(gffn, own_ffn, got_ffn), (gcross, own_cross, got_cross)],
        [(0, 64, 0, 0), (64, 32, 1, 0), (96, 64, 0, 64), (160, 32, 1, 32)],
        pieces, first_a, first_b, second_a, second_b, third, g_ref.at[pl.ds(0, 192)], sems1,
    )
    rest = Summing(
        me, [(gself, None, got_self)], [(0, 64, 0, 0)],
        pieces2, first_a2, first_b2, second_a2, second_b2, third2, g_ref.at[pl.ds(192, 64)], sems2,
    )
    big.load()
    move.wait(*load_first)
    pl.semaphore_wait(barrier, len(others))
    big.core()
    norm_copies = [big.send(vectors.at[0], vectors.at[1], nsend.at[0], nrecv.at[0], big.sibling)]

    def norm_step(stage, target):
        norm_copies[-1].wait_recv()
        vectors[2 * stage] = vectors[2 * stage - 2] + vectors[2 * stage - 1]
        norm_copies.append(
            big.send(vectors.at[2 * stage], vectors.at[2 * stage + 1], nsend.at[stage], nrecv.at[stage], target)
        )

    def norm_last():
        norm_copies[-1].wait_recv()
        vectors[6] = vectors[4] + vectors[5]
        for d in range(1, 4):
            target = me.target(me.x, me.y, big.zs[d], me.c)
            norm_copies.append(big.send(vectors.at[6], vectors.at[6 + d], nsend.at[2 + d], nrecv.at[2 + d], target))

    far, up, down, here = big.order
    steps = [
        lambda: (big.stage1(far), big.stage1(up), norm_step(1, big.x_next)),
        lambda: (big.stage1(down), big.stage1(here)),
        lambda: norm_step(2, big.y_next),
        lambda: (big.stage2(far), big.stage2(up), norm_last()),
        lambda: (big.stage2(down), big.stage3(far)),
        lambda: (big.stage2(here), big.stage3(up)),
        lambda: (big.stage3(down), big.stage3(here)),
    ]

    move.wait(load_mix, *load_rest)
    self_backward(
        tgt, attn, bounds, q, k, v, mix, lse, d1, tgrad, gself.reshape(32, 64, 512),
        query_z, grad_z, key_t, grad_scr, dq_scr, dk_scr, dv_scr, small_scr, d1_scr, steps, lambda: rest.core(),
    )
    move.start(tgrad, tgrad_h)
    for d in rest.order:
        rest.stage1(d)
    big.end()
    for copy in norm_copies[3:]:
        copy.wait_recv()
    vectors[10] = (vectors[6] + vectors[8]) + (vectors[7] + vectors[9])
    lanes = vectors[10, :, pl.ds(pl.multiple_of(me.gx * 128, 128), 128)]
    gn_ref[...] = pltpu.roll(lanes, lax.rem(128 - me.gy * 16, 128), 1)
    rest.stage2(far)
    rest.stage2(up)
    rest.stage3(far)
    rest.stage2(down)
    rest.stage3(up)
    rest.stage2(here)
    rest.stage3(down)
    rest.stage3(here)
    lane = lax.broadcasted_iota(jnp.int32, (1, 128), 1)
    rows = [jnp.zeros((1, 128), f32), jnp.zeros((1, 128), f32)]

    def put(t, pairs):
        for i in range(2):
            square = sum(jnp.sum(pair[i] * pair[i]) for pair in pairs)
            rows[i] = rows[i] + jnp.where(lane == t, square, 0.0)

    def direction(*args):
        return adam_direction(*args)[0]

    def put_attn(j):
        grad = g_ref[attn_rows(j) : attn_rows(j) + 16, :]
        put(j, [(attn_p[j], direction(attn_p[j], grad, (attn_m[0, j], attn_m[1, j])))])

    for j in range(4, 8):
        put_attn(j)
    pairs = []
    for b in range(4):
        cols = slice(512 * b, 512 * b + 512)
        grad = g_ref[16 * b : 16 * b + 16, :]
        pairs.append((inner_p[:, cols], direction(inner_p[:, cols], grad, (in_m[0, :, cols], in_m[1, :, cols]))))
    put(8, pairs)
    put(9, [(outer_p[...], direction(outer_p[...], g_ref[OUTER_ROWS, :], (out_m[0], out_m[1])))])
    master = norm_p[...]
    update = direction(master, gn_ref[0:6, 0:16], (norm_m[0], norm_m[1]))
    for i in range(6):
        put(10 + i, [(master[i : i + 1], update[i : i + 1])])
    rest.end()
    for j in range(4):
        put_attn(j)
    tiles[me.here] = jnp.concatenate([rows[0], rows[1], jnp.zeros((6, 128), f32)], axis=0)
    for i, target in enumerate(others):
        big.send(tiles.at[me.here], tiles.at[me.here], tsend.at[i], trecv.at[me.here], target)
    for i, target in enumerate(others):
        source = target[0] * 8 + target[1]
        remote(tiles.at[source], tiles.at[source], tsend.at[i], trecv.at[source], target).wait_recv()
    totals_ref[...] = jnp.sum(tiles[...], axis=0)
    for copy in big.pending + rest.pending:
        copy.wait_send()
    move.finish()


def backward_scratch(length, width):
    pairs = width // LANES
    row = (length, width)
    zeroed = ((pairs, 2 * length, LANES), bf16)
    return [
        zeroed, zeroed, ((width, length), bf16), (row, bf16), (row, bf16), (row, f32), (row, f32),
        ((pairs, LANES, QB), f32), (row, bf16),
    ]


def finish_and_reduce(full, bounds, tgt, saved, d1, grads, norm_grad, params, moments):
    length, width = tgt.shape
    row = (length, width)
    lse = (length // QB, width // LANES, 2 * QB)

    def sums(half):
        return [
            ((4, 2, 2, 2 * half, 512), bf16), ((4, 2, half, 512), bf16), ((4, 2, half, 512), bf16),
            ((4, half, 512), bf16), ((4, half, 512), bf16), ((3, 2 * half, 512), bf16),
        ]

    scratch = vmem(
        (bounds.shape, jnp.int32), (row, bf16), ((32, 64, 512), bf16), *[(row, bf16)] * 4, (lse, f32), (row, f32),
        (row, bf16), ((4, 4, 2, 64, 512), bf16), *backward_scratch(length, width),
        ((4, 4, 128, 512), bf16), ((4, 4, 64, 512), bf16), ((4, 4, 128, 512), bf16), ((4, 4, 64, 512), bf16), *sums(96),
        ((4, 4, 64, 512), bf16), *sums(32), ((11, 8, 512), f32), ((32, 8, 128), f32),
    )
    round_sems = [dma(4, 2), dma(4, 2), dma(4, 2), dma(4, 2), dma(4, 2), dma(4, 2), dma(4, 2), dma(3), dma(3)]
    split = [grad.reshape(4, 4, 2, grad.shape[1], 512) for grad in grads]
    return pl.pallas_call(
        last_kernel,
        out_shape=(shape(row, bf16), shape((256, 512), f32), shape((8, 128), f32), shape((8, 128), f32)),
        in_specs=[HBM_SPEC] * 12 + [VMEM_SPEC] * 8,
        out_specs=(HBM_SPEC, VMEM_SPEC, VMEM_SPEC, VMEM_SPEC),
        scratch_shapes=scratch + [dma(16), dma(1)] + round_sems + round_sems + [dma(6), dma(6), dma(31), dma(32)],
        compiler_params=pltpu.CompilerParams(collective_id=1, has_side_effects=True, vmem_limit_bytes=GRANT),
    )(full, bounds, tgt, *saved, d1, *split, norm_grad, *params, *moments)


def finish_kernel(
    full, bounds, tgt, q, k, v, mix, lse, d1, tgrad, gself,
    attn, query_z, grad_z, key_t, grad_scr, dq_scr, dk_scr, dv_scr, small_scr, d1_scr, sems,
):
    move = Mover(sems)
    move.wait(move.start(full.at[:, pl.ds(0, attn.shape[1])], attn))
    self_backward(
        tgt, attn, bounds, q, k, v, mix, lse, d1, tgrad, gself,
        query_z, grad_z, key_t, grad_scr, dq_scr, dk_scr, dv_scr, small_scr, d1_scr, (), lambda: None,
    )


def finish_only(full, bounds, tgt, saved, d1):
    length, width = tgt.shape
    gself = ((full.shape[0], 64, width), bf16)
    return pl.pallas_call(
        finish_kernel,
        out_shape=(shape((length, width), bf16), shape(*gself)),
        in_specs=[HBM_SPEC] + [VMEM_SPEC] * 8,
        out_specs=(VMEM_SPEC, VMEM_SPEC),
        scratch_shapes=vmem(gself, *backward_scratch(length, width)) + [dma(2)],
        compiler_params=pltpu.CompilerParams(vmem_limit_bytes=GRANT),
    )(full, bounds, tgt, *saved, d1)


def update_kernel(
    g_ref, gn_ref, totals_ref, attn, inner, outer, norm, attn_m, in_m, out_m, norm_m,
    attn_new, in_new, out_new, norm_new, attn_first, attn_second, in_first, in_second, out_first, out_second,
    norm_first, norm_second, attn_copy, in_copy, out_copy, norm_copy, norms_ref,
):
    roots = jnp.sqrt(totals_ref[...])
    norms_ref[...] = roots[0:2, 0:16]
    ratio = learn_rate * (roots[0:1, :] / roots[1:2, :])

    def step(t, master, gradient, moments, new, first, second, copy, place):
        direction, first_moment, second_moment = adam_direction(master, gradient, moments)
        value = master - ratio[:, t : t + 1] * direction
        new[place] = value
        first[place] = first_moment
        second[place] = second_moment
        copy[place] = value.astype(bf16)

    for j in range(8):
        grad = g_ref[attn_rows(j) : attn_rows(j) + 16, :]
        step(j, attn[j], grad, (attn_m[0, j], attn_m[1, j]), attn_new, attn_first, attn_second, attn_copy, j)
    for b in range(4):
        cols = slice(512 * b, 512 * b + 512)
        place = (slice(None), cols)
        grad = g_ref[16 * b : 16 * b + 16, :]
        step(8, inner[:, cols], grad, (in_m[0, :, cols], in_m[1, :, cols]), in_new, in_first, in_second, in_copy, place)
    step(9, outer[...], g_ref[OUTER_ROWS, :], (out_m[0], out_m[1]), out_new, out_first, out_second, out_copy, ...)
    for i in range(6):
        one = slice(i, i + 1)
        moments = (norm_m[0, one], norm_m[1, one])
        step(10 + i, norm[one], gn_ref[one, 0:16], moments, norm_new, norm_first, norm_second, norm_copy, one)


def update_params(summed, params, moments):
    outs = [shape(p.shape, f32) for p in params]
    outs += [shape(p.shape, f32) for p in params for _ in range(2)]
    outs += [shape(p.shape, bf16) for p in params] + [shape((2, 16), f32)]
    return pl.pallas_call(
        update_kernel,
        out_shape=tuple(outs),
        in_specs=[VMEM_SPEC] * 11,
        out_specs=(VMEM_SPEC,) * len(outs),
        compiler_params=pltpu.CompilerParams(vmem_limit_bytes=GRANT),
    )(*summed, *params, *moments)


def tensor_squares(attn_part, inner_part, outer_part, norm_part):
    return jnp.concatenate(
        [
            jnp.sum(attn_part * attn_part, axis=(1, 2)),
            jnp.sum(inner_part * inner_part)[None],
            jnp.sum(outer_part * outer_part)[None],
            jnp.sum(norm_part * norm_part, axis=1),
        ]
    )


def blocked(matrix, width):
    blocks = matrix.shape[0] // 16
    cols = matrix.shape[1] // width
    return matrix.reshape(blocks, 16, cols, width).transpose(0, 2, 1, 3).reshape(blocks, cols * 16, width)


def unblocked(blocks, width):
    count = blocks.shape[0]
    cols = blocks.shape[1] // 16
    return blocks.reshape(count, cols, 16, width).transpose(0, 2, 1, 3).reshape(count * 16, cols * width)


def gather_any(attn_w, ffn_in, ffn_out, norm_params):
    width = attn_w.shape[2]
    attn = lax.all_gather(attn_w.astype(bf16), AXES, axis=1, tiled=True)
    inner = lax.all_gather(ffn_in.astype(bf16), AXES, axis=0, tiled=True)
    outer = lax.all_gather(ffn_out.astype(bf16), AXES, axis=0, tiled=True)
    norm = lax.all_gather(norm_params.astype(bf16), AXES, axis=1, tiled=True)
    blocks = width // 16
    attn = attn.reshape(8, blocks, 16, width).transpose(1, 0, 2, 3).reshape(blocks, 8 * 16, width)
    full = jnp.concatenate([attn, blocked(inner, width), outer.reshape(blocks, -1, width)], axis=1)
    lanes = jnp.pad(norm, ((0, 10), (0, 0))).reshape(16, 4, width // 4).transpose(1, 0, 2)
    return full, lanes


def reduce_any(grads, norm_grad, params, moments):
    grad_ffn, grad_cross, grad_self = grads
    width = grad_ffn.shape[2]
    blocks = width // 16
    attn_w, ffn_in, ffn_out, norm_params = params
    attn_m, in_m, out_m, norm_m = moments
    stack = jnp.concatenate([grad_self, grad_cross], axis=1)
    stack = stack.reshape(blocks, 8, 16, width).transpose(1, 0, 2, 3).reshape(8, width, width)
    rows = ffn_in.shape[1] // width * 16
    inner = unblocked(grad_ffn[:, :rows], width)
    outer = grad_ffn[:, rows:].reshape(-1, width)
    shard_attn = lax.psum_scatter(stack, AXES, scatter_dimension=1, tiled=True).astype(f32)
    shard_inner = lax.psum_scatter(inner, AXES, scatter_dimension=0, tiled=True).astype(f32)
    shard_outer = lax.psum_scatter(outer, AXES, scatter_dimension=0, tiled=True).astype(f32)
    shard_norm = lax.psum_scatter(norm_grad, AXES, scatter_dimension=1, tiled=True)
    attn_dir, attn_first, attn_second = adam_direction(attn_w, shard_attn, attn_m)
    inner_dir, inner_first, inner_second = adam_direction(ffn_in, shard_inner, in_m)
    outer_dir, outer_first, outer_second = adam_direction(ffn_out, shard_outer, out_m)
    norm_dir, norm_first, norm_second = adam_direction(norm_params, shard_norm, norm_m)
    weight_total, update_total = lax.psum(
        (tensor_squares(*params), tensor_squares(attn_dir, inner_dir, outer_dir, norm_dir)), AXES
    )
    ratio = jnp.sqrt(weight_total) / jnp.sqrt(update_total)
    attn_new = attn_w - learn_rate * ratio[0:8][:, None, None] * attn_dir
    in_new = ffn_in - learn_rate * ratio[8] * inner_dir
    out_new = ffn_out - learn_rate * ratio[9] * outer_dir
    norm_new = norm_params - learn_rate * ratio[10:16][:, None] * norm_dir
    norms = jnp.stack([jnp.sqrt(weight_total), jnp.sqrt(update_total)])
    return (
        attn_new, in_new, out_new, norm_new,
        attn_first, attn_second, inner_first, inner_second, outer_first, outer_second, norm_first, norm_second,
        attn_new.astype(bf16), in_new.astype(bf16), out_new.astype(bf16), norm_new.astype(bf16), norms,
    )


def on_device(
    close, tgt, memory, cotangent, tgt_lengths, src_segments, attn_w, ffn_in, ffn_out, norm_params,
    attn_moments, in_moments, out_moments, norm_moments,
):
    params = (attn_w, ffn_in, ffn_out, norm_params)
    moments = (attn_moments, in_moments, out_moments, norm_moments)
    if close and tgt.shape[0] == 1:
        full, norms, bounds, *state = gather_and_start(params, tgt_lengths, src_segments, tgt[0])
        saved, (n1, s1) = state[:5], state[5:]
        layer_out, d1, mem_grad, grad_ffn, grad_cross, norm_grad = middle(
            bounds, full, norms, memory[0], cotangent[0], n1, s1
        )
        tgt_grad, *summed = finish_and_reduce(
            full, bounds, tgt[0], saved, d1, (grad_ffn, grad_cross), norm_grad, params, moments
        )
        return (layer_out[None], tgt_grad[None], mem_grad[None], *update_params(summed, params, moments))
    full, norms = gather_any(*params)
    parts = []
    for r in range(tgt.shape[0]):
        bounds, *state = start_only(full, tgt_lengths[r : r + 1], src_segments[r : r + 1], tgt[r])
        saved, (n1, s1) = state[:5], state[5:]
        layer_out, d1, mem_grad, grad_ffn, grad_cross, norm_grad = middle(
            bounds, full, norms, memory[r], cotangent[r], n1, s1
        )
        tgt_grad, grad_self = finish_only(full, bounds, tgt[r], saved, d1)
        parts.append((layer_out, tgt_grad, mem_grad, grad_ffn, grad_cross, grad_self, norm_grad[0:6]))
    outs = [jnp.stack([part[i] for part in parts]) for i in range(3)]
    sums = [sum(part[i].astype(f32) for part in parts) for i in range(3, 7)]
    grads = [grad.astype(bf16) for grad in sums[:3]]
    return (*outs, *reduce_any(grads, sums[3], params, moments))


def fits(mesh):
    return mesh.shape["gx"] == 4 and mesh.shape["gy"] == 8


def solution(mesh):
    rows = P(AXES, None, None)
    matrix = P(AXES, None)
    stack = P(None, AXES, None)
    vectors = P(None, AXES)
    return jax.shard_map(
        functools.partial(on_device, fits(mesh)),
        mesh=mesh,
        in_specs=(
            rows, rows, rows, matrix, matrix, stack, matrix, matrix, vectors,
            P(None, None, AXES, None), stack, stack, P(None, None, AXES),
        ),
        out_specs=(
            rows, rows, rows, stack, matrix, matrix, vectors, stack, stack, matrix, matrix, matrix, matrix,
            vectors, vectors, stack, matrix, matrix, vectors, P(),
        ),
        check_vma=False,
    )
```

```python
import functools

import jax
import jax.numpy as jnp
from jax import lax
from jax.experimental import pallas as pl
from jax.experimental.pallas import tpu as pltpu
from jax.sharding import PartitionSpec as P

HEAD_DIM = 64
STEP = 5

beta_first = 0.5
beta_second = 0.5
learn_rate = 0.5
decay_rate = 0.01
norm_eps = 1e-05
adam_eps = 1e-06

f32 = jnp.float32
bf16 = jnp.bfloat16
LANES = 128
QB = 128
KB = 256
RC = 256
LONGEST = 512
MASKED = -1e30
AXES = ("gx", "gy")
GRANT = 63 * 2**20


def nn(left, right):
    return lax.dot_general(left, right, (((1,), (0,)), ((), ())), preferred_element_type=f32)


def nt(left, right):
    return lax.dot_general(left, right, (((1,), (1,)), ((), ())), preferred_element_type=f32)


def tn(left, right):
    return lax.dot_general(left, right, (((0,), (0,)), ((), ())), preferred_element_type=f32)


def rows_of(step, size):
    return pl.ds(pl.multiple_of(step * size, size), size)


def each_chunk(count, body):
    def step(index, carry):
        body(index)
        return carry

    lax.fori_loop(0, count, step, 0)


def spread_heads(dst, src):
    pairs = dst.shape[0]
    first = lax.broadcasted_iota(jnp.int32, (QB, LANES), 1) < HEAD_DIM
    zero = jnp.zeros((QB, LANES), bf16)

    def body(i):
        start = pl.multiple_of(i * 2 * QB, 2 * QB)
        for p in range(pairs):
            tile = src[rows_of(i, QB), p * LANES : (p + 1) * LANES]
            dst[p, pl.ds(start, QB), :] = jnp.where(first, tile, zero)
            dst[p, pl.ds(start + QB, QB), :] = jnp.where(first, zero, tile)

    each_chunk(src.shape[0] // QB, body)


def run_blocks(count, body, steps):
    if not steps:
        each_chunk(count, body)
        return
    for i in range(count):
        body(i)
        if i < len(steps) and steps[i] is not None:
            steps[i]()


def near_window(i):
    first = max(0, i - LONGEST // LANES) if isinstance(i, int) else jnp.maximum(i - LONGEST // LANES, 0)
    return first, (i + 1 - first + KB // LANES - 1) // (KB // LANES)


def bound_window(bounds, which):
    def window(i):
        first = bounds[2 * which, i * QB] // LANES
        last = (bounds[2 * which + 1, i * QB + QB - 1] + LANES - 1) // LANES
        return first, ((last - first) * LANES + KB - 1) // KB

    return window


def key_block(first_key, j, keys):
    nominal = first_key * LANES + j * KB
    return pl.multiple_of(jnp.minimum(nominal, keys - KB), LANES), nominal


def block_bias(low, high, start, nominal):
    place = start + lax.broadcasted_iota(jnp.int32, (KB, QB), 0)
    bias = jnp.where((place >= jnp.maximum(low, nominal)) & (place < high), 0.0, MASKED).astype(f32)
    return jnp.concatenate([bias, bias], axis=1)


def attention(window, which, bounds, key_ref, value_t, query_z, mixed_ref, lse_ref, score_scr, out_scr, steps=()):
    keys = key_ref.shape[0]
    pairs = query_z.shape[0]
    fold = (KB // 8, 8, 2 * QB)

    def query_block(i):
        rows = rows_of(i, QB)
        pair_rows = rows_of(i, 2 * QB)
        low = bounds[2 * which : 2 * which + 1, rows]
        high = bounds[2 * which + 1 : 2 * which + 2, rows]
        first_key, blocks = window(i)
        out_scr[...] = jnp.zeros_like(out_scr)

        def scores(j, tops):
            start, nominal = key_block(first_key, j, keys)
            bias = block_bias(low, high, start, nominal)
            found = []
            raw = [
                nt(key_ref[pl.ds(start, KB), p * LANES : (p + 1) * LANES], query_z[p, pair_rows, :])
                for p in range(pairs)
            ]
            for p in range(pairs):
                score = raw[p] + bias
                score_scr[p, rows_of(j, KB), :] = score
                found.append(jnp.maximum(tops[p], jnp.max(score.reshape(fold), axis=0)))
            return tuple(found)

        tops = lax.fori_loop(
            0, blocks, scores, tuple(jnp.full((8, 2 * QB), MASKED, f32) for _ in range(pairs))
        )
        top = [jnp.max(t, axis=0, keepdims=True) for t in tops]

        def weigh(j, sums):
            start, _ = key_block(first_key, j, keys)
            found = []
            low_exps = []
            for p in range(pairs):
                exponent = jnp.exp(score_scr[p, rows_of(j, KB), :] - top[p])
                found.append(sums[p] + jnp.sum(exponent.reshape(fold), axis=0))
                low_exps.append(exponent.astype(bf16))
            for p in range(pairs):
                for h in range(2):
                    heads = slice(h * HEAD_DIM, (h + 1) * HEAD_DIM)
                    value = value_t[
                        p * LANES + h * HEAD_DIM : p * LANES + (h + 1) * HEAD_DIM, pl.ds(start, KB)
                    ]
                    out_scr[p, heads, :] += nn(value, low_exps[p][:, h * QB : (h + 1) * QB])
            return tuple(found)

        sums = lax.fori_loop(
            0, blocks, weigh, tuple(jnp.zeros((8, 2 * QB), f32) for _ in range(pairs))
        )
        for p in range(pairs):
            total = jnp.sum(sums[p], axis=0, keepdims=True)
            lse_ref[i, p : p + 1, :] = top[p] + jnp.log(total)
            inverse = 1.0 / total
            out = jnp.concatenate(
                [out_scr[p, 0:HEAD_DIM, :] * inverse[:, :QB], out_scr[p, HEAD_DIM:, :] * inverse[:, QB:]],
                axis=0,
            )
            mixed_ref[rows, p * LANES : (p + 1) * LANES] = out.T.astype(bf16)

    run_blocks(query_z.shape[1] // (2 * QB), query_block, steps)


def attention_back(
    window, which, bounds, key_ref, key_t, value_ref, query_z, grad_z, grad_ref, mixed_ref, lse_ref,
    dquery_ref, dkey_scr, dvalue_scr, dq_scr, steps=(),
):
    keys = key_ref.shape[0]
    pairs = query_z.shape[0]

    def query_block(i):
        rows = rows_of(i, QB)
        pair_rows = rows_of(i, 2 * QB)
        low = bounds[2 * which : 2 * which + 1, rows]
        high = bounds[2 * which + 1 : 2 * which + 2, rows]
        first_key, blocks = window(i)
        dq_scr[...] = jnp.zeros_like(dq_scr)
        deltas = []
        for p in range(pairs):
            lanes = slice(p * LANES, (p + 1) * LANES)
            product = (grad_ref[rows, lanes].astype(f32) * mixed_ref[rows, lanes].astype(f32)).T
            deltas.append(
                jnp.concatenate(
                    [
                        jnp.sum(product[:HEAD_DIM], axis=0, keepdims=True),
                        jnp.sum(product[HEAD_DIM:], axis=0, keepdims=True),
                    ],
                    axis=1,
                )
            )

        def key_step(j):
            start, nominal = key_block(first_key, j, keys)
            bias = block_bias(low, high, start, nominal)
            block = pl.ds(start, KB)
            held = {}

            def first(p):
                lanes = slice(p * LANES, (p + 1) * LANES)
                held["s", p] = nt(key_ref[block, lanes], query_z[p, pair_rows, :])
                held["d", p] = nt(value_ref[block, lanes], grad_z[p, pair_rows, :])

            def second(p):
                prob = jnp.exp(held.pop(("s", p)) + bias - lse_ref[i, p : p + 1, :])
                held["ds", p] = (prob * (held.pop(("d", p)) - deltas[p])).astype(bf16)
                held["p", p] = prob.astype(bf16)

            def third(p):
                lanes = slice(p * LANES, (p + 1) * LANES)
                dscore = held["ds", p]
                dvalue_scr[block, lanes] += nn(held["p", p], grad_z[p, pair_rows, :])
                dkey_scr[block, lanes] += nn(dscore, query_z[p, pair_rows, :])
                for h in range(2):
                    heads = slice(h * HEAD_DIM, (h + 1) * HEAD_DIM)
                    key = key_t[
                        p * LANES + h * HEAD_DIM : p * LANES + (h + 1) * HEAD_DIM, block
                    ]
                    dq_scr[p, heads, :] += nn(key, dscore[:, h * QB : (h + 1) * QB])

            for step in (first, second, third):
                for p in range(pairs):
                    step(p)

        each_chunk(blocks, key_step)
        for p in range(pairs):
            dquery_ref[rows, p * LANES : (p + 1) * LANES] = (
                (dq_scr[p] * HEAD_DIM**-0.5).T.astype(bf16)
            )

    run_blocks(query_z.shape[1] // (2 * QB), query_block, steps)


def norm_parts(values):
    average = jnp.mean(values, axis=-1, keepdims=True)
    centred = values - average
    spread = jnp.mean(centred * centred, axis=-1, keepdims=True)
    inverse = lax.rsqrt(spread + norm_eps)
    return centred * inverse, inverse


def norm_back(gradient, normed, inverse, gain):
    scaled = gradient * gain
    first_mean = jnp.mean(scaled, axis=-1, keepdims=True)
    second_mean = jnp.mean(scaled * normed, axis=-1, keepdims=True)
    return inverse * (scaled - first_mean - normed * second_mean)


def fold_rows(values):
    return jnp.sum(values.reshape(values.shape[0] // 8, 8, values.shape[1]), axis=0)


def load_norms(norm_ref):
    group = norm_ref.shape[0] // 4
    blocks = [jnp.sum(norm_ref[group * i : group * (i + 1)].astype(f32), axis=0) for i in range(4)]
    rows = jnp.concatenate(blocks, axis=1)
    return [rows[i : i + 1, :] for i in range(6)]


def weight(ref, index):
    blocks = ref.shape[0]
    return ref[:, 16 * index : 16 * (index + 1), :].reshape(16 * blocks, ref.shape[2])


def put_gradient(ref, index, value):
    blocks = ref.shape[0]
    ref[:, 16 * index : 16 * (index + 1), :] = value.astype(bf16).reshape(blocks, 16, ref.shape[2])


def load_norm_rows(dst, norm_ref):
    for i, vector in enumerate(load_norms(norm_ref)):
        dst[i : i + 1, :] = vector


def sigmoid(values):
    return 0.5 * jnp.tanh(0.5 * values) + 0.5


class Mover:
    def __init__(self, sems):
        self.sems = sems
        self.count = 0
        self.open = []

    def start(self, src, dst):
        copy = pltpu.make_async_copy(src, dst, self.sems.at[self.count])
        self.count += 1
        copy.start()
        self.open.append(copy)
        return copy

    def wait(self, *copies):
        for copy in copies:
            copy.wait()
            self.open = [other for other in self.open if other is not copy]

    def finish(self):
        self.wait(*list(self.open))


def find_bounds(lengths, src_segments, bounds_ref):
    sentences = lengths.shape[1]
    length = bounds_ref.shape[1]
    row = lax.broadcasted_iota(jnp.int32, (sentences, sentences), 0)
    col = lax.broadcasted_iota(jnp.int32, (sentences, sentences), 1)
    sizes = jnp.broadcast_to(lengths[...].astype(f32), (sentences, sentences))

    def total(mask, values):
        return jnp.sum(jnp.where(mask, values, 0.0), axis=1, keepdims=True)

    own = total(col == row, sizes)
    starts = total(col < row, sizes)
    ends = starts + own
    sources = src_segments.shape[1]
    number = lax.broadcasted_iota(jnp.int32, (sentences, sources), 0)
    count = total(jnp.broadcast_to(src_segments[...], (sentences, sources)) == number, 1.0)
    places = lax.broadcasted_iota(jnp.int32, (sentences, length), 1).astype(f32)

    def gather(edges, values):
        return jnp.sum(jnp.where(edges <= places, values, 0.0), axis=0, keepdims=True).astype(jnp.int32)

    bounds_ref[0:1, :] = gather(ends, own)
    bounds_ref[1:2, :] = lax.broadcasted_iota(jnp.int32, (1, length), 1) + 1
    bounds_ref[2:3, :] = gather(ends, count)
    bounds_ref[3:4, :] = gather(starts, count)
    bounds_ref[4:8, :] = jnp.zeros((4, length), jnp.int32)


def self_forward(tgt, attn, bounds, q, k, v, mix, lse, n1, s1, query_z, value_t, score_scr, out_scr, move, outs, steps):
    chunks = tgt.shape[0] // RC
    scale = jnp.array(HEAD_DIM**-0.5, bf16)

    def project(c):
        rows = rows_of(c, RC)
        x = tgt[rows, :]
        q[rows, :] = nn(x, weight(attn, 0)).astype(bf16) * scale
        k[rows, :] = nn(x, weight(attn, 1)).astype(bf16)
        v[rows, :] = nn(x, weight(attn, 2)).astype(bf16)

    each_chunk(chunks, project)
    for i, ref in enumerate((q, k, v)):
        move.start(ref, outs[i])
    spread_heads(query_z, q)
    value_t[...] = v[...].T
    attention(near_window, 0, bounds, k, value_t, query_z, mix, lse, score_scr, out_scr, steps)
    move.start(mix, outs[3])
    move.start(lse, outs[4])

    def middle(c):
        rows = rows_of(c, RC)
        normed, inverse = norm_parts(tgt[rows, :].astype(f32) + nn(mix[rows, :], weight(attn, 3)))
        n1[rows, :] = normed
        s1[rows, :] = inverse

    each_chunk(chunks, middle)
    move.start(n1, outs[5])
    move.start(s1, outs[6])


def middle_kernel(
    bounds_s, bounds_h, full, memory_h, cot_h, n1_h, s1_h,
    out_h, d1_h, mgrad_h, gffn_h, gcross_h, gnorm_ref,
    bounds, norm_b, attn, ffn, memory, cot, n1, s1, cq, ck, cv, cmix, clse, query_z, grad_z, turned, score_scr, small_scr,
    act_scr, dpre_scr, h2_scr, d3_scr, d2_scr, d2b_scr, grad_scr, dq_scr, dk_scr, dv_scr, out_scr, mgrad, gffn, gcross,
    sums, norm, sems,
):
    width = n1.shape[1]
    chunks = n1.shape[0] // RC
    scale = jnp.array(HEAD_DIM**-0.5, bf16)
    move = Mover(sems)
    rows_cross = attn.shape[1]
    norm_rows = pl.ds(full.shape[1] - 16, 16)
    load_small = [move.start(full.at[:, norm_rows, pl.ds(0, width // 4)], norm_b), move.start(bounds_h, bounds)]
    load_cross = move.start(full.at[:, pl.ds(rows_cross, rows_cross)], attn)
    load_n1 = move.start(n1_h, n1)
    load_memory = move.start(memory_h, memory)
    load_ffn = move.start(full.at[:, pl.ds(2 * rows_cross, ffn.shape[1])], ffn)
    load_rest = [move.start(cot_h, cot), move.start(s1_h, s1)]
    sums[...] = jnp.zeros_like(sums)
    move.wait(*load_small)
    load_norm_rows(norm, norm_b)
    move.wait(load_cross, load_n1, load_memory)

    def h1_of(rows):
        return n1[rows, :] * norm[0:1, :] + norm[1:2, :]

    def project(c):
        rows = rows_of(c, RC)
        cq[rows, :] = nn(h1_of(rows).astype(bf16), weight(attn, 0)).astype(bf16) * scale
        mem = memory[rows, :]
        ck[rows, :] = nn(mem, weight(attn, 1)).astype(bf16)
        cv[rows, :] = nn(mem, weight(attn, 2)).astype(bf16)

    each_chunk(chunks, project)
    spread_heads(query_z, cq)
    turned[...] = cv[...].T
    window = bound_window(bounds_s, 1)
    attention(window, 1, bounds, ck, turned, query_z, cmix, clse, score_scr, small_scr)
    move.wait(load_ffn, *load_rest)
    blocks = ffn.shape[0]
    parts = act_scr.shape[1] // width
    share = blocks // parts

    def outer(b):
        return ffn[share * b : share * (b + 1), 16 * parts :, :].reshape(width, width)

    def body(c):
        rows = rows_of(c, RC)
        n2, s2 = norm_parts(h1_of(rows) + nn(cmix[rows, :], weight(attn, 3)))
        h2 = n2 * norm[2:3, :] + norm[3:4, :]
        h2b = h2.astype(bf16)
        h2_scr[rows, :] = h2b
        third = h2
        slopes = []
        for b in range(parts):
            cols = slice(width * b, width * (b + 1))
            pre = nn(h2b, weight(ffn, b))
            sig = sigmoid(pre)
            swish = pre * sig
            act = swish.astype(bf16)
            act_scr[rows, cols] = act
            slopes.append(sig + swish * (1.0 - sig))
            third = third + nn(act, outer(b))
        n3, s3 = norm_parts(third)
        out_scr[rows, :] = (n3 * norm[4:5, :] + norm[5:6, :]).astype(bf16)
        up = cot[rows, :].astype(f32)
        sums[4] += fold_rows(up * n3)
        sums[5] += fold_rows(up)
        d3 = norm_back(up, n3, s3, norm[4:5, :])
        d3b = d3.astype(bf16)
        d3_scr[rows, :] = d3b
        dh2 = d3
        for b in range(parts):
            cols = slice(width * b, width * (b + 1))
            dpre = (nt(d3b, outer(b)) * slopes[b]).astype(bf16)
            dpre_scr[rows, cols] = dpre
            dh2 = dh2 + nt(dpre, weight(ffn, b))
        sums[2] += fold_rows(dh2 * n2)
        sums[3] += fold_rows(dh2)
        d2 = norm_back(dh2, n2, s2, norm[2:3, :])
        d2_scr[rows, :] = d2
        d2b = d2.astype(bf16)
        d2b_scr[rows, :] = d2b
        grad_scr[rows, :] = nt(d2b, weight(attn, 3)).astype(bf16)

    each_chunk(chunks, body)
    move.start(out_scr, out_h)
    for b in range(parts):
        cols = slice(width * b, width * (b + 1))
        gffn[share * b : share * (b + 1), 16 * parts :, :] = (
            tn(act_scr[:, cols], d3_scr[...]).astype(bf16).reshape(share, width // share, width)
        )
        put_gradient(gffn, b, tn(h2_scr[...], dpre_scr[:, cols]))
    move.start(gffn, gffn_h)
    put_gradient(gcross, 3, tn(cmix[...], d2b_scr[...]))
    spread_heads(grad_z, grad_scr)
    turned[...] = ck[...].T
    dk_scr[...] = jnp.zeros_like(dk_scr)
    dv_scr[...] = jnp.zeros_like(dv_scr)
    attention_back(
        window, 1, bounds, ck, turned, cv, query_z, grad_z, grad_scr, cmix, clse, dq_scr, dk_scr, dv_scr, small_scr,
    )

    def leave(c):
        rows = rows_of(c, RC)
        dkb = dk_scr[rows, :].astype(bf16)
        dvb = dv_scr[rows, :].astype(bf16)
        ck[rows, :] = dkb
        cv[rows, :] = dvb
        mgrad[rows, :] = (nt(dkb, weight(attn, 1)) + nt(dvb, weight(attn, 2))).astype(bf16)
        normed = n1[rows, :]
        h2_scr[rows, :] = h1_of(rows).astype(bf16)
        dh1 = d2_scr[rows, :] + nt(dq_scr[rows, :], weight(attn, 0))
        sums[0] += fold_rows(dh1 * normed)
        sums[1] += fold_rows(dh1)
        d2_scr[rows, :] = norm_back(dh1, normed, s1[rows, :], norm[0:1, :])

    each_chunk(chunks, leave)
    move.start(d2_scr, d1_h)
    move.start(mgrad, mgrad_h)
    for i in range(6):
        gnorm_ref[i : i + 1, :] = jnp.sum(sums[i], axis=0, keepdims=True)
    gnorm_ref[6:8, :] = jnp.zeros((2, width), f32)
    put_gradient(gcross, 0, tn(h2_scr[...], dq_scr[...]))
    put_gradient(gcross, 1, tn(memory[...], ck[...]))
    put_gradient(gcross, 2, tn(memory[...], cv[...]))
    move.start(gcross, gcross_h)
    move.finish()


def self_backward(
    tgt, attn, bounds, q, k, v, mix, lse, d1, tgrad, gself,
    query_z, grad_z, key_t, grad_scr, dq_scr, dk_scr, dv_scr, small_scr, d1_scr, steps, begin, late,
):
    chunks = tgt.shape[0] // RC

    def enter(c):
        rows = rows_of(c, RC)
        d1b = d1[rows, :].astype(bf16)
        d1_scr[rows, :] = d1b
        grad_scr[rows, :] = nt(d1b, weight(attn, 3)).astype(bf16)

    each_chunk(chunks, enter)
    put_gradient(gself, 3, tn(mix[...], d1_scr[...]))
    spread_heads(query_z, q)
    spread_heads(grad_z, grad_scr)
    key_t[...] = k[...].T
    dk_scr[...] = jnp.zeros_like(dk_scr)
    dv_scr[...] = jnp.zeros_like(dv_scr)
    begin()
    attention_back(
        near_window, 0, bounds, k, key_t, v, query_z, grad_z, grad_scr, mix, lse, dq_scr, dk_scr, dv_scr, small_scr, steps,
    )
    for i, scr in enumerate((dq_scr, dk_scr, dv_scr)):
        put_gradient(gself, i, tn(tgt[...], scr[...].astype(bf16)))
    late()

    def leave(c):
        rows = rows_of(c, RC)
        tgrad[rows, :] = (
            d1[rows, :]
            + nt(dq_scr[rows, :], weight(attn, 0))
            + nt(dk_scr[rows, :].astype(bf16), weight(attn, 1))
            + nt(dv_scr[rows, :].astype(bf16), weight(attn, 2))
        ).astype(bf16)

    each_chunk(chunks, leave)


def shape(dims, dtype):
    return jax.ShapeDtypeStruct(dims, dtype)


VMEM_SPEC = pl.BlockSpec(memory_space=pltpu.VMEM)
HBM_SPEC = pl.BlockSpec(memory_space=pltpu.HBM)
SMEM_SPEC = pl.BlockSpec(memory_space=pltpu.SMEM)


def vmem(*buffers):
    return [pltpu.VMEM(dims, dtype) for dims, dtype in buffers]


def dma(*dims):
    return pltpu.SemaphoreType.DMA(dims)


def adam_direction(master, gradient, moments):
    first_moment = beta_first * moments[0] + (1.0 - beta_first) * gradient
    second_moment = beta_second * moments[1] + (1.0 - beta_second) * gradient * gradient
    first_fix = 1.0 - beta_first**STEP
    second_fix = 1.0 - beta_second**STEP
    direction = (
        first_moment / first_fix / (jnp.sqrt(second_moment / second_fix) + adam_eps)
        + decay_rate * master
    )
    return (direction, first_moment, second_moment)


MESH = pl.DeviceIdType.MESH


class Place:
    def __init__(self):
        self.gx = lax.axis_index("gx")
        self.gy = lax.axis_index("gy")
        self.x = lax.rem(self.gx, 2)
        self.y = self.gx // 2
        self.z = self.gy // 2
        self.c = lax.rem(self.gy, 2)
        self.here = self.gx * 8 + self.gy

    def target(self, x, y, z, c):
        return (y * 2 + x, z * 2 + c)

    def index(self, x, y, z, c):
        return (y * 2 + x) * 8 + z * 2 + c

    def others(self):
        found = []
        for step in range(1, 32):
            device = lax.rem(self.here + step, 32)
            found.append((device // 8, lax.rem(device, 8)))
        return found


def greet(targets):
    barrier = pltpu.get_barrier_semaphore()
    for target in targets:
        pl.semaphore_signal(barrier, inc=1, device_id=target, device_id_type=MESH)
    pl.semaphore_wait(barrier, len(targets))


def remote(src, dst, send_sem, recv_sem, target):
    return pltpu.make_async_remote_copy(
        src_ref=src, dst_ref=dst, send_sem=send_sem, recv_sem=recv_sem, device_id=target, device_id_type=MESH
    )


def forward_sizes(length, width):
    pairs = width // LANES
    row = (length, width)
    lse = (length // QB, pairs, 2 * QB)
    kept = [(row, bf16)] * 4 + [(lse, f32), (row, f32), ((length, 1), f32)]
    scratch = [
        ((pairs, 2 * length, LANES), bf16), ((width, length), bf16),
        ((pairs, LONGEST + 2 * KB, 2 * QB), f32), ((pairs, LANES, QB), f32),
    ]
    return kept, scratch


class Gathering:
    parts = ((0, 32), (32, 32), (64, 96), (160, 112))

    def __init__(self, me, mine, near, full, zsend, xsend, ysend, csend, recv, crecv):
        self.me, self.mine, self.near, self.full = me, mine, near, full
        self.zsend, self.xsend, self.ysend, self.csend, self.recv, self.crecv = zsend, xsend, ysend, csend, recv, crecv
        x, y, z, c = me.x, me.y, me.z, me.c
        self.ox, self.oy, self.oc = 1 - x, 1 - y, 1 - c
        self.x_next = me.target(self.ox, y, z, c)
        self.y_next = me.target(x, self.oy, z, c)
        self.sibling = me.target(x, y, z, self.oc)
        self.up = me.target(x, y, lax.rem(z + 1, 4), c)
        self.down = me.target(x, y, lax.rem(z + 3, 4), c)

    def held(self, part):
        return self.near if part < 2 else self.full

    def copy(self, column, zz, part, target, sem, own=False):
        rows = pl.ds(*self.parts[part])
        c = self.me.c
        dst = self.held(part).at[column, zz, c, rows]
        return remote(self.mine.at[rows] if own else dst, dst, sem, self.recv.at[column, zz, part], target)

    def arrive(self, column, zz, part):
        self.copy(column, zz, part, self.sibling, self.xsend.at[part]).wait_recv()

    def to_x(self, column, zz, part, own=False):
        self.copy(column, zz, part, self.x_next, self.xsend.at[part], own).start()

    def to_y(self, column, zz, part, own=False):
        self.copy(column, zz, part, self.y_next, self.ysend.at[part], own).start()

    def column(self, x, y):
        return y * 2 + x

    def along(self, zz, part, upward, own=False):
        me = self.me
        target = self.up if upward else self.down
        sem = self.zsend.at[zz, part, 0 if upward else 1]

        @pl.when((me.z < 3) if upward else (me.z > 0))
        def _():
            self.copy(me.gx, zz, part, target, sem, own).start()

    def own_z(self, parts):
        for part in parts:
            self.along(self.me.z, part, True, True)
            self.along(self.me.z, part, False, True)

    def own_sides(self, parts):
        for part in parts:
            self.to_x(self.me.gx, self.me.z, part, True)
            self.to_y(self.me.gx, self.me.z, part, True)

    def at_distance(self, d, action):
        z = self.me.z
        if d == 0:
            action(z, None)
            return

        @pl.when(z >= d)
        def _():
            action(z - d, True)

        @pl.when(z + d <= 3)
        def _():
            action(z + d, False)

    def inline(self, d, parts):
        me = self.me

        def action(zz, upward):
            for part in parts:
                self.arrive(me.gx, zz, part)
                self.along(zz, part, upward)
                self.to_x(me.gx, zz, part)
                self.to_y(me.gx, zz, part)

        self.at_distance(d, action)

    def side(self, d, parts):
        me = self.me

        def action(zz, _):
            for part in parts:
                if part % 2 == 0:
                    column = self.column(self.ox, me.y)
                    self.arrive(column, zz, part)
                    self.to_y(column, zz, part)
                else:
                    column = self.column(me.x, self.oy)
                    self.arrive(column, zz, part)
                    self.to_x(column, zz, part)

        self.at_distance(d, action)

    def last_columns(self, part):
        last = (self.me.x, self.oy) if part % 2 == 0 else (self.ox, self.me.y)
        return (self.column(*last), self.column(self.ox, self.oy))

    def far(self, d, parts):
        def action(zz, _):
            for part in parts:
                for column in self.last_columns(part):
                    self.arrive(column, zz, part)

        self.at_distance(d, action)

    def core(self, column, part):
        rows = pl.ds(*self.parts[part])
        block = self.held(part).at[column, :, self.me.c, rows]
        return remote(block, block, self.csend.at[column, part], self.crecv.at[column, part], self.sibling)

    def core_inline(self, parts):
        for part in parts:
            self.core(self.me.gx, part).start()

    def core_side(self, parts):
        me = self.me
        for part in parts:
            self.core(self.column(self.ox, me.y) if part % 2 == 0 else self.column(me.x, self.oy), part).start()

    def core_far(self, parts):
        for part in parts:
            for column in self.last_columns(part):
                self.core(column, part).start()

    def cores(self, parts):
        for part in parts:
            for column in range(4):
                self.core(column, part).wait_recv()

    def sent(self, parts):
        me = self.me
        for part in parts:
            for zz in range(4):

                @pl.when((me.z < 3) & (zz <= me.z))
                def _():
                    self.copy(me.gx, zz, part, self.up, self.zsend.at[zz, part, 0]).wait_send()

                @pl.when((me.z > 0) & (zz >= me.z))
                def _():
                    self.copy(me.gx, zz, part, self.down, self.zsend.at[zz, part, 1]).wait_send()

            rows = pl.ds(*self.parts[part])
            four, eight = self.held(part).at[0, :, 0, rows], self.held(part).at[pl.ds(0, 2), :, 0, rows]
            sems = (self.xsend.at[part], self.ysend.at[part])
            few, many = sems if part % 2 == 0 else sems[::-1]
            remote(four, four, few, self.recv.at[0, 0, part], self.sibling).wait_send()
            remote(eight, eight, many, self.recv.at[0, 0, part], self.sibling).wait_send()
            for column in range(4):
                self.core(column, part).wait_send()

    def stages(self, parts):
        return [
            lambda: self.inline(1, parts),
            lambda: (self.side(0, parts), self.inline(2, parts)),
            lambda: (self.side(1, parts), self.inline(3, parts), self.core_inline(parts)),
            lambda: (self.side(2, parts), self.far(0, parts)),
            lambda: (self.side(3, parts), self.core_side(parts), self.far(1, parts)),
            lambda: (self.far(2, parts), self.far(3, parts), self.core_far(parts)),
        ]


def first_kernel(
    attn_h, inner_h, outer_h, norm_h, lengths_h, src_h, tgt_h,
    full, bounds_out, q_h, k_h, v_h, mix_h, lse_h, n1_h, s1_h,
    attn_f, inner_f, outer_f, norm_f, lengths, src, mine, bounds, tgt, attn,
    q, k, v, mix, lse, n1, s1, query_z, value_t, score_scr, small_scr,
    sems, zsend, xsend, ysend, csend, recv, crecv,
):
    me = Place()
    move = Mover(sems)
    loads = [
        move.start(a, b)
        for a, b in (
            (attn_h, attn_f), (inner_h, inner_f), (outer_h, outer_f), (norm_h, norm_f), (lengths_h, lengths), (src_h, src),
        )
    ]
    load_tgt = move.start(tgt_h, tgt)
    gathering = Gathering(me, mine, attn, full, zsend, xsend, ysend, csend, recv, crecv)
    barrier = pltpu.get_barrier_semaphore()

    def greet(target):
        pl.semaphore_signal(barrier, inc=1, device_id=target, device_id_type=MESH)

    for target in (gathering.x_next, gathering.y_next, gathering.sibling):
        greet(target)

    @pl.when(me.z < 3)
    def _():
        greet(gathering.up)

    @pl.when(me.z > 0)
    def _():
        greet(gathering.down)

    move.wait(*loads)
    for j in range(8):
        mine[16 * j : 16 * j + 16, :] = attn_f[j].astype(bf16)
    for b in range(4):
        mine[128 + 16 * b : 144 + 16 * b, :] = inner_f[:, 512 * b : 512 * b + 512].astype(bf16)
    mine[192:256, :] = outer_f[...].astype(bf16)
    lanes = jnp.concatenate([norm_f[...], jnp.zeros((6, 112), f32)], axis=1)
    lanes = jnp.concatenate([lanes, jnp.zeros((10, 128), f32)], axis=0)
    lanes = pltpu.roll(lanes, me.gy * 16, 1).astype(bf16)
    mine[256:272, :] = jnp.concatenate([lanes, jnp.zeros((16, 384), bf16)], axis=1)
    attn[me.gx, me.z, me.c] = mine[0:64, :]
    ends = jnp.where(me.z > 0, 1, 0) + jnp.where(me.z < 3, 1, 0)
    pl.semaphore_wait(barrier, 3 + ends)
    early, late = (0, 1), (2, 3)
    gathering.own_z(early)
    gathering.own_sides(early)
    gathering.own_z(late)
    gathering.own_sides(late)
    keep = move.start(mine.at[pl.ds(64, 208)], full.at[me.gx, me.z, me.c, pl.ds(64, 208)])
    find_bounds(lengths, src, bounds)
    move.start(bounds, bounds_out)
    sooner, later = gathering.stages(early), gathering.stages(late)
    for stage in (*sooner[:3], later[0], sooner[3], later[1], sooner[4], sooner[5]):
        stage()
    move.wait(keep)
    later[2]()
    gathering.cores(early)
    move.start(attn, full.at[:, :, :, pl.ds(0, 64)])
    move.wait(load_tgt)
    self_forward(
        tgt, attn.reshape(32, 64, 512), bounds, q, k, v, mix, lse, n1, s1, query_z, value_t, score_scr, small_scr,
        move, (q_h, k_h, v_h, mix_h, lse_h, n1_h, s1_h),
        (None, later[3], None, later[4], None, later[5]),
    )
    gathering.cores(late)
    gathering.sent(early + late)
    move.finish()


def gather_and_start(params, lengths, src_segments, tgt):
    length, width = tgt.shape
    kept, scratch = forward_sizes(length, width)
    row = (length, width)
    bounds = ((8, length), jnp.int32)
    full = ((4, 4, 2, 272, 512), bf16)
    loads = [(p.shape, f32) for p in params] + [(lengths.shape, jnp.int32), (src_segments.shape, jnp.int32)]
    return pl.pallas_call(
        first_kernel,
        out_shape=tuple(shape(*item) for item in [full, bounds] + kept),
        in_specs=[HBM_SPEC] * 7,
        out_specs=(HBM_SPEC,) * 9,
        scratch_shapes=vmem(
            *loads, ((272, 512), bf16), bounds, (row, bf16), ((4, 4, 2, 64, 512), bf16), *kept, *scratch,
        )
        + [dma(24), dma(4, 4, 2), dma(4), dma(4), dma(4, 4), dma(4, 4, 4), dma(4, 4)],
        compiler_params=pltpu.CompilerParams(collective_id=0, has_side_effects=True, vmem_limit_bytes=GRANT),
    )(*params, lengths, src_segments, tgt)


def start_kernel(
    full, lengths, src, tgt, bounds_out, q_h, k_h, v_h, mix_h, lse_h, n1_h, s1_h,
    bounds, attn, q, k, v, mix, lse, n1, s1, query_z, value_t, score_scr, small_scr, sems,
):
    move = Mover(sems)
    load = move.start(full.at[:, pl.ds(0, attn.shape[1])], attn)
    find_bounds(lengths, src, bounds)
    move.start(bounds, bounds_out)
    move.wait(load)
    self_forward(
        tgt, attn, bounds, q, k, v, mix, lse, n1, s1, query_z, value_t, score_scr, small_scr,
        move, (q_h, k_h, v_h, mix_h, lse_h, n1_h, s1_h), (),
    )
    move.finish()


def start_only(full, lengths, src_segments, tgt):
    length, width = tgt.shape
    kept, scratch = forward_sizes(length, width)
    bounds = ((8, length), jnp.int32)
    return pl.pallas_call(
        start_kernel,
        out_shape=tuple(shape(*item) for item in [bounds] + kept),
        in_specs=[HBM_SPEC] + [VMEM_SPEC] * 3,
        out_specs=(HBM_SPEC,) * 8,
        scratch_shapes=vmem(bounds, ((full.shape[0], 64, width), bf16), *kept, *scratch) + [dma(16)],
        compiler_params=pltpu.CompilerParams(vmem_limit_bytes=GRANT),
    )(full, lengths, src_segments, tgt)


def middle(bounds, full, memory, cotangent, n1, s1):
    length, width = n1.shape
    keys = memory.shape[0]
    blocks = full.shape[0]
    ffn_rows = full.shape[1] - 144
    hidden = ffn_rows * blocks // 2 * full.shape[2] // width
    pairs = width // LANES
    row, mem_row = (length, width), (keys, width)
    zeroed = ((pairs, 2 * length, LANES), bf16)
    gffn, gcross = ((blocks, ffn_rows, width), bf16), ((blocks, 64, width), bf16)
    outs = [(row, bf16), (row, f32), (mem_row, bf16), gffn, gcross, ((8, width), f32)]
    scratch = vmem(
        (bounds.shape, jnp.int32), ((blocks, 16, width // 4), bf16), gcross, gffn, (mem_row, bf16), (row, bf16), (row, f32),
        ((length, 1), f32), (row, bf16), (mem_row, bf16), (mem_row, bf16), (row, bf16),
        ((length // QB, pairs, 2 * QB), f32), zeroed, zeroed, ((width, keys), bf16), ((pairs, keys + KB, 2 * QB), f32),
        ((pairs, LANES, QB), f32), ((length, hidden), bf16), ((length, hidden), bf16), (row, bf16), (row, bf16),
        (row, f32), (row, bf16), (row, bf16), (row, bf16), (mem_row, f32), (mem_row, f32), (row, bf16), (mem_row, bf16),
        gffn, gcross, ((6, 8, width), f32), ((8, width), f32),
    )
    return pl.pallas_call(
        middle_kernel,
        out_shape=tuple(shape(*item) for item in outs),
        in_specs=[SMEM_SPEC] + [HBM_SPEC] * 6,
        out_specs=(HBM_SPEC,) * 5 + (VMEM_SPEC,),
        scratch_shapes=scratch + [dma(16)],
        compiler_params=pltpu.CompilerParams(vmem_limit_bytes=GRANT),
    )(bounds, bounds, full, memory, cotangent, n1, s1)


OUTER_ROWS = slice(96, 160)


def attn_rows(j):
    return 192 + 16 * j if j < 4 else 64 + 16 * (j - 4) if j < 6 else 160 + 16 * (j - 6)


def add_rows(dst, *sources):
    total = sources[0][...].astype(f32)
    for source in sources[1:]:
        total = total + source[...].astype(f32)
    dst[...] = total.astype(dst.dtype)


class Summing:
    order = (2, 1, 3, 0)

    def __init__(self, me, sources, rows, pieces, first_a, first_b, second_a, second_b, third, result, sems):
        self.me, self.sources, self.rows, self.pieces = me, sources, rows, pieces
        self.first_a, self.first_b, self.second_a, self.second_b, self.third = first_a, first_b, second_a, second_b, third
        self.result = result
        (self.lsem, self.csend, self.crecv, self.send1, self.recv1, self.send2, self.recv2, self.send3, self.recv3) = sems
        x, y, z, c = me.x, me.y, me.z, me.c
        self.ox, self.oy, self.oc = 1 - x, 1 - y, 1 - c
        self.x_next = me.target(self.ox, y, z, c)
        self.y_next = me.target(x, self.oy, z, c)
        self.sibling = me.target(x, y, z, self.oc)
        self.zs = [lax.rem(z + d, 4) for d in range(4)]
        self.half = first_a.shape[2]
        self.top, self.bottom = pl.ds(0, self.half), pl.ds(self.half, self.half)
        self.pending, self.cores, self.own = [], {}, {}
        self.firsts, self.seconds, self.thirds = {}, {}, {}

    def send(self, *args):
        copy = remote(*args)
        copy.start()
        self.pending.append(copy)
        return copy

    def load(self):
        for d in self.order:
            for k, (source, kept, _) in enumerate(self.sources):
                if kept is not None:
                    copy = pltpu.make_async_copy(source.at[:, self.zs[d], self.me.c], kept.at[d], self.lsem.at[d, k])
                    copy.start()
                    self.own[d, k] = copy

    def core(self):
        for d in self.order:
            for k, (source, _, got) in enumerate(self.sources):
                self.cores[d, k] = self.send(
                    source.at[:, self.zs[d], self.oc], got.at[d], self.csend.at[d, k], self.crecv.at[d, k], self.sibling
                )

    def stage1(self, d):
        me = self.me
        for k in range(len(self.sources)):
            if (d, k) in self.own:
                self.own[d, k].wait()
            self.cores[d, k].wait_recv()

        def add(i):
            piece = self.pieces.at[d, i // 2, lax.rem(i, 2)]
            for start, count, k, first in self.rows:
                source, kept, got = self.sources[k]
                held = source.at[i, self.zs[d], me.c] if kept is None else kept.at[d, i]
                part = pl.ds(first, count)
                add_rows(piece.at[pl.ds(start, count)], held.at[part], got.at[d, i, part])

        each_chunk(4, add)
        self.firsts[d] = (
            self.send(
                self.pieces.at[d, self.oy, :, self.top], self.first_a.at[d], self.send1.at[d, 0], self.recv1.at[d, 0],
                self.y_next,
            ),
            self.send(
                self.pieces.at[d, :, self.ox, self.bottom], self.first_b.at[d], self.send1.at[d, 1],
                self.recv1.at[d, 1], self.x_next,
            ),
        )

    def stage2(self, d):
        me = self.me
        self.firsts[d][0].wait_recv()
        part = self.pieces.at[d, me.y, self.ox, self.top]
        add_rows(part, part, self.first_a.at[d, self.ox])
        one = self.send(part, self.second_a.at[d], self.send2.at[d, 0], self.recv2.at[d, 0], self.x_next)
        self.firsts[d][1].wait_recv()
        part = self.pieces.at[d, self.oy, me.x, self.bottom]
        add_rows(part, part, self.first_b.at[d, self.oy])
        two = self.send(part, self.second_b.at[d], self.send2.at[d, 1], self.recv2.at[d, 1], self.y_next)
        self.seconds[d] = (one, two)

    def stage3(self, d):
        me = self.me
        for copy in self.seconds[d]:
            copy.wait_recv()
        for rows, first, second, at in (
            (self.top, self.first_a, self.second_a, me.x), (self.bottom, self.first_b, self.second_b, me.y),
        ):
            part = self.pieces.at[d, me.y, me.x, rows]
            add_rows(part if d else self.result.at[rows], part, first.at[d, at], second.at[d])
        if d:
            self.thirds[d] = self.send(
                self.pieces.at[d, me.y, me.x], self.third.at[d - 1], self.send3.at[d - 1], self.recv3.at[d - 1],
                me.target(me.x, me.y, self.zs[d], me.c),
            )

    def end(self):
        for d in (1, 2, 3):
            self.thirds[d].wait_recv()
        add_rows(self.result, self.result, self.third.at[0], self.third.at[1], self.third.at[2])


def last_kernel(
    full, bounds_h, tgt_h, q_h, k_h, v_h, mix_h, lse_h, d1_h, gffn, gcross, gnorm_h,
    attn_p, inner_p, outer_p, norm_p, attn_m, in_m, out_m, norm_m,
    tgrad_h, g_ref, gn_ref, totals_ref,
    bounds, tgt, attn, q, k, v, mix, lse, d1, tgrad, gself, query_z, grad_z, key_t, grad_scr, dq_scr, dk_scr, dv_scr,
    small_scr, d1_scr, own_ffn, own_cross, got_ffn, got_cross, pieces, first_a, first_b, second_a, second_b, third,
    got_self, pieces2, first_a2, first_b2, second_a2, second_b2, third2, vectors, tiles,
    msems, psems, *sems,
):
    me = Place()
    move = Mover(msems)
    others = me.others()
    barrier = pltpu.get_barrier_semaphore()
    for target in others:
        pl.semaphore_signal(barrier, inc=1, device_id=target, device_id_type=MESH)
    load_first = [move.start(a, b) for a, b in ((d1_h, d1), (full.at[:, pl.ds(0, 64)], attn), (gnorm_h, vectors.at[0]))]
    load_mix = move.start(mix_h, mix)
    load_rest = [
        move.start(a, b)
        for a, b in ((q_h, q), (k_h, k), (v_h, v), (lse_h, lse), (bounds_h, bounds), (tgt_h, tgt))
    ]
    sems1, sems2, (nsend, nrecv, tsend, trecv) = sems[0:9], sems[9:18], sems[18:22]
    big = Summing(
        me, [(gffn, own_ffn, got_ffn), (gcross, own_cross, got_cross)],
        [(0, 64, 0, 0), (64, 32, 1, 0), (96, 64, 0, 64), (160, 32, 1, 32)],
        pieces, first_a, first_b, second_a, second_b, third, g_ref.at[pl.ds(0, 192)], sems1,
    )
    rest = Summing(
        me, [(gself, None, got_self)], [(0, 64, 0, 0)],
        pieces2, first_a2, first_b2, second_a2, second_b2, third2, g_ref.at[pl.ds(192, 64)], sems2,
    )
    big.load()
    move.wait(*load_first)
    pl.semaphore_wait(barrier, len(others))
    big.core()
    norm_copies = [big.send(vectors.at[0], vectors.at[1], nsend.at[0], nrecv.at[0], big.sibling)]

    def norm_step(stage, target):
        norm_copies[-1].wait_recv()
        vectors[2 * stage] = vectors[2 * stage - 2] + vectors[2 * stage - 1]
        norm_copies.append(
            big.send(vectors.at[2 * stage], vectors.at[2 * stage + 1], nsend.at[stage], nrecv.at[stage], target)
        )

    def norm_last():
        norm_copies[-1].wait_recv()
        vectors[6] = vectors[4] + vectors[5]
        for d in range(1, 4):
            target = me.target(me.x, me.y, big.zs[d], me.c)
            norm_copies.append(big.send(vectors.at[6], vectors.at[6 + d], nsend.at[2 + d], nrecv.at[2 + d], target))

    far, up, down, here = big.order
    steps = [
        None,
        lambda: norm_step(1, big.x_next),
        None,
        lambda: (big.stage2(far), big.stage1(down), norm_step(2, big.y_next)),
        None,
        lambda: (big.stage2(up), big.stage3(far), big.stage1(here), norm_last()),
        None,
        lambda: (big.stage2(down), big.stage3(up)),
    ]

    def begin():
        big.stage1(far)
        big.stage1(up)

    def late():
        rest.core()
        big.stage2(here)
        big.stage3(down)

    move.wait(load_mix, *load_rest)
    self_backward(
        tgt, attn, bounds, q, k, v, mix, lse, d1, tgrad, gself.reshape(32, 64, 512),
        query_z, grad_z, key_t, grad_scr, dq_scr, dk_scr, dv_scr, small_scr, d1_scr, steps, begin, late,
    )
    move.start(tgrad, tgrad_h)
    rest.stage1(far)
    rest.stage1(up)
    big.stage3(here)
    rest.stage2(far)
    rest.stage1(down)
    rest.stage2(up)
    rest.stage3(far)
    rest.stage1(here)
    rest.stage2(down)
    rest.stage3(up)
    rest.stage2(here)
    rest.stage3(down)
    rest.stage3(here)
    big.end()
    for copy in norm_copies[3:]:
        copy.wait_recv()
    vectors[10] = (vectors[6] + vectors[8]) + (vectors[7] + vectors[9])
    lanes = vectors[10, :, pl.ds(pl.multiple_of(me.gx * 128, 128), 128)]
    gn_ref[...] = pltpu.roll(lanes, lax.rem(128 - me.gy * 16, 128), 1)
    lane = lax.broadcasted_iota(jnp.int32, (1, 128), 1)
    rows = [jnp.zeros((1, 128), f32), jnp.zeros((1, 128), f32)]

    def put(t, pairs):
        for i in range(2):
            square = sum(jnp.sum(pair[i] * pair[i]) for pair in pairs)
            rows[i] = rows[i] + jnp.where(lane == t, square, 0.0)

    def direction(*args):
        return adam_direction(*args)[0]

    def put_attn(j):
        grad = g_ref[attn_rows(j) : attn_rows(j) + 16, :]
        put(j, [(attn_p[j], direction(attn_p[j], grad, (attn_m[0, j], attn_m[1, j])))])

    for j in range(4, 8):
        put_attn(j)
    pairs = []
    for b in range(4):
        cols = slice(512 * b, 512 * b + 512)
        grad = g_ref[16 * b : 16 * b + 16, :]
        pairs.append((inner_p[:, cols], direction(inner_p[:, cols], grad, (in_m[0, :, cols], in_m[1, :, cols]))))
    put(8, pairs)
    put(9, [(outer_p[...], direction(outer_p[...], g_ref[OUTER_ROWS, :], (out_m[0], out_m[1])))])
    master = norm_p[...]
    update = direction(master, gn_ref[0:6, 0:16], (norm_m[0], norm_m[1]))
    for i in range(6):
        put(10 + i, [(master[i : i + 1], update[i : i + 1])])
    rest.end()
    for j in range(4):
        put_attn(j)
    tiles[me.here] = jnp.concatenate([rows[0], rows[1], jnp.zeros((6, 128), f32)], axis=0)
    for i, target in enumerate(others):
        big.send(tiles.at[me.here], tiles.at[me.here], tsend.at[i], trecv.at[me.here], target)
    for i, target in enumerate(others):
        source = target[0] * 8 + target[1]
        remote(tiles.at[source], tiles.at[source], tsend.at[i], trecv.at[source], target).wait_recv()
    totals_ref[...] = jnp.sum(tiles[...], axis=0)
    for copy in big.pending + rest.pending:
        copy.wait_send()
    move.finish()


def backward_scratch(length, width):
    pairs = width // LANES
    row = (length, width)
    zeroed = ((pairs, 2 * length, LANES), bf16)
    return [
        zeroed, zeroed, ((width, length), bf16), (row, bf16), (row, bf16), (row, f32), (row, f32),
        ((pairs, LANES, QB), f32), (row, bf16),
    ]


def finish_and_reduce(full, bounds, tgt, saved, d1, grads, norm_grad, params, moments):
    length, width = tgt.shape
    row = (length, width)
    lse = (length // QB, width // LANES, 2 * QB)

    def sums(half):
        return [
            ((4, 2, 2, 2 * half, 512), bf16), ((4, 2, half, 512), bf16), ((4, 2, half, 512), bf16),
            ((4, half, 512), bf16), ((4, half, 512), bf16), ((3, 2 * half, 512), bf16),
        ]

    scratch = vmem(
        (bounds.shape, jnp.int32), (row, bf16), ((32, 64, 512), bf16), *[(row, bf16)] * 4, (lse, f32), (row, f32),
        (row, bf16), ((4, 4, 2, 64, 512), bf16), *backward_scratch(length, width),
        ((4, 4, 128, 512), bf16), ((4, 4, 64, 512), bf16), ((4, 4, 128, 512), bf16), ((4, 4, 64, 512), bf16), *sums(96),
        ((4, 4, 64, 512), bf16), *sums(32), ((11, 8, 512), f32), ((32, 8, 128), f32),
    )
    round_sems = [dma(4, 2), dma(4, 2), dma(4, 2), dma(4, 2), dma(4, 2), dma(4, 2), dma(4, 2), dma(3), dma(3)]
    split = [grad.reshape(4, 4, 2, grad.shape[1], 512) for grad in grads]
    return pl.pallas_call(
        last_kernel,
        out_shape=(shape(row, bf16), shape((256, 512), f32), shape((8, 128), f32), shape((8, 128), f32)),
        in_specs=[HBM_SPEC] * 12 + [VMEM_SPEC] * 8,
        out_specs=(HBM_SPEC, VMEM_SPEC, VMEM_SPEC, VMEM_SPEC),
        scratch_shapes=scratch + [dma(16), dma(1)] + round_sems + round_sems + [dma(6), dma(6), dma(31), dma(32)],
        compiler_params=pltpu.CompilerParams(collective_id=1, has_side_effects=True, vmem_limit_bytes=GRANT),
    )(full, bounds, tgt, *saved, d1, *split, norm_grad, *params, *moments)


def finish_kernel(
    full, bounds, tgt, q, k, v, mix, lse, d1, tgrad, gself,
    attn, query_z, grad_z, key_t, grad_scr, dq_scr, dk_scr, dv_scr, small_scr, d1_scr, sems,
):
    move = Mover(sems)
    move.wait(move.start(full.at[:, pl.ds(0, attn.shape[1])], attn))
    self_backward(
        tgt, attn, bounds, q, k, v, mix, lse, d1, tgrad, gself,
        query_z, grad_z, key_t, grad_scr, dq_scr, dk_scr, dv_scr, small_scr, d1_scr, (), lambda: None, lambda: None,
    )


def finish_only(full, bounds, tgt, saved, d1):
    length, width = tgt.shape
    gself = ((full.shape[0], 64, width), bf16)
    return pl.pallas_call(
        finish_kernel,
        out_shape=(shape((length, width), bf16), shape(*gself)),
        in_specs=[HBM_SPEC] + [VMEM_SPEC] * 8,
        out_specs=(VMEM_SPEC, VMEM_SPEC),
        scratch_shapes=vmem(gself, *backward_scratch(length, width)) + [dma(2)],
        compiler_params=pltpu.CompilerParams(vmem_limit_bytes=GRANT),
    )(full, bounds, tgt, *saved, d1)


def update_kernel(
    g_ref, gn_ref, totals_ref, attn, inner, outer, norm, attn_m, in_m, out_m, norm_m,
    attn_new, in_new, out_new, norm_new, attn_first, attn_second, in_first, in_second, out_first, out_second,
    norm_first, norm_second, attn_copy, in_copy, out_copy, norm_copy, norms_ref,
):
    roots = jnp.sqrt(totals_ref[...])
    norms_ref[...] = roots[0:2, 0:16]
    ratio = learn_rate * (roots[0:1, :] / roots[1:2, :])

    def step(t, master, gradient, moments, new, first, second, copy, place):
        direction, first_moment, second_moment = adam_direction(master, gradient, moments)
        value = master - ratio[:, t : t + 1] * direction
        new[place] = value
        first[place] = first_moment
        second[place] = second_moment
        copy[place] = value.astype(bf16)

    for j in range(8):
        grad = g_ref[attn_rows(j) : attn_rows(j) + 16, :]
        step(j, attn[j], grad, (attn_m[0, j], attn_m[1, j]), attn_new, attn_first, attn_second, attn_copy, j)
    for b in range(4):
        cols = slice(512 * b, 512 * b + 512)
        place = (slice(None), cols)
        grad = g_ref[16 * b : 16 * b + 16, :]
        step(8, inner[:, cols], grad, (in_m[0, :, cols], in_m[1, :, cols]), in_new, in_first, in_second, in_copy, place)
    step(9, outer[...], g_ref[OUTER_ROWS, :], (out_m[0], out_m[1]), out_new, out_first, out_second, out_copy, ...)
    for i in range(6):
        one = slice(i, i + 1)
        moments = (norm_m[0, one], norm_m[1, one])
        step(10 + i, norm[one], gn_ref[one, 0:16], moments, norm_new, norm_first, norm_second, norm_copy, one)


def update_params(summed, params, moments):
    outs = [shape(p.shape, f32) for p in params]
    outs += [shape(p.shape, f32) for p in params for _ in range(2)]
    outs += [shape(p.shape, bf16) for p in params] + [shape((2, 16), f32)]
    return pl.pallas_call(
        update_kernel,
        out_shape=tuple(outs),
        in_specs=[VMEM_SPEC] * 11,
        out_specs=(VMEM_SPEC,) * len(outs),
        compiler_params=pltpu.CompilerParams(vmem_limit_bytes=GRANT),
    )(*summed, *params, *moments)


def tensor_squares(attn_part, inner_part, outer_part, norm_part):
    return jnp.concatenate(
        [
            jnp.sum(attn_part * attn_part, axis=(1, 2)),
            jnp.sum(inner_part * inner_part)[None],
            jnp.sum(outer_part * outer_part)[None],
            jnp.sum(norm_part * norm_part, axis=1),
        ]
    )


def blocked(matrix, width):
    blocks = matrix.shape[0] // 16
    cols = matrix.shape[1] // width
    return matrix.reshape(blocks, 16, cols, width).transpose(0, 2, 1, 3).reshape(blocks, cols * 16, width)


def unblocked(blocks, width):
    count = blocks.shape[0]
    cols = blocks.shape[1] // 16
    return blocks.reshape(count, cols, 16, width).transpose(0, 2, 1, 3).reshape(count * 16, cols * width)


def gather_any(attn_w, ffn_in, ffn_out, norm_params):
    width = attn_w.shape[2]
    attn = lax.all_gather(attn_w.astype(bf16), AXES, axis=1, tiled=True)
    inner = lax.all_gather(ffn_in.astype(bf16), AXES, axis=0, tiled=True)
    outer = lax.all_gather(ffn_out.astype(bf16), AXES, axis=0, tiled=True)
    norm = lax.all_gather(norm_params.astype(bf16), AXES, axis=1, tiled=True)
    blocks = width // 16
    attn = attn.reshape(8, blocks, 16, width).transpose(1, 0, 2, 3).reshape(blocks, 8 * 16, width)
    lanes = jnp.pad(norm, ((0, 10), (0, 0))).reshape(16, 4, 1, width // 4).transpose(1, 2, 0, 3)
    lanes = jnp.pad(lanes, ((0, 0), (0, blocks // 4 - 1), (0, 0), (0, width - width // 4))).reshape(blocks, 16, width)
    return jnp.concatenate([attn, blocked(inner, width), outer.reshape(blocks, -1, width), lanes], axis=1)


def reduce_any(grads, norm_grad, params, moments):
    grad_ffn, grad_cross, grad_self = grads
    width = grad_ffn.shape[2]
    blocks = width // 16
    attn_w, ffn_in, ffn_out, norm_params = params
    attn_m, in_m, out_m, norm_m = moments
    stack = jnp.concatenate([grad_self, grad_cross], axis=1)
    stack = stack.reshape(blocks, 8, 16, width).transpose(1, 0, 2, 3).reshape(8, width, width)
    rows = ffn_in.shape[1] // width * 16
    inner = unblocked(grad_ffn[:, :rows], width)
    outer = grad_ffn[:, rows:].reshape(-1, width)
    shard_attn = lax.psum_scatter(stack, AXES, scatter_dimension=1, tiled=True).astype(f32)
    shard_inner = lax.psum_scatter(inner, AXES, scatter_dimension=0, tiled=True).astype(f32)
    shard_outer = lax.psum_scatter(outer, AXES, scatter_dimension=0, tiled=True).astype(f32)
    shard_norm = lax.psum_scatter(norm_grad, AXES, scatter_dimension=1, tiled=True)
    attn_dir, attn_first, attn_second = adam_direction(attn_w, shard_attn, attn_m)
    inner_dir, inner_first, inner_second = adam_direction(ffn_in, shard_inner, in_m)
    outer_dir, outer_first, outer_second = adam_direction(ffn_out, shard_outer, out_m)
    norm_dir, norm_first, norm_second = adam_direction(norm_params, shard_norm, norm_m)
    weight_total, update_total = lax.psum(
        (tensor_squares(*params), tensor_squares(attn_dir, inner_dir, outer_dir, norm_dir)), AXES
    )
    ratio = jnp.sqrt(weight_total) / jnp.sqrt(update_total)
    attn_new = attn_w - learn_rate * ratio[0:8][:, None, None] * attn_dir
    in_new = ffn_in - learn_rate * ratio[8] * inner_dir
    out_new = ffn_out - learn_rate * ratio[9] * outer_dir
    norm_new = norm_params - learn_rate * ratio[10:16][:, None] * norm_dir
    norms = jnp.stack([jnp.sqrt(weight_total), jnp.sqrt(update_total)])
    return (
        attn_new, in_new, out_new, norm_new,
        attn_first, attn_second, inner_first, inner_second, outer_first, outer_second, norm_first, norm_second,
        attn_new.astype(bf16), in_new.astype(bf16), out_new.astype(bf16), norm_new.astype(bf16), norms,
    )


def on_device(
    close, tgt, memory, cotangent, tgt_lengths, src_segments, attn_w, ffn_in, ffn_out, norm_params,
    attn_moments, in_moments, out_moments, norm_moments,
):
    params = (attn_w, ffn_in, ffn_out, norm_params)
    moments = (attn_moments, in_moments, out_moments, norm_moments)
    if close and tgt.shape[0] == 1:
        full, bounds, *state = gather_and_start(params, tgt_lengths, src_segments, tgt[0])
        full = full.reshape(32, *full.shape[3:])
        saved, (n1, s1) = state[:5], state[5:]
        layer_out, d1, mem_grad, grad_ffn, grad_cross, norm_grad = middle(
            bounds, full, memory[0], cotangent[0], n1, s1
        )
        tgt_grad, *summed = finish_and_reduce(
            full, bounds, tgt[0], saved, d1, (grad_ffn, grad_cross), norm_grad, params, moments
        )
        return (layer_out[None], tgt_grad[None], mem_grad[None], *update_params(summed, params, moments))
    full = gather_any(*params)
    parts = []
    for r in range(tgt.shape[0]):
        bounds, *state = start_only(full, tgt_lengths[r : r + 1], src_segments[r : r + 1], tgt[r])
        saved, (n1, s1) = state[:5], state[5:]
        layer_out, d1, mem_grad, grad_ffn, grad_cross, norm_grad = middle(
            bounds, full, memory[r], cotangent[r], n1, s1
        )
        tgt_grad, grad_self = finish_only(full, bounds, tgt[r], saved, d1)
        parts.append((layer_out, tgt_grad, mem_grad, grad_ffn, grad_cross, grad_self, norm_grad[0:6]))
    outs = [jnp.stack([part[i] for part in parts]) for i in range(3)]
    sums = [sum(part[i].astype(f32) for part in parts) for i in range(3, 7)]
    grads = [grad.astype(bf16) for grad in sums[:3]]
    return (*outs, *reduce_any(grads, sums[3], params, moments))


def fits(mesh):
    return mesh.shape["gx"] == 4 and mesh.shape["gy"] == 8


def solution(mesh):
    rows = P(AXES, None, None)
    matrix = P(AXES, None)
    stack = P(None, AXES, None)
    vectors = P(None, AXES)
    return jax.shard_map(
        functools.partial(on_device, fits(mesh)),
        mesh=mesh,
        in_specs=(
            rows, rows, rows, matrix, matrix, stack, matrix, matrix, vectors,
            P(None, None, AXES, None), stack, stack, P(None, None, AXES),
        ),
        out_specs=(
            rows, rows, rows, stack, matrix, matrix, vectors, stack, stack, matrix, matrix, matrix, matrix,
            vectors, vectors, stack, matrix, matrix, vectors, P(),
        ),
        check_vma=False,
    )
```

```python
import functools

import jax
import jax.numpy as jnp
from jax import lax
from jax.experimental import pallas as pl
from jax.experimental.pallas import tpu as pltpu
from jax.sharding import PartitionSpec as P

HEAD_DIM = 64
STEP = 5

beta_first = 0.5
beta_second = 0.5
learn_rate = 0.5
decay_rate = 0.01
norm_eps = 1e-05
adam_eps = 1e-06

f32 = jnp.float32
bf16 = jnp.bfloat16
LANES = 128
QB = 128
KB = 256
RC = 256
LONGEST = 512
WAYS = 2
MASKED = -1e30
AXES = ("gx", "gy")
GRANT = 63 * 2**20


def nn(left, right):
    return lax.dot_general(left, right, (((1,), (0,)), ((), ())), preferred_element_type=f32)


def nt(left, right):
    return lax.dot_general(left, right, (((1,), (1,)), ((), ())), preferred_element_type=f32)


def tn(left, right):
    return lax.dot_general(left, right, (((0,), (0,)), ((), ())), preferred_element_type=f32)


def rows_of(step, size):
    return pl.ds(pl.multiple_of(step * size, size), size)


def each_chunk(count, body):
    def step(index, carry):
        body(index)
        return carry

    lax.fori_loop(0, count, step, 0)


def spread_heads(dst, src):
    pairs = dst.shape[0]
    first = lax.broadcasted_iota(jnp.int32, (QB, LANES), 1) < HEAD_DIM
    zero = jnp.zeros((QB, LANES), bf16)

    def body(i):
        start = pl.multiple_of(i * 2 * QB, 2 * QB)
        for p in range(pairs):
            tile = src[rows_of(i, QB), p * LANES : (p + 1) * LANES]
            dst[p, pl.ds(start, QB), :] = jnp.where(first, tile, zero)
            dst[p, pl.ds(start + QB, QB), :] = jnp.where(first, zero, tile)

    each_chunk(src.shape[0] // QB, body)


def run_blocks(count, body, steps):
    if not steps:
        each_chunk(count, body)
        return
    for i in range(count):
        body(i)
        if i < len(steps) and steps[i] is not None:
            steps[i]()


def near_window(i):
    first = max(0, i - LONGEST // LANES) if isinstance(i, int) else jnp.maximum(i - LONGEST // LANES, 0)
    return first, (i + 1 - first + KB // LANES - 1) // (KB // LANES)


def bound_window(bounds, which):
    def window(i):
        first = bounds[2 * which, i * QB] // LANES
        last = (bounds[2 * which + 1, i * QB + QB - 1] + LANES - 1) // LANES
        return first, ((last - first) * LANES + KB - 1) // KB

    return window


def key_block(first_key, j, keys):
    nominal = first_key * LANES + j * KB
    return pl.multiple_of(jnp.minimum(nominal, keys - KB), LANES), nominal


def block_bias(low, high, start, nominal):
    place = start + lax.broadcasted_iota(jnp.int32, (KB, QB), 0)
    bias = jnp.where((place >= jnp.maximum(low, nominal)) & (place < high), 0.0, MASKED).astype(f32)
    return jnp.concatenate([bias, bias], axis=1)


def attention(window, which, bounds, key_ref, value_t, query_z, mixed_ref, lse_ref, score_scr, out_scr, steps=()):
    keys = key_ref.shape[0]
    pairs = query_z.shape[0]
    fold = (KB // 8, 8, 2 * QB)

    def query_block(i):
        rows = rows_of(i, QB)
        pair_rows = rows_of(i, 2 * QB)
        low = bounds[2 * which : 2 * which + 1, rows]
        high = bounds[2 * which + 1 : 2 * which + 2, rows]
        first_key, blocks = window(i)
        out_scr[...] = jnp.zeros_like(out_scr)

        def scores(j, tops):
            start, nominal = key_block(first_key, j, keys)
            bias = block_bias(low, high, start, nominal)
            found = []
            raw = [
                nt(key_ref[pl.ds(start, KB), p * LANES : (p + 1) * LANES], query_z[p, pair_rows, :])
                for p in range(pairs)
            ]
            for p in range(pairs):
                score = raw[p] + bias
                score_scr[p, rows_of(j, KB), :] = score
                found.append(jnp.maximum(tops[p], jnp.max(score.reshape(fold), axis=0)))
            return tuple(found)

        tops = lax.fori_loop(
            0, blocks, scores, tuple(jnp.full((8, 2 * QB), MASKED, f32) for _ in range(pairs))
        )
        top = [jnp.max(t, axis=0, keepdims=True) for t in tops]

        def weigh(j, sums):
            start, _ = key_block(first_key, j, keys)
            found = []
            low_exps = []
            for p in range(pairs):
                exponent = jnp.exp(score_scr[p, rows_of(j, KB), :] - top[p])
                found.append(sums[p] + jnp.sum(exponent.reshape(fold), axis=0))
                low_exps.append(exponent.astype(bf16))
            for p in range(pairs):
                for h in range(2):
                    heads = slice(h * HEAD_DIM, (h + 1) * HEAD_DIM)
                    value = value_t[
                        p * LANES + h * HEAD_DIM : p * LANES + (h + 1) * HEAD_DIM, pl.ds(start, KB)
                    ]
                    out_scr[p, heads, :] += nn(value, low_exps[p][:, h * QB : (h + 1) * QB])
            return tuple(found)

        sums = lax.fori_loop(
            0, blocks, weigh, tuple(jnp.zeros((8, 2 * QB), f32) for _ in range(pairs))
        )
        for p in range(pairs):
            total = jnp.sum(sums[p], axis=0, keepdims=True)
            lse_ref[i, p : p + 1, :] = top[p] + jnp.log(total)
            inverse = 1.0 / total
            out = jnp.concatenate(
                [out_scr[p, 0:HEAD_DIM, :] * inverse[:, :QB], out_scr[p, HEAD_DIM:, :] * inverse[:, QB:]],
                axis=0,
            )
            mixed_ref[rows, p * LANES : (p + 1) * LANES] = out.T.astype(bf16)

    run_blocks(query_z.shape[1] // (2 * QB), query_block, steps)


def attention_back(
    window, which, bounds, key_ref, key_t, value_ref, query_z, grad_z, grad_ref, mixed_ref, lse_ref,
    dquery_ref, dkey_scr, dvalue_scr, dq_scr, steps=(),
):
    keys = key_ref.shape[0]
    pairs = query_z.shape[0]

    def query_block(i):
        rows = rows_of(i, QB)
        pair_rows = rows_of(i, 2 * QB)
        low = bounds[2 * which : 2 * which + 1, rows]
        high = bounds[2 * which + 1 : 2 * which + 2, rows]
        first_key, blocks = window(i)
        dq_scr[...] = jnp.zeros_like(dq_scr)
        deltas = []
        for p in range(pairs):
            lanes = slice(p * LANES, (p + 1) * LANES)
            product = (grad_ref[rows, lanes].astype(f32) * mixed_ref[rows, lanes].astype(f32)).T
            deltas.append(
                jnp.concatenate(
                    [
                        jnp.sum(product[:HEAD_DIM], axis=0, keepdims=True),
                        jnp.sum(product[HEAD_DIM:], axis=0, keepdims=True),
                    ],
                    axis=1,
                )
            )

        def key_step(j):
            start, nominal = key_block(first_key, j, keys)
            bias = block_bias(low, high, start, nominal)
            block = pl.ds(start, KB)
            held = {}

            def first(p):
                lanes = slice(p * LANES, (p + 1) * LANES)
                held["s", p] = nt(key_ref[block, lanes], query_z[p, pair_rows, :])
                held["d", p] = nt(value_ref[block, lanes], grad_z[p, pair_rows, :])

            def second(p):
                prob = jnp.exp(held.pop(("s", p)) + bias - lse_ref[i, p : p + 1, :])
                held["ds", p] = (prob * (held.pop(("d", p)) - deltas[p])).astype(bf16)
                held["p", p] = prob.astype(bf16)

            def third(p):
                lanes = slice(p * LANES, (p + 1) * LANES)
                dscore = held["ds", p]
                dvalue_scr[block, lanes] += nn(held["p", p], grad_z[p, pair_rows, :])
                dkey_scr[block, lanes] += nn(dscore, query_z[p, pair_rows, :])
                for h in range(2):
                    heads = slice(h * HEAD_DIM, (h + 1) * HEAD_DIM)
                    key = key_t[
                        p * LANES + h * HEAD_DIM : p * LANES + (h + 1) * HEAD_DIM, block
                    ]
                    dq_scr[p, heads, :] += nn(key, dscore[:, h * QB : (h + 1) * QB])

            for step in (first, second, third):
                for p in range(pairs):
                    step(p)

        each_chunk(blocks, key_step)
        for p in range(pairs):
            dquery_ref[rows, p * LANES : (p + 1) * LANES] = (
                (dq_scr[p] * HEAD_DIM**-0.5).T.astype(bf16)
            )

    run_blocks(query_z.shape[1] // (2 * QB), query_block, steps)


def norm_parts(values):
    average = jnp.mean(values, axis=-1, keepdims=True)
    centred = values - average
    spread = jnp.mean(centred * centred, axis=-1, keepdims=True)
    inverse = lax.rsqrt(spread + norm_eps)
    return centred * inverse, inverse


def norm_back(gradient, normed, inverse, gain):
    scaled = gradient * gain
    first_mean = jnp.mean(scaled, axis=-1, keepdims=True)
    second_mean = jnp.mean(scaled * normed, axis=-1, keepdims=True)
    return inverse * (scaled - first_mean - normed * second_mean)


def fold_rows(values):
    return jnp.sum(values.reshape(values.shape[0] // 8, 8, values.shape[1]), axis=0)


def load_norms(norm_ref):
    group = norm_ref.shape[0] // 4
    blocks = [jnp.sum(norm_ref[group * i : group * (i + 1)].astype(f32), axis=0) for i in range(4)]
    rows = jnp.concatenate(blocks, axis=1)
    return [rows[i : i + 1, :] for i in range(6)]


def weight(ref, index):
    blocks = ref.shape[0]
    return ref[:, 16 * index : 16 * (index + 1), :].reshape(16 * blocks, ref.shape[2])


def put_gradient(ref, index, value):
    blocks = ref.shape[0]
    ref[:, 16 * index : 16 * (index + 1), :] = value.astype(bf16).reshape(blocks, 16, ref.shape[2])


def load_norm_rows(dst, norm_ref):
    for i, vector in enumerate(load_norms(norm_ref)):
        dst[i : i + 1, :] = vector


def sigmoid(values):
    return 0.5 * jnp.tanh(0.5 * values) + 0.5


class Mover:
    def __init__(self, sems):
        self.sems = sems
        self.count = 0
        self.open = []

    def start(self, src, dst):
        copy = pltpu.make_async_copy(src, dst, self.sems.at[self.count])
        self.count += 1
        copy.start()
        self.open.append(copy)
        return copy

    def wait(self, *copies):
        for copy in copies:
            copy.wait()
            self.open = [other for other in self.open if other is not copy]

    def finish(self):
        self.wait(*list(self.open))


def find_bounds(lengths, src_segments, bounds_ref):
    sentences = lengths.shape[1]
    length = bounds_ref.shape[1]
    row = lax.broadcasted_iota(jnp.int32, (sentences, sentences), 0)
    col = lax.broadcasted_iota(jnp.int32, (sentences, sentences), 1)
    sizes = jnp.broadcast_to(lengths[...].astype(f32), (sentences, sentences))

    def total(mask, values):
        return jnp.sum(jnp.where(mask, values, 0.0), axis=1, keepdims=True)

    own = total(col == row, sizes)
    starts = total(col < row, sizes)
    ends = starts + own
    sources = src_segments.shape[1]
    number = lax.broadcasted_iota(jnp.int32, (sentences, sources), 0)
    count = total(jnp.broadcast_to(src_segments[...], (sentences, sources)) == number, 1.0)
    places = lax.broadcasted_iota(jnp.int32, (sentences, length), 1).astype(f32)

    def gather(edges, values):
        return jnp.sum(jnp.where(edges <= places, values, 0.0), axis=0, keepdims=True).astype(jnp.int32)

    bounds_ref[0:1, :] = gather(ends, own)
    bounds_ref[1:2, :] = lax.broadcasted_iota(jnp.int32, (1, length), 1) + 1
    bounds_ref[2:3, :] = gather(ends, count)
    bounds_ref[3:4, :] = gather(starts, count)
    bounds_ref[4:8, :] = jnp.zeros((4, length), jnp.int32)


def self_forward(tgt, attn, bounds, q, k, v, mix, lse, n1, s1, query_z, value_t, score_scr, out_scr, move, outs, steps):
    chunks = tgt.shape[0] // RC
    scale = jnp.array(HEAD_DIM**-0.5, bf16)

    def project(c):
        rows = rows_of(c, RC)
        x = tgt[rows, :]
        q[rows, :] = nn(x, weight(attn, 0)).astype(bf16) * scale
        k[rows, :] = nn(x, weight(attn, 1)).astype(bf16)
        v[rows, :] = nn(x, weight(attn, 2)).astype(bf16)

    each_chunk(chunks, project)
    for i, ref in enumerate((q, k, v)):
        move.start(ref, outs[i])
    spread_heads(query_z, q)
    value_t[...] = v[...].T
    attention(near_window, 0, bounds, k, value_t, query_z, mix, lse, score_scr, out_scr, steps)
    move.start(mix, outs[3])
    move.start(lse, outs[4])

    def middle(c):
        rows = rows_of(c, RC)
        normed, inverse = norm_parts(tgt[rows, :].astype(f32) + nn(mix[rows, :], weight(attn, 3)))
        n1[rows, :] = normed
        s1[rows, :] = inverse

    each_chunk(chunks, middle)
    move.start(n1, outs[5])
    move.start(s1, outs[6])


def middle_kernel(
    bounds_s, bounds_h, full, memory_h, cot_h, n1_h, s1_h,
    out_h, d1_h, mgrad_h, gffn_h, gcross_h, gnorm_ref,
    bounds, norm_b, attn, ffn, memory, cot, n1, s1, cq, ck, cv, cmix, clse, query_z, grad_z, turned, score_scr, small_scr,
    act_scr, dpre_scr, h2_scr, d3_scr, d2_scr, d2b_scr, grad_scr, dq_scr, dk_scr, dv_scr, out_scr, mgrad, gffn, gcross,
    sums, norm, sems,
):
    width = n1.shape[1]
    chunks = n1.shape[0] // RC
    scale = jnp.array(HEAD_DIM**-0.5, bf16)
    move = Mover(sems)
    rows_cross = attn.shape[1]
    norm_rows = pl.ds(full.shape[1] - 16, 16)
    load_small = [move.start(full.at[:, norm_rows, pl.ds(0, width // 4)], norm_b), move.start(bounds_h, bounds)]
    load_cross = move.start(full.at[:, pl.ds(rows_cross, rows_cross)], attn)
    load_memory = move.start(memory_h, memory)
    load_n1 = move.start(n1_h, n1)
    load_ffn = move.start(full.at[:, pl.ds(2 * rows_cross, ffn.shape[1])], ffn)
    load_rest = [move.start(cot_h, cot), move.start(s1_h, s1)]
    sums[...] = jnp.zeros_like(sums)
    move.wait(*load_small)
    load_norm_rows(norm, norm_b)
    move.wait(load_cross, load_memory)

    def h1_of(rows):
        return n1[rows, :] * norm[0:1, :] + norm[1:2, :]

    def project(c):
        rows = rows_of(c, RC)
        mem = memory[rows, :]
        ck[rows, :] = nn(mem, weight(attn, 1)).astype(bf16)
        cv[rows, :] = nn(mem, weight(attn, 2)).astype(bf16)

    def project_queries(c):
        rows = rows_of(c, RC)
        cq[rows, :] = nn(h1_of(rows).astype(bf16), weight(attn, 0)).astype(bf16) * scale

    each_chunk(chunks, project)
    turned[...] = cv[...].T
    move.wait(load_n1)
    each_chunk(chunks, project_queries)
    spread_heads(query_z, cq)
    window = bound_window(bounds_s, 1)
    attention(window, 1, bounds, ck, turned, query_z, cmix, clse, score_scr, small_scr)
    move.wait(load_ffn, *load_rest)
    blocks = ffn.shape[0]
    parts = act_scr.shape[1] // width
    share = blocks // parts

    def outer(b):
        return ffn[share * b : share * (b + 1), 16 * parts :, :].reshape(width, width)

    def body(c):
        rows = [pl.ds(pl.multiple_of((c * WAYS + w) * RC, RC), RC) for w in range(WAYS)]
        ways = range(WAYS)
        state = [{} for _ in ways]

        def enter(w):
            st = state[w]
            st["n2"], st["s2"] = norm_parts(h1_of(rows[w]) + nn(cmix[rows[w], :], weight(attn, 3)))
            st["third"] = st["n2"] * norm[2:3, :] + norm[3:4, :]
            st["h2b"] = st["third"].astype(bf16)
            h2_scr[rows[w], :] = st["h2b"]

        def pre(w, b):
            state[w]["pre", b] = nn(state[w]["h2b"], weight(ffn, b))

        def act(w, b):
            st = state[w]
            sig = sigmoid(st["pre", b])
            swish = st.pop(("pre", b)) * sig
            st["act", b] = swish.astype(bf16)
            act_scr[rows[w], width * b : width * (b + 1)] = st["act", b]
            st["slope", b] = sig + swish * (1.0 - sig)

        def out(w, b):
            st = state[w]
            st["third"] = st["third"] + nn(st.pop(("act", b)), outer(b))

        def turn(w):
            st = state[w]
            n3, s3 = norm_parts(st.pop("third"))
            out_scr[rows[w], :] = (n3 * norm[4:5, :] + norm[5:6, :]).astype(bf16)
            up = cot[rows[w], :].astype(f32)
            sums[4] += fold_rows(up * n3)
            sums[5] += fold_rows(up)
            st["dh2"] = norm_back(up, n3, s3, norm[4:5, :])
            st["d3b"] = st["dh2"].astype(bf16)
            d3_scr[rows[w], :] = st["d3b"]

        def dact(w, b):
            state[w]["dact", b] = nt(state[w]["d3b"], outer(b))

        def dpre(w, b):
            st = state[w]
            st["dpre", b] = (st.pop(("dact", b)) * st.pop(("slope", b))).astype(bf16)
            dpre_scr[rows[w], width * b : width * (b + 1)] = st["dpre", b]

        def back(w, b):
            st = state[w]
            st["dh2"] = st["dh2"] + nt(st.pop(("dpre", b)), weight(ffn, b))

        def leave(w):
            st = state[w]
            dh2 = st["dh2"]
            sums[2] += fold_rows(dh2 * st["n2"])
            sums[3] += fold_rows(dh2)
            d2 = norm_back(dh2, st["n2"], st["s2"], norm[2:3, :])
            d2_scr[rows[w], :] = d2
            d2b = d2.astype(bf16)
            d2b_scr[rows[w], :] = d2b
            grad_scr[rows[w], :] = nt(d2b, weight(attn, 3)).astype(bf16)

        def skewed(w, first, second, third):
            for t in range(parts + 2):
                if t < parts:
                    first(w, t)
                if 0 <= t - 1 < parts:
                    second(w, t - 1)
                if 0 <= t - 2 < parts:
                    third(w, t - 2)

        for w in ways:
            enter(w)
            skewed(w, pre, act, out)
        for w in ways:
            turn(w)
            skewed(w, dact, dpre, back)
        for w in ways:
            leave(w)

    each_chunk(chunks // WAYS, body)
    move.start(out_scr, out_h)
    for b in range(parts):
        cols = slice(width * b, width * (b + 1))
        gffn[share * b : share * (b + 1), 16 * parts :, :] = (
            tn(act_scr[:, cols], d3_scr[...]).astype(bf16).reshape(share, width // share, width)
        )
        put_gradient(gffn, b, tn(h2_scr[...], dpre_scr[:, cols]))
    move.start(gffn, gffn_h)

    def put_cross(i, value):
        put_gradient(gcross, i, value)
        part = pl.ds(16 * i, 16)
        move.start(gcross.at[:, part], gcross_h.at[:, part])

    put_cross(3, tn(cmix[...], d2b_scr[...]))
    spread_heads(grad_z, grad_scr)
    turned[...] = ck[...].T
    dk_scr[...] = jnp.zeros_like(dk_scr)
    dv_scr[...] = jnp.zeros_like(dv_scr)
    attention_back(
        window, 1, bounds, ck, turned, cv, query_z, grad_z, grad_scr, cmix, clse, dq_scr, dk_scr, dv_scr, small_scr,
    )

    def leave(c):
        rows = rows_of(c, RC)
        dkb = dk_scr[rows, :].astype(bf16)
        dvb = dv_scr[rows, :].astype(bf16)
        ck[rows, :] = dkb
        cv[rows, :] = dvb
        mgrad[rows, :] = (nt(dkb, weight(attn, 1)) + nt(dvb, weight(attn, 2))).astype(bf16)
        normed = n1[rows, :]
        h2_scr[rows, :] = h1_of(rows).astype(bf16)
        dh1 = d2_scr[rows, :] + nt(dq_scr[rows, :], weight(attn, 0))
        sums[0] += fold_rows(dh1 * normed)
        sums[1] += fold_rows(dh1)
        d2_scr[rows, :] = norm_back(dh1, normed, s1[rows, :], norm[0:1, :])

    each_chunk(chunks, leave)
    move.start(d2_scr, d1_h)
    move.start(mgrad, mgrad_h)
    for i in range(6):
        gnorm_ref[i : i + 1, :] = jnp.sum(sums[i], axis=0, keepdims=True)
    gnorm_ref[6:8, :] = jnp.zeros((2, width), f32)
    put_cross(0, tn(h2_scr[...], dq_scr[...]))
    put_cross(1, tn(memory[...], ck[...]))
    put_cross(2, tn(memory[...], cv[...]))
    move.finish()


def self_backward(
    tgt, attn, bounds, q, k, v, mix, lse, d1, tgrad, gself,
    query_z, grad_z, key_t, grad_scr, dq_scr, dk_scr, dv_scr, small_scr, d1_scr, steps, begin, late,
):
    chunks = tgt.shape[0] // RC

    def enter(c):
        rows = rows_of(c, RC)
        d1b = d1[rows, :].astype(bf16)
        d1_scr[rows, :] = d1b
        grad_scr[rows, :] = nt(d1b, weight(attn, 3)).astype(bf16)

    each_chunk(chunks, enter)
    begin[0]()
    put_gradient(gself, 3, tn(mix[...], d1_scr[...]))
    begin[1]()
    spread_heads(query_z, q)
    spread_heads(grad_z, grad_scr)
    key_t[...] = k[...].T
    dk_scr[...] = jnp.zeros_like(dk_scr)
    dv_scr[...] = jnp.zeros_like(dv_scr)
    attention_back(
        near_window, 0, bounds, k, key_t, v, query_z, grad_z, grad_scr, mix, lse, dq_scr, dk_scr, dv_scr, small_scr, steps,
    )
    for i, scr in enumerate((dq_scr, dk_scr, dv_scr)):
        put_gradient(gself, i, tn(tgt[...], scr[...].astype(bf16)))
    late()

    def leave(c):
        rows = rows_of(c, RC)
        tgrad[rows, :] = (
            d1[rows, :]
            + nt(dq_scr[rows, :], weight(attn, 0))
            + nt(dk_scr[rows, :].astype(bf16), weight(attn, 1))
            + nt(dv_scr[rows, :].astype(bf16), weight(attn, 2))
        ).astype(bf16)

    each_chunk(chunks, leave)


def shape(dims, dtype):
    return jax.ShapeDtypeStruct(dims, dtype)


VMEM_SPEC = pl.BlockSpec(memory_space=pltpu.VMEM)
HBM_SPEC = pl.BlockSpec(memory_space=pltpu.HBM)
SMEM_SPEC = pl.BlockSpec(memory_space=pltpu.SMEM)


def vmem(*buffers):
    return [pltpu.VMEM(dims, dtype) for dims, dtype in buffers]


def dma(*dims):
    return pltpu.SemaphoreType.DMA(dims)


def adam_direction(master, gradient, moments):
    first_moment = beta_first * moments[0] + (1.0 - beta_first) * gradient
    second_moment = beta_second * moments[1] + (1.0 - beta_second) * gradient * gradient
    first_fix = 1.0 - beta_first**STEP
    second_fix = 1.0 - beta_second**STEP
    direction = (
        first_moment / first_fix / (jnp.sqrt(second_moment / second_fix) + adam_eps)
        + decay_rate * master
    )
    return (direction, first_moment, second_moment)


MESH = pl.DeviceIdType.MESH


class Place:
    def __init__(self):
        self.gx = lax.axis_index("gx")
        self.gy = lax.axis_index("gy")
        self.x = lax.rem(self.gx, 2)
        self.y = self.gx // 2
        self.z = self.gy // 2
        self.c = lax.rem(self.gy, 2)
        self.here = self.gx * 8 + self.gy

    def target(self, x, y, z, c):
        return (y * 2 + x, z * 2 + c)

    def index(self, x, y, z, c):
        return (y * 2 + x) * 8 + z * 2 + c

    def others(self):
        found = []
        for step in range(1, 32):
            device = lax.rem(self.here + step, 32)
            found.append((device // 8, lax.rem(device, 8)))
        return found


def greet(targets):
    barrier = pltpu.get_barrier_semaphore()
    for target in targets:
        pl.semaphore_signal(barrier, inc=1, device_id=target, device_id_type=MESH)
    pl.semaphore_wait(barrier, len(targets))


def remote(src, dst, send_sem, recv_sem, target):
    return pltpu.make_async_remote_copy(
        src_ref=src, dst_ref=dst, send_sem=send_sem, recv_sem=recv_sem, device_id=target, device_id_type=MESH
    )


def forward_sizes(length, width):
    pairs = width // LANES
    row = (length, width)
    lse = (length // QB, pairs, 2 * QB)
    kept = [(row, bf16)] * 4 + [(lse, f32), (row, f32), ((length, 1), f32)]
    scratch = [
        ((pairs, 2 * length, LANES), bf16), ((width, length), bf16),
        ((pairs, LONGEST + 2 * KB, 2 * QB), f32), ((pairs, LANES, QB), f32),
    ]
    return kept, scratch


class Gathering:
    parts = ((0, 32), (32, 32), (64, 96), (160, 112))

    def __init__(self, me, mine, near, full, zsend, xsend, ysend, csend, recv, crecv):
        self.me, self.mine, self.near, self.full = me, mine, near, full
        self.zsend, self.xsend, self.ysend, self.csend, self.recv, self.crecv = zsend, xsend, ysend, csend, recv, crecv
        x, y, z, c = me.x, me.y, me.z, me.c
        self.ox, self.oy, self.oc = 1 - x, 1 - y, 1 - c
        self.x_next = me.target(self.ox, y, z, c)
        self.y_next = me.target(x, self.oy, z, c)
        self.sibling = me.target(x, y, z, self.oc)
        self.up = me.target(x, y, lax.rem(z + 1, 4), c)
        self.down = me.target(x, y, lax.rem(z + 3, 4), c)

    def held(self, part):
        return self.near if part < 2 else self.full

    def copy(self, column, zz, part, target, sem, own=False):
        rows = pl.ds(*self.parts[part])
        c = self.me.c
        dst = self.held(part).at[column, zz, c, rows]
        return remote(self.mine.at[rows] if own else dst, dst, sem, self.recv.at[column, zz, part], target)

    def arrive(self, column, zz, part):
        self.copy(column, zz, part, self.sibling, self.xsend.at[part]).wait_recv()

    def to_x(self, column, zz, part, own=False):
        self.copy(column, zz, part, self.x_next, self.xsend.at[part], own).start()

    def to_y(self, column, zz, part, own=False):
        self.copy(column, zz, part, self.y_next, self.ysend.at[part], own).start()

    def column(self, x, y):
        return y * 2 + x

    def along(self, zz, part, upward, own=False):
        me = self.me
        target = self.up if upward else self.down
        sem = self.zsend.at[zz, part, 0 if upward else 1]

        @pl.when((me.z < 3) if upward else (me.z > 0))
        def _():
            self.copy(me.gx, zz, part, target, sem, own).start()

    def own_z(self, parts):
        for part in parts:
            self.along(self.me.z, part, True, True)
            self.along(self.me.z, part, False, True)

    def own_sides(self, parts):
        for part in parts:
            self.to_x(self.me.gx, self.me.z, part, True)
            self.to_y(self.me.gx, self.me.z, part, True)

    def at_distance(self, d, action):
        z = self.me.z
        if d == 0:
            action(z, None)
            return

        @pl.when(z >= d)
        def _():
            action(z - d, True)

        @pl.when(z + d <= 3)
        def _():
            action(z + d, False)

    def inline(self, d, parts):
        me = self.me

        def action(zz, upward):
            for part in parts:
                self.arrive(me.gx, zz, part)
                self.along(zz, part, upward)
                self.to_x(me.gx, zz, part)
                self.to_y(me.gx, zz, part)

        self.at_distance(d, action)

    def side(self, d, parts):
        me = self.me

        def action(zz, _):
            for part in parts:
                if part % 2 == 0:
                    column = self.column(self.ox, me.y)
                    self.arrive(column, zz, part)
                    self.to_y(column, zz, part)
                else:
                    column = self.column(me.x, self.oy)
                    self.arrive(column, zz, part)
                    self.to_x(column, zz, part)

        self.at_distance(d, action)

    def last_columns(self, part):
        last = (self.me.x, self.oy) if part % 2 == 0 else (self.ox, self.me.y)
        return (self.column(*last), self.column(self.ox, self.oy))

    def far(self, d, parts):
        def action(zz, _):
            for part in parts:
                for column in self.last_columns(part):
                    self.arrive(column, zz, part)

        self.at_distance(d, action)

    def core(self, column, part):
        rows = pl.ds(*self.parts[part])
        block = self.held(part).at[column, :, self.me.c, rows]
        return remote(block, block, self.csend.at[column, part], self.crecv.at[column, part], self.sibling)

    def core_inline(self, parts):
        for part in parts:
            self.core(self.me.gx, part).start()

    def core_side(self, parts):
        me = self.me
        for part in parts:
            self.core(self.column(self.ox, me.y) if part % 2 == 0 else self.column(me.x, self.oy), part).start()

    def core_far(self, parts):
        for part in parts:
            for column in self.last_columns(part):
                self.core(column, part).start()

    def cores(self, parts):
        for part in parts:
            for column in range(4):
                self.core(column, part).wait_recv()

    def sent(self, parts):
        me = self.me
        for part in parts:
            for zz in range(4):

                @pl.when((me.z < 3) & (zz <= me.z))
                def _():
                    self.copy(me.gx, zz, part, self.up, self.zsend.at[zz, part, 0]).wait_send()

                @pl.when((me.z > 0) & (zz >= me.z))
                def _():
                    self.copy(me.gx, zz, part, self.down, self.zsend.at[zz, part, 1]).wait_send()

            rows = pl.ds(*self.parts[part])
            four, eight = self.held(part).at[0, :, 0, rows], self.held(part).at[pl.ds(0, 2), :, 0, rows]
            sems = (self.xsend.at[part], self.ysend.at[part])
            few, many = sems if part % 2 == 0 else sems[::-1]
            remote(four, four, few, self.recv.at[0, 0, part], self.sibling).wait_send()
            remote(eight, eight, many, self.recv.at[0, 0, part], self.sibling).wait_send()
            for column in range(4):
                self.core(column, part).wait_send()

    def stages(self, parts):
        return [
            lambda: self.inline(1, parts),
            lambda: (self.side(0, parts), self.inline(2, parts)),
            lambda: (self.side(1, parts), self.inline(3, parts), self.core_inline(parts)),
            lambda: (self.side(2, parts), self.far(0, parts)),
            lambda: (self.side(3, parts), self.core_side(parts), self.far(1, parts)),
            lambda: (self.far(2, parts), self.far(3, parts), self.core_far(parts)),
        ]


def first_kernel(
    attn_h, inner_h, outer_h, norm_h, lengths_h, src_h, tgt_h,
    full, bounds_out, q_h, k_h, v_h, mix_h, lse_h, n1_h, s1_h,
    attn_f, inner_f, outer_f, norm_f, lengths, src, mine, bounds, tgt, attn,
    q, k, v, mix, lse, n1, s1, query_z, value_t, score_scr, small_scr,
    sems, zsend, xsend, ysend, csend, recv, crecv,
):
    me = Place()
    move = Mover(sems)
    loads = [
        move.start(a, b)
        for a, b in (
            (attn_h, attn_f), (inner_h, inner_f), (outer_h, outer_f), (norm_h, norm_f), (lengths_h, lengths), (src_h, src),
        )
    ]
    load_tgt = move.start(tgt_h, tgt)
    gathering = Gathering(me, mine, attn, full, zsend, xsend, ysend, csend, recv, crecv)
    barrier = pltpu.get_barrier_semaphore()

    def greet(target):
        pl.semaphore_signal(barrier, inc=1, device_id=target, device_id_type=MESH)

    for target in (gathering.x_next, gathering.y_next, gathering.sibling):
        greet(target)

    @pl.when(me.z < 3)
    def _():
        greet(gathering.up)

    @pl.when(me.z > 0)
    def _():
        greet(gathering.down)

    move.wait(*loads)
    for j in range(8):
        mine[16 * j : 16 * j + 16, :] = attn_f[j].astype(bf16)
    for b in range(4):
        mine[128 + 16 * b : 144 + 16 * b, :] = inner_f[:, 512 * b : 512 * b + 512].astype(bf16)
    mine[192:256, :] = outer_f[...].astype(bf16)
    lanes = jnp.concatenate([norm_f[...], jnp.zeros((6, 112), f32)], axis=1)
    lanes = jnp.concatenate([lanes, jnp.zeros((10, 128), f32)], axis=0)
    lanes = pltpu.roll(lanes, me.gy * 16, 1).astype(bf16)
    mine[256:272, :] = jnp.concatenate([lanes, jnp.zeros((16, 384), bf16)], axis=1)
    attn[me.gx, me.z, me.c] = mine[0:64, :]
    ends = jnp.where(me.z > 0, 1, 0) + jnp.where(me.z < 3, 1, 0)
    pl.semaphore_wait(barrier, 3 + ends)
    early, late = (0, 1), (2, 3)
    gathering.own_z(early)
    gathering.own_sides(early)
    gathering.own_z(late)
    gathering.own_sides(late)
    keep = move.start(mine.at[pl.ds(64, 208)], full.at[me.gx, me.z, me.c, pl.ds(64, 208)])
    find_bounds(lengths, src, bounds)
    move.start(bounds, bounds_out)
    sooner, later = gathering.stages(early), gathering.stages(late)
    for stage in (*sooner[:3], later[0], sooner[3], later[1], sooner[4], sooner[5]):
        stage()
    move.wait(keep)
    later[2]()
    gathering.cores(early)
    move.start(attn, full.at[:, :, :, pl.ds(0, 64)])
    move.wait(load_tgt)
    self_forward(
        tgt, attn.reshape(32, 64, 512), bounds, q, k, v, mix, lse, n1, s1, query_z, value_t, score_scr, small_scr,
        move, (q_h, k_h, v_h, mix_h, lse_h, n1_h, s1_h),
        (None, later[3], None, later[4], None, later[5]),
    )
    gathering.cores(late)
    gathering.sent(early + late)
    move.finish()


def gather_and_start(params, lengths, src_segments, tgt):
    length, width = tgt.shape
    kept, scratch = forward_sizes(length, width)
    row = (length, width)
    bounds = ((8, length), jnp.int32)
    full = ((4, 4, 2, 272, 512), bf16)
    loads = [(p.shape, f32) for p in params] + [(lengths.shape, jnp.int32), (src_segments.shape, jnp.int32)]
    return pl.pallas_call(
        first_kernel,
        out_shape=tuple(shape(*item) for item in [full, bounds] + kept),
        in_specs=[HBM_SPEC] * 7,
        out_specs=(HBM_SPEC,) * 9,
        scratch_shapes=vmem(
            *loads, ((272, 512), bf16), bounds, (row, bf16), ((4, 4, 2, 64, 512), bf16), *kept, *scratch,
        )
        + [dma(24), dma(4, 4, 2), dma(4), dma(4), dma(4, 4), dma(4, 4, 4), dma(4, 4)],
        compiler_params=pltpu.CompilerParams(collective_id=0, has_side_effects=True, vmem_limit_bytes=GRANT),
    )(*params, lengths, src_segments, tgt)


def start_kernel(
    full, lengths, src, tgt, bounds_out, q_h, k_h, v_h, mix_h, lse_h, n1_h, s1_h,
    bounds, attn, q, k, v, mix, lse, n1, s1, query_z, value_t, score_scr, small_scr, sems,
):
    move = Mover(sems)
    load = move.start(full.at[:, pl.ds(0, attn.shape[1])], attn)
    find_bounds(lengths, src, bounds)
    move.start(bounds, bounds_out)
    move.wait(load)
    self_forward(
        tgt, attn, bounds, q, k, v, mix, lse, n1, s1, query_z, value_t, score_scr, small_scr,
        move, (q_h, k_h, v_h, mix_h, lse_h, n1_h, s1_h), (),
    )
    move.finish()


def start_only(full, lengths, src_segments, tgt):
    length, width = tgt.shape
    kept, scratch = forward_sizes(length, width)
    bounds = ((8, length), jnp.int32)
    return pl.pallas_call(
        start_kernel,
        out_shape=tuple(shape(*item) for item in [bounds] + kept),
        in_specs=[HBM_SPEC] + [VMEM_SPEC] * 3,
        out_specs=(HBM_SPEC,) * 8,
        scratch_shapes=vmem(bounds, ((full.shape[0], 64, width), bf16), *kept, *scratch) + [dma(16)],
        compiler_params=pltpu.CompilerParams(vmem_limit_bytes=GRANT),
    )(full, lengths, src_segments, tgt)


def middle(bounds, full, memory, cotangent, n1, s1):
    length, width = n1.shape
    keys = memory.shape[0]
    blocks = full.shape[0]
    ffn_rows = full.shape[1] - 144
    hidden = ffn_rows * blocks // 2 * full.shape[2] // width
    pairs = width // LANES
    row, mem_row = (length, width), (keys, width)
    zeroed = ((pairs, 2 * length, LANES), bf16)
    gffn, gcross = ((blocks, ffn_rows, width), bf16), ((blocks, 64, width), bf16)
    outs = [(row, bf16), (row, f32), (mem_row, bf16), gffn, gcross, ((8, width), f32)]
    scratch = vmem(
        (bounds.shape, jnp.int32), ((blocks, 16, width // 4), bf16), gcross, gffn, (mem_row, bf16), (row, bf16), (row, f32),
        ((length, 1), f32), (row, bf16), (mem_row, bf16), (mem_row, bf16), (row, bf16),
        ((length // QB, pairs, 2 * QB), f32), zeroed, zeroed, ((width, keys), bf16), ((pairs, keys + KB, 2 * QB), f32),
        ((pairs, LANES, QB), f32), ((length, hidden), bf16), ((length, hidden), bf16), (row, bf16), (row, bf16),
        (row, f32), (row, bf16), (row, bf16), (row, bf16), (mem_row, f32), (mem_row, f32), (row, bf16), (mem_row, bf16),
        gffn, gcross, ((6, 8, width), f32), ((8, width), f32),
    )
    return pl.pallas_call(
        middle_kernel,
        out_shape=tuple(shape(*item) for item in outs),
        in_specs=[SMEM_SPEC] + [HBM_SPEC] * 6,
        out_specs=(HBM_SPEC,) * 5 + (VMEM_SPEC,),
        scratch_shapes=scratch + [dma(16)],
        compiler_params=pltpu.CompilerParams(vmem_limit_bytes=GRANT),
    )(bounds, bounds, full, memory, cotangent, n1, s1)


OUTER_ROWS = slice(96, 160)


def attn_rows(j):
    return 192 + 16 * j if j < 4 else 64 + 16 * (j - 4) if j < 6 else 160 + 16 * (j - 6)


def add_rows(dst, *sources):
    total = sources[0][...].astype(f32)
    for source in sources[1:]:
        total = total + source[...].astype(f32)
    dst[...] = total.astype(dst.dtype)


class Summing:
    order = (2, 1, 3, 0)

    def __init__(self, me, sources, rows, pieces, first_a, first_b, second_a, second_b, third, result, sems):
        self.me, self.sources, self.rows, self.pieces = me, sources, rows, pieces
        self.first_a, self.first_b, self.second_a, self.second_b, self.third = first_a, first_b, second_a, second_b, third
        self.result = result
        (self.lsem, self.csend, self.crecv, self.send1, self.recv1, self.send2, self.recv2, self.send3, self.recv3) = sems
        x, y, z, c = me.x, me.y, me.z, me.c
        self.ox, self.oy, self.oc = 1 - x, 1 - y, 1 - c
        self.x_next = me.target(self.ox, y, z, c)
        self.y_next = me.target(x, self.oy, z, c)
        self.sibling = me.target(x, y, z, self.oc)
        self.zs = [lax.rem(z + d, 4) for d in range(4)]
        self.half = first_a.shape[2]
        self.top, self.bottom = pl.ds(0, self.half), pl.ds(self.half, self.half)
        self.pending, self.cores, self.own = [], {}, {}
        self.firsts, self.seconds, self.thirds = {}, {}, {}

    def send(self, *args):
        copy = remote(*args)
        copy.start()
        self.pending.append(copy)
        return copy

    def load(self):
        for d in self.order:
            for k, (source, kept, _) in enumerate(self.sources):
                if kept is not None:
                    copy = pltpu.make_async_copy(source.at[:, self.zs[d], self.me.c], kept.at[d], self.lsem.at[d, k])
                    copy.start()
                    self.own[d, k] = copy

    def core(self):
        for d in self.order:
            for k, (source, _, got) in enumerate(self.sources):
                self.cores[d, k] = self.send(
                    source.at[:, self.zs[d], self.oc], got.at[d], self.csend.at[d, k], self.crecv.at[d, k], self.sibling
                )

    def stage1(self, d):
        me = self.me
        for k in range(len(self.sources)):
            if (d, k) in self.own:
                self.own[d, k].wait()
            self.cores[d, k].wait_recv()

        def add(i):
            piece = self.pieces.at[d, i // 2, lax.rem(i, 2)]
            for start, count, k, first in self.rows:
                source, kept, got = self.sources[k]
                held = source.at[i, self.zs[d], me.c] if kept is None else kept.at[d, i]
                part = pl.ds(first, count)
                add_rows(piece.at[pl.ds(start, count)], held.at[part], got.at[d, i, part])

        each_chunk(4, add)
        self.firsts[d] = (
            self.send(
                self.pieces.at[d, self.oy, :, self.top], self.first_a.at[d], self.send1.at[d, 0], self.recv1.at[d, 0],
                self.y_next,
            ),
            self.send(
                self.pieces.at[d, :, self.ox, self.bottom], self.first_b.at[d], self.send1.at[d, 1],
                self.recv1.at[d, 1], self.x_next,
            ),
        )

    def stage2(self, d):
        me = self.me
        self.firsts[d][0].wait_recv()
        part = self.pieces.at[d, me.y, self.ox, self.top]
        add_rows(part, part, self.first_a.at[d, self.ox])
        one = self.send(part, self.second_a.at[d], self.send2.at[d, 0], self.recv2.at[d, 0], self.x_next)
        self.firsts[d][1].wait_recv()
        part = self.pieces.at[d, self.oy, me.x, self.bottom]
        add_rows(part, part, self.first_b.at[d, self.oy])
        two = self.send(part, self.second_b.at[d], self.send2.at[d, 1], self.recv2.at[d, 1], self.y_next)
        self.seconds[d] = (one, two)

    def stage3(self, d):
        me = self.me
        for copy in self.seconds[d]:
            copy.wait_recv()
        for rows, first, second, at in (
            (self.top, self.first_a, self.second_a, me.x), (self.bottom, self.first_b, self.second_b, me.y),
        ):
            part = self.pieces.at[d, me.y, me.x, rows]
            add_rows(part if d else self.result.at[rows], part, first.at[d, at], second.at[d])
        if d:
            self.thirds[d] = self.send(
                self.pieces.at[d, me.y, me.x], self.third.at[d - 1], self.send3.at[d - 1], self.recv3.at[d - 1],
                me.target(me.x, me.y, self.zs[d], me.c),
            )

    def end(self):
        for d in (1, 2, 3):
            self.thirds[d].wait_recv()
        add_rows(self.result, self.result, self.third.at[0], self.third.at[1], self.third.at[2])


def last_kernel(
    full, bounds_h, tgt_h, q_h, k_h, v_h, mix_h, lse_h, d1_h, gffn, gcross, gnorm_h,
    attn_p, inner_p, outer_p, norm_p, attn_m, in_m, out_m, norm_m,
    tgrad_h, g_ref, gn_ref, totals_ref,
    bounds, tgt, attn, q, k, v, mix, lse, d1, tgrad, gself, query_z, grad_z, key_t, grad_scr, dq_scr, dk_scr, dv_scr,
    small_scr, d1_scr, own_ffn, own_cross, got_ffn, got_cross, pieces, first_a, first_b, second_a, second_b, third,
    got_self, pieces2, first_a2, first_b2, second_a2, second_b2, third2, vectors, squares, tiles,
    msems, psems, *sems,
):
    me = Place()
    move = Mover(msems)
    others = me.others()
    barrier = pltpu.get_barrier_semaphore()
    for target in others:
        pl.semaphore_signal(barrier, inc=1, device_id=target, device_id_type=MESH)
    load_first = [move.start(a, b) for a, b in ((d1_h, d1), (full.at[:, pl.ds(0, 64)], attn), (gnorm_h, vectors.at[0]))]
    load_mix = move.start(mix_h, mix)
    load_rest = [
        move.start(a, b)
        for a, b in ((q_h, q), (k_h, k), (v_h, v), (lse_h, lse), (bounds_h, bounds), (tgt_h, tgt))
    ]
    sems1, sems2, (nsend, nrecv, tsend, trecv) = sems[0:9], sems[9:18], sems[18:22]
    big = Summing(
        me, [(gffn, own_ffn, got_ffn), (gcross, own_cross, got_cross)],
        [(0, 64, 0, 0), (64, 32, 1, 0), (96, 64, 0, 64), (160, 32, 1, 32)],
        pieces, first_a, first_b, second_a, second_b, third, g_ref.at[pl.ds(0, 192)], sems1,
    )
    rest = Summing(
        me, [(gself, None, got_self)], [(0, 64, 0, 0)],
        pieces2, first_a2, first_b2, second_a2, second_b2, third2, g_ref.at[pl.ds(192, 64)], sems2,
    )
    big.load()
    move.wait(*load_first)
    pl.semaphore_wait(barrier, len(others))
    big.core()
    norm_copies = [big.send(vectors.at[0], vectors.at[1], nsend.at[0], nrecv.at[0], big.sibling)]

    def norm_step(stage, target):
        norm_copies[-1].wait_recv()
        vectors[2 * stage] = vectors[2 * stage - 2] + vectors[2 * stage - 1]
        norm_copies.append(
            big.send(vectors.at[2 * stage], vectors.at[2 * stage + 1], nsend.at[stage], nrecv.at[stage], target)
        )

    def norm_last():
        norm_copies[-1].wait_recv()
        vectors[6] = vectors[4] + vectors[5]
        for d in range(1, 4):
            target = me.target(me.x, me.y, big.zs[d], me.c)
            norm_copies.append(big.send(vectors.at[6], vectors.at[6 + d], nsend.at[2 + d], nrecv.at[2 + d], target))

    far, up, down, here = big.order
    steps = [
        None,
        lambda: norm_step(1, big.x_next),
        None,
        lambda: (big.stage2(far), big.stage1(down), norm_step(2, big.y_next)),
        None,
        lambda: (big.stage2(up), big.stage3(far), big.stage1(here), norm_last()),
        None,
        lambda: (big.stage2(down), big.stage3(up)),
    ]

    begin = (lambda: big.stage1(far), lambda: big.stage1(up))

    def late():
        rest.core()
        big.stage2(here)
        big.stage3(down)

    move.wait(load_mix, *load_rest)
    self_backward(
        tgt, attn, bounds, q, k, v, mix, lse, d1, tgrad, gself.reshape(32, 64, 512),
        query_z, grad_z, key_t, grad_scr, dq_scr, dk_scr, dv_scr, small_scr, d1_scr, steps, begin, late,
    )
    move.start(tgrad, tgrad_h)
    rest.stage1(far)
    rest.stage1(up)
    big.stage3(here)
    rest.stage2(far)
    rest.stage1(down)
    rest.stage2(up)
    rest.stage3(far)
    rest.stage1(here)
    rest.stage2(down)
    rest.stage3(up)
    rest.stage2(here)
    rest.stage3(down)
    rest.stage3(here)
    big.end()
    for copy in norm_copies[3:]:
        copy.wait_recv()
    vectors[10] = (vectors[6] + vectors[8]) + (vectors[7] + vectors[9])
    lanes = vectors[10, :, pl.ds(pl.multiple_of(me.gx * 128, 128), 128)]
    gn_ref[...] = pltpu.roll(lanes, lax.rem(128 - me.gy * 16, 128), 1)

    def put(t, pairs):
        for i in range(2):
            squares[16 * i + t : 16 * i + t + 1, :] = sum(
                jnp.sum(pair[i] * pair[i], axis=0, keepdims=True) for pair in pairs
            )

    def direction(*args):
        return adam_direction(*args)[0]

    def put_attn(j):
        grad = g_ref[attn_rows(j) : attn_rows(j) + 16, :]
        put(j, [(attn_p[j], direction(attn_p[j], grad, (attn_m[0, j], attn_m[1, j])))])

    for j in range(4, 8):
        put_attn(j)
    pairs = []
    for b in range(4):
        cols = slice(512 * b, 512 * b + 512)
        grad = g_ref[16 * b : 16 * b + 16, :]
        pairs.append((inner_p[:, cols], direction(inner_p[:, cols], grad, (in_m[0, :, cols], in_m[1, :, cols]))))
    put(8, pairs)
    put(9, [(outer_p[...], direction(outer_p[...], g_ref[OUTER_ROWS, :], (out_m[0], out_m[1])))])
    master = norm_p[...]
    update = direction(master, gn_ref[0:6, 0:16], (norm_m[:, 0, :], norm_m[:, 1, :]))
    rest_lanes = jnp.zeros((6, 512 - 16), f32)
    master, update = (jnp.concatenate([item, rest_lanes], axis=1) for item in (master, update))
    for i in range(6):
        put(10 + i, [(master[i : i + 1], update[i : i + 1])])
    rest.end()
    for j in range(4):
        put_attn(j)
    folded = (squares[:, 0:128] + squares[:, 128:256]) + (squares[:, 256:384] + squares[:, 384:512])
    row = jnp.sum(folded.T, axis=0, keepdims=True)
    row = jnp.concatenate([row, jnp.zeros((1, 96), f32)], axis=1)
    tiles[me.here] = jnp.concatenate([row, jnp.zeros((7, 128), f32)], axis=0)
    for i, target in enumerate(others):
        big.send(tiles.at[me.here], tiles.at[me.here], tsend.at[i], trecv.at[me.here], target)
    for i, target in enumerate(others):
        source = target[0] * 8 + target[1]
        remote(tiles.at[source], tiles.at[source], tsend.at[i], trecv.at[source], target).wait_recv()
    totals_ref[...] = jnp.sum(tiles[...], axis=0)
    for copy in big.pending + rest.pending:
        copy.wait_send()
    move.finish()


def backward_scratch(length, width):
    pairs = width // LANES
    row = (length, width)
    zeroed = ((pairs, 2 * length, LANES), bf16)
    return [
        zeroed, zeroed, ((width, length), bf16), (row, bf16), (row, bf16), (row, f32), (row, f32),
        ((pairs, LANES, QB), f32), (row, bf16),
    ]


def finish_and_reduce(full, bounds, tgt, saved, d1, grads, norm_grad, params, moments):
    length, width = tgt.shape
    row = (length, width)
    lse = (length // QB, width // LANES, 2 * QB)

    def sums(half):
        return [
            ((4, 2, 2, 2 * half, 512), bf16), ((4, 2, half, 512), bf16), ((4, 2, half, 512), bf16),
            ((4, half, 512), bf16), ((4, half, 512), bf16), ((3, 2 * half, 512), bf16),
        ]

    scratch = vmem(
        (bounds.shape, jnp.int32), (row, bf16), ((32, 64, 512), bf16), *[(row, bf16)] * 4, (lse, f32), (row, f32),
        (row, bf16), ((4, 4, 2, 64, 512), bf16), *backward_scratch(length, width),
        ((4, 4, 128, 512), bf16), ((4, 4, 64, 512), bf16), ((4, 4, 128, 512), bf16), ((4, 4, 64, 512), bf16), *sums(96),
        ((4, 4, 64, 512), bf16), *sums(32), ((11, 8, 512), f32), ((32, 512), f32), ((32, 8, 128), f32),
    )
    round_sems = [dma(4, 2), dma(4, 2), dma(4, 2), dma(4, 2), dma(4, 2), dma(4, 2), dma(4, 2), dma(3), dma(3)]
    split = [grad.reshape(4, 4, 2, grad.shape[1], 512) for grad in grads]
    return pl.pallas_call(
        last_kernel,
        out_shape=(shape(row, bf16), shape((256, 512), f32), shape((8, 128), f32), shape((8, 128), f32)),
        in_specs=[HBM_SPEC] * 12 + [VMEM_SPEC] * 8,
        out_specs=(HBM_SPEC, VMEM_SPEC, VMEM_SPEC, VMEM_SPEC),
        scratch_shapes=scratch + [dma(16), dma(1)] + round_sems + round_sems + [dma(6), dma(6), dma(31), dma(32)],
        compiler_params=pltpu.CompilerParams(collective_id=1, has_side_effects=True, vmem_limit_bytes=GRANT),
    )(full, bounds, tgt, *saved, d1, *split, norm_grad, *params, *moments)


def finish_kernel(
    full, bounds, tgt, q, k, v, mix, lse, d1, tgrad, gself,
    attn, query_z, grad_z, key_t, grad_scr, dq_scr, dk_scr, dv_scr, small_scr, d1_scr, sems,
):
    move = Mover(sems)
    move.wait(move.start(full.at[:, pl.ds(0, attn.shape[1])], attn))
    self_backward(
        tgt, attn, bounds, q, k, v, mix, lse, d1, tgrad, gself,
        query_z, grad_z, key_t, grad_scr, dq_scr, dk_scr, dv_scr, small_scr, d1_scr, (), (lambda: None,) * 2, lambda: None,
    )


def finish_only(full, bounds, tgt, saved, d1):
    length, width = tgt.shape
    gself = ((full.shape[0], 64, width), bf16)
    return pl.pallas_call(
        finish_kernel,
        out_shape=(shape((length, width), bf16), shape(*gself)),
        in_specs=[HBM_SPEC] + [VMEM_SPEC] * 8,
        out_specs=(VMEM_SPEC, VMEM_SPEC),
        scratch_shapes=vmem(gself, *backward_scratch(length, width)) + [dma(2)],
        compiler_params=pltpu.CompilerParams(vmem_limit_bytes=GRANT),
    )(full, bounds, tgt, *saved, d1)


def update_kernel(*refs):
    ins, outs = refs[:12], refs[12:30]
    held, made, sems = refs[30:42], refs[42:59], refs[59]
    move = Mover(sems)
    order = (3, 2, 1, 7, 11, 6, 10, 5, 9, 4, 8, 0)
    loads = {i: move.start(ins[i], held[i]) for i in order}
    g_ref, gn_ref, totals_ref, attn, inner, outer, norm, attn_m, in_m, out_m, norm_m = held[1:]
    norms_ref = made[16]

    def results(t):
        return [(made[i], outs[1 + i]) for i in (t, 4 + 2 * t, 5 + 2 * t, 12 + t)]

    def step(t, master, gradient, moments, ratio, refs, place):
        direction, first_moment, second_moment = adam_direction(master, gradient, moments)
        value = master - ratio * direction
        for (ref, _), item in zip(refs, (value, first_moment, second_moment, value.astype(bf16))):
            ref[place] = item

    def leave(refs):
        for ref, out in refs:
            move.start(ref, out)

    move.wait(loads[3], loads[2], loads[7], loads[11])
    roots = jnp.sqrt(totals_ref[0:1, 0:32])
    norms_ref[0:1, :] = roots[:, 0:16]
    norms_ref[1:2, :] = roots[:, 16:32]
    move.start(norms_ref, outs[17])
    ratio = learn_rate * (roots[:, 0:16] / roots[:, 16:32])
    vectors = results(3)
    for i in range(6):
        one = slice(i, i + 1)
        moments = (norm_m[i, 0:1], norm_m[i, 1:2])
        step(10 + i, norm[one], gn_ref[one, 0:16], moments, ratio[:, 10 + i : 11 + i], vectors, one)
    leave(vectors)
    move.wait(loads[1], loads[6], loads[10])
    moments = (out_m[0], out_m[1])
    step(2, outer[...], g_ref[OUTER_ROWS, :], moments, ratio[:, 9:10], results(2), ...)
    leave(results(2))
    move.wait(loads[5], loads[9])
    for b in range(4):
        cols = slice(512 * b, 512 * b + 512)
        moments = (in_m[0, :, cols], in_m[1, :, cols])
        step(1, inner[:, cols], g_ref[16 * b : 16 * b + 16, :], moments, ratio[:, 8:9], results(1), (slice(None), cols))
    leave(results(1))
    move.wait(loads[4], loads[8], loads[0])
    move.start(held[0], outs[0])
    for j in range(8):
        grad = g_ref[attn_rows(j) : attn_rows(j) + 16, :]
        step(0, attn[j], grad, (attn_m[0, j], attn_m[1, j]), ratio[:, j : j + 1], results(0), j)
    leave(results(0))
    move.finish()


def update_params(summed, params, moments):
    args = (*summed, *params, *moments)
    outs = [shape(p.shape, f32) for p in params]
    outs += [shape(p.shape, f32) for p in params for _ in range(2)]
    outs += [shape(p.shape, bf16) for p in params] + [shape((2, 16), f32)]
    return pl.pallas_call(
        update_kernel,
        out_shape=(shape(summed[0].shape, bf16), *outs),
        in_specs=[HBM_SPEC] * len(args),
        out_specs=(HBM_SPEC,) * (1 + len(outs)),
        scratch_shapes=vmem(*((item.shape, item.dtype) for item in (*args, *outs))) + [dma(32)],
        compiler_params=pltpu.CompilerParams(vmem_limit_bytes=GRANT),
    )(*args)


def tensor_squares(attn_part, inner_part, outer_part, norm_part):
    return jnp.concatenate(
        [
            jnp.sum(attn_part * attn_part, axis=(1, 2)),
            jnp.sum(inner_part * inner_part)[None],
            jnp.sum(outer_part * outer_part)[None],
            jnp.sum(norm_part * norm_part, axis=1),
        ]
    )


def blocked(matrix, width):
    blocks = matrix.shape[0] // 16
    cols = matrix.shape[1] // width
    return matrix.reshape(blocks, 16, cols, width).transpose(0, 2, 1, 3).reshape(blocks, cols * 16, width)


def unblocked(blocks, width):
    count = blocks.shape[0]
    cols = blocks.shape[1] // 16
    return blocks.reshape(count, cols, 16, width).transpose(0, 2, 1, 3).reshape(count * 16, cols * width)


def gather_any(attn_w, ffn_in, ffn_out, norm_params):
    width = attn_w.shape[2]
    attn = lax.all_gather(attn_w.astype(bf16), AXES, axis=1, tiled=True)
    inner = lax.all_gather(ffn_in.astype(bf16), AXES, axis=0, tiled=True)
    outer = lax.all_gather(ffn_out.astype(bf16), AXES, axis=0, tiled=True)
    norm = lax.all_gather(norm_params.astype(bf16), AXES, axis=1, tiled=True)
    blocks = width // 16
    attn = attn.reshape(8, blocks, 16, width).transpose(1, 0, 2, 3).reshape(blocks, 8 * 16, width)
    lanes = jnp.pad(norm, ((0, 10), (0, 0))).reshape(16, 4, 1, width // 4).transpose(1, 2, 0, 3)
    lanes = jnp.pad(lanes, ((0, 0), (0, blocks // 4 - 1), (0, 0), (0, width - width // 4))).reshape(blocks, 16, width)
    return jnp.concatenate([attn, blocked(inner, width), outer.reshape(blocks, -1, width), lanes], axis=1)


def reduce_any(grads, norm_grad, params, moments):
    grad_ffn, grad_cross, grad_self = grads
    width = grad_ffn.shape[2]
    blocks = width // 16
    attn_w, ffn_in, ffn_out, norm_params = params
    attn_m, in_m, out_m, norm_m = moments
    stack = jnp.concatenate([grad_self, grad_cross], axis=1)
    stack = stack.reshape(blocks, 8, 16, width).transpose(1, 0, 2, 3).reshape(8, width, width)
    rows = ffn_in.shape[1] // width * 16
    inner = unblocked(grad_ffn[:, :rows], width)
    outer = grad_ffn[:, rows:].reshape(-1, width)
    shard_attn = lax.psum_scatter(stack, AXES, scatter_dimension=1, tiled=True).astype(f32)
    shard_inner = lax.psum_scatter(inner, AXES, scatter_dimension=0, tiled=True).astype(f32)
    shard_outer = lax.psum_scatter(outer, AXES, scatter_dimension=0, tiled=True).astype(f32)
    shard_norm = lax.psum_scatter(norm_grad, AXES, scatter_dimension=1, tiled=True)
    attn_dir, attn_first, attn_second = adam_direction(attn_w, shard_attn, attn_m)
    inner_dir, inner_first, inner_second = adam_direction(ffn_in, shard_inner, in_m)
    outer_dir, outer_first, outer_second = adam_direction(ffn_out, shard_outer, out_m)
    norm_dir, norm_first, norm_second = adam_direction(norm_params, shard_norm, norm_m)
    weight_total, update_total = lax.psum(
        (tensor_squares(*params), tensor_squares(attn_dir, inner_dir, outer_dir, norm_dir)), AXES
    )
    ratio = jnp.sqrt(weight_total) / jnp.sqrt(update_total)
    attn_new = attn_w - learn_rate * ratio[0:8][:, None, None] * attn_dir
    in_new = ffn_in - learn_rate * ratio[8] * inner_dir
    out_new = ffn_out - learn_rate * ratio[9] * outer_dir
    norm_new = norm_params - learn_rate * ratio[10:16][:, None] * norm_dir
    norms = jnp.stack([jnp.sqrt(weight_total), jnp.sqrt(update_total)])
    return (
        attn_new, in_new, out_new, norm_new,
        attn_first, attn_second, inner_first, inner_second, outer_first, outer_second, norm_first, norm_second,
        attn_new.astype(bf16), in_new.astype(bf16), out_new.astype(bf16), norm_new.astype(bf16), norms,
    )


def on_device(
    close, tgt, memory, cotangent, tgt_lengths, src_segments, attn_w, ffn_in, ffn_out, norm_params,
    attn_moments, in_moments, out_moments, norm_moments,
):
    params = (attn_w, ffn_in, ffn_out, norm_params)
    moments = (attn_moments, in_moments, out_moments, norm_moments)
    if close and tgt.shape[0] == 1:
        full, bounds, *state = gather_and_start(params, tgt_lengths, src_segments, tgt[0])
        full = full.reshape(32, *full.shape[3:])
        saved, (n1, s1) = state[:5], state[5:]
        layer_out, d1, mem_grad, grad_ffn, grad_cross, norm_grad = middle(
            bounds, full, memory[0], cotangent[0], n1, s1
        )
        moments = (*moments[:3], norm_moments.transpose(1, 0, 2))
        summed = finish_and_reduce(
            full, bounds, tgt[0], saved, d1, (grad_ffn, grad_cross), norm_grad, params, moments
        )
        tgt_grad, *updated = update_params(summed, params, moments)
        return (layer_out[None], tgt_grad[None], mem_grad[None], *updated)
    full = gather_any(*params)
    parts = []
    for r in range(tgt.shape[0]):
        bounds, *state = start_only(full, tgt_lengths[r : r + 1], src_segments[r : r + 1], tgt[r])
        saved, (n1, s1) = state[:5], state[5:]
        layer_out, d1, mem_grad, grad_ffn, grad_cross, norm_grad = middle(
            bounds, full, memory[r], cotangent[r], n1, s1
        )
        tgt_grad, grad_self = finish_only(full, bounds, tgt[r], saved, d1)
        parts.append((layer_out, tgt_grad, mem_grad, grad_ffn, grad_cross, grad_self, norm_grad[0:6]))
    outs = [jnp.stack([part[i] for part in parts]) for i in range(3)]
    sums = [sum(part[i].astype(f32) for part in parts) for i in range(3, 7)]
    grads = [grad.astype(bf16) for grad in sums[:3]]
    return (*outs, *reduce_any(grads, sums[3], params, moments))


def fits(mesh):
    return mesh.shape["gx"] == 4 and mesh.shape["gy"] == 8


def solution(mesh):
    rows = P(AXES, None, None)
    matrix = P(AXES, None)
    stack = P(None, AXES, None)
    vectors = P(None, AXES)
    return jax.shard_map(
        functools.partial(on_device, fits(mesh)),
        mesh=mesh,
        in_specs=(
            rows, rows, rows, matrix, matrix, stack, matrix, matrix, vectors,
            P(None, None, AXES, None), stack, stack, P(None, None, AXES),
        ),
        out_specs=(
            rows, rows, rows, stack, matrix, matrix, vectors, stack, stack, matrix, matrix, matrix, matrix,
            vectors, vectors, stack, matrix, matrix, vectors, P(),
        ),
        check_vma=False,
    )
```

```python
import functools

import jax
import jax.numpy as jnp
from jax import lax
from jax.experimental import pallas as pl
from jax.experimental.pallas import tpu as pltpu
from jax.sharding import PartitionSpec as P

HEAD_DIM = 64
STEP = 5

beta_first = 0.5
beta_second = 0.5
learn_rate = 0.5
decay_rate = 0.01
norm_eps = 1e-05
adam_eps = 1e-06

f32 = jnp.float32
bf16 = jnp.bfloat16
LANES = 128
QB = 128
KB = 256
RC = 256
LONGEST = 512
WAYS = 2
MASKED = -1e30
AXES = ("gx", "gy")
GRANT = 63 * 2**20


def nn(left, right):
    return lax.dot_general(left, right, (((1,), (0,)), ((), ())), preferred_element_type=f32)


def nt(left, right):
    return lax.dot_general(left, right, (((1,), (1,)), ((), ())), preferred_element_type=f32)


def tn(left, right):
    return lax.dot_general(left, right, (((0,), (0,)), ((), ())), preferred_element_type=f32)


def rows_of(step, size):
    return pl.ds(pl.multiple_of(step * size, size), size)


def each_chunk(count, body):
    def step(index, carry):
        body(index)
        return carry

    lax.fori_loop(0, count, step, 0)


def spread_heads(dst, src):
    pairs = dst.shape[0]
    first = lax.broadcasted_iota(jnp.int32, (QB, LANES), 1) < HEAD_DIM
    zero = jnp.zeros((QB, LANES), bf16)

    def body(i):
        start = pl.multiple_of(i * 2 * QB, 2 * QB)
        for p in range(pairs):
            tile = src[rows_of(i, QB), p * LANES : (p + 1) * LANES]
            dst[p, pl.ds(start, QB), :] = jnp.where(first, tile, zero)
            dst[p, pl.ds(start + QB, QB), :] = jnp.where(first, zero, tile)

    each_chunk(src.shape[0] // QB, body)


def run_blocks(count, body, steps):
    if not steps:
        each_chunk(count, body)
        return
    for i in range(count):
        body(i)
        if i < len(steps) and steps[i] is not None:
            steps[i]()


def near_window(i):
    first = max(0, i - LONGEST // LANES) if isinstance(i, int) else jnp.maximum(i - LONGEST // LANES, 0)
    return first, (i + 1 - first + KB // LANES - 1) // (KB // LANES)


def bound_window(bounds, which):
    def window(i):
        first = bounds[2 * which, i * QB] // LANES
        last = (bounds[2 * which + 1, i * QB + QB - 1] + LANES - 1) // LANES
        return first, ((last - first) * LANES + KB - 1) // KB

    return window


def key_block(first_key, j, keys):
    nominal = first_key * LANES + j * KB
    return pl.multiple_of(jnp.minimum(nominal, keys - KB), LANES), nominal


def block_bias(low, high, start, nominal):
    place = start + lax.broadcasted_iota(jnp.int32, (KB, QB), 0)
    bias = jnp.where((place >= jnp.maximum(low, nominal)) & (place < high), 0.0, MASKED).astype(f32)
    return jnp.concatenate([bias, bias], axis=1)


def attention(window, which, bounds, key_ref, value_t, query_z, mixed_ref, lse_ref, score_scr, out_scr, steps=()):
    keys = key_ref.shape[0]
    pairs = query_z.shape[0]
    fold = (KB // 8, 8, 2 * QB)

    def query_block(i):
        rows = rows_of(i, QB)
        pair_rows = rows_of(i, 2 * QB)
        low = bounds[2 * which : 2 * which + 1, rows]
        high = bounds[2 * which + 1 : 2 * which + 2, rows]
        first_key, blocks = window(i)
        out_scr[...] = jnp.zeros_like(out_scr)

        def scores(j, tops):
            start, nominal = key_block(first_key, j, keys)
            bias = block_bias(low, high, start, nominal)
            found = []
            raw = [
                nt(key_ref[pl.ds(start, KB), p * LANES : (p + 1) * LANES], query_z[p, pair_rows, :])
                for p in range(pairs)
            ]
            for p in range(pairs):
                score = raw[p] + bias
                score_scr[p, rows_of(j, KB), :] = score
                found.append(jnp.maximum(tops[p], jnp.max(score.reshape(fold), axis=0)))
            return tuple(found)

        tops = lax.fori_loop(
            0, blocks, scores, tuple(jnp.full((8, 2 * QB), MASKED, f32) for _ in range(pairs))
        )
        top = [jnp.max(t, axis=0, keepdims=True) for t in tops]

        def weigh(j, sums):
            start, _ = key_block(first_key, j, keys)
            found = []
            low_exps = []
            for p in range(pairs):
                exponent = jnp.exp(score_scr[p, rows_of(j, KB), :] - top[p])
                found.append(sums[p] + jnp.sum(exponent.reshape(fold), axis=0))
                low_exps.append(exponent.astype(bf16))
            for p in range(pairs):
                for h in range(2):
                    heads = slice(h * HEAD_DIM, (h + 1) * HEAD_DIM)
                    value = value_t[
                        p * LANES + h * HEAD_DIM : p * LANES + (h + 1) * HEAD_DIM, pl.ds(start, KB)
                    ]
                    out_scr[p, heads, :] += nn(value, low_exps[p][:, h * QB : (h + 1) * QB])
            return tuple(found)

        sums = lax.fori_loop(
            0, blocks, weigh, tuple(jnp.zeros((8, 2 * QB), f32) for _ in range(pairs))
        )
        for p in range(pairs):
            total = jnp.sum(sums[p], axis=0, keepdims=True)
            lse_ref[i, p : p + 1, :] = top[p] + jnp.log(total)
            inverse = 1.0 / total
            out = jnp.concatenate(
                [out_scr[p, 0:HEAD_DIM, :] * inverse[:, :QB], out_scr[p, HEAD_DIM:, :] * inverse[:, QB:]],
                axis=0,
            )
            mixed_ref[rows, p * LANES : (p + 1) * LANES] = out.T.astype(bf16)

    run_blocks(query_z.shape[1] // (2 * QB), query_block, steps)


def attention_back(
    window, which, bounds, key_ref, key_t, value_ref, query_z, grad_z, grad_ref, mixed_ref, lse_ref,
    dquery_ref, dkey_scr, dvalue_scr, dq_scr, steps=(),
):
    keys = key_ref.shape[0]
    pairs = query_z.shape[0]

    def query_block(i):
        rows = rows_of(i, QB)
        pair_rows = rows_of(i, 2 * QB)
        low = bounds[2 * which : 2 * which + 1, rows]
        high = bounds[2 * which + 1 : 2 * which + 2, rows]
        first_key, blocks = window(i)
        dq_scr[...] = jnp.zeros_like(dq_scr)
        deltas = []
        for p in range(pairs):
            lanes = slice(p * LANES, (p + 1) * LANES)
            product = (grad_ref[rows, lanes].astype(f32) * mixed_ref[rows, lanes].astype(f32)).T
            deltas.append(
                jnp.concatenate(
                    [
                        jnp.sum(product[:HEAD_DIM], axis=0, keepdims=True),
                        jnp.sum(product[HEAD_DIM:], axis=0, keepdims=True),
                    ],
                    axis=1,
                )
            )

        def key_step(j):
            start, nominal = key_block(first_key, j, keys)
            bias = block_bias(low, high, start, nominal)
            block = pl.ds(start, KB)
            held = {}

            def first(p):
                lanes = slice(p * LANES, (p + 1) * LANES)
                held["s", p] = nt(key_ref[block, lanes], query_z[p, pair_rows, :])
                held["d", p] = nt(value_ref[block, lanes], grad_z[p, pair_rows, :])

            def second(p):
                prob = jnp.exp(held.pop(("s", p)) + bias - lse_ref[i, p : p + 1, :])
                held["ds", p] = (prob * (held.pop(("d", p)) - deltas[p])).astype(bf16)
                held["p", p] = prob.astype(bf16)

            def third(p):
                lanes = slice(p * LANES, (p + 1) * LANES)
                dscore = held["ds", p]
                dvalue_scr[block, lanes] += nn(held["p", p], grad_z[p, pair_rows, :])
                dkey_scr[block, lanes] += nn(dscore, query_z[p, pair_rows, :])
                for h in range(2):
                    heads = slice(h * HEAD_DIM, (h + 1) * HEAD_DIM)
                    key = key_t[
                        p * LANES + h * HEAD_DIM : p * LANES + (h + 1) * HEAD_DIM, block
                    ]
                    dq_scr[p, heads, :] += nn(key, dscore[:, h * QB : (h + 1) * QB])

            for step in (first, second, third):
                for p in range(pairs):
                    step(p)

        each_chunk(blocks, key_step)
        for p in range(pairs):
            dquery_ref[rows, p * LANES : (p + 1) * LANES] = (
                (dq_scr[p] * HEAD_DIM**-0.5).T.astype(bf16)
            )

    run_blocks(query_z.shape[1] // (2 * QB), query_block, steps)


def norm_parts(values):
    average = jnp.mean(values, axis=-1, keepdims=True)
    centred = values - average
    spread = jnp.mean(centred * centred, axis=-1, keepdims=True)
    inverse = lax.rsqrt(spread + norm_eps)
    return centred * inverse, inverse


def norm_back(gradient, normed, inverse, gain):
    scaled = gradient * gain
    first_mean = jnp.mean(scaled, axis=-1, keepdims=True)
    second_mean = jnp.mean(scaled * normed, axis=-1, keepdims=True)
    return inverse * (scaled - first_mean - normed * second_mean)


def fold_rows(values):
    return jnp.sum(values.reshape(values.shape[0] // 8, 8, values.shape[1]), axis=0)


def load_norms(norm_ref):
    group = norm_ref.shape[0] // 4
    blocks = [jnp.sum(norm_ref[group * i : group * (i + 1)].astype(f32), axis=0) for i in range(4)]
    rows = jnp.concatenate(blocks, axis=1)
    return [rows[i : i + 1, :] for i in range(6)]


def weight(ref, index):
    blocks = ref.shape[0]
    return ref[:, 16 * index : 16 * (index + 1), :].reshape(16 * blocks, ref.shape[2])


def put_gradient(ref, index, value):
    blocks = ref.shape[0]
    ref[:, 16 * index : 16 * (index + 1), :] = value.astype(bf16).reshape(blocks, 16, ref.shape[2])


def load_norm_rows(dst, norm_ref):
    for i, vector in enumerate(load_norms(norm_ref)):
        dst[i : i + 1, :] = vector


def sigmoid(values):
    return 0.5 * jnp.tanh(0.5 * values) + 0.5


class Mover:
    def __init__(self, sems):
        self.sems = sems
        self.count = 0
        self.open = []

    def start(self, src, dst):
        copy = pltpu.make_async_copy(src, dst, self.sems.at[self.count])
        self.count += 1
        copy.start()
        self.open.append(copy)
        return copy

    def wait(self, *copies):
        for copy in copies:
            copy.wait()
            self.open = [other for other in self.open if other is not copy]

    def finish(self):
        self.wait(*list(self.open))


def find_bounds(lengths, src_segments, bounds_ref):
    sentences = lengths.shape[1]
    length = bounds_ref.shape[1]
    row = lax.broadcasted_iota(jnp.int32, (sentences, sentences), 0)
    col = lax.broadcasted_iota(jnp.int32, (sentences, sentences), 1)
    sizes = jnp.broadcast_to(lengths[...].astype(f32), (sentences, sentences))

    def total(mask, values):
        return jnp.sum(jnp.where(mask, values, 0.0), axis=1, keepdims=True)

    own = total(col == row, sizes)
    starts = total(col < row, sizes)
    ends = starts + own
    sources = src_segments.shape[1]
    number = lax.broadcasted_iota(jnp.int32, (sentences, sources), 0)
    count = total(jnp.broadcast_to(src_segments[...], (sentences, sources)) == number, 1.0)
    places = lax.broadcasted_iota(jnp.int32, (sentences, length), 1).astype(f32)

    def gather(edges, values):
        return jnp.sum(jnp.where(edges <= places, values, 0.0), axis=0, keepdims=True).astype(jnp.int32)

    bounds_ref[0:1, :] = gather(ends, own)
    bounds_ref[1:2, :] = lax.broadcasted_iota(jnp.int32, (1, length), 1) + 1
    bounds_ref[2:3, :] = gather(ends, count)
    bounds_ref[3:4, :] = gather(starts, count)
    bounds_ref[4:8, :] = jnp.zeros((4, length), jnp.int32)


def self_forward(tgt, attn, bounds, q, k, v, mix, lse, n1, s1, query_z, value_t, score_scr, out_scr, move, outs, steps):
    chunks = tgt.shape[0] // RC
    scale = jnp.array(HEAD_DIM**-0.5, bf16)

    def project(c):
        rows = rows_of(c, RC)
        x = tgt[rows, :]
        q[rows, :] = nn(x, weight(attn, 0)).astype(bf16) * scale
        k[rows, :] = nn(x, weight(attn, 1)).astype(bf16)
        v[rows, :] = nn(x, weight(attn, 2)).astype(bf16)

    each_chunk(chunks, project)
    for i, ref in enumerate((q, k, v)):
        move.start(ref, outs[i])
    spread_heads(query_z, q)
    value_t[...] = v[...].T
    attention(near_window, 0, bounds, k, value_t, query_z, mix, lse, score_scr, out_scr, steps)
    move.start(mix, outs[3])
    move.start(lse, outs[4])

    def middle(c):
        rows = rows_of(c, RC)
        normed, inverse = norm_parts(tgt[rows, :].astype(f32) + nn(mix[rows, :], weight(attn, 3)))
        n1[rows, :] = normed
        s1[rows, :] = inverse

    each_chunk(chunks, middle)
    move.start(n1, outs[5])
    move.start(s1, outs[6])


def middle_kernel(
    bounds_s, bounds_h, full, memory_h, cot_h, n1_h, s1_h,
    out_h, d1_h, mgrad_h, gffn_h, gcross_h, gnorm_ref,
    bounds, norm_b, attn, ffn, memory, cot, n1, s1, cq, ck, cv, cmix, clse, query_z, grad_z, turned, score_scr, small_scr,
    act_scr, dpre_scr, h2_scr, d3_scr, d2_scr, d2b_scr, grad_scr, dq_scr, dk_scr, dv_scr, out_scr, mgrad, gffn, gcross,
    sums, norm, sems,
):
    width = n1.shape[1]
    chunks = n1.shape[0] // RC
    scale = jnp.array(HEAD_DIM**-0.5, bf16)
    move = Mover(sems)
    rows_cross = attn.shape[1]
    norm_rows = pl.ds(full.shape[1] - 16, 16)
    load_small = [move.start(full.at[:, norm_rows, pl.ds(0, width // 4)], norm_b), move.start(bounds_h, bounds)]
    load_cross = move.start(full.at[:, pl.ds(rows_cross, rows_cross)], attn)
    load_memory = move.start(memory_h, memory)
    load_n1 = move.start(n1_h, n1)
    load_ffn = move.start(full.at[:, pl.ds(2 * rows_cross, ffn.shape[1])], ffn)
    load_rest = [move.start(cot_h, cot), move.start(s1_h, s1)]
    sums[...] = jnp.zeros_like(sums)
    move.wait(*load_small)
    load_norm_rows(norm, norm_b)
    move.wait(load_cross, load_memory)

    def h1_of(rows):
        return n1[rows, :] * norm[0:1, :] + norm[1:2, :]

    def project(c):
        rows = rows_of(c, RC)
        mem = memory[rows, :]
        ck[rows, :] = nn(mem, weight(attn, 1)).astype(bf16)
        cv[rows, :] = nn(mem, weight(attn, 2)).astype(bf16)

    def project_queries(c):
        rows = rows_of(c, RC)
        cq[rows, :] = nn(h1_of(rows).astype(bf16), weight(attn, 0)).astype(bf16) * scale

    each_chunk(chunks, project)
    turned[...] = cv[...].T
    move.wait(load_n1)
    each_chunk(chunks, project_queries)
    spread_heads(query_z, cq)
    window = bound_window(bounds_s, 1)
    attention(window, 1, bounds, ck, turned, query_z, cmix, clse, score_scr, small_scr)
    move.wait(load_ffn, *load_rest)
    blocks = ffn.shape[0]
    parts = act_scr.shape[1] // width
    share = blocks // parts

    def outer(b):
        return ffn[share * b : share * (b + 1), 16 * parts :, :].reshape(width, width)

    def body(c):
        rows = [pl.ds(pl.multiple_of((c * WAYS + w) * RC, RC), RC) for w in range(WAYS)]
        ways = range(WAYS)
        state = [{} for _ in ways]

        def enter(w):
            st = state[w]
            st["n2"], st["s2"] = norm_parts(h1_of(rows[w]) + nn(cmix[rows[w], :], weight(attn, 3)))
            st["third"] = st["n2"] * norm[2:3, :] + norm[3:4, :]
            st["h2b"] = st["third"].astype(bf16)
            h2_scr[rows[w], :] = st["h2b"]

        def pre(w, b):
            state[w]["pre", b] = nn(state[w]["h2b"], weight(ffn, b))

        def act(w, b):
            st = state[w]
            sig = sigmoid(st["pre", b])
            swish = st.pop(("pre", b)) * sig
            st["act", b] = swish.astype(bf16)
            act_scr[rows[w], width * b : width * (b + 1)] = st["act", b]
            st["slope", b] = sig + swish * (1.0 - sig)

        def out(w, b):
            st = state[w]
            st["third"] = st["third"] + nn(st.pop(("act", b)), outer(b))

        def turn(w):
            st = state[w]
            n3, s3 = norm_parts(st.pop("third"))
            out_scr[rows[w], :] = (n3 * norm[4:5, :] + norm[5:6, :]).astype(bf16)
            up = cot[rows[w], :].astype(f32)
            sums[4] += fold_rows(up * n3)
            sums[5] += fold_rows(up)
            st["dh2"] = norm_back(up, n3, s3, norm[4:5, :])
            st["d3b"] = st["dh2"].astype(bf16)
            d3_scr[rows[w], :] = st["d3b"]

        def dact(w, b):
            state[w]["dact", b] = nt(state[w]["d3b"], outer(b))

        def dpre(w, b):
            st = state[w]
            st["dpre", b] = (st.pop(("dact", b)) * st.pop(("slope", b))).astype(bf16)
            dpre_scr[rows[w], width * b : width * (b + 1)] = st["dpre", b]

        def back(w, b):
            st = state[w]
            st["dh2"] = st["dh2"] + nt(st.pop(("dpre", b)), weight(ffn, b))

        def leave(w):
            st = state[w]
            dh2 = st["dh2"]
            sums[2] += fold_rows(dh2 * st["n2"])
            sums[3] += fold_rows(dh2)
            d2 = norm_back(dh2, st["n2"], st["s2"], norm[2:3, :])
            d2_scr[rows[w], :] = d2
            d2b = d2.astype(bf16)
            d2b_scr[rows[w], :] = d2b
            grad_scr[rows[w], :] = nt(d2b, weight(attn, 3)).astype(bf16)

        def skewed(w, first, second, third):
            for t in range(parts + 2):
                if t < parts:
                    first(w, t)
                if 0 <= t - 1 < parts:
                    second(w, t - 1)
                if 0 <= t - 2 < parts:
                    third(w, t - 2)

        for w in ways:
            enter(w)
            skewed(w, pre, act, out)
        for w in ways:
            turn(w)
            skewed(w, dact, dpre, back)
        for w in ways:
            leave(w)

    each_chunk(chunks // WAYS, body)
    move.start(out_scr, out_h)
    for b in range(parts):
        cols = slice(width * b, width * (b + 1))
        gffn[share * b : share * (b + 1), 16 * parts :, :] = (
            tn(act_scr[:, cols], d3_scr[...]).astype(bf16).reshape(share, width // share, width)
        )
        put_gradient(gffn, b, tn(h2_scr[...], dpre_scr[:, cols]))
    move.start(gffn, gffn_h)

    def put_cross(i, value):
        put_gradient(gcross, i, value)
        part = pl.ds(16 * i, 16)
        move.start(gcross.at[:, part], gcross_h.at[:, part])

    put_cross(3, tn(cmix[...], d2b_scr[...]))
    spread_heads(grad_z, grad_scr)
    turned[...] = ck[...].T
    dk_scr[...] = jnp.zeros_like(dk_scr)
    dv_scr[...] = jnp.zeros_like(dv_scr)
    attention_back(
        window, 1, bounds, ck, turned, cv, query_z, grad_z, grad_scr, cmix, clse, dq_scr, dk_scr, dv_scr, small_scr,
    )

    def leave(c):
        rows = rows_of(c, RC)
        dkb = dk_scr[rows, :].astype(bf16)
        dvb = dv_scr[rows, :].astype(bf16)
        ck[rows, :] = dkb
        cv[rows, :] = dvb
        mgrad[rows, :] = (nt(dkb, weight(attn, 1)) + nt(dvb, weight(attn, 2))).astype(bf16)
        normed = n1[rows, :]
        h2_scr[rows, :] = h1_of(rows).astype(bf16)
        dh1 = d2_scr[rows, :] + nt(dq_scr[rows, :], weight(attn, 0))
        sums[0] += fold_rows(dh1 * normed)
        sums[1] += fold_rows(dh1)
        d2_scr[rows, :] = norm_back(dh1, normed, s1[rows, :], norm[0:1, :])

    each_chunk(chunks, leave)
    move.start(d2_scr, d1_h)
    move.start(mgrad, mgrad_h)
    for i in range(6):
        gnorm_ref[i : i + 1, :] = jnp.sum(sums[i], axis=0, keepdims=True)
    gnorm_ref[6:8, :] = jnp.zeros((2, width), f32)
    put_cross(0, tn(h2_scr[...], dq_scr[...]))
    put_cross(1, tn(memory[...], ck[...]))
    put_cross(2, tn(memory[...], cv[...]))
    move.finish()


def self_backward(
    tgt, attn, bounds, q, k, v, mix, lse, d1, tgrad, gself,
    query_z, grad_z, key_t, grad_scr, dq_scr, dk_scr, dv_scr, small_scr, d1_scr, steps, begin, late,
):
    chunks = tgt.shape[0] // RC

    def enter(c):
        rows = rows_of(c, RC)
        d1b = d1[rows, :].astype(bf16)
        d1_scr[rows, :] = d1b
        grad_scr[rows, :] = nt(d1b, weight(attn, 3)).astype(bf16)

    each_chunk(chunks, enter)
    begin[0]()
    put_gradient(gself, 3, tn(mix[...], d1_scr[...]))
    begin[1]()
    spread_heads(query_z, q)
    spread_heads(grad_z, grad_scr)
    key_t[...] = k[...].T
    dk_scr[...] = jnp.zeros_like(dk_scr)
    dv_scr[...] = jnp.zeros_like(dv_scr)
    attention_back(
        near_window, 0, bounds, k, key_t, v, query_z, grad_z, grad_scr, mix, lse, dq_scr, dk_scr, dv_scr, small_scr, steps,
    )
    for i, scr in enumerate((dq_scr, dk_scr, dv_scr)):
        put_gradient(gself, i, tn(tgt[...], scr[...].astype(bf16)))
    late()

    def leave(c):
        rows = rows_of(c, RC)
        tgrad[rows, :] = (
            d1[rows, :]
            + nt(dq_scr[rows, :], weight(attn, 0))
            + nt(dk_scr[rows, :].astype(bf16), weight(attn, 1))
            + nt(dv_scr[rows, :].astype(bf16), weight(attn, 2))
        ).astype(bf16)

    each_chunk(chunks, leave)


def shape(dims, dtype):
    return jax.ShapeDtypeStruct(dims, dtype)


VMEM_SPEC = pl.BlockSpec(memory_space=pltpu.VMEM)
HBM_SPEC = pl.BlockSpec(memory_space=pltpu.HBM)
SMEM_SPEC = pl.BlockSpec(memory_space=pltpu.SMEM)


def vmem(*buffers):
    return [pltpu.VMEM(dims, dtype) for dims, dtype in buffers]


def dma(*dims):
    return pltpu.SemaphoreType.DMA(dims)


def adam_direction(master, gradient, moments):
    first_moment = beta_first * moments[0] + (1.0 - beta_first) * gradient
    second_moment = beta_second * moments[1] + (1.0 - beta_second) * gradient * gradient
    first_fix = 1.0 - beta_first**STEP
    second_fix = 1.0 - beta_second**STEP
    direction = (
        first_moment / first_fix / (jnp.sqrt(second_moment / second_fix) + adam_eps)
        + decay_rate * master
    )
    return (direction, first_moment, second_moment)


MESH = pl.DeviceIdType.MESH


class Place:
    def __init__(self):
        self.gx = lax.axis_index("gx")
        self.gy = lax.axis_index("gy")
        self.x = lax.rem(self.gx, 2)
        self.y = self.gx // 2
        self.z = self.gy // 2
        self.c = lax.rem(self.gy, 2)
        self.here = self.gx * 8 + self.gy

    def target(self, x, y, z, c):
        return (y * 2 + x, z * 2 + c)

    def index(self, x, y, z, c):
        return (y * 2 + x) * 8 + z * 2 + c

    def others(self):
        found = []
        for step in range(1, 32):
            device = lax.rem(self.here + step, 32)
            found.append((device // 8, lax.rem(device, 8)))
        return found


def greet(targets):
    barrier = pltpu.get_barrier_semaphore()
    for target in targets:
        pl.semaphore_signal(barrier, inc=1, device_id=target, device_id_type=MESH)
    pl.semaphore_wait(barrier, len(targets))


def remote(src, dst, send_sem, recv_sem, target):
    return pltpu.make_async_remote_copy(
        src_ref=src, dst_ref=dst, send_sem=send_sem, recv_sem=recv_sem, device_id=target, device_id_type=MESH
    )


def forward_sizes(length, width):
    pairs = width // LANES
    row = (length, width)
    lse = (length // QB, pairs, 2 * QB)
    kept = [(row, bf16)] * 4 + [(lse, f32), (row, f32), ((length, 1), f32)]
    scratch = [
        ((pairs, 2 * length, LANES), bf16), ((width, length), bf16),
        ((pairs, LONGEST + 2 * KB, 2 * QB), f32), ((pairs, LANES, QB), f32),
    ]
    return kept, scratch


class Gathering:
    parts = ((0, 32), (32, 32), (64, 96), (160, 112))

    def __init__(self, me, mine, near, full, zsend, xsend, ysend, csend, recv, crecv):
        self.me, self.mine, self.near, self.full = me, mine, near, full
        self.zsend, self.xsend, self.ysend, self.csend, self.recv, self.crecv = zsend, xsend, ysend, csend, recv, crecv
        x, y, z, c = me.x, me.y, me.z, me.c
        self.ox, self.oy, self.oc = 1 - x, 1 - y, 1 - c
        self.x_next = me.target(self.ox, y, z, c)
        self.y_next = me.target(x, self.oy, z, c)
        self.sibling = me.target(x, y, z, self.oc)
        self.up = me.target(x, y, lax.rem(z + 1, 4), c)
        self.down = me.target(x, y, lax.rem(z + 3, 4), c)

    def held(self, part):
        return self.near if part < 2 else self.full

    def copy(self, column, zz, part, target, sem, own=False):
        rows = pl.ds(*self.parts[part])
        c = self.me.c
        dst = self.held(part).at[column, zz, c, rows]
        return remote(self.mine.at[rows] if own else dst, dst, sem, self.recv.at[column, zz, part], target)

    def arrive(self, column, zz, part):
        self.copy(column, zz, part, self.sibling, self.xsend.at[part]).wait_recv()

    def to_x(self, column, zz, part, own=False):
        self.copy(column, zz, part, self.x_next, self.xsend.at[part], own).start()

    def to_y(self, column, zz, part, own=False):
        self.copy(column, zz, part, self.y_next, self.ysend.at[part], own).start()

    def column(self, x, y):
        return y * 2 + x

    def along(self, zz, part, upward, own=False):
        me = self.me
        target = self.up if upward else self.down
        sem = self.zsend.at[zz, part, 0 if upward else 1]

        if part < 2:
            return

        @pl.when((me.z < 3) if upward else (me.z > 0))
        def _():
            self.copy(me.gx, zz, part, target, sem, own).start()

    def straight(self, d, part):
        me = self.me
        target = me.target(me.x, me.y, lax.rem(me.z + d, 4), me.c)
        return self.copy(me.gx, me.z, part, target, self.zsend.at[d, part, 0], True)

    def own_straight(self, parts):
        for d in (1, 3, 2):
            for part in parts:
                self.straight(d, part).start()

    def own_z(self, parts):
        for part in parts:
            self.along(self.me.z, part, True, True)
            self.along(self.me.z, part, False, True)

    def own_sides(self, parts):
        for part in parts:
            self.to_x(self.me.gx, self.me.z, part, True)
            self.to_y(self.me.gx, self.me.z, part, True)

    def at_distance(self, d, action):
        z = self.me.z
        if d == 0:
            action(z, None)
            return

        @pl.when(z >= d)
        def _():
            action(z - d, True)

        @pl.when(z + d <= 3)
        def _():
            action(z + d, False)

    def inline(self, d, parts):
        me = self.me

        def action(zz, upward):
            for part in parts:
                self.arrive(me.gx, zz, part)
                self.along(zz, part, upward)
                self.to_x(me.gx, zz, part)
                self.to_y(me.gx, zz, part)

        self.at_distance(d, action)

    def side(self, d, parts):
        me = self.me

        def action(zz, _):
            for part in parts:
                if part % 2 == 0:
                    column = self.column(self.ox, me.y)
                    self.arrive(column, zz, part)
                    self.to_y(column, zz, part)
                else:
                    column = self.column(me.x, self.oy)
                    self.arrive(column, zz, part)
                    self.to_x(column, zz, part)

        self.at_distance(d, action)

    def last_columns(self, part):
        last = (self.me.x, self.oy) if part % 2 == 0 else (self.ox, self.me.y)
        return (self.column(*last), self.column(self.ox, self.oy))

    def far(self, d, parts):
        def action(zz, _):
            for part in parts:
                for column in self.last_columns(part):
                    self.arrive(column, zz, part)

        self.at_distance(d, action)

    def core(self, column, part):
        rows = pl.ds(*self.parts[part])
        block = self.held(part).at[column, :, self.me.c, rows]
        return remote(block, block, self.csend.at[column, part], self.crecv.at[column, part], self.sibling)

    def core_inline(self, parts):
        for part in parts:
            self.core(self.me.gx, part).start()

    def core_side(self, parts):
        me = self.me
        for part in parts:
            self.core(self.column(self.ox, me.y) if part % 2 == 0 else self.column(me.x, self.oy), part).start()

    def core_far(self, parts):
        for part in parts:
            for column in self.last_columns(part):
                self.core(column, part).start()

    def cores(self, parts):
        for part in parts:
            for column in range(4):
                self.core(column, part).wait_recv()

    def sent(self, parts):
        me = self.me
        for part in parts:
            if part < 2:
                for d in (1, 2, 3):
                    self.straight(d, part).wait_send()
            for zz in range(4 if part >= 2 else 0):

                @pl.when((me.z < 3) & (zz <= me.z))
                def _():
                    self.copy(me.gx, zz, part, self.up, self.zsend.at[zz, part, 0]).wait_send()

                @pl.when((me.z > 0) & (zz >= me.z))
                def _():
                    self.copy(me.gx, zz, part, self.down, self.zsend.at[zz, part, 1]).wait_send()

            rows = pl.ds(*self.parts[part])
            four, eight = self.held(part).at[0, :, 0, rows], self.held(part).at[pl.ds(0, 2), :, 0, rows]
            sems = (self.xsend.at[part], self.ysend.at[part])
            few, many = sems if part % 2 == 0 else sems[::-1]
            remote(four, four, few, self.recv.at[0, 0, part], self.sibling).wait_send()
            remote(eight, eight, many, self.recv.at[0, 0, part], self.sibling).wait_send()

    def cores_sent(self, parts):
        for part in parts:
            for column in range(4):
                self.core(column, part).wait_send()

    def stages(self, parts):
        return [
            lambda: self.inline(1, parts),
            lambda: (self.side(0, parts), self.inline(2, parts)),
            lambda: (self.side(1, parts), self.inline(3, parts), self.core_inline(parts)),
            lambda: (self.side(2, parts), self.far(0, parts)),
            lambda: (self.side(3, parts), self.core_side(parts), self.far(1, parts)),
            lambda: (self.far(2, parts), self.far(3, parts), self.core_far(parts)),
        ]


def first_kernel(
    attn_h, inner_h, outer_h, norm_h, lengths_h, src_h, tgt_h,
    full, bounds_out, q_h, k_h, v_h, mix_h, lse_h, n1_h, s1_h,
    attn_f, inner_f, outer_f, norm_f, lengths, src, mine, bounds, tgt, attn,
    q, k, v, mix, lse, n1, s1, query_z, value_t, score_scr, small_scr,
    sems, zsend, xsend, ysend, csend, recv, crecv,
):
    me = Place()
    move = Mover(sems)
    loads = [
        move.start(a, b)
        for a, b in (
            (attn_h, attn_f), (inner_h, inner_f), (outer_h, outer_f), (norm_h, norm_f), (lengths_h, lengths), (src_h, src),
        )
    ]
    load_tgt = move.start(tgt_h, tgt)
    gathering = Gathering(me, mine, attn, full, zsend, xsend, ysend, csend, recv, crecv)
    barrier = pltpu.get_barrier_semaphore()

    def greet(target):
        pl.semaphore_signal(barrier, inc=1, device_id=target, device_id_type=MESH)

    peers = [gathering.x_next, gathering.y_next, gathering.sibling]
    peers += [me.target(me.x, me.y, lax.rem(me.z + d, 4), me.c) for d in (1, 2, 3)]
    for target in peers:
        greet(target)
    move.wait(loads[0])
    for j in range(8):
        mine[16 * j : 16 * j + 16, :] = attn_f[j].astype(bf16)
    attn[me.gx, me.z, me.c] = mine[0:64, :]
    pl.semaphore_wait(barrier, len(peers))
    early, late = (0, 1), (2, 3)
    gathering.own_straight(early)
    gathering.own_sides(early)
    move.wait(*loads[1:])
    for b in range(4):
        mine[128 + 16 * b : 144 + 16 * b, :] = inner_f[:, 512 * b : 512 * b + 512].astype(bf16)
    mine[192:256, :] = outer_f[...].astype(bf16)
    lanes = jnp.concatenate([norm_f[...], jnp.zeros((6, 112), f32)], axis=1)
    lanes = jnp.concatenate([lanes, jnp.zeros((10, 128), f32)], axis=0)
    lanes = pltpu.roll(lanes, me.gy * 16, 1).astype(bf16)
    mine[256:272, :] = jnp.concatenate([lanes, jnp.zeros((16, 384), bf16)], axis=1)
    gathering.own_z(late)
    gathering.own_sides(late)
    keep = move.start(mine.at[pl.ds(64, 208)], full.at[me.gx, me.z, me.c, pl.ds(64, 208)])
    find_bounds(lengths, src, bounds)
    move.start(bounds, bounds_out)
    sooner, later = gathering.stages(early), gathering.stages(late)
    for stage in (*sooner[:3], later[0], sooner[3], later[1], sooner[4], sooner[5]):
        stage()
    move.wait(keep)
    later[2]()
    gathering.cores(early)
    move.start(attn, full.at[:, :, :, pl.ds(0, 64)])
    move.wait(load_tgt)
    self_forward(
        tgt, attn.reshape(32, 64, 512), bounds, q, k, v, mix, lse, n1, s1, query_z, value_t, score_scr, small_scr,
        move, (q_h, k_h, v_h, mix_h, lse_h, n1_h, s1_h),
        (None, later[3], None, later[4], None, later[5]),
    )
    gathering.sent(early + late)
    gathering.cores_sent(early)
    gathering.cores(late)
    gathering.cores_sent(late)
    move.finish()


def gather_and_start(params, lengths, src_segments, tgt):
    length, width = tgt.shape
    kept, scratch = forward_sizes(length, width)
    row = (length, width)
    bounds = ((8, length), jnp.int32)
    full = ((4, 4, 2, 272, 512), bf16)
    loads = [(p.shape, f32) for p in params] + [(lengths.shape, jnp.int32), (src_segments.shape, jnp.int32)]
    return pl.pallas_call(
        first_kernel,
        out_shape=tuple(shape(*item) for item in [full, bounds] + kept),
        in_specs=[HBM_SPEC] * 7,
        out_specs=(HBM_SPEC,) * 9,
        scratch_shapes=vmem(
            *loads, ((272, 512), bf16), bounds, (row, bf16), ((4, 4, 2, 64, 512), bf16), *kept, *scratch,
        )
        + [dma(24), dma(4, 4, 2), dma(4), dma(4), dma(4, 4), dma(4, 4, 4), dma(4, 4)],
        compiler_params=pltpu.CompilerParams(collective_id=0, has_side_effects=True, vmem_limit_bytes=GRANT),
    )(*params, lengths, src_segments, tgt)


def start_kernel(
    full, lengths, src, tgt, bounds_out, q_h, k_h, v_h, mix_h, lse_h, n1_h, s1_h,
    bounds, attn, q, k, v, mix, lse, n1, s1, query_z, value_t, score_scr, small_scr, sems,
):
    move = Mover(sems)
    load = move.start(full.at[:, pl.ds(0, attn.shape[1])], attn)
    find_bounds(lengths, src, bounds)
    move.start(bounds, bounds_out)
    move.wait(load)
    self_forward(
        tgt, attn, bounds, q, k, v, mix, lse, n1, s1, query_z, value_t, score_scr, small_scr,
        move, (q_h, k_h, v_h, mix_h, lse_h, n1_h, s1_h), (),
    )
    move.finish()


def start_only(full, lengths, src_segments, tgt):
    length, width = tgt.shape
    kept, scratch = forward_sizes(length, width)
    bounds = ((8, length), jnp.int32)
    return pl.pallas_call(
        start_kernel,
        out_shape=tuple(shape(*item) for item in [bounds] + kept),
        in_specs=[HBM_SPEC] + [VMEM_SPEC] * 3,
        out_specs=(HBM_SPEC,) * 8,
        scratch_shapes=vmem(bounds, ((full.shape[0], 64, width), bf16), *kept, *scratch) + [dma(16)],
        compiler_params=pltpu.CompilerParams(vmem_limit_bytes=GRANT),
    )(full, lengths, src_segments, tgt)


def middle(bounds, full, memory, cotangent, n1, s1):
    length, width = n1.shape
    keys = memory.shape[0]
    blocks = full.shape[0]
    ffn_rows = full.shape[1] - 144
    hidden = ffn_rows * blocks // 2 * full.shape[2] // width
    pairs = width // LANES
    row, mem_row = (length, width), (keys, width)
    zeroed = ((pairs, 2 * length, LANES), bf16)
    gffn, gcross = ((blocks, ffn_rows, width), bf16), ((blocks, 64, width), bf16)
    outs = [(row, bf16), (row, f32), (mem_row, bf16), gffn, gcross, ((8, width), f32)]
    scratch = vmem(
        (bounds.shape, jnp.int32), ((blocks, 16, width // 4), bf16), gcross, gffn, (mem_row, bf16), (row, bf16), (row, f32),
        ((length, 1), f32), (row, bf16), (mem_row, bf16), (mem_row, bf16), (row, bf16),
        ((length // QB, pairs, 2 * QB), f32), zeroed, zeroed, ((width, keys), bf16), ((pairs, keys + KB, 2 * QB), f32),
        ((pairs, LANES, QB), f32), ((length, hidden), bf16), ((length, hidden), bf16), (row, bf16), (row, bf16),
        (row, f32), (row, bf16), (row, bf16), (row, bf16), (mem_row, f32), (mem_row, f32), (row, bf16), (mem_row, bf16),
        gffn, gcross, ((6, 8, width), f32), ((8, width), f32),
    )
    return pl.pallas_call(
        middle_kernel,
        out_shape=tuple(shape(*item) for item in outs),
        in_specs=[SMEM_SPEC] + [HBM_SPEC] * 6,
        out_specs=(HBM_SPEC,) * 5 + (VMEM_SPEC,),
        scratch_shapes=scratch + [dma(16)],
        compiler_params=pltpu.CompilerParams(vmem_limit_bytes=GRANT),
    )(bounds, bounds, full, memory, cotangent, n1, s1)


OUTER_ROWS = slice(96, 160)


def attn_rows(j):
    return 192 + 16 * j if j < 4 else 64 + 16 * (j - 4) if j < 6 else 160 + 16 * (j - 6)


def add_rows(dst, *sources):
    total = sources[0][...].astype(f32)
    for source in sources[1:]:
        total = total + source[...].astype(f32)
    dst[...] = total.astype(dst.dtype)


class Summing:
    order = (2, 1, 3, 0)

    def __init__(self, me, sources, rows, pieces, first_a, first_b, second_a, second_b, third, result, sems):
        self.me, self.sources, self.rows, self.pieces = me, sources, rows, pieces
        self.first_a, self.first_b, self.second_a, self.second_b, self.third = first_a, first_b, second_a, second_b, third
        self.result = result
        (self.lsem, self.csend, self.crecv, self.send1, self.recv1, self.send2, self.recv2, self.send3, self.recv3) = sems
        x, y, z, c = me.x, me.y, me.z, me.c
        self.ox, self.oy, self.oc = 1 - x, 1 - y, 1 - c
        self.x_next = me.target(self.ox, y, z, c)
        self.y_next = me.target(x, self.oy, z, c)
        self.sibling = me.target(x, y, z, self.oc)
        self.zs = [lax.rem(z + d, 4) for d in range(4)]
        self.half = first_a.shape[2]
        self.top, self.bottom = pl.ds(0, self.half), pl.ds(self.half, self.half)
        self.pending, self.cores, self.own = [], {}, {}
        self.firsts, self.seconds, self.thirds = {}, {}, {}

    def send(self, *args):
        copy = remote(*args)
        copy.start()
        self.pending.append(copy)
        return copy

    def load(self):
        for d in self.order:
            for k, (source, kept, _) in enumerate(self.sources):
                if kept is not None:
                    copy = pltpu.make_async_copy(source.at[:, self.zs[d], self.me.c], kept.at[d], self.lsem.at[d, k])
                    copy.start()
                    self.own[d, k] = copy

    def core(self):
        for d in self.order:
            for k, (source, _, got) in enumerate(self.sources):
                self.cores[d, k] = self.send(
                    source.at[:, self.zs[d], self.oc], got.at[d], self.csend.at[d, k], self.crecv.at[d, k], self.sibling
                )

    def stage1(self, d):
        me = self.me
        for k in range(len(self.sources)):
            if (d, k) in self.own:
                self.own[d, k].wait()
            self.cores[d, k].wait_recv()

        def add(i):
            piece = self.pieces.at[d, i // 2, lax.rem(i, 2)]
            for start, count, k, first in self.rows:
                source, kept, got = self.sources[k]
                held = source.at[i, self.zs[d], me.c] if kept is None else kept.at[d, i]
                part = pl.ds(first, count)
                add_rows(piece.at[pl.ds(start, count)], held.at[part], got.at[d, i, part])

        each_chunk(4, add)
        self.firsts[d] = (
            self.send(
                self.pieces.at[d, self.oy, :, self.top], self.first_a.at[d], self.send1.at[d, 0], self.recv1.at[d, 0],
                self.y_next,
            ),
            self.send(
                self.pieces.at[d, :, self.ox, self.bottom], self.first_b.at[d], self.send1.at[d, 1],
                self.recv1.at[d, 1], self.x_next,
            ),
        )

    def stage2(self, d):
        me = self.me
        self.firsts[d][0].wait_recv()
        part = self.pieces.at[d, me.y, self.ox, self.top]
        add_rows(part, part, self.first_a.at[d, self.ox])
        one = self.send(part, self.second_a.at[d], self.send2.at[d, 0], self.recv2.at[d, 0], self.x_next)
        self.firsts[d][1].wait_recv()
        part = self.pieces.at[d, self.oy, me.x, self.bottom]
        add_rows(part, part, self.first_b.at[d, self.oy])
        two = self.send(part, self.second_b.at[d], self.send2.at[d, 1], self.recv2.at[d, 1], self.y_next)
        self.seconds[d] = (one, two)

    def stage3(self, d):
        me = self.me
        for copy in self.seconds[d]:
            copy.wait_recv()
        for rows, first, second, at in (
            (self.top, self.first_a, self.second_a, me.x), (self.bottom, self.first_b, self.second_b, me.y),
        ):
            part = self.pieces.at[d, me.y, me.x, rows]
            add_rows(part if d else self.result.at[rows], part, first.at[d, at], second.at[d])
        if d:
            self.thirds[d] = self.send(
                self.pieces.at[d, me.y, me.x], self.third.at[d - 1], self.send3.at[d - 1], self.recv3.at[d - 1],
                me.target(me.x, me.y, self.zs[d], me.c),
            )

    def end(self):
        for d in (1, 2, 3):
            self.thirds[d].wait_recv()
        add_rows(self.result, self.result, self.third.at[0], self.third.at[1], self.third.at[2])


def last_kernel(
    full, bounds_h, tgt_h, q_h, k_h, v_h, mix_h, lse_h, d1_h, gffn, gcross, gnorm_h,
    attn_p, inner_p, outer_p, norm_p, attn_m, in_m, out_m, norm_m,
    tgrad_h, g_ref, gn_ref, totals_ref,
    bounds, tgt, attn, q, k, v, mix, lse, d1, tgrad, gself, query_z, grad_z, key_t, grad_scr, dq_scr, dk_scr, dv_scr,
    small_scr, d1_scr, own_ffn, own_cross, got_ffn, got_cross, pieces, first_a, first_b, second_a, second_b, third,
    got_self, pieces2, first_a2, first_b2, second_a2, second_b2, third2, vectors, squares, tiles,
    msems, psems, *sems,
):
    me = Place()
    move = Mover(msems)
    others = me.others()
    barrier = pltpu.get_barrier_semaphore()
    for target in others:
        pl.semaphore_signal(barrier, inc=1, device_id=target, device_id_type=MESH)
    load_first = [move.start(a, b) for a, b in ((gnorm_h, vectors.at[0]), (d1_h, d1), (full.at[:, pl.ds(0, 64)], attn))]
    load_mix = move.start(mix_h, mix)
    load_rest = [
        move.start(a, b)
        for a, b in ((q_h, q), (k_h, k), (v_h, v), (lse_h, lse), (bounds_h, bounds), (tgt_h, tgt))
    ]
    sems1, sems2, (nsend, nrecv, tsend, trecv) = sems[0:9], sems[9:18], sems[18:22]
    big = Summing(
        me, [(gffn, own_ffn, got_ffn), (gcross, own_cross, got_cross)],
        [(0, 64, 0, 0), (64, 32, 1, 0), (96, 64, 0, 64), (160, 32, 1, 32)],
        pieces, first_a, first_b, second_a, second_b, third, g_ref.at[pl.ds(0, 192)], sems1,
    )
    rest = Summing(
        me, [(gself, None, got_self)], [(0, 64, 0, 0)],
        pieces2, first_a2, first_b2, second_a2, second_b2, third2, g_ref.at[pl.ds(192, 64)], sems2,
    )
    big.load()
    pl.semaphore_wait(barrier, len(others))
    big.core()
    move.wait(*load_first)
    norm_copies = [big.send(vectors.at[0], vectors.at[1], nsend.at[0], nrecv.at[0], big.sibling)]

    def norm_step(stage, target):
        norm_copies[-1].wait_recv()
        vectors[2 * stage] = vectors[2 * stage - 2] + vectors[2 * stage - 1]
        norm_copies.append(
            big.send(vectors.at[2 * stage], vectors.at[2 * stage + 1], nsend.at[stage], nrecv.at[stage], target)
        )

    def norm_last():
        norm_copies[-1].wait_recv()
        vectors[6] = vectors[4] + vectors[5]
        for d in range(1, 4):
            target = me.target(me.x, me.y, big.zs[d], me.c)
            norm_copies.append(big.send(vectors.at[6], vectors.at[6 + d], nsend.at[2 + d], nrecv.at[2 + d], target))

    far, up, down, here = big.order
    steps = [
        None,
        lambda: norm_step(1, big.x_next),
        None,
        lambda: (big.stage2(far), big.stage1(down)),
        None,
        lambda: (big.stage2(up), big.stage3(far), big.stage1(here), norm_step(2, big.y_next)),
        None,
        lambda: (big.stage2(down), big.stage3(up)),
    ]

    begin = (lambda: big.stage1(far), lambda: big.stage1(up))

    def late():
        rest.core()
        big.stage2(here)
        rest.stage1(far)
        rest.stage1(up)
        big.stage3(down)
        norm_last()

    move.wait(load_mix, *load_rest)
    self_backward(
        tgt, attn, bounds, q, k, v, mix, lse, d1, tgrad, gself.reshape(32, 64, 512),
        query_z, grad_z, key_t, grad_scr, dq_scr, dk_scr, dv_scr, small_scr, d1_scr, steps, begin, late,
    )
    move.start(tgrad, tgrad_h)
    rest.stage1(down)
    rest.stage1(here)
    big.stage3(here)
    rest.stage2(far)
    rest.stage2(up)
    rest.stage3(far)
    rest.stage2(down)
    rest.stage3(up)
    rest.stage2(here)
    rest.stage3(down)
    rest.stage3(here)
    big.end()
    for copy in norm_copies[3:]:
        copy.wait_recv()
    vectors[10] = (vectors[6] + vectors[8]) + (vectors[7] + vectors[9])
    lanes = vectors[10, :, pl.ds(pl.multiple_of(me.gx * 128, 128), 128)]
    gn_ref[...] = pltpu.roll(lanes, lax.rem(128 - me.gy * 16, 128), 1)

    def put(t, pairs):
        for i in range(2):
            squares[16 * i + t : 16 * i + t + 1, :] = sum(
                jnp.sum(pair[i] * pair[i], axis=0, keepdims=True) for pair in pairs
            )

    def direction(*args):
        return adam_direction(*args)[0]

    def put_attn(j):
        grad = g_ref[attn_rows(j) : attn_rows(j) + 16, :]
        put(j, [(attn_p[j], direction(attn_p[j], grad, (attn_m[0, j], attn_m[1, j])))])

    for j in range(4, 8):
        put_attn(j)
    pairs = []
    for b in range(4):
        cols = slice(512 * b, 512 * b + 512)
        grad = g_ref[16 * b : 16 * b + 16, :]
        pairs.append((inner_p[:, cols], direction(inner_p[:, cols], grad, (in_m[0, :, cols], in_m[1, :, cols]))))
    put(8, pairs)
    put(9, [(outer_p[...], direction(outer_p[...], g_ref[OUTER_ROWS, :], (out_m[0], out_m[1])))])
    master = norm_p[...]
    update = direction(master, gn_ref[0:6, 0:16], (norm_m[:, 0, :], norm_m[:, 1, :]))
    rest_lanes = jnp.zeros((6, 512 - 16), f32)
    master, update = (jnp.concatenate([item, rest_lanes], axis=1) for item in (master, update))
    for i in range(6):
        put(10 + i, [(master[i : i + 1], update[i : i + 1])])
    rest.end()
    for j in range(4):
        put_attn(j)
    folded = (squares[:, 0:128] + squares[:, 128:256]) + (squares[:, 256:384] + squares[:, 384:512])
    row = jnp.sum(folded.T, axis=0, keepdims=True)
    row = jnp.concatenate([row, jnp.zeros((1, 96), f32)], axis=1)
    tiles[me.here] = jnp.concatenate([row, jnp.zeros((7, 128), f32)], axis=0)
    for target in others:
        remote(tiles.at[me.here], tiles.at[me.here], tsend, trecv, target).start()
    for copy in big.pending + rest.pending:
        copy.wait_send()
    received = tiles.at[pl.ds(0, 31)]
    every = remote(received, received, tsend, trecv, big.sibling)
    every.wait_recv()
    every.wait_send()
    totals_ref[...] = jnp.sum(tiles[...], axis=0)
    move.finish()


def backward_scratch(length, width):
    pairs = width // LANES
    row = (length, width)
    zeroed = ((pairs, 2 * length, LANES), bf16)
    return [
        zeroed, zeroed, ((width, length), bf16), (row, bf16), (row, bf16), (row, f32), (row, f32),
        ((pairs, LANES, QB), f32), (row, bf16),
    ]


def finish_and_reduce(full, bounds, tgt, saved, d1, grads, norm_grad, params, moments):
    length, width = tgt.shape
    row = (length, width)
    lse = (length // QB, width // LANES, 2 * QB)

    def sums(half):
        return [
            ((4, 2, 2, 2 * half, 512), bf16), ((4, 2, half, 512), bf16), ((4, 2, half, 512), bf16),
            ((4, half, 512), bf16), ((4, half, 512), bf16), ((3, 2 * half, 512), bf16),
        ]

    scratch = vmem(
        (bounds.shape, jnp.int32), (row, bf16), ((32, 64, 512), bf16), *[(row, bf16)] * 4, (lse, f32), (row, f32),
        (row, bf16), ((4, 4, 2, 64, 512), bf16), *backward_scratch(length, width),
        ((4, 4, 128, 512), bf16), ((4, 4, 64, 512), bf16), ((4, 4, 128, 512), bf16), ((4, 4, 64, 512), bf16), *sums(96),
        ((4, 4, 64, 512), bf16), *sums(32), ((11, 8, 512), f32), ((32, 512), f32), ((32, 8, 128), f32),
    )
    round_sems = [dma(4, 2), dma(4, 2), dma(4, 2), dma(4, 2), dma(4, 2), dma(4, 2), dma(4, 2), dma(3), dma(3)]
    split = [grad.reshape(4, 4, 2, grad.shape[1], 512) for grad in grads]
    return pl.pallas_call(
        last_kernel,
        out_shape=(shape(row, bf16), shape((256, 512), f32), shape((8, 128), f32), shape((8, 128), f32)),
        in_specs=[HBM_SPEC] * 12 + [VMEM_SPEC] * 8,
        out_specs=(HBM_SPEC, VMEM_SPEC, VMEM_SPEC, VMEM_SPEC),
        scratch_shapes=scratch + [dma(16), dma(1)] + round_sems + round_sems + [dma(6), dma(6)] + [pltpu.SemaphoreType.DMA] * 2,
        compiler_params=pltpu.CompilerParams(collective_id=1, has_side_effects=True, vmem_limit_bytes=GRANT),
    )(full, bounds, tgt, *saved, d1, *split, norm_grad, *params, *moments)


def finish_kernel(
    full, bounds, tgt, q, k, v, mix, lse, d1, tgrad, gself,
    attn, query_z, grad_z, key_t, grad_scr, dq_scr, dk_scr, dv_scr, small_scr, d1_scr, sems,
):
    move = Mover(sems)
    move.wait(move.start(full.at[:, pl.ds(0, attn.shape[1])], attn))
    self_backward(
        tgt, attn, bounds, q, k, v, mix, lse, d1, tgrad, gself,
        query_z, grad_z, key_t, grad_scr, dq_scr, dk_scr, dv_scr, small_scr, d1_scr, (), (lambda: None,) * 2, lambda: None,
    )


def finish_only(full, bounds, tgt, saved, d1):
    length, width = tgt.shape
    gself = ((full.shape[0], 64, width), bf16)
    return pl.pallas_call(
        finish_kernel,
        out_shape=(shape((length, width), bf16), shape(*gself)),
        in_specs=[HBM_SPEC] + [VMEM_SPEC] * 8,
        out_specs=(VMEM_SPEC, VMEM_SPEC),
        scratch_shapes=vmem(gself, *backward_scratch(length, width)) + [dma(2)],
        compiler_params=pltpu.CompilerParams(vmem_limit_bytes=GRANT),
    )(full, bounds, tgt, *saved, d1)


def update_kernel(*refs):
    ins, outs = refs[:12], refs[12:30]
    held, made, sems = refs[30:42], refs[42:59], refs[59]
    move = Mover(sems)
    order = (3, 2, 1, 7, 11, 6, 10, 5, 9, 4, 8, 0)
    loads = {i: move.start(ins[i], held[i]) for i in order}
    g_ref, gn_ref, totals_ref, attn, inner, outer, norm, attn_m, in_m, out_m, norm_m = held[1:]
    norms_ref = made[16]

    def results(t):
        return [(made[i], outs[1 + i]) for i in (t, 4 + 2 * t, 5 + 2 * t, 12 + t)]

    def step(t, master, gradient, moments, ratio, refs, place):
        direction, first_moment, second_moment = adam_direction(master, gradient, moments)
        value = master - ratio * direction
        for (ref, _), item in zip(refs, (value, first_moment, second_moment, value.astype(bf16))):
            ref[place] = item

    def leave(refs):
        for ref, out in refs:
            move.start(ref, out)

    move.wait(loads[3], loads[2], loads[7], loads[11])
    roots = jnp.sqrt(totals_ref[0:1, 0:32])
    norms_ref[0:1, :] = roots[:, 0:16]
    norms_ref[1:2, :] = roots[:, 16:32]
    move.start(norms_ref, outs[17])
    ratio = learn_rate * (roots[:, 0:16] / roots[:, 16:32])
    vectors = results(3)
    for i in range(6):
        one = slice(i, i + 1)
        moments = (norm_m[i, 0:1], norm_m[i, 1:2])
        step(10 + i, norm[one], gn_ref[one, 0:16], moments, ratio[:, 10 + i : 11 + i], vectors, one)
    leave(vectors)
    move.wait(loads[1], loads[6], loads[10])
    moments = (out_m[0], out_m[1])
    step(2, outer[...], g_ref[OUTER_ROWS, :], moments, ratio[:, 9:10], results(2), ...)
    leave(results(2))
    move.wait(loads[5], loads[9])
    for b in range(4):
        cols = slice(512 * b, 512 * b + 512)
        moments = (in_m[0, :, cols], in_m[1, :, cols])
        step(1, inner[:, cols], g_ref[16 * b : 16 * b + 16, :], moments, ratio[:, 8:9], results(1), (slice(None), cols))
    leave(results(1))
    move.wait(loads[4], loads[8], loads[0])
    move.start(held[0], outs[0])
    for j in range(8):
        grad = g_ref[attn_rows(j) : attn_rows(j) + 16, :]
        step(0, attn[j], grad, (attn_m[0, j], attn_m[1, j]), ratio[:, j : j + 1], results(0), j)
    leave(results(0))
    move.finish()


def update_params(summed, params, moments):
    args = (*summed, *params, *moments)
    outs = [shape(p.shape, f32) for p in params]
    outs += [shape(p.shape, f32) for p in params for _ in range(2)]
    outs += [shape(p.shape, bf16) for p in params] + [shape((2, 16), f32)]
    return pl.pallas_call(
        update_kernel,
        out_shape=(shape(summed[0].shape, bf16), *outs),
        in_specs=[HBM_SPEC] * len(args),
        out_specs=(HBM_SPEC,) * (1 + len(outs)),
        scratch_shapes=vmem(*((item.shape, item.dtype) for item in (*args, *outs))) + [dma(32)],
        compiler_params=pltpu.CompilerParams(vmem_limit_bytes=GRANT),
    )(*args)


def tensor_squares(attn_part, inner_part, outer_part, norm_part):
    return jnp.concatenate(
        [
            jnp.sum(attn_part * attn_part, axis=(1, 2)),
            jnp.sum(inner_part * inner_part)[None],
            jnp.sum(outer_part * outer_part)[None],
            jnp.sum(norm_part * norm_part, axis=1),
        ]
    )


def blocked(matrix, width):
    blocks = matrix.shape[0] // 16
    cols = matrix.shape[1] // width
    return matrix.reshape(blocks, 16, cols, width).transpose(0, 2, 1, 3).reshape(blocks, cols * 16, width)


def unblocked(blocks, width):
    count = blocks.shape[0]
    cols = blocks.shape[1] // 16
    return blocks.reshape(count, cols, 16, width).transpose(0, 2, 1, 3).reshape(count * 16, cols * width)


def gather_any(attn_w, ffn_in, ffn_out, norm_params):
    width = attn_w.shape[2]
    attn = lax.all_gather(attn_w.astype(bf16), AXES, axis=1, tiled=True)
    inner = lax.all_gather(ffn_in.astype(bf16), AXES, axis=0, tiled=True)
    outer = lax.all_gather(ffn_out.astype(bf16), AXES, axis=0, tiled=True)
    norm = lax.all_gather(norm_params.astype(bf16), AXES, axis=1, tiled=True)
    blocks = width // 16
    attn = attn.reshape(8, blocks, 16, width).transpose(1, 0, 2, 3).reshape(blocks, 8 * 16, width)
    lanes = jnp.pad(norm, ((0, 10), (0, 0))).reshape(16, 4, 1, width // 4).transpose(1, 2, 0, 3)
    lanes = jnp.pad(lanes, ((0, 0), (0, blocks // 4 - 1), (0, 0), (0, width - width // 4))).reshape(blocks, 16, width)
    return jnp.concatenate([attn, blocked(inner, width), outer.reshape(blocks, -1, width), lanes], axis=1)


def reduce_any(grads, norm_grad, params, moments):
    grad_ffn, grad_cross, grad_self = grads
    width = grad_ffn.shape[2]
    blocks = width // 16
    attn_w, ffn_in, ffn_out, norm_params = params
    attn_m, in_m, out_m, norm_m = moments
    stack = jnp.concatenate([grad_self, grad_cross], axis=1)
    stack = stack.reshape(blocks, 8, 16, width).transpose(1, 0, 2, 3).reshape(8, width, width)
    rows = ffn_in.shape[1] // width * 16
    inner = unblocked(grad_ffn[:, :rows], width)
    outer = grad_ffn[:, rows:].reshape(-1, width)
    shard_attn = lax.psum_scatter(stack, AXES, scatter_dimension=1, tiled=True).astype(f32)
    shard_inner = lax.psum_scatter(inner, AXES, scatter_dimension=0, tiled=True).astype(f32)
    shard_outer = lax.psum_scatter(outer, AXES, scatter_dimension=0, tiled=True).astype(f32)
    shard_norm = lax.psum_scatter(norm_grad, AXES, scatter_dimension=1, tiled=True)
    attn_dir, attn_first, attn_second = adam_direction(attn_w, shard_attn, attn_m)
    inner_dir, inner_first, inner_second = adam_direction(ffn_in, shard_inner, in_m)
    outer_dir, outer_first, outer_second = adam_direction(ffn_out, shard_outer, out_m)
    norm_dir, norm_first, norm_second = adam_direction(norm_params, shard_norm, norm_m)
    weight_total, update_total = lax.psum(
        (tensor_squares(*params), tensor_squares(attn_dir, inner_dir, outer_dir, norm_dir)), AXES
    )
    ratio = jnp.sqrt(weight_total) / jnp.sqrt(update_total)
    attn_new = attn_w - learn_rate * ratio[0:8][:, None, None] * attn_dir
    in_new = ffn_in - learn_rate * ratio[8] * inner_dir
    out_new = ffn_out - learn_rate * ratio[9] * outer_dir
    norm_new = norm_params - learn_rate * ratio[10:16][:, None] * norm_dir
    norms = jnp.stack([jnp.sqrt(weight_total), jnp.sqrt(update_total)])
    return (
        attn_new, in_new, out_new, norm_new,
        attn_first, attn_second, inner_first, inner_second, outer_first, outer_second, norm_first, norm_second,
        attn_new.astype(bf16), in_new.astype(bf16), out_new.astype(bf16), norm_new.astype(bf16), norms,
    )


def on_device(
    close, tgt, memory, cotangent, tgt_lengths, src_segments, attn_w, ffn_in, ffn_out, norm_params,
    attn_moments, in_moments, out_moments, norm_moments,
):
    params = (attn_w, ffn_in, ffn_out, norm_params)
    moments = (attn_moments, in_moments, out_moments, norm_moments)
    if close and tgt.shape[0] == 1:
        full, bounds, *state = gather_and_start(params, tgt_lengths, src_segments, tgt[0])
        full = full.reshape(32, *full.shape[3:])
        saved, (n1, s1) = state[:5], state[5:]
        layer_out, d1, mem_grad, grad_ffn, grad_cross, norm_grad = middle(
            bounds, full, memory[0], cotangent[0], n1, s1
        )
        moments = (*moments[:3], norm_moments.transpose(1, 0, 2))
        summed = finish_and_reduce(
            full, bounds, tgt[0], saved, d1, (grad_ffn, grad_cross), norm_grad, params, moments
        )
        tgt_grad, *updated = update_params(summed, params, moments)
        return (layer_out[None], tgt_grad[None], mem_grad[None], *updated)
    full = gather_any(*params)
    parts = []
    for r in range(tgt.shape[0]):
        bounds, *state = start_only(full, tgt_lengths[r : r + 1], src_segments[r : r + 1], tgt[r])
        saved, (n1, s1) = state[:5], state[5:]
        layer_out, d1, mem_grad, grad_ffn, grad_cross, norm_grad = middle(
            bounds, full, memory[r], cotangent[r], n1, s1
        )
        tgt_grad, grad_self = finish_only(full, bounds, tgt[r], saved, d1)
        parts.append((layer_out, tgt_grad, mem_grad, grad_ffn, grad_cross, grad_self, norm_grad[0:6]))
    outs = [jnp.stack([part[i] for part in parts]) for i in range(3)]
    sums = [sum(part[i].astype(f32) for part in parts) for i in range(3, 7)]
    grads = [grad.astype(bf16) for grad in sums[:3]]
    return (*outs, *reduce_any(grads, sums[3], params, moments))


def fits(mesh):
    return mesh.shape["gx"] == 4 and mesh.shape["gy"] == 8


def solution(mesh):
    rows = P(AXES, None, None)
    matrix = P(AXES, None)
    stack = P(None, AXES, None)
    vectors = P(None, AXES)
    return jax.shard_map(
        functools.partial(on_device, fits(mesh)),
        mesh=mesh,
        in_specs=(
            rows, rows, rows, matrix, matrix, stack, matrix, matrix, vectors,
            P(None, None, AXES, None), stack, stack, P(None, None, AXES),
        ),
        out_specs=(
            rows, rows, rows, stack, matrix, matrix, vectors, stack, stack, matrix, matrix, matrix, matrix,
            vectors, vectors, stack, matrix, matrix, vectors, P(),
        ),
        check_vma=False,
    )
```

```python
import functools

import jax
import jax.numpy as jnp
from jax import lax
from jax.experimental import pallas as pl
from jax.experimental.pallas import tpu as pltpu
from jax.sharding import PartitionSpec as P

HEAD_DIM = 64
STEP = 5

beta_first = 0.5
beta_second = 0.5
learn_rate = 0.5
decay_rate = 0.01
norm_eps = 1e-05
adam_eps = 1e-06

f32 = jnp.float32
bf16 = jnp.bfloat16
LANES = 128
QB = 128
KB = 256
RC = 256
LONGEST = 512
WAYS = 2
MASKED = -1e30
AXES = ("gx", "gy")
GRANT = 63 * 2**20


def nn(left, right):
    return lax.dot_general(left, right, (((1,), (0,)), ((), ())), preferred_element_type=f32)


def nt(left, right):
    return lax.dot_general(left, right, (((1,), (1,)), ((), ())), preferred_element_type=f32)


def tn(left, right):
    return lax.dot_general(left, right, (((0,), (0,)), ((), ())), preferred_element_type=f32)


def rows_of(step, size):
    return pl.ds(pl.multiple_of(step * size, size), size)


def each_chunk(count, body, ways=1):
    def step(index, carry):
        for way in range(ways):
            body(index * ways + way)
        return carry

    lax.fori_loop(0, count // ways, step, 0)


def spread_heads(dst, src):
    pairs = dst.shape[0]
    first = lax.broadcasted_iota(jnp.int32, (QB, LANES), 1) < HEAD_DIM
    zero = jnp.zeros((QB, LANES), bf16)

    def body(i):
        start = pl.multiple_of(i * 2 * QB, 2 * QB)
        for p in range(pairs):
            tile = src[rows_of(i, QB), p * LANES : (p + 1) * LANES]
            dst[p, pl.ds(start, QB), :] = jnp.where(first, tile, zero)
            dst[p, pl.ds(start + QB, QB), :] = jnp.where(first, zero, tile)

    each_chunk(src.shape[0] // QB, body)


def run_blocks(count, body, steps):
    if not steps:
        each_chunk(count, body)
        return
    for i in range(count):
        body(i)
        if i < len(steps) and steps[i] is not None:
            steps[i]()


def near_window(i):
    first = max(0, i - LONGEST // LANES) if isinstance(i, int) else jnp.maximum(i - LONGEST // LANES, 0)
    return first, (i + 1 - first + KB // LANES - 1) // (KB // LANES)


def bound_window(spans, count):
    def window(i):
        first = spans[i, 0] // LANES
        last = (spans[count + i, QB - 1] + LANES - 1) // LANES
        return first, ((last - first) * LANES + KB - 1) // KB

    return window


def key_block(first_key, j, keys):
    nominal = first_key * LANES + j * KB
    return pl.multiple_of(jnp.minimum(nominal, keys - KB), LANES), nominal


def block_bias(low, high, start, nominal):
    place = start + lax.broadcasted_iota(jnp.int32, (KB, QB), 0)
    bias = jnp.where((place >= jnp.maximum(low, nominal)) & (place < high), 0.0, MASKED).astype(f32)
    return jnp.concatenate([bias, bias], axis=1)


def attention(window, which, bounds, key_ref, value_t, query_z, mixed_ref, lse_ref, score_scr, out_scr, steps=()):
    keys = key_ref.shape[0]
    pairs = query_z.shape[0]
    fold = (KB // 8, 8, 2 * QB)

    def query_block(i):
        rows = rows_of(i, QB)
        pair_rows = rows_of(i, 2 * QB)
        low = bounds[2 * which : 2 * which + 1, rows]
        high = bounds[2 * which + 1 : 2 * which + 2, rows]
        first_key, blocks = window(i)
        out_scr[...] = jnp.zeros_like(out_scr)

        def scores(j, tops):
            start, nominal = key_block(first_key, j, keys)
            bias = block_bias(low, high, start, nominal)
            found = []
            raw = [
                nt(key_ref[pl.ds(start, KB), p * LANES : (p + 1) * LANES], query_z[p, pair_rows, :])
                for p in range(pairs)
            ]
            for p in range(pairs):
                score = raw[p] + bias
                score_scr[p, rows_of(j, KB), :] = score
                found.append(jnp.maximum(tops[p], jnp.max(score.reshape(fold), axis=0)))
            return tuple(found)

        tops = lax.fori_loop(
            0, blocks, scores, tuple(jnp.full((8, 2 * QB), MASKED, f32) for _ in range(pairs))
        )
        top = [jnp.max(t, axis=0, keepdims=True) for t in tops]

        def weigh(j, sums):
            start, _ = key_block(first_key, j, keys)
            found = []
            low_exps = []
            for p in range(pairs):
                exponent = jnp.exp(score_scr[p, rows_of(j, KB), :] - top[p])
                found.append(sums[p] + jnp.sum(exponent.reshape(fold), axis=0))
                low_exps.append(exponent.astype(bf16))
            for p in range(pairs):
                for h in range(2):
                    heads = slice(h * HEAD_DIM, (h + 1) * HEAD_DIM)
                    value = value_t[
                        p * LANES + h * HEAD_DIM : p * LANES + (h + 1) * HEAD_DIM, pl.ds(start, KB)
                    ]
                    out_scr[p, heads, :] += nn(value, low_exps[p][:, h * QB : (h + 1) * QB])
            return tuple(found)

        sums = lax.fori_loop(
            0, blocks, weigh, tuple(jnp.zeros((8, 2 * QB), f32) for _ in range(pairs))
        )
        for p in range(pairs):
            total = jnp.sum(sums[p], axis=0, keepdims=True)
            lse_ref[i, p : p + 1, :] = top[p] + jnp.log(total)
            inverse = 1.0 / total
            out = jnp.concatenate(
                [out_scr[p, 0:HEAD_DIM, :] * inverse[:, :QB], out_scr[p, HEAD_DIM:, :] * inverse[:, QB:]],
                axis=0,
            )
            mixed_ref[rows, p * LANES : (p + 1) * LANES] = out.T.astype(bf16)

    run_blocks(query_z.shape[1] // (2 * QB), query_block, steps)


def put_deltas(delta_ref, first_block, grad, mixed):
    for b in range(grad.shape[0] // QB):
        for p in range(grad.shape[1] // LANES):
            place = (slice(b * QB, (b + 1) * QB), slice(p * LANES, (p + 1) * LANES))
            product = (grad[place].astype(f32) * mixed[place].astype(f32)).T
            for h in range(2):
                delta_ref[first_block + b, p : p + 1, h * QB : (h + 1) * QB] = jnp.sum(
                    product[h * HEAD_DIM : (h + 1) * HEAD_DIM], axis=0, keepdims=True
                )


def attention_back(
    window, which, bounds, key_ref, key_t, value_ref, query_z, grad_z, delta_ref, lse_ref,
    dquery_ref, dkey_scr, dvalue_scr, dq_scr, steps=(),
):
    keys = key_ref.shape[0]
    pairs = query_z.shape[0]

    def query_block(i):
        rows = rows_of(i, QB)
        pair_rows = rows_of(i, 2 * QB)
        low = bounds[2 * which : 2 * which + 1, rows]
        high = bounds[2 * which + 1 : 2 * which + 2, rows]
        first_key, blocks = window(i)
        dq_scr[...] = jnp.zeros_like(dq_scr)
        deltas = [delta_ref[i, p : p + 1, :] for p in range(pairs)]

        def key_step(j):
            start, nominal = key_block(first_key, j, keys)
            bias = block_bias(low, high, start, nominal)
            block = pl.ds(start, KB)
            held = {}

            def first(p):
                lanes = slice(p * LANES, (p + 1) * LANES)
                held["s", p] = nt(key_ref[block, lanes], query_z[p, pair_rows, :])
                held["d", p] = nt(value_ref[block, lanes], grad_z[p, pair_rows, :])

            def second(p):
                prob = jnp.exp(held.pop(("s", p)) + bias - lse_ref[i, p : p + 1, :])
                held["ds", p] = (prob * (held.pop(("d", p)) - deltas[p])).astype(bf16)
                held["p", p] = prob.astype(bf16)

            def third(p):
                lanes = slice(p * LANES, (p + 1) * LANES)
                dscore = held["ds", p]
                dvalue_scr[block, lanes] += nn(held["p", p], grad_z[p, pair_rows, :])
                dkey_scr[block, lanes] += nn(dscore, query_z[p, pair_rows, :])
                for h in range(2):
                    heads = slice(h * HEAD_DIM, (h + 1) * HEAD_DIM)
                    key = key_t[
                        p * LANES + h * HEAD_DIM : p * LANES + (h + 1) * HEAD_DIM, block
                    ]
                    dq_scr[p, heads, :] += nn(key, dscore[:, h * QB : (h + 1) * QB])

            for step in (first, second, third):
                for p in range(pairs):
                    step(p)

        each_chunk(blocks, key_step)
        for p in range(pairs):
            dquery_ref[rows, p * LANES : (p + 1) * LANES] = (
                (dq_scr[p] * HEAD_DIM**-0.5).T.astype(bf16)
            )

    run_blocks(query_z.shape[1] // (2 * QB), query_block, steps)


def norm_parts(values):
    average = jnp.mean(values, axis=-1, keepdims=True)
    centred = values - average
    spread = jnp.mean(centred * centred, axis=-1, keepdims=True)
    inverse = lax.rsqrt(spread + norm_eps)
    return centred * inverse, inverse


def norm_back(gradient, normed, inverse, gain):
    scaled = gradient * gain
    first_mean = jnp.mean(scaled, axis=-1, keepdims=True)
    second_mean = jnp.mean(scaled * normed, axis=-1, keepdims=True)
    return inverse * (scaled - first_mean - normed * second_mean)


def fold_rows(values):
    return jnp.sum(values.reshape(values.shape[0] // 8, 8, values.shape[1]), axis=0)


def load_norms(norm_ref):
    group = norm_ref.shape[0] // 4
    blocks = [jnp.sum(norm_ref[group * i : group * (i + 1)].astype(f32), axis=0) for i in range(4)]
    rows = jnp.concatenate(blocks, axis=1)
    return [rows[i : i + 1, :] for i in range(6)]


def weight(ref, index):
    blocks = ref.shape[0]
    return ref[:, 16 * index : 16 * (index + 1), :].reshape(16 * blocks, ref.shape[2])


def put_gradient(ref, index, value):
    blocks = ref.shape[0]
    ref[:, 16 * index : 16 * (index + 1), :] = value.astype(bf16).reshape(blocks, 16, ref.shape[2])


def load_norm_rows(dst, norm_ref):
    for i, vector in enumerate(load_norms(norm_ref)):
        dst[i : i + 1, :] = vector


def sigmoid(values):
    return 0.5 * jnp.tanh(0.5 * values) + 0.5


class Mover:
    def __init__(self, sems):
        self.sems = sems
        self.count = 0
        self.open = []

    def start(self, src, dst):
        copy = pltpu.make_async_copy(src, dst, self.sems.at[self.count])
        self.count += 1
        copy.start()
        self.open.append(copy)
        return copy

    def wait(self, *copies):
        for copy in copies:
            copy.wait()
            self.open = [other for other in self.open if other is not copy]

    def finish(self):
        self.wait(*list(self.open))


def find_bounds(lengths, src_segments, bounds_ref, spans_ref):
    sentences = lengths.shape[1]
    length = bounds_ref.shape[1]
    row = lax.broadcasted_iota(jnp.int32, (sentences, sentences), 0)
    col = lax.broadcasted_iota(jnp.int32, (sentences, sentences), 1)
    sizes = jnp.broadcast_to(lengths[...].astype(f32), (sentences, sentences))

    def total(mask, values):
        return jnp.sum(jnp.where(mask, values, 0.0), axis=1, keepdims=True)

    own = total(col == row, sizes)
    starts = total(col < row, sizes)
    ends = starts + own
    sources = src_segments.shape[1]
    number = lax.broadcasted_iota(jnp.int32, (sentences, sources), 0)
    count = total(jnp.broadcast_to(src_segments[...], (sentences, sources)) == number, 1.0)
    places = lax.broadcasted_iota(jnp.int32, (sentences, length), 1).astype(f32)

    def gather(edges, values):
        return jnp.sum(jnp.where(edges <= places, values, 0.0), axis=0, keepdims=True).astype(jnp.int32)

    bounds_ref[0:1, :] = gather(ends, own)
    bounds_ref[1:2, :] = lax.broadcasted_iota(jnp.int32, (1, length), 1) + 1
    bounds_ref[2:3, :] = gather(ends, count)
    bounds_ref[3:4, :] = gather(starts, count)
    bounds_ref[4:8, :] = jnp.zeros((4, length), jnp.int32)
    blocks = length // QB
    for i in range(blocks):
        spans_ref[i : i + 1, :] = bounds_ref[2:3, i * QB : (i + 1) * QB]
        spans_ref[blocks + i : blocks + i + 1, :] = bounds_ref[3:4, i * QB : (i + 1) * QB]


def self_forward(tgt, attn, bounds, q, k, v, mix, lse, n1, s1, query_z, value_t, score_scr, out_scr, move, outs, steps):
    chunks = tgt.shape[0] // RC
    scale = jnp.array(HEAD_DIM**-0.5, bf16)

    def project(c):
        rows = rows_of(c, RC)
        x = tgt[rows, :]
        q[rows, :] = nn(x, weight(attn, 0)).astype(bf16) * scale
        k[rows, :] = nn(x, weight(attn, 1)).astype(bf16)
        v[rows, :] = nn(x, weight(attn, 2)).astype(bf16)

    each_chunk(chunks, project, 2)
    for i, ref in enumerate((q, k, v)):
        move.start(ref, outs[i])
    spread_heads(query_z, q)
    value_t[...] = v[...].T
    attention(near_window, 0, bounds, k, value_t, query_z, mix, lse, score_scr, out_scr, steps)
    move.start(mix, outs[3])
    move.start(lse, outs[4])

    def middle(c):
        rows = rows_of(c, RC)
        normed, inverse = norm_parts(tgt[rows, :].astype(f32) + nn(mix[rows, :], weight(attn, 3)))
        n1[rows, :] = normed
        s1[rows, :] = inverse

    each_chunk(chunks, middle, 2)
    move.start(n1, outs[5])
    move.start(s1, outs[6])


def middle_kernel(
    spans, bounds_h, full, memory_h, cot_h, n1_h, s1_h,
    out_h, d1_h, mgrad_h, gffn_h, gcross_h, gnorm_ref,
    bounds, norm_b, attn, ffn, memory, cot, n1, s1, cq, ck, cv, cmix, clse, query_z, grad_z, turned, score_scr, small_scr,
    act_scr, dpre_scr, h2_scr, d3_scr, d2_scr, d2b_scr, grad_scr, dq_scr, dk_scr, dv_scr, out_scr, mgrad, gffn, gcross,
    sums, norm, delta, sems,
):
    width = n1.shape[1]
    chunks = n1.shape[0] // RC
    scale = jnp.array(HEAD_DIM**-0.5, bf16)
    move = Mover(sems)
    rows_cross = attn.shape[1]
    norm_rows = pl.ds(full.shape[1] - 16, 16)
    load_small = [move.start(full.at[:, norm_rows, pl.ds(0, width // 4)], norm_b), move.start(bounds_h, bounds)]
    load_cross = move.start(full.at[:, pl.ds(rows_cross, rows_cross)], attn)
    load_memory = move.start(memory_h, memory)
    load_n1 = move.start(n1_h, n1)
    load_ffn = move.start(full.at[:, pl.ds(2 * rows_cross, ffn.shape[1])], ffn)
    load_rest = [move.start(cot_h, cot), move.start(s1_h, s1)]
    sums[...] = jnp.zeros_like(sums)
    move.wait(*load_small)
    load_norm_rows(norm, norm_b)
    move.wait(load_cross, load_memory)

    def h1_of(rows):
        return n1[rows, :] * norm[0:1, :] + norm[1:2, :]

    def project(c):
        rows = rows_of(c, RC)
        mem = memory[rows, :]
        ck[rows, :] = nn(mem, weight(attn, 1)).astype(bf16)
        cv[rows, :] = nn(mem, weight(attn, 2)).astype(bf16)

    def project_queries(c):
        rows = rows_of(c, RC)
        cq[rows, :] = nn(h1_of(rows).astype(bf16), weight(attn, 0)).astype(bf16) * scale

    each_chunk(chunks, project, 2)
    turned[...] = cv[...].T
    move.wait(load_n1)
    each_chunk(chunks, project_queries, 2)
    spread_heads(query_z, cq)
    window = bound_window(spans, n1.shape[0] // QB)
    attention(window, 1, bounds, ck, turned, query_z, cmix, clse, score_scr, small_scr)
    move.wait(load_ffn, *load_rest)
    blocks = ffn.shape[0]
    parts = act_scr.shape[1] // width
    share = blocks // parts

    def outer(b):
        return ffn[share * b : share * (b + 1), 16 * parts :, :].reshape(width, width)

    def body(c):
        rows = [pl.ds(pl.multiple_of((c * WAYS + w) * RC, RC), RC) for w in range(WAYS)]
        ways = range(WAYS)
        state = [{} for _ in ways]

        def enter(w):
            st = state[w]
            st["n2"], st["s2"] = norm_parts(h1_of(rows[w]) + nn(cmix[rows[w], :], weight(attn, 3)))
            st["third"] = st["n2"] * norm[2:3, :] + norm[3:4, :]
            st["h2b"] = st["third"].astype(bf16)
            h2_scr[rows[w], :] = st["h2b"]

        def pre(w, b):
            state[w]["pre", b] = nn(state[w]["h2b"], weight(ffn, b))

        def act(w, b):
            st = state[w]
            sig = sigmoid(st["pre", b])
            swish = st.pop(("pre", b)) * sig
            st["act", b] = swish.astype(bf16)
            act_scr[rows[w], width * b : width * (b + 1)] = st["act", b]
            st["slope", b] = sig + swish * (1.0 - sig)

        def out(w, b):
            st = state[w]
            st["third"] = st["third"] + nn(st.pop(("act", b)), outer(b))

        def turn(w):
            st = state[w]
            n3, s3 = norm_parts(st.pop("third"))
            out_scr[rows[w], :] = (n3 * norm[4:5, :] + norm[5:6, :]).astype(bf16)
            up = cot[rows[w], :].astype(f32)
            sums[4] += fold_rows(up * n3)
            sums[5] += fold_rows(up)
            st["dh2"] = norm_back(up, n3, s3, norm[4:5, :])
            st["d3b"] = st["dh2"].astype(bf16)
            d3_scr[rows[w], :] = st["d3b"]

        def dact(w, b):
            state[w]["dact", b] = nt(state[w]["d3b"], outer(b))

        def dpre(w, b):
            st = state[w]
            st["dpre", b] = (st.pop(("dact", b)) * st.pop(("slope", b))).astype(bf16)
            dpre_scr[rows[w], width * b : width * (b + 1)] = st["dpre", b]

        def back(w, b):
            st = state[w]
            st["dh2"] = st["dh2"] + nt(st.pop(("dpre", b)), weight(ffn, b))

        def leave(w):
            st = state[w]
            dh2 = st["dh2"]
            sums[2] += fold_rows(dh2 * st["n2"])
            sums[3] += fold_rows(dh2)
            d2 = norm_back(dh2, st["n2"], st["s2"], norm[2:3, :])
            d2_scr[rows[w], :] = d2
            d2b = d2.astype(bf16)
            d2b_scr[rows[w], :] = d2b
            grad = nt(d2b, weight(attn, 3)).astype(bf16)
            grad_scr[rows[w], :] = grad
            put_deltas(delta, (c * WAYS + w) * (RC // QB), grad, cmix[rows[w], :])

        def skewed(w, first, second, third):
            for t in range(parts + 2):
                if t < parts:
                    first(w, t)
                if 0 <= t - 1 < parts:
                    second(w, t - 1)
                if 0 <= t - 2 < parts:
                    third(w, t - 2)

        for w in ways:
            enter(w)
            skewed(w, pre, act, out)
        for w in ways:
            turn(w)
            skewed(w, dact, dpre, back)
        for w in ways:
            leave(w)

    each_chunk(chunks // WAYS, body)
    move.start(out_scr, out_h)
    for b in range(parts):
        cols = slice(width * b, width * (b + 1))
        gffn[share * b : share * (b + 1), 16 * parts :, :] = (
            tn(act_scr[:, cols], d3_scr[...]).astype(bf16).reshape(share, width // share, width)
        )
        put_gradient(gffn, b, tn(h2_scr[...], dpre_scr[:, cols]))
    move.start(gffn, gffn_h)

    def put_cross(i, value):
        put_gradient(gcross, i, value)
        part = pl.ds(16 * i, 16)
        move.start(gcross.at[:, part], gcross_h.at[:, part])

    put_cross(3, tn(cmix[...], d2b_scr[...]))
    spread_heads(grad_z, grad_scr)
    turned[...] = ck[...].T
    dk_scr[...] = jnp.zeros_like(dk_scr)
    dv_scr[...] = jnp.zeros_like(dv_scr)
    attention_back(
        window, 1, bounds, ck, turned, cv, query_z, grad_z, delta, clse, dq_scr, dk_scr, dv_scr, small_scr,
    )

    def leave(c):
        rows = rows_of(c, RC)
        dkb = dk_scr[rows, :].astype(bf16)
        dvb = dv_scr[rows, :].astype(bf16)
        ck[rows, :] = dkb
        cv[rows, :] = dvb
        mgrad[rows, :] = (nt(dkb, weight(attn, 1)) + nt(dvb, weight(attn, 2))).astype(bf16)
        normed = n1[rows, :]
        h2_scr[rows, :] = h1_of(rows).astype(bf16)
        dh1 = d2_scr[rows, :] + nt(dq_scr[rows, :], weight(attn, 0))
        sums[0] += fold_rows(dh1 * normed)
        sums[1] += fold_rows(dh1)
        d2_scr[rows, :] = norm_back(dh1, normed, s1[rows, :], norm[0:1, :])

    each_chunk(chunks, leave, 2)
    move.start(d2_scr, d1_h)
    move.start(mgrad, mgrad_h)
    for i in range(6):
        gnorm_ref[i : i + 1, :] = jnp.sum(sums[i], axis=0, keepdims=True)
    gnorm_ref[6:8, :] = jnp.zeros((2, width), f32)
    put_cross(0, tn(h2_scr[...], dq_scr[...]))
    put_cross(1, tn(memory[...], ck[...]))
    put_cross(2, tn(memory[...], cv[...]))
    move.finish()


def self_backward(
    tgt, attn, bounds, q, k, v, mix, lse, d1, tgrad, gself,
    query_z, grad_z, key_t, grad_scr, dq_scr, dk_scr, dv_scr, small_scr, d1_scr, delta, steps, begin, late,
):
    chunks = tgt.shape[0] // RC

    def enter(c):
        rows = rows_of(c, RC)
        d1b = d1[rows, :].astype(bf16)
        d1_scr[rows, :] = d1b
        grad = nt(d1b, weight(attn, 3)).astype(bf16)
        grad_scr[rows, :] = grad
        put_deltas(delta, c * (RC // QB), grad, mix[rows, :])

    each_chunk(chunks, enter, 2)
    begin[0]()
    put_gradient(gself, 3, tn(mix[...], d1_scr[...]))
    begin[1]()
    spread_heads(query_z, q)
    spread_heads(grad_z, grad_scr)
    key_t[...] = k[...].T
    dk_scr[...] = jnp.zeros_like(dk_scr)
    dv_scr[...] = jnp.zeros_like(dv_scr)
    attention_back(
        near_window, 0, bounds, k, key_t, v, query_z, grad_z, delta, lse, dq_scr, dk_scr, dv_scr, small_scr, steps,
    )
    for i, scr in enumerate((dq_scr, dk_scr, dv_scr)):
        put_gradient(gself, i, tn(tgt[...], scr[...].astype(bf16)))
    late()

    def leave(c):
        rows = rows_of(c, RC)
        tgrad[rows, :] = (
            d1[rows, :]
            + nt(dq_scr[rows, :], weight(attn, 0))
            + nt(dk_scr[rows, :].astype(bf16), weight(attn, 1))
            + nt(dv_scr[rows, :].astype(bf16), weight(attn, 2))
        ).astype(bf16)

    each_chunk(chunks, leave, 2)


def shape(dims, dtype):
    return jax.ShapeDtypeStruct(dims, dtype)


VMEM_SPEC = pl.BlockSpec(memory_space=pltpu.VMEM)
HBM_SPEC = pl.BlockSpec(memory_space=pltpu.HBM)
SMEM_SPEC = pl.BlockSpec(memory_space=pltpu.SMEM)


def vmem(*buffers):
    return [pltpu.VMEM(dims, dtype) for dims, dtype in buffers]


def dma(*dims):
    return pltpu.SemaphoreType.DMA(dims)


def adam_direction(master, gradient, moments):
    first_moment = beta_first * moments[0] + (1.0 - beta_first) * gradient
    second_moment = beta_second * moments[1] + (1.0 - beta_second) * gradient * gradient
    first_fix = 1.0 - beta_first**STEP
    second_fix = 1.0 - beta_second**STEP
    direction = (
        first_moment / first_fix / (jnp.sqrt(second_moment / second_fix) + adam_eps)
        + decay_rate * master
    )
    return (direction, first_moment, second_moment)


MESH = pl.DeviceIdType.MESH


class Place:
    def __init__(self):
        self.gx = lax.axis_index("gx")
        self.gy = lax.axis_index("gy")
        self.x = lax.rem(self.gx, 2)
        self.y = self.gx // 2
        self.z = self.gy // 2
        self.c = lax.rem(self.gy, 2)
        self.here = self.gx * 8 + self.gy

    def target(self, x, y, z, c):
        return (y * 2 + x, z * 2 + c)

    def index(self, x, y, z, c):
        return (y * 2 + x) * 8 + z * 2 + c

    def others(self):
        found = []
        for step in range(1, 32):
            device = lax.rem(self.here + step, 32)
            found.append((device // 8, lax.rem(device, 8)))
        return found


def greet(targets):
    barrier = pltpu.get_barrier_semaphore()
    for target in targets:
        pl.semaphore_signal(barrier, inc=1, device_id=target, device_id_type=MESH)
    pl.semaphore_wait(barrier, len(targets))


def remote(src, dst, send_sem, recv_sem, target):
    return pltpu.make_async_remote_copy(
        src_ref=src, dst_ref=dst, send_sem=send_sem, recv_sem=recv_sem, device_id=target, device_id_type=MESH
    )


def forward_sizes(length, width):
    pairs = width // LANES
    row = (length, width)
    lse = (length // QB, pairs, 2 * QB)
    kept = [(row, bf16)] * 4 + [(lse, f32), (row, f32), ((length, 1), f32)]
    scratch = [
        ((pairs, 2 * length, LANES), bf16), ((width, length), bf16),
        ((pairs, LONGEST + 2 * KB, 2 * QB), f32), ((pairs, LANES, QB), f32),
    ]
    return kept, scratch


class Gathering:
    parts = ((0, 32), (32, 32), (64, 96), (160, 112))

    def __init__(self, me, mine, near, full, zsend, xsend, ysend, csend, recv, crecv):
        self.me, self.mine, self.near, self.full = me, mine, near, full
        self.zsend, self.xsend, self.ysend, self.csend, self.recv, self.crecv = zsend, xsend, ysend, csend, recv, crecv
        x, y, z, c = me.x, me.y, me.z, me.c
        self.ox, self.oy, self.oc = 1 - x, 1 - y, 1 - c
        self.x_next = me.target(self.ox, y, z, c)
        self.y_next = me.target(x, self.oy, z, c)
        self.sibling = me.target(x, y, z, self.oc)
        self.up = me.target(x, y, lax.rem(z + 1, 4), c)
        self.down = me.target(x, y, lax.rem(z + 3, 4), c)

    def held(self, part):
        return self.near if part < 2 else self.full

    def copy(self, column, zz, part, target, sem, own=False):
        rows = pl.ds(*self.parts[part])
        c = self.me.c
        dst = self.held(part).at[column, zz, c, rows]
        return remote(self.mine.at[rows] if own else dst, dst, sem, self.recv.at[column, zz, part], target)

    def arrive(self, column, zz, part):
        self.copy(column, zz, part, self.sibling, self.xsend.at[part]).wait_recv()

    def to_x(self, column, zz, part, own=False):
        self.copy(column, zz, part, self.x_next, self.xsend.at[part], own).start()

    def to_y(self, column, zz, part, own=False):
        self.copy(column, zz, part, self.y_next, self.ysend.at[part], own).start()

    def column(self, x, y):
        return y * 2 + x

    def along(self, zz, part, upward, own=False):
        me = self.me
        target = self.up if upward else self.down
        sem = self.zsend.at[zz, part, 0 if upward else 1]

        if part < 2:
            return

        @pl.when((me.z < 3) if upward else (me.z > 0))
        def _():
            self.copy(me.gx, zz, part, target, sem, own).start()

    def straight(self, d, part):
        me = self.me
        target = me.target(me.x, me.y, lax.rem(me.z + d, 4), me.c)
        return self.copy(me.gx, me.z, part, target, self.zsend.at[d, part, 0], True)

    def own_straight(self, parts):
        for d in (1, 3, 2):
            for part in parts:
                self.straight(d, part).start()

    def own_z(self, parts):
        for part in parts:
            self.along(self.me.z, part, True, True)
            self.along(self.me.z, part, False, True)

    def own_sides(self, parts):
        for part in parts:
            self.to_x(self.me.gx, self.me.z, part, True)
            self.to_y(self.me.gx, self.me.z, part, True)

    def at_distance(self, d, action):
        z = self.me.z
        if d == 0:
            action(z, None)
            return

        @pl.when(z >= d)
        def _():
            action(z - d, True)

        @pl.when(z + d <= 3)
        def _():
            action(z + d, False)

    def inline(self, d, parts):
        me = self.me

        def action(zz, upward):
            for part in parts:
                self.arrive(me.gx, zz, part)
                self.along(zz, part, upward)
                self.to_x(me.gx, zz, part)
                self.to_y(me.gx, zz, part)

        self.at_distance(d, action)

    def side(self, d, parts):
        me = self.me

        def action(zz, _):
            for part in parts:
                if part % 2 == 0:
                    column = self.column(self.ox, me.y)
                    self.arrive(column, zz, part)
                    self.to_y(column, zz, part)
                else:
                    column = self.column(me.x, self.oy)
                    self.arrive(column, zz, part)
                    self.to_x(column, zz, part)

        self.at_distance(d, action)

    def last_columns(self, part):
        last = (self.me.x, self.oy) if part % 2 == 0 else (self.ox, self.me.y)
        return (self.column(*last), self.column(self.ox, self.oy))

    def far(self, d, parts):
        def action(zz, _):
            for part in parts:
                for column in self.last_columns(part):
                    self.arrive(column, zz, part)

        self.at_distance(d, action)

    def core(self, column, part):
        rows = pl.ds(*self.parts[part])
        block = self.held(part).at[column, :, self.me.c, rows]
        return remote(block, block, self.csend.at[column, part], self.crecv.at[column, part], self.sibling)

    def core_inline(self, parts):
        for part in parts:
            self.core(self.me.gx, part).start()

    def core_side(self, parts):
        me = self.me
        for part in parts:
            self.core(self.column(self.ox, me.y) if part % 2 == 0 else self.column(me.x, self.oy), part).start()

    def core_far(self, parts):
        for part in parts:
            for column in self.last_columns(part):
                self.core(column, part).start()

    def cores(self, parts):
        for part in parts:
            for column in range(4):
                self.core(column, part).wait_recv()

    def sent(self, parts):
        me = self.me
        for part in parts:
            if part < 2:
                for d in (1, 2, 3):
                    self.straight(d, part).wait_send()
            for zz in range(4 if part >= 2 else 0):

                @pl.when((me.z < 3) & (zz <= me.z))
                def _():
                    self.copy(me.gx, zz, part, self.up, self.zsend.at[zz, part, 0]).wait_send()

                @pl.when((me.z > 0) & (zz >= me.z))
                def _():
                    self.copy(me.gx, zz, part, self.down, self.zsend.at[zz, part, 1]).wait_send()

            rows = pl.ds(*self.parts[part])
            four, eight = self.held(part).at[0, :, 0, rows], self.held(part).at[pl.ds(0, 2), :, 0, rows]
            sems = (self.xsend.at[part], self.ysend.at[part])
            few, many = sems if part % 2 == 0 else sems[::-1]
            remote(four, four, few, self.recv.at[0, 0, part], self.sibling).wait_send()
            remote(eight, eight, many, self.recv.at[0, 0, part], self.sibling).wait_send()

    def cores_sent(self, parts):
        for part in parts:
            for column in range(4):
                self.core(column, part).wait_send()

    def stages(self, parts):
        return [
            lambda: self.inline(1, parts),
            lambda: (self.side(0, parts), self.inline(2, parts)),
            lambda: (self.side(1, parts), self.inline(3, parts), self.core_inline(parts)),
            lambda: (self.side(2, parts), self.far(0, parts)),
            lambda: (self.side(3, parts), self.core_side(parts), self.far(1, parts)),
            lambda: (self.far(2, parts), self.far(3, parts), self.core_far(parts)),
        ]


def first_kernel(
    attn_h, inner_h, outer_h, norm_h, lengths_h, src_h, tgt_h,
    full, bounds_out, spans_out, q_h, k_h, v_h, mix_h, lse_h, n1_h, s1_h,
    attn_f, inner_f, outer_f, norm_f, lengths, src, mine, bounds, spans, tgt, attn,
    q, k, v, mix, lse, n1, s1, query_z, value_t, score_scr, small_scr,
    sems, zsend, xsend, ysend, csend, recv, crecv,
):
    me = Place()
    move = Mover(sems)
    loads = [
        move.start(a, b)
        for a, b in (
            (attn_h, attn_f), (inner_h, inner_f), (outer_h, outer_f), (norm_h, norm_f), (lengths_h, lengths), (src_h, src),
        )
    ]
    load_tgt = move.start(tgt_h, tgt)
    gathering = Gathering(me, mine, attn, full, zsend, xsend, ysend, csend, recv, crecv)
    barrier = pltpu.get_barrier_semaphore()

    def greet(target):
        pl.semaphore_signal(barrier, inc=1, device_id=target, device_id_type=MESH)

    peers = [gathering.x_next, gathering.y_next, gathering.sibling]
    peers += [me.target(me.x, me.y, lax.rem(me.z + d, 4), me.c) for d in (1, 2, 3)]
    for target in peers:
        greet(target)
    move.wait(loads[0])
    for j in range(8):
        mine[16 * j : 16 * j + 16, :] = attn_f[j].astype(bf16)
    attn[me.gx, me.z, me.c] = mine[0:64, :]
    pl.semaphore_wait(barrier, len(peers))
    early, late = (0, 1), (2, 3)
    gathering.own_straight(early)
    gathering.own_sides(early)
    move.wait(*loads[1:])
    for b in range(4):
        mine[128 + 16 * b : 144 + 16 * b, :] = inner_f[:, 512 * b : 512 * b + 512].astype(bf16)
    mine[192:256, :] = outer_f[...].astype(bf16)
    lanes = jnp.concatenate([norm_f[...], jnp.zeros((6, 112), f32)], axis=1)
    lanes = jnp.concatenate([lanes, jnp.zeros((10, 128), f32)], axis=0)
    lanes = pltpu.roll(lanes, me.gy * 16, 1).astype(bf16)
    mine[256:272, :] = jnp.concatenate([lanes, jnp.zeros((16, 384), bf16)], axis=1)
    gathering.own_z(late)
    gathering.own_sides(late)
    keep = move.start(mine.at[pl.ds(64, 208)], full.at[me.gx, me.z, me.c, pl.ds(64, 208)])
    find_bounds(lengths, src, bounds, spans)
    move.start(bounds, bounds_out)
    move.start(spans, spans_out)
    sooner, later = gathering.stages(early), gathering.stages(late)
    for stage in (*sooner[:3], later[0], sooner[3], later[1], sooner[4], sooner[5]):
        stage()
    move.wait(keep)
    later[2]()
    gathering.cores(early)
    move.start(attn, full.at[:, :, :, pl.ds(0, 64)])
    move.wait(load_tgt)
    self_forward(
        tgt, attn.reshape(32, 64, 512), bounds, q, k, v, mix, lse, n1, s1, query_z, value_t, score_scr, small_scr,
        move, (q_h, k_h, v_h, mix_h, lse_h, n1_h, s1_h),
        (None, later[3], None, later[4], None, later[5]),
    )
    gathering.sent(early + late)
    gathering.cores_sent(early)
    gathering.cores(late)
    gathering.cores_sent(late)
    move.finish()


def gather_and_start(params, lengths, src_segments, tgt):
    length, width = tgt.shape
    kept, scratch = forward_sizes(length, width)
    row = (length, width)
    bounds, spans = ((8, length), jnp.int32), ((2 * length // QB, QB), jnp.int32)
    full = ((4, 4, 2, 272, 512), bf16)
    loads = [(p.shape, f32) for p in params] + [(lengths.shape, jnp.int32), (src_segments.shape, jnp.int32)]
    return pl.pallas_call(
        first_kernel,
        out_shape=tuple(shape(*item) for item in [full, bounds, spans] + kept),
        in_specs=[HBM_SPEC] * 7,
        out_specs=(HBM_SPEC,) * 10,
        scratch_shapes=vmem(
            *loads, ((272, 512), bf16), bounds, spans, (row, bf16), ((4, 4, 2, 64, 512), bf16), *kept, *scratch,
        )
        + [dma(24), dma(4, 4, 2), dma(4), dma(4), dma(4, 4), dma(4, 4, 4), dma(4, 4)],
        compiler_params=pltpu.CompilerParams(collective_id=0, has_side_effects=True, vmem_limit_bytes=GRANT),
    )(*params, lengths, src_segments, tgt)


def start_kernel(
    full, lengths, src, tgt, bounds_out, spans_out, q_h, k_h, v_h, mix_h, lse_h, n1_h, s1_h,
    bounds, spans, attn, q, k, v, mix, lse, n1, s1, query_z, value_t, score_scr, small_scr, sems,
):
    move = Mover(sems)
    load = move.start(full.at[:, pl.ds(0, attn.shape[1])], attn)
    find_bounds(lengths, src, bounds, spans)
    move.start(bounds, bounds_out)
    move.start(spans, spans_out)
    move.wait(load)
    self_forward(
        tgt, attn, bounds, q, k, v, mix, lse, n1, s1, query_z, value_t, score_scr, small_scr,
        move, (q_h, k_h, v_h, mix_h, lse_h, n1_h, s1_h), (),
    )
    move.finish()


def start_only(full, lengths, src_segments, tgt):
    length, width = tgt.shape
    kept, scratch = forward_sizes(length, width)
    bounds, spans = ((8, length), jnp.int32), ((2 * length // QB, QB), jnp.int32)
    return pl.pallas_call(
        start_kernel,
        out_shape=tuple(shape(*item) for item in [bounds, spans] + kept),
        in_specs=[HBM_SPEC] + [VMEM_SPEC] * 3,
        out_specs=(HBM_SPEC,) * 9,
        scratch_shapes=vmem(bounds, spans, ((full.shape[0], 64, width), bf16), *kept, *scratch) + [dma(16)],
        compiler_params=pltpu.CompilerParams(vmem_limit_bytes=GRANT),
    )(full, lengths, src_segments, tgt)


def middle(spans, bounds, full, memory, cotangent, n1, s1):
    length, width = n1.shape
    keys = memory.shape[0]
    blocks = full.shape[0]
    ffn_rows = full.shape[1] - 144
    hidden = ffn_rows * blocks // 2 * full.shape[2] // width
    pairs = width // LANES
    row, mem_row = (length, width), (keys, width)
    zeroed = ((pairs, 2 * length, LANES), bf16)
    gffn, gcross = ((blocks, ffn_rows, width), bf16), ((blocks, 64, width), bf16)
    outs = [(row, bf16), (row, f32), (mem_row, bf16), gffn, gcross, ((8, width), f32)]
    scratch = vmem(
        (bounds.shape, jnp.int32), ((blocks, 16, width // 4), bf16), gcross, gffn, (mem_row, bf16), (row, bf16), (row, f32),
        ((length, 1), f32), (row, bf16), (mem_row, bf16), (mem_row, bf16), (row, bf16),
        ((length // QB, pairs, 2 * QB), f32), zeroed, zeroed, ((width, keys), bf16), ((pairs, keys + KB, 2 * QB), f32),
        ((pairs, LANES, QB), f32), ((length, hidden), bf16), ((length, hidden), bf16), (row, bf16), (row, bf16),
        (row, f32), (row, bf16), (row, bf16), (row, bf16), (mem_row, f32), (mem_row, f32), (row, bf16), (mem_row, bf16),
        gffn, gcross, ((6, 8, width), f32), ((8, width), f32),
        ((length // QB, pairs, 2 * QB), f32),
    )
    return pl.pallas_call(
        middle_kernel,
        out_shape=tuple(shape(*item) for item in outs),
        in_specs=[SMEM_SPEC] + [HBM_SPEC] * 6,
        out_specs=(HBM_SPEC,) * 5 + (VMEM_SPEC,),
        scratch_shapes=scratch + [dma(16)],
        compiler_params=pltpu.CompilerParams(vmem_limit_bytes=GRANT),
    )(spans, bounds, full, memory, cotangent, n1, s1)


OUTER_ROWS = slice(96, 160)


def attn_rows(j):
    return 192 + 16 * j if j < 4 else 64 + 16 * (j - 4) if j < 6 else 160 + 16 * (j - 6)


def add_rows(dst, *sources):
    total = sources[0][...].astype(f32)
    for source in sources[1:]:
        total = total + source[...].astype(f32)
    dst[...] = total.astype(dst.dtype)


class Summing:
    order = (2, 1, 3, 0)

    def __init__(self, me, sources, rows, pieces, first_a, first_b, second_a, second_b, third, result, sems):
        self.me, self.sources, self.rows, self.pieces = me, sources, rows, pieces
        self.first_a, self.first_b, self.second_a, self.second_b, self.third = first_a, first_b, second_a, second_b, third
        self.result = result
        (self.lsem, self.csend, self.crecv, self.send1, self.recv1, self.send2, self.recv2, self.send3, self.recv3) = sems
        x, y, z, c = me.x, me.y, me.z, me.c
        self.ox, self.oy, self.oc = 1 - x, 1 - y, 1 - c
        self.x_next = me.target(self.ox, y, z, c)
        self.y_next = me.target(x, self.oy, z, c)
        self.sibling = me.target(x, y, z, self.oc)
        self.zs = [lax.rem(z + d, 4) for d in range(4)]
        self.half = first_a.shape[2]
        self.top, self.bottom = pl.ds(0, self.half), pl.ds(self.half, self.half)
        self.pending, self.cores, self.own = [], {}, {}
        self.firsts, self.seconds, self.thirds = {}, {}, {}

    def send(self, *args):
        copy = remote(*args)
        copy.start()
        self.pending.append(copy)
        return copy

    def load(self):
        for d in self.order:
            for k, (source, kept, _) in enumerate(self.sources):
                if kept is not None:
                    copy = pltpu.make_async_copy(source.at[:, self.zs[d], self.me.c], kept.at[d], self.lsem.at[d, k])
                    copy.start()
                    self.own[d, k] = copy

    def core(self):
        for d in self.order:
            for k, (source, _, got) in enumerate(self.sources):
                self.cores[d, k] = self.send(
                    source.at[:, self.zs[d], self.oc], got.at[d], self.csend.at[d, k], self.crecv.at[d, k], self.sibling
                )

    def stage1(self, d):
        me = self.me
        for k in range(len(self.sources)):
            if (d, k) in self.own:
                self.own[d, k].wait()
            self.cores[d, k].wait_recv()

        def add(i):
            piece = self.pieces.at[d, i // 2, lax.rem(i, 2)]
            for start, count, k, first in self.rows:
                source, kept, got = self.sources[k]
                held = source.at[i, self.zs[d], me.c] if kept is None else kept.at[d, i]
                part = pl.ds(first, count)
                add_rows(piece.at[pl.ds(start, count)], held.at[part], got.at[d, i, part])

        each_chunk(4, add)
        self.firsts[d] = (
            self.send(
                self.pieces.at[d, self.oy, :, self.top], self.first_a.at[d], self.send1.at[d, 0], self.recv1.at[d, 0],
                self.y_next,
            ),
            self.send(
                self.pieces.at[d, :, self.ox, self.bottom], self.first_b.at[d], self.send1.at[d, 1],
                self.recv1.at[d, 1], self.x_next,
            ),
        )

    def stage2(self, d):
        me = self.me
        self.firsts[d][0].wait_recv()
        part = self.pieces.at[d, me.y, self.ox, self.top]
        add_rows(part, part, self.first_a.at[d, self.ox])
        one = self.send(part, self.second_a.at[d], self.send2.at[d, 0], self.recv2.at[d, 0], self.x_next)
        self.firsts[d][1].wait_recv()
        part = self.pieces.at[d, self.oy, me.x, self.bottom]
        add_rows(part, part, self.first_b.at[d, self.oy])
        two = self.send(part, self.second_b.at[d], self.send2.at[d, 1], self.recv2.at[d, 1], self.y_next)
        self.seconds[d] = (one, two)

    def stage3(self, d):
        me = self.me
        for copy in self.seconds[d]:
            copy.wait_recv()
        for rows, first, second, at in (
            (self.top, self.first_a, self.second_a, me.x), (self.bottom, self.first_b, self.second_b, me.y),
        ):
            part = self.pieces.at[d, me.y, me.x, rows]
            add_rows(part if d else self.result.at[rows], part, first.at[d, at], second.at[d])
        if d:
            self.thirds[d] = self.send(
                self.pieces.at[d, me.y, me.x], self.third.at[d - 1], self.send3.at[d - 1], self.recv3.at[d - 1],
                me.target(me.x, me.y, self.zs[d], me.c),
            )

    def end(self):
        for d in (1, 2, 3):
            self.thirds[d].wait_recv()
        add_rows(self.result, self.result, self.third.at[0], self.third.at[1], self.third.at[2])


def last_kernel(
    full, bounds_h, tgt_h, q_h, k_h, v_h, mix_h, lse_h, d1_h, gffn, gcross, gnorm_h,
    attn_ph, inner_ph, outer_ph, norm_ph, attn_mh, in_mh, out_mh, norm_mh,
    tgrad_h, g_h, gn_ref, totals_ref,
    g_ref, attn_p, inner_p, outer_p, norm_p, attn_m, in_m, out_m, norm_m,
    bounds, tgt, attn, q, k, v, mix, lse, d1, tgrad, gself, query_z, grad_z, key_t, grad_scr, dq_scr, dk_scr, dv_scr,
    small_scr, d1_scr, delta, own_ffn, own_cross, got_ffn, got_cross, pieces, first_a, first_b, second_a, second_b, third,
    got_self, pieces2, first_a2, first_b2, second_a2, second_b2, third2, vectors, squares, tiles,
    msems, psems, *sems,
):
    me = Place()
    move = Mover(msems)
    others = me.others()
    barrier = pltpu.get_barrier_semaphore()
    for target in others:
        pl.semaphore_signal(barrier, inc=1, device_id=target, device_id_type=MESH)
    load_first = [move.start(a, b) for a, b in ((gnorm_h, vectors.at[0]), (d1_h, d1), (full.at[:, pl.ds(0, 64)], attn))]
    load_mix = move.start(mix_h, mix)
    load_rest = [
        move.start(a, b)
        for a, b in ((q_h, q), (k_h, k), (v_h, v), (lse_h, lse), (bounds_h, bounds), (tgt_h, tgt))
    ]
    sems1, sems2, (nsend, nrecv, tsend, trecv) = sems[0:9], sems[9:18], sems[18:22]
    big = Summing(
        me, [(gffn, own_ffn, got_ffn), (gcross, own_cross, got_cross)],
        [(0, 64, 0, 0), (64, 32, 1, 0), (96, 64, 0, 64), (160, 32, 1, 32)],
        pieces, first_a, first_b, second_a, second_b, third, g_ref.at[pl.ds(0, 192)], sems1,
    )
    rest = Summing(
        me, [(gself, None, got_self)], [(0, 64, 0, 0)],
        pieces2, first_a2, first_b2, second_a2, second_b2, third2, g_ref.at[pl.ds(192, 64)], sems2,
    )
    big.load()
    pl.semaphore_wait(barrier, len(others))
    big.core()
    load_last = [
        move.start(a, b)
        for a, b in (
            (attn_ph, attn_p), (inner_ph, inner_p), (outer_ph, outer_p), (norm_ph, norm_p),
            (attn_mh, attn_m), (in_mh, in_m), (out_mh, out_m), (norm_mh, norm_m),
        )
    ]
    move.wait(*load_first, load_mix)
    norm_copies = [big.send(vectors.at[0], vectors.at[1], nsend.at[0], nrecv.at[0], big.sibling)]

    def norm_step(stage, target):
        norm_copies[-1].wait_recv()
        vectors[2 * stage] = vectors[2 * stage - 2] + vectors[2 * stage - 1]
        norm_copies.append(
            big.send(vectors.at[2 * stage], vectors.at[2 * stage + 1], nsend.at[stage], nrecv.at[stage], target)
        )

    def norm_last():
        norm_copies[-1].wait_recv()
        vectors[6] = vectors[4] + vectors[5]
        for d in range(1, 4):
            target = me.target(me.x, me.y, big.zs[d], me.c)
            norm_copies.append(big.send(vectors.at[6], vectors.at[6 + d], nsend.at[2 + d], nrecv.at[2 + d], target))

    far, up, down, here = big.order
    steps = [
        None,
        lambda: norm_step(1, big.x_next),
        None,
        lambda: (big.stage2(far), big.stage1(down)),
        None,
        lambda: (big.stage2(up), big.stage3(far), big.stage1(here), norm_step(2, big.y_next)),
        None,
        lambda: (big.stage2(down), big.stage3(up)),
    ]

    begin = (lambda: big.stage1(far), lambda: big.stage1(up))

    def late():
        rest.core()
        big.stage2(here)
        rest.stage1(far)
        rest.stage1(up)
        big.stage3(down)
        norm_last()

    move.wait(*load_rest)
    self_backward(
        tgt, attn, bounds, q, k, v, mix, lse, d1, tgrad, gself.reshape(32, 64, 512),
        query_z, grad_z, key_t, grad_scr, dq_scr, dk_scr, dv_scr, small_scr, d1_scr, delta, steps, begin, late,
    )
    move.start(tgrad, tgrad_h)
    rest.stage1(down)
    rest.stage1(here)
    big.stage3(here)
    rest.stage2(far)
    rest.stage2(up)
    rest.stage3(far)
    rest.stage2(down)
    rest.stage3(up)
    rest.stage2(here)
    rest.stage3(down)
    rest.stage3(here)
    big.end()
    for copy in norm_copies[3:]:
        copy.wait_recv()
    vectors[10] = (vectors[6] + vectors[8]) + (vectors[7] + vectors[9])
    lanes = vectors[10, :, pl.ds(pl.multiple_of(me.gx * 128, 128), 128)]
    gn_ref[...] = pltpu.roll(lanes, lax.rem(128 - me.gy * 16, 128), 1)

    def put(t, pairs):
        for i in range(2):
            squares[16 * i + t : 16 * i + t + 1, :] = sum(
                jnp.sum(pair[i] * pair[i], axis=0, keepdims=True) for pair in pairs
            )

    move.wait(*load_last)

    def direction(*args):
        return adam_direction(*args)[0]

    def put_attn(j):
        grad = g_ref[attn_rows(j) : attn_rows(j) + 16, :]
        put(j, [(attn_p[j], direction(attn_p[j], grad, (attn_m[0, j], attn_m[1, j])))])

    for j in range(4, 8):
        put_attn(j)
    pairs = []
    for b in range(4):
        cols = slice(512 * b, 512 * b + 512)
        grad = g_ref[16 * b : 16 * b + 16, :]
        pairs.append((inner_p[:, cols], direction(inner_p[:, cols], grad, (in_m[0, :, cols], in_m[1, :, cols]))))
    put(8, pairs)
    put(9, [(outer_p[...], direction(outer_p[...], g_ref[OUTER_ROWS, :], (out_m[0], out_m[1])))])
    master = norm_p[...]
    update = direction(master, gn_ref[0:6, 0:16], (norm_m[:, 0, :], norm_m[:, 1, :]))
    rest_lanes = jnp.zeros((6, 512 - 16), f32)
    master, update = (jnp.concatenate([item, rest_lanes], axis=1) for item in (master, update))
    for i in range(6):
        put(10 + i, [(master[i : i + 1], update[i : i + 1])])
    rest.end()
    move.start(g_ref, g_h)
    for j in range(4):
        put_attn(j)
    folded = (squares[:, 0:128] + squares[:, 128:256]) + (squares[:, 256:384] + squares[:, 384:512])
    row = jnp.sum(folded.T, axis=0, keepdims=True)
    row = jnp.concatenate([row, jnp.zeros((1, 96), f32)], axis=1)
    tiles[me.here] = jnp.concatenate([row, jnp.zeros((7, 128), f32)], axis=0)
    for target in others:
        remote(tiles.at[me.here], tiles.at[me.here], tsend, trecv, target).start()
    for copy in big.pending + rest.pending:
        copy.wait_send()
    received = tiles.at[pl.ds(0, 31)]
    every = remote(received, received, tsend, trecv, big.sibling)
    every.wait_recv()
    every.wait_send()
    totals_ref[...] = jnp.sum(tiles[...], axis=0)
    move.finish()


def backward_scratch(length, width):
    pairs = width // LANES
    row = (length, width)
    zeroed = ((pairs, 2 * length, LANES), bf16)
    return [
        zeroed, zeroed, ((width, length), bf16), (row, bf16), (row, bf16), (row, f32), (row, f32),
        ((pairs, LANES, QB), f32), (row, bf16), ((length // QB, pairs, 2 * QB), f32),
    ]


def finish_and_reduce(full, bounds, tgt, saved, d1, grads, norm_grad, params, moments):
    length, width = tgt.shape
    row = (length, width)
    lse = (length // QB, width // LANES, 2 * QB)

    def sums(half):
        return [
            ((4, 2, 2, 2 * half, 512), bf16), ((4, 2, half, 512), bf16), ((4, 2, half, 512), bf16),
            ((4, half, 512), bf16), ((4, half, 512), bf16), ((3, 2 * half, 512), bf16),
        ]

    scratch = vmem(
        ((256, 512), f32), *((item.shape, f32) for item in (*params, *moments)),
        (bounds.shape, jnp.int32), (row, bf16), ((32, 64, 512), bf16), *[(row, bf16)] * 4, (lse, f32), (row, f32),
        (row, bf16), ((4, 4, 2, 64, 512), bf16), *backward_scratch(length, width),
        ((4, 4, 128, 512), bf16), ((4, 4, 64, 512), bf16), ((4, 4, 128, 512), bf16), ((4, 4, 64, 512), bf16), *sums(96),
        ((4, 4, 64, 512), bf16), *sums(32), ((11, 8, 512), f32), ((32, 512), f32), ((32, 8, 128), f32),
    )
    round_sems = [dma(4, 2), dma(4, 2), dma(4, 2), dma(4, 2), dma(4, 2), dma(4, 2), dma(4, 2), dma(3), dma(3)]
    split = [grad.reshape(4, 4, 2, grad.shape[1], 512) for grad in grads]
    return pl.pallas_call(
        last_kernel,
        out_shape=(shape(row, bf16), shape((256, 512), f32), shape((8, 128), f32), shape((8, 128), f32)),
        in_specs=[HBM_SPEC] * 20,
        out_specs=(HBM_SPEC, HBM_SPEC, VMEM_SPEC, VMEM_SPEC),
        scratch_shapes=scratch + [dma(24), dma(1)] + round_sems + round_sems + [dma(6), dma(6)] + [pltpu.SemaphoreType.DMA] * 2,
        compiler_params=pltpu.CompilerParams(collective_id=1, has_side_effects=True, vmem_limit_bytes=GRANT),
    )(full, bounds, tgt, *saved, d1, *split, norm_grad, *params, *moments)


def finish_kernel(
    full, bounds, tgt, q, k, v, mix, lse, d1, tgrad, gself,
    attn, query_z, grad_z, key_t, grad_scr, dq_scr, dk_scr, dv_scr, small_scr, d1_scr, delta, sems,
):
    move = Mover(sems)
    move.wait(move.start(full.at[:, pl.ds(0, attn.shape[1])], attn))
    self_backward(
        tgt, attn, bounds, q, k, v, mix, lse, d1, tgrad, gself,
        query_z, grad_z, key_t, grad_scr, dq_scr, dk_scr, dv_scr, small_scr, d1_scr, delta, (), (lambda: None,) * 2, lambda: None,
    )


def finish_only(full, bounds, tgt, saved, d1):
    length, width = tgt.shape
    gself = ((full.shape[0], 64, width), bf16)
    return pl.pallas_call(
        finish_kernel,
        out_shape=(shape((length, width), bf16), shape(*gself)),
        in_specs=[HBM_SPEC] + [VMEM_SPEC] * 8,
        out_specs=(VMEM_SPEC, VMEM_SPEC),
        scratch_shapes=vmem(gself, *backward_scratch(length, width)) + [dma(2)],
        compiler_params=pltpu.CompilerParams(vmem_limit_bytes=GRANT),
    )(full, bounds, tgt, *saved, d1)


def update_kernel(*refs):
    ins, outs = refs[:12], refs[12:30]
    held, made, sems = refs[30:42], refs[42:59], refs[59]
    move = Mover(sems)
    order = (3, 2, 1, 7, 11, 6, 10, 5, 9, 4, 8, 0)
    loads = {i: move.start(ins[i], held[i]) for i in order}
    g_ref, gn_ref, totals_ref, attn, inner, outer, norm, attn_m, in_m, out_m, norm_m = held[1:]
    norms_ref = made[16]

    def results(t):
        return [(made[i], outs[1 + i]) for i in (t, 4 + 2 * t, 5 + 2 * t, 12 + t)]

    def step(t, master, gradient, moments, ratio, refs, place):
        direction, first_moment, second_moment = adam_direction(master, gradient, moments)
        value = master - ratio * direction
        for (ref, _), item in zip(refs, (value, first_moment, second_moment, value.astype(bf16))):
            ref[place] = item

    def leave(refs):
        for ref, out in refs:
            move.start(ref, out)

    move.wait(loads[3], loads[2], loads[7], loads[11])
    roots = jnp.sqrt(totals_ref[0:1, 0:32])
    norms_ref[0:1, :] = roots[:, 0:16]
    norms_ref[1:2, :] = roots[:, 16:32]
    move.start(norms_ref, outs[17])
    ratio = learn_rate * (roots[:, 0:16] / roots[:, 16:32])
    vectors = results(3)
    for i in range(6):
        one = slice(i, i + 1)
        moments = (norm_m[i, 0:1], norm_m[i, 1:2])
        step(10 + i, norm[one], gn_ref[one, 0:16], moments, ratio[:, 10 + i : 11 + i], vectors, one)
    leave(vectors)
    move.wait(loads[1], loads[6], loads[10])
    moments = (out_m[0], out_m[1])
    step(2, outer[...], g_ref[OUTER_ROWS, :], moments, ratio[:, 9:10], results(2), ...)
    leave(results(2))
    move.wait(loads[5], loads[9])
    for b in range(4):
        cols = slice(512 * b, 512 * b + 512)
        moments = (in_m[0, :, cols], in_m[1, :, cols])
        step(1, inner[:, cols], g_ref[16 * b : 16 * b + 16, :], moments, ratio[:, 8:9], results(1), (slice(None), cols))
    leave(results(1))
    move.wait(loads[4], loads[8], loads[0])
    move.start(held[0], outs[0])
    for j in range(8):
        grad = g_ref[attn_rows(j) : attn_rows(j) + 16, :]
        step(0, attn[j], grad, (attn_m[0, j], attn_m[1, j]), ratio[:, j : j + 1], results(0), j)
    leave(results(0))
    move.finish()


def update_params(summed, params, moments):
    args = (*summed, *params, *moments)
    outs = [shape(p.shape, f32) for p in params]
    outs += [shape(p.shape, f32) for p in params for _ in range(2)]
    outs += [shape(p.shape, bf16) for p in params] + [shape((2, 16), f32)]
    return pl.pallas_call(
        update_kernel,
        out_shape=(shape(summed[0].shape, bf16), *outs),
        in_specs=[HBM_SPEC] * len(args),
        out_specs=(HBM_SPEC,) * (1 + len(outs)),
        scratch_shapes=vmem(*((item.shape, item.dtype) for item in (*args, *outs))) + [dma(32)],
        compiler_params=pltpu.CompilerParams(vmem_limit_bytes=GRANT),
    )(*args)


def tensor_squares(attn_part, inner_part, outer_part, norm_part):
    return jnp.concatenate(
        [
            jnp.sum(attn_part * attn_part, axis=(1, 2)),
            jnp.sum(inner_part * inner_part)[None],
            jnp.sum(outer_part * outer_part)[None],
            jnp.sum(norm_part * norm_part, axis=1),
        ]
    )


def blocked(matrix, width):
    blocks = matrix.shape[0] // 16
    cols = matrix.shape[1] // width
    return matrix.reshape(blocks, 16, cols, width).transpose(0, 2, 1, 3).reshape(blocks, cols * 16, width)


def unblocked(blocks, width):
    count = blocks.shape[0]
    cols = blocks.shape[1] // 16
    return blocks.reshape(count, cols, 16, width).transpose(0, 2, 1, 3).reshape(count * 16, cols * width)


def gather_any(attn_w, ffn_in, ffn_out, norm_params):
    width = attn_w.shape[2]
    attn = lax.all_gather(attn_w.astype(bf16), AXES, axis=1, tiled=True)
    inner = lax.all_gather(ffn_in.astype(bf16), AXES, axis=0, tiled=True)
    outer = lax.all_gather(ffn_out.astype(bf16), AXES, axis=0, tiled=True)
    norm = lax.all_gather(norm_params.astype(bf16), AXES, axis=1, tiled=True)
    blocks = width // 16
    attn = attn.reshape(8, blocks, 16, width).transpose(1, 0, 2, 3).reshape(blocks, 8 * 16, width)
    lanes = jnp.pad(norm, ((0, 10), (0, 0))).reshape(16, 4, 1, width // 4).transpose(1, 2, 0, 3)
    lanes = jnp.pad(lanes, ((0, 0), (0, blocks // 4 - 1), (0, 0), (0, width - width // 4))).reshape(blocks, 16, width)
    return jnp.concatenate([attn, blocked(inner, width), outer.reshape(blocks, -1, width), lanes], axis=1)


def reduce_any(grads, norm_grad, params, moments):
    grad_ffn, grad_cross, grad_self = grads
    width = grad_ffn.shape[2]
    blocks = width // 16
    attn_w, ffn_in, ffn_out, norm_params = params
    attn_m, in_m, out_m, norm_m = moments
    stack = jnp.concatenate([grad_self, grad_cross], axis=1)
    stack = stack.reshape(blocks, 8, 16, width).transpose(1, 0, 2, 3).reshape(8, width, width)
    rows = ffn_in.shape[1] // width * 16
    inner = unblocked(grad_ffn[:, :rows], width)
    outer = grad_ffn[:, rows:].reshape(-1, width)
    shard_attn = lax.psum_scatter(stack, AXES, scatter_dimension=1, tiled=True).astype(f32)
    shard_inner = lax.psum_scatter(inner, AXES, scatter_dimension=0, tiled=True).astype(f32)
    shard_outer = lax.psum_scatter(outer, AXES, scatter_dimension=0, tiled=True).astype(f32)
    shard_norm = lax.psum_scatter(norm_grad, AXES, scatter_dimension=1, tiled=True)
    attn_dir, attn_first, attn_second = adam_direction(attn_w, shard_attn, attn_m)
    inner_dir, inner_first, inner_second = adam_direction(ffn_in, shard_inner, in_m)
    outer_dir, outer_first, outer_second = adam_direction(ffn_out, shard_outer, out_m)
    norm_dir, norm_first, norm_second = adam_direction(norm_params, shard_norm, norm_m)
    weight_total, update_total = lax.psum(
        (tensor_squares(*params), tensor_squares(attn_dir, inner_dir, outer_dir, norm_dir)), AXES
    )
    ratio = jnp.sqrt(weight_total) / jnp.sqrt(update_total)
    attn_new = attn_w - learn_rate * ratio[0:8][:, None, None] * attn_dir
    in_new = ffn_in - learn_rate * ratio[8] * inner_dir
    out_new = ffn_out - learn_rate * ratio[9] * outer_dir
    norm_new = norm_params - learn_rate * ratio[10:16][:, None] * norm_dir
    norms = jnp.stack([jnp.sqrt(weight_total), jnp.sqrt(update_total)])
    return (
        attn_new, in_new, out_new, norm_new,
        attn_first, attn_second, inner_first, inner_second, outer_first, outer_second, norm_first, norm_second,
        attn_new.astype(bf16), in_new.astype(bf16), out_new.astype(bf16), norm_new.astype(bf16), norms,
    )


def on_device(
    close, tgt, memory, cotangent, tgt_lengths, src_segments, attn_w, ffn_in, ffn_out, norm_params,
    attn_moments, in_moments, out_moments, norm_moments,
):
    params = (attn_w, ffn_in, ffn_out, norm_params)
    moments = (attn_moments, in_moments, out_moments, norm_moments)
    if close and tgt.shape[0] == 1:
        full, bounds, spans, *state = gather_and_start(params, tgt_lengths, src_segments, tgt[0])
        full = full.reshape(32, *full.shape[3:])
        saved, (n1, s1) = state[:5], state[5:]
        layer_out, d1, mem_grad, grad_ffn, grad_cross, norm_grad = middle(
            spans, bounds, full, memory[0], cotangent[0], n1, s1
        )
        moments = (*moments[:3], norm_moments.transpose(1, 0, 2))
        summed = finish_and_reduce(
            full, bounds, tgt[0], saved, d1, (grad_ffn, grad_cross), norm_grad, params, moments
        )
        tgt_grad, *updated = update_params(summed, params, moments)
        return (layer_out[None], tgt_grad[None], mem_grad[None], *updated)
    full = gather_any(*params)
    parts = []
    for r in range(tgt.shape[0]):
        bounds, spans, *state = start_only(full, tgt_lengths[r : r + 1], src_segments[r : r + 1], tgt[r])
        saved, (n1, s1) = state[:5], state[5:]
        layer_out, d1, mem_grad, grad_ffn, grad_cross, norm_grad = middle(
            spans, bounds, full, memory[r], cotangent[r], n1, s1
        )
        tgt_grad, grad_self = finish_only(full, bounds, tgt[r], saved, d1)
        parts.append((layer_out, tgt_grad, mem_grad, grad_ffn, grad_cross, grad_self, norm_grad[0:6]))
    outs = [jnp.stack([part[i] for part in parts]) for i in range(3)]
    sums = [sum(part[i].astype(f32) for part in parts) for i in range(3, 7)]
    grads = [grad.astype(bf16) for grad in sums[:3]]
    return (*outs, *reduce_any(grads, sums[3], params, moments))


def fits(mesh):
    return mesh.shape["gx"] == 4 and mesh.shape["gy"] == 8


def solution(mesh):
    rows = P(AXES, None, None)
    matrix = P(AXES, None)
    stack = P(None, AXES, None)
    vectors = P(None, AXES)
    return jax.shard_map(
        functools.partial(on_device, fits(mesh)),
        mesh=mesh,
        in_specs=(
            rows, rows, rows, matrix, matrix, stack, matrix, matrix, vectors,
            P(None, None, AXES, None), stack, stack, P(None, None, AXES),
        ),
        out_specs=(
            rows, rows, rows, stack, matrix, matrix, vectors, stack, stack, matrix, matrix, matrix, matrix,
            vectors, vectors, stack, matrix, matrix, vectors, P(),
        ),
        check_vma=False,
    )
```

```python
import functools

import jax
import jax.numpy as jnp
from jax import lax
from jax.experimental import pallas as pl
from jax.experimental.pallas import tpu as pltpu
from jax.sharding import PartitionSpec as P

HEAD_DIM = 64
STEP = 5

beta_first = 0.5
beta_second = 0.5
learn_rate = 0.5
decay_rate = 0.01
norm_eps = 1e-05
adam_eps = 1e-06

f32 = jnp.float32
bf16 = jnp.bfloat16
LANES = 128
QB = 128
KB = 256
RC = 256
LONGEST = 512
WAYS = 2
KEY_STEP = 16
MASKED = -1e30
AXES = ("gx", "gy")
GRANT = 63 * 2**20


def nn(left, right):
    return lax.dot_general(left, right, (((1,), (0,)), ((), ())), preferred_element_type=f32)


def nt(left, right):
    return lax.dot_general(left, right, (((1,), (1,)), ((), ())), preferred_element_type=f32)


def tn(left, right):
    return lax.dot_general(left, right, (((0,), (0,)), ((), ())), preferred_element_type=f32)


def rows_of(step, size):
    return pl.ds(pl.multiple_of(step * size, size), size)


def each_chunk(count, body, ways=1):
    def step(index, carry):
        for way in range(ways):
            body(index * ways + way)
        return carry

    lax.fori_loop(0, count // ways, step, 0)


def spread_heads(dst, src):
    pairs = dst.shape[0]
    first = lax.broadcasted_iota(jnp.int32, (QB, LANES), 1) < HEAD_DIM
    zero = jnp.zeros((QB, LANES), bf16)

    def body(i):
        start = pl.multiple_of(i * 2 * QB, 2 * QB)
        for p in range(pairs):
            tile = src[rows_of(i, QB), p * LANES : (p + 1) * LANES]
            dst[p, pl.ds(start, QB), :] = jnp.where(first, tile, zero)
            dst[p, pl.ds(start + QB, QB), :] = jnp.where(first, zero, tile)

    each_chunk(src.shape[0] // QB, body)


def run_blocks(count, body, steps):
    if not steps:
        each_chunk(count, body)
        return
    for i in range(count):
        body(i)
        if i < len(steps) and steps[i] is not None:
            steps[i]()


def near_window(i):
    first = max(0, i - LONGEST // LANES) if isinstance(i, int) else jnp.maximum(i - LONGEST // LANES, 0)
    return first * LANES, (i + 1 - first + KB // LANES - 1) // (KB // LANES)


def bound_window(spans, count):
    def window(i):
        first = spans[i, 0] // KEY_STEP * KEY_STEP
        return first, (spans[count + i, QB - 1] - first + KB - 1) // KB

    return window


def key_block(first_key, j, keys, step):
    nominal = first_key + j * KB
    return pl.multiple_of(jnp.minimum(nominal, keys - KB), step), nominal


def block_bias(low, high, start, nominal):
    place = start + lax.broadcasted_iota(jnp.int32, (KB, QB), 0)
    bias = jnp.where((place >= jnp.maximum(low, nominal)) & (place < high), 0.0, MASKED).astype(f32)
    return jnp.concatenate([bias, bias], axis=1)


def attention(
    window, which, bounds, key_ref, value_t, value_ref, query_z, mixed_ref, lse_ref, score_scr, out_scr, steps=()
):
    keys = key_ref.shape[0]
    pairs = query_z.shape[0]
    fold = (KB // 8, 8, 2 * QB)
    step = KEY_STEP if value_t is None else LANES

    def query_block(i):
        rows = rows_of(i, QB)
        pair_rows = rows_of(i, 2 * QB)
        low = bounds[2 * which : 2 * which + 1, rows]
        high = bounds[2 * which + 1 : 2 * which + 2, rows]
        first_key, blocks = window(i)
        out_scr[...] = jnp.zeros_like(out_scr)

        def scores(j, tops):
            start, nominal = key_block(first_key, j, keys, step)
            bias = block_bias(low, high, start, nominal)
            found = []
            raw = [
                nt(key_ref[pl.ds(start, KB), p * LANES : (p + 1) * LANES], query_z[p, pair_rows, :])
                for p in range(pairs)
            ]
            for p in range(pairs):
                score = raw[p] + bias
                score_scr[p, rows_of(j, KB), :] = score
                found.append(jnp.maximum(tops[p], jnp.max(score.reshape(fold), axis=0)))
            return tuple(found)

        tops = lax.fori_loop(
            0, blocks, scores, tuple(jnp.full((8, 2 * QB), MASKED, f32) for _ in range(pairs))
        )
        top = [jnp.max(t, axis=0, keepdims=True) for t in tops]

        def weigh(j, sums):
            start, _ = key_block(first_key, j, keys, step)
            found = []
            low_exps = []
            for p in range(pairs):
                exponent = jnp.exp(score_scr[p, rows_of(j, KB), :] - top[p])
                found.append(sums[p] + jnp.sum(exponent.reshape(fold), axis=0))
                low_exps.append(exponent.astype(bf16))
            for p in range(pairs):
                if value_t is None:
                    both = tn(value_ref[pl.ds(start, KB), p * LANES : (p + 1) * LANES], low_exps[p])
                    out_scr[p, 0:HEAD_DIM, :] += both[0:HEAD_DIM, :QB]
                    out_scr[p, HEAD_DIM:, :] += both[HEAD_DIM:, QB:]
                    continue
                for h in range(2):
                    heads = slice(h * HEAD_DIM, (h + 1) * HEAD_DIM)
                    value = value_t[
                        p * LANES + h * HEAD_DIM : p * LANES + (h + 1) * HEAD_DIM, pl.ds(start, KB)
                    ]
                    out_scr[p, heads, :] += nn(value, low_exps[p][:, h * QB : (h + 1) * QB])
            return tuple(found)

        sums = lax.fori_loop(
            0, blocks, weigh, tuple(jnp.zeros((8, 2 * QB), f32) for _ in range(pairs))
        )
        for p in range(pairs):
            total = jnp.sum(sums[p], axis=0, keepdims=True)
            lse_ref[i, p : p + 1, :] = top[p] + jnp.log(total)
            inverse = 1.0 / total
            out = jnp.concatenate(
                [out_scr[p, 0:HEAD_DIM, :] * inverse[:, :QB], out_scr[p, HEAD_DIM:, :] * inverse[:, QB:]],
                axis=0,
            )
            mixed_ref[rows, p * LANES : (p + 1) * LANES] = out.T.astype(bf16)

    run_blocks(query_z.shape[1] // (2 * QB), query_block, steps)


def put_deltas(delta_ref, first_block, grad, mixed):
    for b in range(grad.shape[0] // QB):
        for p in range(grad.shape[1] // LANES):
            place = (slice(b * QB, (b + 1) * QB), slice(p * LANES, (p + 1) * LANES))
            product = (grad[place].astype(f32) * mixed[place].astype(f32)).T
            for h in range(2):
                delta_ref[first_block + b, p : p + 1, h * QB : (h + 1) * QB] = jnp.sum(
                    product[h * HEAD_DIM : (h + 1) * HEAD_DIM], axis=0, keepdims=True
                )


def attention_back(
    window, which, bounds, key_ref, key_t, value_ref, query_z, grad_z, delta_ref, lse_ref,
    dquery_ref, dkey_scr, dvalue_scr, dq_scr, steps=(),
):
    keys = key_ref.shape[0]
    pairs = query_z.shape[0]
    step = KEY_STEP if key_t is None else LANES

    def query_block(i):
        rows = rows_of(i, QB)
        pair_rows = rows_of(i, 2 * QB)
        low = bounds[2 * which : 2 * which + 1, rows]
        high = bounds[2 * which + 1 : 2 * which + 2, rows]
        first_key, blocks = window(i)
        dq_scr[...] = jnp.zeros_like(dq_scr)
        deltas = [delta_ref[i, p : p + 1, :] for p in range(pairs)]

        def key_step(j):
            start, nominal = key_block(first_key, j, keys, step)
            bias = block_bias(low, high, start, nominal)
            block = pl.ds(start, KB)
            held = {}

            def first(p):
                lanes = slice(p * LANES, (p + 1) * LANES)
                held["s", p] = nt(key_ref[block, lanes], query_z[p, pair_rows, :])
                held["d", p] = nt(value_ref[block, lanes], grad_z[p, pair_rows, :])

            def second(p):
                prob = jnp.exp(held.pop(("s", p)) + bias - lse_ref[i, p : p + 1, :])
                held["ds", p] = (prob * (held.pop(("d", p)) - deltas[p])).astype(bf16)
                held["p", p] = prob.astype(bf16)

            def third(p):
                lanes = slice(p * LANES, (p + 1) * LANES)
                dscore = held["ds", p]
                dvalue_scr[block, lanes] += nn(held["p", p], grad_z[p, pair_rows, :])
                dkey_scr[block, lanes] += nn(dscore, query_z[p, pair_rows, :])
                if key_t is None:
                    both = tn(key_ref[block, lanes], dscore)
                    dq_scr[p, 0:HEAD_DIM, :] += both[0:HEAD_DIM, :QB]
                    dq_scr[p, HEAD_DIM:, :] += both[HEAD_DIM:, QB:]
                    return
                for h in range(2):
                    heads = slice(h * HEAD_DIM, (h + 1) * HEAD_DIM)
                    key = key_t[
                        p * LANES + h * HEAD_DIM : p * LANES + (h + 1) * HEAD_DIM, block
                    ]
                    dq_scr[p, heads, :] += nn(key, dscore[:, h * QB : (h + 1) * QB])

            for stage in (first, second, third):
                for p in range(pairs):
                    stage(p)

        each_chunk(blocks, key_step)
        for p in range(pairs):
            dquery_ref[rows, p * LANES : (p + 1) * LANES] = (
                (dq_scr[p] * HEAD_DIM**-0.5).T.astype(bf16)
            )

    run_blocks(query_z.shape[1] // (2 * QB), query_block, steps)


def norm_parts(values):
    average = jnp.mean(values, axis=-1, keepdims=True)
    centred = values - average
    spread = jnp.mean(centred * centred, axis=-1, keepdims=True)
    inverse = lax.rsqrt(spread + norm_eps)
    return centred * inverse, inverse


def norm_back(gradient, normed, inverse, gain):
    scaled = gradient * gain
    first_mean = jnp.mean(scaled, axis=-1, keepdims=True)
    second_mean = jnp.mean(scaled * normed, axis=-1, keepdims=True)
    return inverse * (scaled - first_mean - normed * second_mean)


def fold_rows(values):
    return jnp.sum(values.reshape(values.shape[0] // 8, 8, values.shape[1]), axis=0)


def load_norms(norm_ref):
    group = norm_ref.shape[0] // 4
    blocks = [jnp.sum(norm_ref[group * i : group * (i + 1)].astype(f32), axis=0) for i in range(4)]
    rows = jnp.concatenate(blocks, axis=1)
    return [rows[i : i + 1, :] for i in range(6)]


def weight(ref, index):
    blocks = ref.shape[0]
    return ref[:, 16 * index : 16 * (index + 1), :].reshape(16 * blocks, ref.shape[2])


def put_gradient(ref, index, value):
    blocks = ref.shape[0]
    ref[:, 16 * index : 16 * (index + 1), :] = value.astype(bf16).reshape(blocks, 16, ref.shape[2])


def load_norm_rows(dst, norm_ref):
    for i, vector in enumerate(load_norms(norm_ref)):
        dst[i : i + 1, :] = vector


def sigmoid(values):
    return 0.5 * jnp.tanh(0.5 * values) + 0.5


class Mover:
    def __init__(self, sems):
        self.sems = sems
        self.count = 0
        self.open = []

    def start(self, src, dst):
        copy = pltpu.make_async_copy(src, dst, self.sems.at[self.count])
        self.count += 1
        copy.start()
        self.open.append(copy)
        return copy

    def wait(self, *copies):
        for copy in copies:
            copy.wait()
            self.open = [other for other in self.open if other is not copy]

    def finish(self):
        self.wait(*list(self.open))


def find_bounds(lengths, src_segments, bounds_ref, spans_ref):
    sentences = lengths.shape[1]
    length = bounds_ref.shape[1]
    row = lax.broadcasted_iota(jnp.int32, (sentences, sentences), 0)
    col = lax.broadcasted_iota(jnp.int32, (sentences, sentences), 1)
    sizes = jnp.broadcast_to(lengths[...].astype(f32), (sentences, sentences))

    def total(mask, values):
        return jnp.sum(jnp.where(mask, values, 0.0), axis=1, keepdims=True)

    own = total(col == row, sizes)
    starts = total(col < row, sizes)
    ends = starts + own
    sources = src_segments.shape[1]
    number = lax.broadcasted_iota(jnp.int32, (sentences, sources), 0)
    count = total(jnp.broadcast_to(src_segments[...], (sentences, sources)) == number, 1.0)
    places = lax.broadcasted_iota(jnp.int32, (sentences, length), 1).astype(f32)

    def gather(edges, values):
        return jnp.sum(jnp.where(edges <= places, values, 0.0), axis=0, keepdims=True).astype(jnp.int32)

    bounds_ref[0:1, :] = gather(ends, own)
    bounds_ref[1:2, :] = lax.broadcasted_iota(jnp.int32, (1, length), 1) + 1
    bounds_ref[2:3, :] = gather(ends, count)
    bounds_ref[3:4, :] = gather(starts, count)
    bounds_ref[4:8, :] = jnp.zeros((4, length), jnp.int32)
    blocks = length // QB
    for i in range(blocks):
        spans_ref[i : i + 1, :] = bounds_ref[2:3, i * QB : (i + 1) * QB]
        spans_ref[blocks + i : blocks + i + 1, :] = bounds_ref[3:4, i * QB : (i + 1) * QB]


def self_forward(tgt, attn, bounds, q, k, v, mix, lse, n1, s1, query_z, value_t, score_scr, out_scr, move, outs, steps):
    chunks = tgt.shape[0] // RC
    scale = jnp.array(HEAD_DIM**-0.5, bf16)

    def project(c):
        rows = rows_of(c, RC)
        x = tgt[rows, :]
        q[rows, :] = nn(x, weight(attn, 0)).astype(bf16) * scale
        k[rows, :] = nn(x, weight(attn, 1)).astype(bf16)
        v[rows, :] = nn(x, weight(attn, 2)).astype(bf16)

    each_chunk(chunks, project, 2)
    for i, ref in enumerate((q, k, v)):
        move.start(ref, outs[i])
    spread_heads(query_z, q)
    value_t[...] = v[...].T
    attention(near_window, 0, bounds, k, value_t, None, query_z, mix, lse, score_scr, out_scr, steps)
    move.start(mix, outs[3])
    move.start(lse, outs[4])

    def middle(c):
        rows = rows_of(c, RC)
        normed, inverse = norm_parts(tgt[rows, :].astype(f32) + nn(mix[rows, :], weight(attn, 3)))
        n1[rows, :] = normed
        s1[rows, :] = inverse

    each_chunk(chunks, middle, 2)
    move.start(n1, outs[5])
    move.start(s1, outs[6])


def middle_kernel(
    spans, bounds_h, full, memory_h, cot_h, n1_h, s1_h,
    out_h, d1_h, mgrad_h, gffn_h, gcross_h, gnorm_ref,
    bounds, norm_b, attn, ffn, memory, cot, n1, s1, cq, ck, cv, cmix, clse, query_z, grad_z, score_scr, small_scr,
    act_scr, dpre_scr, h2_scr, d3_scr, d2_scr, d2b_scr, grad_scr, dq_scr, dk_scr, dv_scr, out_scr, mgrad, gffn, gcross,
    sums, norm, delta, sems,
):
    width = n1.shape[1]
    chunks = n1.shape[0] // RC
    scale = jnp.array(HEAD_DIM**-0.5, bf16)
    move = Mover(sems)
    rows_cross = attn.shape[1]
    norm_rows = pl.ds(full.shape[1] - 16, 16)
    load_small = [move.start(full.at[:, norm_rows, pl.ds(0, width // 4)], norm_b), move.start(bounds_h, bounds)]
    load_cross = move.start(full.at[:, pl.ds(rows_cross, rows_cross)], attn)
    load_memory = move.start(memory_h, memory)
    load_n1 = move.start(n1_h, n1)
    load_ffn = move.start(full.at[:, pl.ds(2 * rows_cross, ffn.shape[1])], ffn)
    load_rest = [move.start(cot_h, cot), move.start(s1_h, s1)]
    sums[...] = jnp.zeros_like(sums)
    move.wait(*load_small)
    load_norm_rows(norm, norm_b)
    move.wait(load_cross, load_memory)

    def h1_of(rows):
        return n1[rows, :] * norm[0:1, :] + norm[1:2, :]

    def project(c):
        rows = rows_of(c, RC)
        mem = memory[rows, :]
        ck[rows, :] = nn(mem, weight(attn, 1)).astype(bf16)
        cv[rows, :] = nn(mem, weight(attn, 2)).astype(bf16)

    def project_queries(c):
        rows = rows_of(c, RC)
        cq[rows, :] = nn(h1_of(rows).astype(bf16), weight(attn, 0)).astype(bf16) * scale

    each_chunk(chunks, project, 2)
    move.wait(load_n1)
    each_chunk(chunks, project_queries, 2)
    spread_heads(query_z, cq)
    window = bound_window(spans, n1.shape[0] // QB)
    attention(window, 1, bounds, ck, None, cv, query_z, cmix, clse, score_scr, small_scr)
    move.wait(load_ffn, *load_rest)
    blocks = ffn.shape[0]
    parts = act_scr.shape[1] // width
    share = blocks // parts

    def outer(b):
        return ffn[share * b : share * (b + 1), 16 * parts :, :].reshape(width, width)

    def body(c):
        rows = [pl.ds(pl.multiple_of((c * WAYS + w) * RC, RC), RC) for w in range(WAYS)]
        ways = range(WAYS)
        state = [{} for _ in ways]

        def enter(w):
            st = state[w]
            st["n2"], st["s2"] = norm_parts(h1_of(rows[w]) + nn(cmix[rows[w], :], weight(attn, 3)))
            st["third"] = st["n2"] * norm[2:3, :] + norm[3:4, :]
            st["h2b"] = st["third"].astype(bf16)
            h2_scr[rows[w], :] = st["h2b"]

        def pre(w, b):
            state[w]["pre", b] = nn(state[w]["h2b"], weight(ffn, b))

        def act(w, b):
            st = state[w]
            sig = sigmoid(st["pre", b])
            swish = st.pop(("pre", b)) * sig
            st["act", b] = swish.astype(bf16)
            act_scr[rows[w], width * b : width * (b + 1)] = st["act", b]
            st["slope", b] = sig + swish * (1.0 - sig)

        def out(w, b):
            st = state[w]
            st["third"] = st["third"] + nn(st.pop(("act", b)), outer(b))

        def turn(w):
            st = state[w]
            n3, s3 = norm_parts(st.pop("third"))
            out_scr[rows[w], :] = (n3 * norm[4:5, :] + norm[5:6, :]).astype(bf16)
            up = cot[rows[w], :].astype(f32)
            sums[4] += fold_rows(up * n3)
            sums[5] += fold_rows(up)
            st["dh2"] = norm_back(up, n3, s3, norm[4:5, :])
            st["d3b"] = st["dh2"].astype(bf16)
            d3_scr[rows[w], :] = st["d3b"]

        def dact(w, b):
            state[w]["dact", b] = nt(state[w]["d3b"], outer(b))

        def dpre(w, b):
            st = state[w]
            st["dpre", b] = (st.pop(("dact", b)) * st.pop(("slope", b))).astype(bf16)
            dpre_scr[rows[w], width * b : width * (b + 1)] = st["dpre", b]

        def back(w, b):
            st = state[w]
            st["dh2"] = st["dh2"] + nt(st.pop(("dpre", b)), weight(ffn, b))

        def leave(w):
            st = state[w]
            dh2 = st["dh2"]
            sums[2] += fold_rows(dh2 * st["n2"])
            sums[3] += fold_rows(dh2)
            d2 = norm_back(dh2, st["n2"], st["s2"], norm[2:3, :])
            d2_scr[rows[w], :] = d2
            d2b = d2.astype(bf16)
            d2b_scr[rows[w], :] = d2b
            grad = nt(d2b, weight(attn, 3)).astype(bf16)
            grad_scr[rows[w], :] = grad
            put_deltas(delta, (c * WAYS + w) * (RC // QB), grad, cmix[rows[w], :])

        def skewed(w, first, second, third):
            for t in range(parts + 2):
                if t < parts:
                    first(w, t)
                if 0 <= t - 1 < parts:
                    second(w, t - 1)
                if 0 <= t - 2 < parts:
                    third(w, t - 2)

        for w in ways:
            enter(w)
            skewed(w, pre, act, out)
        for w in ways:
            turn(w)
            skewed(w, dact, dpre, back)
        for w in ways:
            leave(w)

    each_chunk(chunks // WAYS, body)
    move.start(out_scr, out_h)
    for b in range(parts):
        cols = slice(width * b, width * (b + 1))
        gffn[share * b : share * (b + 1), 16 * parts :, :] = (
            tn(act_scr[:, cols], d3_scr[...]).astype(bf16).reshape(share, width // share, width)
        )
        put_gradient(gffn, b, tn(h2_scr[...], dpre_scr[:, cols]))
    move.start(gffn, gffn_h)

    def put_cross(i, value):
        put_gradient(gcross, i, value)
        part = pl.ds(16 * i, 16)
        move.start(gcross.at[:, part], gcross_h.at[:, part])

    put_cross(3, tn(cmix[...], d2b_scr[...]))
    spread_heads(grad_z, grad_scr)
    dk_scr[...] = jnp.zeros_like(dk_scr)
    dv_scr[...] = jnp.zeros_like(dv_scr)
    attention_back(
        window, 1, bounds, ck, None, cv, query_z, grad_z, delta, clse, dq_scr, dk_scr, dv_scr, small_scr,
    )

    def leave(c):
        rows = rows_of(c, RC)
        dkb = dk_scr[rows, :].astype(bf16)
        dvb = dv_scr[rows, :].astype(bf16)
        ck[rows, :] = dkb
        cv[rows, :] = dvb
        mgrad[rows, :] = (nt(dkb, weight(attn, 1)) + nt(dvb, weight(attn, 2))).astype(bf16)
        normed = n1[rows, :]
        h2_scr[rows, :] = h1_of(rows).astype(bf16)
        dh1 = d2_scr[rows, :] + nt(dq_scr[rows, :], weight(attn, 0))
        sums[0] += fold_rows(dh1 * normed)
        sums[1] += fold_rows(dh1)
        d2_scr[rows, :] = norm_back(dh1, normed, s1[rows, :], norm[0:1, :])

    each_chunk(chunks, leave, 2)
    move.start(d2_scr, d1_h)
    move.start(mgrad, mgrad_h)
    for i in range(6):
        gnorm_ref[i : i + 1, :] = jnp.sum(sums[i], axis=0, keepdims=True)
    gnorm_ref[6:8, :] = jnp.zeros((2, width), f32)
    put_cross(0, tn(h2_scr[...], dq_scr[...]))
    put_cross(1, tn(memory[...], ck[...]))
    put_cross(2, tn(memory[...], cv[...]))
    move.finish()


def self_backward(
    tgt, attn, bounds, q, k, v, mix, lse, d1, tgrad, gself,
    query_z, grad_z, key_t, grad_scr, dq_scr, dk_scr, dv_scr, small_scr, d1_scr, delta, steps, begin, late,
):
    chunks = tgt.shape[0] // RC

    def enter(c):
        rows = rows_of(c, RC)
        d1b = d1[rows, :].astype(bf16)
        d1_scr[rows, :] = d1b
        grad = nt(d1b, weight(attn, 3)).astype(bf16)
        grad_scr[rows, :] = grad
        put_deltas(delta, c * (RC // QB), grad, mix[rows, :])

    each_chunk(chunks, enter, 2)
    begin[0]()
    put_gradient(gself, 3, tn(mix[...], d1_scr[...]))
    begin[1]()
    spread_heads(query_z, q)
    spread_heads(grad_z, grad_scr)
    key_t[...] = k[...].T
    dk_scr[...] = jnp.zeros_like(dk_scr)
    dv_scr[...] = jnp.zeros_like(dv_scr)
    attention_back(
        near_window, 0, bounds, k, key_t, v, query_z, grad_z, delta, lse, dq_scr, dk_scr, dv_scr, small_scr, steps,
    )
    for i, scr in enumerate((dq_scr, dk_scr, dv_scr)):
        put_gradient(gself, i, tn(tgt[...], scr[...].astype(bf16)))
    late()

    def leave(c):
        rows = rows_of(c, RC)
        tgrad[rows, :] = (
            d1[rows, :]
            + nt(dq_scr[rows, :], weight(attn, 0))
            + nt(dk_scr[rows, :].astype(bf16), weight(attn, 1))
            + nt(dv_scr[rows, :].astype(bf16), weight(attn, 2))
        ).astype(bf16)

    each_chunk(chunks, leave, 2)


def shape(dims, dtype):
    return jax.ShapeDtypeStruct(dims, dtype)


VMEM_SPEC = pl.BlockSpec(memory_space=pltpu.VMEM)
HBM_SPEC = pl.BlockSpec(memory_space=pltpu.HBM)
SMEM_SPEC = pl.BlockSpec(memory_space=pltpu.SMEM)


def vmem(*buffers):
    return [pltpu.VMEM(dims, dtype) for dims, dtype in buffers]


def dma(*dims):
    return pltpu.SemaphoreType.DMA(dims)


def adam_direction(master, gradient, moments):
    first_moment = beta_first * moments[0] + (1.0 - beta_first) * gradient
    second_moment = beta_second * moments[1] + (1.0 - beta_second) * gradient * gradient
    first_fix = 1.0 - beta_first**STEP
    second_fix = 1.0 - beta_second**STEP
    direction = (
        first_moment / first_fix / (jnp.sqrt(second_moment / second_fix) + adam_eps)
        + decay_rate * master
    )
    return (direction, first_moment, second_moment)


MESH = pl.DeviceIdType.MESH


class Place:
    def __init__(self):
        self.gx = lax.axis_index("gx")
        self.gy = lax.axis_index("gy")
        self.x = lax.rem(self.gx, 2)
        self.y = self.gx // 2
        self.z = self.gy // 2
        self.c = lax.rem(self.gy, 2)
        self.here = self.gx * 8 + self.gy

    def target(self, x, y, z, c):
        return (y * 2 + x, z * 2 + c)

    def index(self, x, y, z, c):
        return (y * 2 + x) * 8 + z * 2 + c

    def others(self):
        found = []
        for step in range(1, 32):
            device = lax.rem(self.here + step, 32)
            found.append((device // 8, lax.rem(device, 8)))
        return found


def greet(targets):
    barrier = pltpu.get_barrier_semaphore()
    for target in targets:
        pl.semaphore_signal(barrier, inc=1, device_id=target, device_id_type=MESH)
    pl.semaphore_wait(barrier, len(targets))


def remote(src, dst, send_sem, recv_sem, target):
    return pltpu.make_async_remote_copy(
        src_ref=src, dst_ref=dst, send_sem=send_sem, recv_sem=recv_sem, device_id=target, device_id_type=MESH
    )


def forward_sizes(length, width):
    pairs = width // LANES
    row = (length, width)
    lse = (length // QB, pairs, 2 * QB)
    kept = [(row, bf16)] * 4 + [(lse, f32), (row, f32), ((length, 1), f32)]
    scratch = [
        ((pairs, 2 * length, LANES), bf16), ((width, length), bf16),
        ((pairs, LONGEST + 2 * KB, 2 * QB), f32), ((pairs, LANES, QB), f32),
    ]
    return kept, scratch


class Gathering:
    parts = ((0, 32), (32, 32), (64, 96), (160, 112))

    def __init__(self, me, mine, near, full, zsend, xsend, ysend, csend, recv, crecv):
        self.me, self.mine, self.near, self.full = me, mine, near, full
        self.zsend, self.xsend, self.ysend, self.csend, self.recv, self.crecv = zsend, xsend, ysend, csend, recv, crecv
        x, y, z, c = me.x, me.y, me.z, me.c
        self.ox, self.oy, self.oc = 1 - x, 1 - y, 1 - c
        self.x_next = me.target(self.ox, y, z, c)
        self.y_next = me.target(x, self.oy, z, c)
        self.sibling = me.target(x, y, z, self.oc)
        self.up = me.target(x, y, lax.rem(z + 1, 4), c)
        self.down = me.target(x, y, lax.rem(z + 3, 4), c)

    def held(self, part):
        return self.near if part < 2 else self.full

    def copy(self, column, zz, part, target, sem, own=False):
        rows = pl.ds(*self.parts[part])
        c = self.me.c
        dst = self.held(part).at[column, zz, c, rows]
        return remote(self.mine.at[rows] if own else dst, dst, sem, self.recv.at[column, zz, part], target)

    def arrive(self, column, zz, part):
        self.copy(column, zz, part, self.sibling, self.xsend.at[part]).wait_recv()

    def to_x(self, column, zz, part, own=False):
        self.copy(column, zz, part, self.x_next, self.xsend.at[part], own).start()

    def to_y(self, column, zz, part, own=False):
        self.copy(column, zz, part, self.y_next, self.ysend.at[part], own).start()

    def column(self, x, y):
        return y * 2 + x

    def along(self, zz, part, upward, own=False):
        me = self.me
        target = self.up if upward else self.down
        sem = self.zsend.at[zz, part, 0 if upward else 1]

        if part < 2:
            return

        @pl.when((me.z < 3) if upward else (me.z > 0))
        def _():
            self.copy(me.gx, zz, part, target, sem, own).start()

    def straight(self, d, part):
        me = self.me
        target = me.target(me.x, me.y, lax.rem(me.z + d, 4), me.c)
        return self.copy(me.gx, me.z, part, target, self.zsend.at[d, part, 0], True)

    def own_straight(self, parts):
        for d in (1, 3, 2):
            for part in parts:
                self.straight(d, part).start()

    def own_z(self, parts):
        for part in parts:
            self.along(self.me.z, part, True, True)
            self.along(self.me.z, part, False, True)

    def own_sides(self, parts):
        for part in parts:
            self.to_x(self.me.gx, self.me.z, part, True)
            self.to_y(self.me.gx, self.me.z, part, True)

    def at_distance(self, d, action):
        z = self.me.z
        if d == 0:
            action(z, None)
            return

        @pl.when(z >= d)
        def _():
            action(z - d, True)

        @pl.when(z + d <= 3)
        def _():
            action(z + d, False)

    def inline(self, d, parts):
        me = self.me

        def action(zz, upward):
            for part in parts:
                self.arrive(me.gx, zz, part)
                self.along(zz, part, upward)
                self.to_x(me.gx, zz, part)
                self.to_y(me.gx, zz, part)

        self.at_distance(d, action)

    def side(self, d, parts):
        me = self.me

        def action(zz, _):
            for part in parts:
                if part % 2 == 0:
                    column = self.column(self.ox, me.y)
                    self.arrive(column, zz, part)
                    self.to_y(column, zz, part)
                else:
                    column = self.column(me.x, self.oy)
                    self.arrive(column, zz, part)
                    self.to_x(column, zz, part)

        self.at_distance(d, action)

    def last_columns(self, part):
        last = (self.me.x, self.oy) if part % 2 == 0 else (self.ox, self.me.y)
        return (self.column(*last), self.column(self.ox, self.oy))

    def far(self, d, parts):
        def action(zz, _):
            for part in parts:
                for column in self.last_columns(part):
                    self.arrive(column, zz, part)

        self.at_distance(d, action)

    def core(self, column, part):
        rows = pl.ds(*self.parts[part])
        block = self.held(part).at[column, :, self.me.c, rows]
        return remote(block, block, self.csend.at[column, part], self.crecv.at[column, part], self.sibling)

    def core_inline(self, parts):
        for part in parts:
            self.core(self.me.gx, part).start()

    def core_side(self, parts):
        me = self.me
        for part in parts:
            self.core(self.column(self.ox, me.y) if part % 2 == 0 else self.column(me.x, self.oy), part).start()

    def core_far(self, parts):
        for part in parts:
            for column in self.last_columns(part):
                self.core(column, part).start()

    def cores(self, parts):
        for part in parts:
            for column in range(4):
                self.core(column, part).wait_recv()

    def sent(self, parts):
        me = self.me
        for part in parts:
            if part < 2:
                for d in (1, 2, 3):
                    self.straight(d, part).wait_send()
            for zz in range(4 if part >= 2 else 0):

                @pl.when((me.z < 3) & (zz <= me.z))
                def _():
                    self.copy(me.gx, zz, part, self.up, self.zsend.at[zz, part, 0]).wait_send()

                @pl.when((me.z > 0) & (zz >= me.z))
                def _():
                    self.copy(me.gx, zz, part, self.down, self.zsend.at[zz, part, 1]).wait_send()

            rows = pl.ds(*self.parts[part])
            four, eight = self.held(part).at[0, :, 0, rows], self.held(part).at[pl.ds(0, 2), :, 0, rows]
            sems = (self.xsend.at[part], self.ysend.at[part])
            few, many = sems if part % 2 == 0 else sems[::-1]
            remote(four, four, few, self.recv.at[0, 0, part], self.sibling).wait_send()
            remote(eight, eight, many, self.recv.at[0, 0, part], self.sibling).wait_send()

    def cores_sent(self, parts):
        for part in parts:
            for column in range(4):
                self.core(column, part).wait_send()

    def stages(self, parts):
        return [
            lambda: self.inline(1, parts),
            lambda: (self.side(0, parts), self.inline(2, parts)),
            lambda: (self.side(1, parts), self.inline(3, parts), self.core_inline(parts)),
            lambda: (self.side(2, parts), self.far(0, parts)),
            lambda: (self.side(3, parts), self.core_side(parts), self.far(1, parts)),
            lambda: (self.far(2, parts), self.far(3, parts), self.core_far(parts)),
        ]


def first_kernel(
    attn_h, inner_h, outer_h, norm_h, lengths_h, src_h, tgt_h,
    full, bounds_out, spans_out, q_h, k_h, v_h, mix_h, lse_h, n1_h, s1_h,
    attn_f, inner_f, outer_f, norm_f, lengths, src, mine, bounds, spans, tgt, attn,
    q, k, v, mix, lse, n1, s1, query_z, value_t, score_scr, small_scr,
    sems, zsend, xsend, ysend, csend, recv, crecv,
):
    me = Place()
    move = Mover(sems)
    loads = [
        move.start(a, b)
        for a, b in (
            (attn_h, attn_f), (inner_h, inner_f), (outer_h, outer_f), (norm_h, norm_f), (lengths_h, lengths), (src_h, src),
        )
    ]
    load_tgt = move.start(tgt_h, tgt)
    gathering = Gathering(me, mine, attn, full, zsend, xsend, ysend, csend, recv, crecv)
    barrier = pltpu.get_barrier_semaphore()

    def greet(target):
        pl.semaphore_signal(barrier, inc=1, device_id=target, device_id_type=MESH)

    peers = [gathering.x_next, gathering.y_next, gathering.sibling]
    peers += [me.target(me.x, me.y, lax.rem(me.z + d, 4), me.c) for d in (1, 2, 3)]
    for target in peers:
        greet(target)
    move.wait(loads[0])
    for j in range(8):
        mine[16 * j : 16 * j + 16, :] = attn_f[j].astype(bf16)
    attn[me.gx, me.z, me.c] = mine[0:64, :]
    pl.semaphore_wait(barrier, len(peers))
    early, late = (0, 1), (2, 3)
    gathering.own_straight(early)
    gathering.own_sides(early)
    move.wait(*loads[1:])
    for b in range(4):
        mine[128 + 16 * b : 144 + 16 * b, :] = inner_f[:, 512 * b : 512 * b + 512].astype(bf16)
    mine[192:256, :] = outer_f[...].astype(bf16)
    lanes = jnp.concatenate([norm_f[...], jnp.zeros((6, 112), f32)], axis=1)
    lanes = jnp.concatenate([lanes, jnp.zeros((10, 128), f32)], axis=0)
    lanes = pltpu.roll(lanes, me.gy * 16, 1).astype(bf16)
    mine[256:272, :] = jnp.concatenate([lanes, jnp.zeros((16, 384), bf16)], axis=1)
    gathering.own_z(late)
    gathering.own_sides(late)
    keep = move.start(mine.at[pl.ds(64, 208)], full.at[me.gx, me.z, me.c, pl.ds(64, 208)])
    find_bounds(lengths, src, bounds, spans)
    move.start(bounds, bounds_out)
    move.start(spans, spans_out)
    sooner, later = gathering.stages(early), gathering.stages(late)
    for stage in (*sooner[:3], later[0], sooner[3], later[1], sooner[4], sooner[5]):
        stage()
    move.wait(keep)
    later[2]()
    gathering.cores(early)
    move.start(attn, full.at[:, :, :, pl.ds(0, 64)])
    move.wait(load_tgt)
    self_forward(
        tgt, attn.reshape(32, 64, 512), bounds, q, k, v, mix, lse, n1, s1, query_z, value_t, score_scr, small_scr,
        move, (q_h, k_h, v_h, mix_h, lse_h, n1_h, s1_h),
        (None, later[3], None, later[4], None, later[5]),
    )
    gathering.sent(early + late)
    gathering.cores_sent(early)
    gathering.cores(late)
    gathering.cores_sent(late)
    move.finish()


def gather_and_start(params, lengths, src_segments, tgt):
    length, width = tgt.shape
    kept, scratch = forward_sizes(length, width)
    row = (length, width)
    bounds, spans = ((8, length), jnp.int32), ((2 * length // QB, QB), jnp.int32)
    full = ((4, 4, 2, 272, 512), bf16)
    loads = [(p.shape, f32) for p in params] + [(lengths.shape, jnp.int32), (src_segments.shape, jnp.int32)]
    return pl.pallas_call(
        first_kernel,
        out_shape=tuple(shape(*item) for item in [full, bounds, spans] + kept),
        in_specs=[HBM_SPEC] * 7,
        out_specs=(HBM_SPEC,) * 10,
        scratch_shapes=vmem(
            *loads, ((272, 512), bf16), bounds, spans, (row, bf16), ((4, 4, 2, 64, 512), bf16), *kept, *scratch,
        )
        + [dma(24), dma(4, 4, 2), dma(4), dma(4), dma(4, 4), dma(4, 4, 4), dma(4, 4)],
        compiler_params=pltpu.CompilerParams(collective_id=0, has_side_effects=True, vmem_limit_bytes=GRANT),
    )(*params, lengths, src_segments, tgt)


def start_kernel(
    full, lengths, src, tgt, bounds_out, spans_out, q_h, k_h, v_h, mix_h, lse_h, n1_h, s1_h,
    bounds, spans, attn, q, k, v, mix, lse, n1, s1, query_z, value_t, score_scr, small_scr, sems,
):
    move = Mover(sems)
    load = move.start(full.at[:, pl.ds(0, attn.shape[1])], attn)
    find_bounds(lengths, src, bounds, spans)
    move.start(bounds, bounds_out)
    move.start(spans, spans_out)
    move.wait(load)
    self_forward(
        tgt, attn, bounds, q, k, v, mix, lse, n1, s1, query_z, value_t, score_scr, small_scr,
        move, (q_h, k_h, v_h, mix_h, lse_h, n1_h, s1_h), (),
    )
    move.finish()


def start_only(full, lengths, src_segments, tgt):
    length, width = tgt.shape
    kept, scratch = forward_sizes(length, width)
    bounds, spans = ((8, length), jnp.int32), ((2 * length // QB, QB), jnp.int32)
    return pl.pallas_call(
        start_kernel,
        out_shape=tuple(shape(*item) for item in [bounds, spans] + kept),
        in_specs=[HBM_SPEC] + [VMEM_SPEC] * 3,
        out_specs=(HBM_SPEC,) * 9,
        scratch_shapes=vmem(bounds, spans, ((full.shape[0], 64, width), bf16), *kept, *scratch) + [dma(16)],
        compiler_params=pltpu.CompilerParams(vmem_limit_bytes=GRANT),
    )(full, lengths, src_segments, tgt)


def middle(spans, bounds, full, memory, cotangent, n1, s1):
    length, width = n1.shape
    keys = memory.shape[0]
    blocks = full.shape[0]
    ffn_rows = full.shape[1] - 144
    hidden = ffn_rows * blocks // 2 * full.shape[2] // width
    pairs = width // LANES
    row, mem_row = (length, width), (keys, width)
    zeroed = ((pairs, 2 * length, LANES), bf16)
    gffn, gcross = ((blocks, ffn_rows, width), bf16), ((blocks, 64, width), bf16)
    outs = [(row, bf16), (row, f32), (mem_row, bf16), gffn, gcross, ((8, width), f32)]
    scratch = vmem(
        (bounds.shape, jnp.int32), ((blocks, 16, width // 4), bf16), gcross, gffn, (mem_row, bf16), (row, bf16), (row, f32),
        ((length, 1), f32), (row, bf16), (mem_row, bf16), (mem_row, bf16), (row, bf16),
        ((length // QB, pairs, 2 * QB), f32), zeroed, zeroed, ((pairs, keys + KB, 2 * QB), f32),
        ((pairs, LANES, QB), f32), ((length, hidden), bf16), ((length, hidden), bf16), (row, bf16), (row, bf16),
        (row, f32), (row, bf16), (row, bf16), (row, bf16), (mem_row, f32), (mem_row, f32), (row, bf16), (mem_row, bf16),
        gffn, gcross, ((6, 8, width), f32), ((8, width), f32),
        ((length // QB, pairs, 2 * QB), f32),
    )
    return pl.pallas_call(
        middle_kernel,
        out_shape=tuple(shape(*item) for item in outs),
        in_specs=[SMEM_SPEC] + [HBM_SPEC] * 6,
        out_specs=(HBM_SPEC,) * 5 + (VMEM_SPEC,),
        scratch_shapes=scratch + [dma(16)],
        compiler_params=pltpu.CompilerParams(vmem_limit_bytes=GRANT),
    )(spans, bounds, full, memory, cotangent, n1, s1)


OUTER_ROWS = slice(96, 160)


def attn_rows(j):
    return 192 + 16 * j if j < 4 else 64 + 16 * (j - 4) if j < 6 else 160 + 16 * (j - 6)


def add_rows(dst, *sources):
    total = sources[0][...].astype(f32)
    for source in sources[1:]:
        total = total + source[...].astype(f32)
    dst[...] = total.astype(dst.dtype)


class Summing:
    order = (2, 1, 3, 0)

    def __init__(self, me, sources, rows, pieces, first_a, first_b, second_a, second_b, third, result, sems):
        self.me, self.sources, self.rows, self.pieces = me, sources, rows, pieces
        self.first_a, self.first_b, self.second_a, self.second_b, self.third = first_a, first_b, second_a, second_b, third
        self.result = result
        (self.lsem, self.csend, self.crecv, self.send1, self.recv1, self.send2, self.recv2, self.send3, self.recv3) = sems
        x, y, z, c = me.x, me.y, me.z, me.c
        self.ox, self.oy, self.oc = 1 - x, 1 - y, 1 - c
        self.x_next = me.target(self.ox, y, z, c)
        self.y_next = me.target(x, self.oy, z, c)
        self.sibling = me.target(x, y, z, self.oc)
        self.zs = [lax.rem(z + d, 4) for d in range(4)]
        self.half = first_a.shape[2]
        self.top, self.bottom = pl.ds(0, self.half), pl.ds(self.half, self.half)
        self.pending, self.cores, self.own = [], {}, {}
        self.firsts, self.seconds, self.thirds = {}, {}, {}

    def send(self, *args):
        copy = remote(*args)
        copy.start()
        self.pending.append(copy)
        return copy

    def load(self):
        for d in self.order:
            for k, (source, kept, _) in enumerate(self.sources):
                if kept is not None:
                    copy = pltpu.make_async_copy(source.at[:, self.zs[d], self.me.c], kept.at[d], self.lsem.at[d, k])
                    copy.start()
                    self.own[d, k] = copy

    def core(self):
        for d in self.order:
            for k, (source, _, got) in enumerate(self.sources):
                self.cores[d, k] = self.send(
                    source.at[:, self.zs[d], self.oc], got.at[d], self.csend.at[d, k], self.crecv.at[d, k], self.sibling
                )

    def stage1(self, d):
        me = self.me
        for k in range(len(self.sources)):
            if (d, k) in self.own:
                self.own[d, k].wait()
            self.cores[d, k].wait_recv()

        def add(i):
            piece = self.pieces.at[d, i // 2, lax.rem(i, 2)]
            for start, count, k, first in self.rows:
                source, kept, got = self.sources[k]
                held = source.at[i, self.zs[d], me.c] if kept is None else kept.at[d, i]
                part = pl.ds(first, count)
                add_rows(piece.at[pl.ds(start, count)], held.at[part], got.at[d, i, part])

        each_chunk(4, add)
        self.firsts[d] = (
            self.send(
                self.pieces.at[d, self.oy, :, self.top], self.first_a.at[d], self.send1.at[d, 0], self.recv1.at[d, 0],
                self.y_next,
            ),
            self.send(
                self.pieces.at[d, :, self.ox, self.bottom], self.first_b.at[d], self.send1.at[d, 1],
                self.recv1.at[d, 1], self.x_next,
            ),
        )

    def stage2(self, d):
        me = self.me
        self.firsts[d][0].wait_recv()
        part = self.pieces.at[d, me.y, self.ox, self.top]
        add_rows(part, part, self.first_a.at[d, self.ox])
        one = self.send(part, self.second_a.at[d], self.send2.at[d, 0], self.recv2.at[d, 0], self.x_next)
        self.firsts[d][1].wait_recv()
        part = self.pieces.at[d, self.oy, me.x, self.bottom]
        add_rows(part, part, self.first_b.at[d, self.oy])
        two = self.send(part, self.second_b.at[d], self.send2.at[d, 1], self.recv2.at[d, 1], self.y_next)
        self.seconds[d] = (one, two)

    def stage3(self, d):
        me = self.me
        for copy in self.seconds[d]:
            copy.wait_recv()
        for rows, first, second, at in (
            (self.top, self.first_a, self.second_a, me.x), (self.bottom, self.first_b, self.second_b, me.y),
        ):
            part = self.pieces.at[d, me.y, me.x, rows]
            add_rows(part if d else self.result.at[rows], part, first.at[d, at], second.at[d])
        if d:
            self.thirds[d] = self.send(
                self.pieces.at[d, me.y, me.x], self.third.at[d - 1], self.send3.at[d - 1], self.recv3.at[d - 1],
                me.target(me.x, me.y, self.zs[d], me.c),
            )

    def end(self):
        for d in (1, 2, 3):
            self.thirds[d].wait_recv()
        add_rows(self.result, self.result, self.third.at[0], self.third.at[1], self.third.at[2])


def last_kernel(
    full, bounds_h, tgt_h, q_h, k_h, v_h, mix_h, lse_h, d1_h, gffn, gcross, gnorm_h,
    attn_ph, inner_ph, outer_ph, norm_ph, attn_mh, in_mh, out_mh, norm_mh,
    tgrad_h, g_h, gn_ref, totals_ref,
    g_ref, attn_p, inner_p, outer_p, norm_p, attn_m, in_m, out_m, norm_m,
    bounds, tgt, attn, q, k, v, mix, lse, d1, tgrad, gself, query_z, grad_z, key_t, grad_scr, dq_scr, dk_scr, dv_scr,
    small_scr, d1_scr, delta, own_ffn, own_cross, got_ffn, got_cross, pieces, first_a, first_b, second_a, second_b, third,
    got_self, pieces2, first_a2, first_b2, second_a2, second_b2, third2, vectors, squares, tiles,
    msems, psems, *sems,
):
    me = Place()
    move = Mover(msems)
    others = me.others()
    barrier = pltpu.get_barrier_semaphore()
    for target in others:
        pl.semaphore_signal(barrier, inc=1, device_id=target, device_id_type=MESH)
    load_first = [move.start(a, b) for a, b in ((gnorm_h, vectors.at[0]), (d1_h, d1), (full.at[:, pl.ds(0, 64)], attn))]
    load_mix = move.start(mix_h, mix)
    load_rest = [
        move.start(a, b)
        for a, b in ((q_h, q), (k_h, k), (v_h, v), (lse_h, lse), (bounds_h, bounds), (tgt_h, tgt))
    ]
    sems1, sems2, (nsend, nrecv, tsend, trecv) = sems[0:9], sems[9:18], sems[18:22]
    big = Summing(
        me, [(gffn, own_ffn, got_ffn), (gcross, own_cross, got_cross)],
        [(0, 64, 0, 0), (64, 32, 1, 0), (96, 64, 0, 64), (160, 32, 1, 32)],
        pieces, first_a, first_b, second_a, second_b, third, g_ref.at[pl.ds(0, 192)], sems1,
    )
    rest = Summing(
        me, [(gself, None, got_self)], [(0, 64, 0, 0)],
        pieces2, first_a2, first_b2, second_a2, second_b2, third2, g_ref.at[pl.ds(192, 64)], sems2,
    )
    big.load()
    pl.semaphore_wait(barrier, len(others))
    big.core()
    load_last = [
        move.start(a, b)
        for a, b in (
            (attn_ph, attn_p), (inner_ph, inner_p), (outer_ph, outer_p), (norm_ph, norm_p),
            (attn_mh, attn_m), (in_mh, in_m), (out_mh, out_m), (norm_mh, norm_m),
        )
    ]
    move.wait(*load_first, load_mix)
    norm_copies = [big.send(vectors.at[0], vectors.at[1], nsend.at[0], nrecv.at[0], big.sibling)]

    def norm_step(stage, target):
        norm_copies[-1].wait_recv()
        vectors[2 * stage] = vectors[2 * stage - 2] + vectors[2 * stage - 1]
        norm_copies.append(
            big.send(vectors.at[2 * stage], vectors.at[2 * stage + 1], nsend.at[stage], nrecv.at[stage], target)
        )

    def norm_last():
        norm_copies[-1].wait_recv()
        vectors[6] = vectors[4] + vectors[5]
        for d in range(1, 4):
            target = me.target(me.x, me.y, big.zs[d], me.c)
            norm_copies.append(big.send(vectors.at[6], vectors.at[6 + d], nsend.at[2 + d], nrecv.at[2 + d], target))

    far, up, down, here = big.order
    steps = [
        None,
        lambda: norm_step(1, big.x_next),
        None,
        lambda: (big.stage2(far), big.stage1(down)),
        None,
        lambda: (big.stage2(up), big.stage3(far), big.stage1(here), norm_step(2, big.y_next)),
        None,
        lambda: (big.stage2(down), big.stage3(up)),
    ]

    begin = (lambda: big.stage1(far), lambda: big.stage1(up))

    def late():
        rest.core()
        big.stage2(here)
        rest.stage1(far)
        rest.stage1(up)
        big.stage3(down)
        norm_last()

    move.wait(*load_rest)
    self_backward(
        tgt, attn, bounds, q, k, v, mix, lse, d1, tgrad, gself.reshape(32, 64, 512),
        query_z, grad_z, key_t, grad_scr, dq_scr, dk_scr, dv_scr, small_scr, d1_scr, delta, steps, begin, late,
    )
    move.start(tgrad, tgrad_h)
    rest.stage1(down)
    rest.stage1(here)
    big.stage3(here)
    rest.stage2(far)
    rest.stage2(up)
    rest.stage3(far)
    rest.stage2(down)
    rest.stage3(up)
    rest.stage2(here)
    rest.stage3(down)
    rest.stage3(here)
    big.end()
    for copy in norm_copies[3:]:
        copy.wait_recv()
    vectors[10] = (vectors[6] + vectors[8]) + (vectors[7] + vectors[9])
    lanes = vectors[10, :, pl.ds(pl.multiple_of(me.gx * 128, 128), 128)]
    gn_ref[...] = pltpu.roll(lanes, lax.rem(128 - me.gy * 16, 128), 1)

    def put(t, pairs):
        for i in range(2):
            squares[16 * i + t : 16 * i + t + 1, :] = sum(
                jnp.sum(pair[i] * pair[i], axis=0, keepdims=True) for pair in pairs
            )

    move.wait(*load_last)

    def direction(*args):
        return adam_direction(*args)[0]

    def put_attn(j):
        grad = g_ref[attn_rows(j) : attn_rows(j) + 16, :]
        put(j, [(attn_p[j], direction(attn_p[j], grad, (attn_m[0, j], attn_m[1, j])))])

    for j in range(4, 8):
        put_attn(j)
    pairs = []
    for b in range(4):
        cols = slice(512 * b, 512 * b + 512)
        grad = g_ref[16 * b : 16 * b + 16, :]
        pairs.append((inner_p[:, cols], direction(inner_p[:, cols], grad, (in_m[0, :, cols], in_m[1, :, cols]))))
    put(8, pairs)
    put(9, [(outer_p[...], direction(outer_p[...], g_ref[OUTER_ROWS, :], (out_m[0], out_m[1])))])
    master = norm_p[...]
    update = direction(master, gn_ref[0:6, 0:16], (norm_m[:, 0, :], norm_m[:, 1, :]))
    rest_lanes = jnp.zeros((6, 512 - 16), f32)
    master, update = (jnp.concatenate([item, rest_lanes], axis=1) for item in (master, update))
    for i in range(6):
        put(10 + i, [(master[i : i + 1], update[i : i + 1])])
    rest.end()
    move.start(g_ref, g_h)
    for j in range(4):
        put_attn(j)
    folded = (squares[:, 0:128] + squares[:, 128:256]) + (squares[:, 256:384] + squares[:, 384:512])
    row = jnp.sum(folded.T, axis=0, keepdims=True)
    row = jnp.concatenate([row, jnp.zeros((1, 96), f32)], axis=1)
    tiles[me.here] = jnp.concatenate([row, jnp.zeros((7, 128), f32)], axis=0)
    for target in others:
        remote(tiles.at[me.here], tiles.at[me.here], tsend, trecv, target).start()
    for copy in big.pending + rest.pending:
        copy.wait_send()
    received = tiles.at[pl.ds(0, 31)]
    every = remote(received, received, tsend, trecv, big.sibling)
    every.wait_recv()
    every.wait_send()
    totals_ref[...] = jnp.sum(tiles[...], axis=0)
    move.finish()


def backward_scratch(length, width):
    pairs = width // LANES
    row = (length, width)
    zeroed = ((pairs, 2 * length, LANES), bf16)
    return [
        zeroed, zeroed, ((width, length), bf16), (row, bf16), (row, bf16), (row, f32), (row, f32),
        ((pairs, LANES, QB), f32), (row, bf16), ((length // QB, pairs, 2 * QB), f32),
    ]


def finish_and_reduce(full, bounds, tgt, saved, d1, grads, norm_grad, params, moments):
    length, width = tgt.shape
    row = (length, width)
    lse = (length // QB, width // LANES, 2 * QB)

    def sums(half):
        return [
            ((4, 2, 2, 2 * half, 512), bf16), ((4, 2, half, 512), bf16), ((4, 2, half, 512), bf16),
            ((4, half, 512), bf16), ((4, half, 512), bf16), ((3, 2 * half, 512), bf16),
        ]

    scratch = vmem(
        ((256, 512), f32), *((item.shape, f32) for item in (*params, *moments)),
        (bounds.shape, jnp.int32), (row, bf16), ((32, 64, 512), bf16), *[(row, bf16)] * 4, (lse, f32), (row, f32),
        (row, bf16), ((4, 4, 2, 64, 512), bf16), *backward_scratch(length, width),
        ((4, 4, 128, 512), bf16), ((4, 4, 64, 512), bf16), ((4, 4, 128, 512), bf16), ((4, 4, 64, 512), bf16), *sums(96),
        ((4, 4, 64, 512), bf16), *sums(32), ((11, 8, 512), f32), ((32, 512), f32), ((32, 8, 128), f32),
    )
    round_sems = [dma(4, 2), dma(4, 2), dma(4, 2), dma(4, 2), dma(4, 2), dma(4, 2), dma(4, 2), dma(3), dma(3)]
    split = [grad.reshape(4, 4, 2, grad.shape[1], 512) for grad in grads]
    return pl.pallas_call(
        last_kernel,
        out_shape=(shape(row, bf16), shape((256, 512), f32), shape((8, 128), f32), shape((8, 128), f32)),
        in_specs=[HBM_SPEC] * 20,
        out_specs=(HBM_SPEC, HBM_SPEC, VMEM_SPEC, VMEM_SPEC),
        scratch_shapes=scratch + [dma(24), dma(1)] + round_sems + round_sems + [dma(6), dma(6)] + [pltpu.SemaphoreType.DMA] * 2,
        compiler_params=pltpu.CompilerParams(collective_id=1, has_side_effects=True, vmem_limit_bytes=GRANT),
    )(full, bounds, tgt, *saved, d1, *split, norm_grad, *params, *moments)


def finish_kernel(
    full, bounds, tgt, q, k, v, mix, lse, d1, tgrad, gself,
    attn, query_z, grad_z, key_t, grad_scr, dq_scr, dk_scr, dv_scr, small_scr, d1_scr, delta, sems,
):
    move = Mover(sems)
    move.wait(move.start(full.at[:, pl.ds(0, attn.shape[1])], attn))
    self_backward(
        tgt, attn, bounds, q, k, v, mix, lse, d1, tgrad, gself,
        query_z, grad_z, key_t, grad_scr, dq_scr, dk_scr, dv_scr, small_scr, d1_scr, delta, (), (lambda: None,) * 2, lambda: None,
    )


def finish_only(full, bounds, tgt, saved, d1):
    length, width = tgt.shape
    gself = ((full.shape[0], 64, width), bf16)
    return pl.pallas_call(
        finish_kernel,
        out_shape=(shape((length, width), bf16), shape(*gself)),
        in_specs=[HBM_SPEC] + [VMEM_SPEC] * 8,
        out_specs=(VMEM_SPEC, VMEM_SPEC),
        scratch_shapes=vmem(gself, *backward_scratch(length, width)) + [dma(2)],
        compiler_params=pltpu.CompilerParams(vmem_limit_bytes=GRANT),
    )(full, bounds, tgt, *saved, d1)


def update_kernel(*refs):
    ins, outs = refs[:12], refs[12:30]
    held, made, sems = refs[30:42], refs[42:59], refs[59]
    move = Mover(sems)
    order = (3, 2, 1, 7, 11, 6, 10, 5, 9, 4, 8, 0)
    loads = {i: move.start(ins[i], held[i]) for i in order}
    g_ref, gn_ref, totals_ref, attn, inner, outer, norm, attn_m, in_m, out_m, norm_m = held[1:]
    norms_ref = made[16]

    def results(t):
        return [(made[i], outs[1 + i]) for i in (t, 4 + 2 * t, 5 + 2 * t, 12 + t)]

    def step(t, master, gradient, moments, ratio, refs, place):
        direction, first_moment, second_moment = adam_direction(master, gradient, moments)
        value = master - ratio * direction
        for (ref, _), item in zip(refs, (value, first_moment, second_moment, value.astype(bf16))):
            ref[place] = item

    def leave(refs):
        for ref, out in refs:
            move.start(ref, out)

    move.wait(loads[3], loads[2], loads[7], loads[11])
    roots = jnp.sqrt(totals_ref[0:1, 0:32])
    norms_ref[0:1, :] = roots[:, 0:16]
    norms_ref[1:2, :] = roots[:, 16:32]
    move.start(norms_ref, outs[17])
    ratio = learn_rate * (roots[:, 0:16] / roots[:, 16:32])
    vectors = results(3)
    for i in range(6):
        one = slice(i, i + 1)
        moments = (norm_m[i, 0:1], norm_m[i, 1:2])
        step(10 + i, norm[one], gn_ref[one, 0:16], moments, ratio[:, 10 + i : 11 + i], vectors, one)
    leave(vectors)
    move.wait(loads[1], loads[6], loads[10])
    moments = (out_m[0], out_m[1])
    step(2, outer[...], g_ref[OUTER_ROWS, :], moments, ratio[:, 9:10], results(2), ...)
    leave(results(2))
    move.wait(loads[5], loads[9])
    for b in range(4):
        cols = slice(512 * b, 512 * b + 512)
        moments = (in_m[0, :, cols], in_m[1, :, cols])
        step(1, inner[:, cols], g_ref[16 * b : 16 * b + 16, :], moments, ratio[:, 8:9], results(1), (slice(None), cols))
    leave(results(1))
    move.wait(loads[4], loads[8], loads[0])
    move.start(held[0], outs[0])
    for j in range(8):
        grad = g_ref[attn_rows(j) : attn_rows(j) + 16, :]
        step(0, attn[j], grad, (attn_m[0, j], attn_m[1, j]), ratio[:, j : j + 1], results(0), j)
    leave(results(0))
    move.finish()


def update_params(summed, params, moments):
    args = (*summed, *params, *moments)
    outs = [shape(p.shape, f32) for p in params]
    outs += [shape(p.shape, f32) for p in params for _ in range(2)]
    outs += [shape(p.shape, bf16) for p in params] + [shape((2, 16), f32)]
    return pl.pallas_call(
        update_kernel,
        out_shape=(shape(summed[0].shape, bf16), *outs),
        in_specs=[HBM_SPEC] * len(args),
        out_specs=(HBM_SPEC,) * (1 + len(outs)),
        scratch_shapes=vmem(*((item.shape, item.dtype) for item in (*args, *outs))) + [dma(32)],
        compiler_params=pltpu.CompilerParams(vmem_limit_bytes=GRANT),
    )(*args)


def tensor_squares(attn_part, inner_part, outer_part, norm_part):
    return jnp.concatenate(
        [
            jnp.sum(attn_part * attn_part, axis=(1, 2)),
            jnp.sum(inner_part * inner_part)[None],
            jnp.sum(outer_part * outer_part)[None],
            jnp.sum(norm_part * norm_part, axis=1),
        ]
    )


def blocked(matrix, width):
    blocks = matrix.shape[0] // 16
    cols = matrix.shape[1] // width
    return matrix.reshape(blocks, 16, cols, width).transpose(0, 2, 1, 3).reshape(blocks, cols * 16, width)


def unblocked(blocks, width):
    count = blocks.shape[0]
    cols = blocks.shape[1] // 16
    return blocks.reshape(count, cols, 16, width).transpose(0, 2, 1, 3).reshape(count * 16, cols * width)


def gather_any(attn_w, ffn_in, ffn_out, norm_params):
    width = attn_w.shape[2]
    attn = lax.all_gather(attn_w.astype(bf16), AXES, axis=1, tiled=True)
    inner = lax.all_gather(ffn_in.astype(bf16), AXES, axis=0, tiled=True)
    outer = lax.all_gather(ffn_out.astype(bf16), AXES, axis=0, tiled=True)
    norm = lax.all_gather(norm_params.astype(bf16), AXES, axis=1, tiled=True)
    blocks = width // 16
    attn = attn.reshape(8, blocks, 16, width).transpose(1, 0, 2, 3).reshape(blocks, 8 * 16, width)
    lanes = jnp.pad(norm, ((0, 10), (0, 0))).reshape(16, 4, 1, width // 4).transpose(1, 2, 0, 3)
    lanes = jnp.pad(lanes, ((0, 0), (0, blocks // 4 - 1), (0, 0), (0, width - width // 4))).reshape(blocks, 16, width)
    return jnp.concatenate([attn, blocked(inner, width), outer.reshape(blocks, -1, width), lanes], axis=1)


def reduce_any(grads, norm_grad, params, moments):
    grad_ffn, grad_cross, grad_self = grads
    width = grad_ffn.shape[2]
    blocks = width // 16
    attn_w, ffn_in, ffn_out, norm_params = params
    attn_m, in_m, out_m, norm_m = moments
    stack = jnp.concatenate([grad_self, grad_cross], axis=1)
    stack = stack.reshape(blocks, 8, 16, width).transpose(1, 0, 2, 3).reshape(8, width, width)
    rows = ffn_in.shape[1] // width * 16
    inner = unblocked(grad_ffn[:, :rows], width)
    outer = grad_ffn[:, rows:].reshape(-1, width)
    shard_attn = lax.psum_scatter(stack, AXES, scatter_dimension=1, tiled=True).astype(f32)
    shard_inner = lax.psum_scatter(inner, AXES, scatter_dimension=0, tiled=True).astype(f32)
    shard_outer = lax.psum_scatter(outer, AXES, scatter_dimension=0, tiled=True).astype(f32)
    shard_norm = lax.psum_scatter(norm_grad, AXES, scatter_dimension=1, tiled=True)
    attn_dir, attn_first, attn_second = adam_direction(attn_w, shard_attn, attn_m)
    inner_dir, inner_first, inner_second = adam_direction(ffn_in, shard_inner, in_m)
    outer_dir, outer_first, outer_second = adam_direction(ffn_out, shard_outer, out_m)
    norm_dir, norm_first, norm_second = adam_direction(norm_params, shard_norm, norm_m)
    weight_total, update_total = lax.psum(
        (tensor_squares(*params), tensor_squares(attn_dir, inner_dir, outer_dir, norm_dir)), AXES
    )
    ratio = jnp.sqrt(weight_total) / jnp.sqrt(update_total)
    attn_new = attn_w - learn_rate * ratio[0:8][:, None, None] * attn_dir
    in_new = ffn_in - learn_rate * ratio[8] * inner_dir
    out_new = ffn_out - learn_rate * ratio[9] * outer_dir
    norm_new = norm_params - learn_rate * ratio[10:16][:, None] * norm_dir
    norms = jnp.stack([jnp.sqrt(weight_total), jnp.sqrt(update_total)])
    return (
        attn_new, in_new, out_new, norm_new,
        attn_first, attn_second, inner_first, inner_second, outer_first, outer_second, norm_first, norm_second,
        attn_new.astype(bf16), in_new.astype(bf16), out_new.astype(bf16), norm_new.astype(bf16), norms,
    )


def on_device(
    close, tgt, memory, cotangent, tgt_lengths, src_segments, attn_w, ffn_in, ffn_out, norm_params,
    attn_moments, in_moments, out_moments, norm_moments,
):
    params = (attn_w, ffn_in, ffn_out, norm_params)
    moments = (attn_moments, in_moments, out_moments, norm_moments)
    if close and tgt.shape[0] == 1:
        full, bounds, spans, *state = gather_and_start(params, tgt_lengths, src_segments, tgt[0])
        full = full.reshape(32, *full.shape[3:])
        saved, (n1, s1) = state[:5], state[5:]
        layer_out, d1, mem_grad, grad_ffn, grad_cross, norm_grad = middle(
            spans, bounds, full, memory[0], cotangent[0], n1, s1
        )
        moments = (*moments[:3], norm_moments.transpose(1, 0, 2))
        summed = finish_and_reduce(
            full, bounds, tgt[0], saved, d1, (grad_ffn, grad_cross), norm_grad, params, moments
        )
        tgt_grad, *updated = update_params(summed, params, moments)
        return (layer_out[None], tgt_grad[None], mem_grad[None], *updated)
    full = gather_any(*params)
    parts = []
    for r in range(tgt.shape[0]):
        bounds, spans, *state = start_only(full, tgt_lengths[r : r + 1], src_segments[r : r + 1], tgt[r])
        saved, (n1, s1) = state[:5], state[5:]
        layer_out, d1, mem_grad, grad_ffn, grad_cross, norm_grad = middle(
            spans, bounds, full, memory[r], cotangent[r], n1, s1
        )
        tgt_grad, grad_self = finish_only(full, bounds, tgt[r], saved, d1)
        parts.append((layer_out, tgt_grad, mem_grad, grad_ffn, grad_cross, grad_self, norm_grad[0:6]))
    outs = [jnp.stack([part[i] for part in parts]) for i in range(3)]
    sums = [sum(part[i].astype(f32) for part in parts) for i in range(3, 7)]
    grads = [grad.astype(bf16) for grad in sums[:3]]
    return (*outs, *reduce_any(grads, sums[3], params, moments))


def fits(mesh):
    return mesh.shape["gx"] == 4 and mesh.shape["gy"] == 8


def solution(mesh):
    rows = P(AXES, None, None)
    matrix = P(AXES, None)
    stack = P(None, AXES, None)
    vectors = P(None, AXES)
    return jax.shard_map(
        functools.partial(on_device, fits(mesh)),
        mesh=mesh,
        in_specs=(
            rows, rows, rows, matrix, matrix, stack, matrix, matrix, vectors,
            P(None, None, AXES, None), stack, stack, P(None, None, AXES),
        ),
        out_specs=(
            rows, rows, rows, stack, matrix, matrix, vectors, stack, stack, matrix, matrix, matrix, matrix,
            vectors, vectors, stack, matrix, matrix, vectors, P(),
        ),
        check_vma=False,
    )
```

```python
import functools

import jax
import jax.numpy as jnp
from jax import lax
from jax.experimental import pallas as pl
from jax.experimental.pallas import tpu as pltpu
from jax.sharding import PartitionSpec as P

HEAD_DIM = 64
STEP = 5

beta_first = 0.5
beta_second = 0.5
learn_rate = 0.5
decay_rate = 0.01
norm_eps = 1e-05
adam_eps = 1e-06

f32 = jnp.float32
bf16 = jnp.bfloat16
LANES = 128
QB = 128
KB = 256
RC = 256
LONGEST = 512
WAYS = 2
KEY_STEP = 16
MASKED = -1e30
AXES = ("gx", "gy")
GRANT = 63 * 2**20


def nn(left, right):
    return lax.dot_general(left, right, (((1,), (0,)), ((), ())), preferred_element_type=f32)


def nt(left, right):
    return lax.dot_general(left, right, (((1,), (1,)), ((), ())), preferred_element_type=f32)


def tn(left, right):
    return lax.dot_general(left, right, (((0,), (0,)), ((), ())), preferred_element_type=f32)


def rows_of(step, size):
    return pl.ds(pl.multiple_of(step * size, size), size)


def each_chunk(count, body, ways=1):
    def step(index, carry):
        for way in range(ways):
            body(index * ways + way)
        return carry

    lax.fori_loop(0, count // ways, step, 0)


def spread_heads(dst, src):
    pairs = dst.shape[0]
    first = lax.broadcasted_iota(jnp.int32, (QB, LANES), 1) < HEAD_DIM
    zero = jnp.zeros((QB, LANES), bf16)

    def body(i):
        start = pl.multiple_of(i * 2 * QB, 2 * QB)
        for p in range(pairs):
            tile = src[rows_of(i, QB), p * LANES : (p + 1) * LANES]
            dst[p, pl.ds(start, QB), :] = jnp.where(first, tile, zero)
            dst[p, pl.ds(start + QB, QB), :] = jnp.where(first, zero, tile)

    each_chunk(src.shape[0] // QB, body, 2)


def run_blocks(count, body, steps):
    if not steps:
        each_chunk(count, body)
        return
    for i in range(count):
        body(i)
        if i < len(steps) and steps[i] is not None:
            steps[i]()


def near_window(i):
    first = max(0, i - LONGEST // LANES) if isinstance(i, int) else jnp.maximum(i - LONGEST // LANES, 0)
    return first * LANES, (i + 1 - first + KB // LANES - 1) // (KB // LANES)


def bound_window(spans, count):
    def window(i):
        first = spans[i, 0] // KEY_STEP * KEY_STEP
        return first, (spans[count + i, QB - 1] - first + KB - 1) // KB

    return window


def key_block(first_key, j, keys, step):
    nominal = first_key + j * KB
    return pl.multiple_of(jnp.minimum(nominal, keys - KB), step), nominal


def block_bias(low, high, start, nominal):
    place = start + lax.broadcasted_iota(jnp.int32, (KB, QB), 0)
    bias = jnp.where((place >= jnp.maximum(low, nominal)) & (place < high), 0.0, MASKED).astype(f32)
    return jnp.concatenate([bias, bias], axis=1)


def attention(
    window, which, bounds, key_ref, value_t, value_ref, query_z, mixed_ref, lse_ref, score_scr, out_scr, steps=()
):
    keys = key_ref.shape[0]
    pairs = query_z.shape[0]
    fold = (KB // 8, 8, 2 * QB)
    step = KEY_STEP if value_t is None else LANES

    def query_block(i):
        rows = rows_of(i, QB)
        pair_rows = rows_of(i, 2 * QB)
        low = bounds[2 * which : 2 * which + 1, rows]
        high = bounds[2 * which + 1 : 2 * which + 2, rows]
        first_key, blocks = window(i)
        out_scr[...] = jnp.zeros_like(out_scr)

        def scores(j, tops):
            start, nominal = key_block(first_key, j, keys, step)
            bias = block_bias(low, high, start, nominal)
            found = []
            raw = [
                nt(key_ref[pl.ds(start, KB), p * LANES : (p + 1) * LANES], query_z[p, pair_rows, :])
                for p in range(pairs)
            ]
            for p in range(pairs):
                score = raw[p] + bias
                score_scr[p, rows_of(j, KB), :] = score
                found.append(jnp.maximum(tops[p], jnp.max(score.reshape(fold), axis=0)))
            return tuple(found)

        tops = lax.fori_loop(
            0, blocks, scores, tuple(jnp.full((8, 2 * QB), MASKED, f32) for _ in range(pairs))
        )
        top = [jnp.max(t, axis=0, keepdims=True) for t in tops]

        def weigh(j, sums):
            start, _ = key_block(first_key, j, keys, step)
            found = []
            low_exps = []
            for p in range(pairs):
                exponent = jnp.exp(score_scr[p, rows_of(j, KB), :] - top[p])
                found.append(sums[p] + jnp.sum(exponent.reshape(fold), axis=0))
                low_exps.append(exponent.astype(bf16))
            for p in range(pairs):
                if value_t is None:
                    both = tn(value_ref[pl.ds(start, KB), p * LANES : (p + 1) * LANES], low_exps[p])
                    out_scr[p, 0:HEAD_DIM, :] += both[0:HEAD_DIM, :QB]
                    out_scr[p, HEAD_DIM:, :] += both[HEAD_DIM:, QB:]
                    continue
                for h in range(2):
                    heads = slice(h * HEAD_DIM, (h + 1) * HEAD_DIM)
                    value = value_t[
                        p * LANES + h * HEAD_DIM : p * LANES + (h + 1) * HEAD_DIM, pl.ds(start, KB)
                    ]
                    out_scr[p, heads, :] += nn(value, low_exps[p][:, h * QB : (h + 1) * QB])
            return tuple(found)

        sums = lax.fori_loop(
            0, blocks, weigh, tuple(jnp.zeros((8, 2 * QB), f32) for _ in range(pairs))
        )
        for p in range(pairs):
            total = jnp.sum(sums[p], axis=0, keepdims=True)
            lse_ref[i, p : p + 1, :] = top[p] + jnp.log(total)
            inverse = 1.0 / total
            out = jnp.concatenate(
                [out_scr[p, 0:HEAD_DIM, :] * inverse[:, :QB], out_scr[p, HEAD_DIM:, :] * inverse[:, QB:]],
                axis=0,
            )
            mixed_ref[rows, p * LANES : (p + 1) * LANES] = out.T.astype(bf16)

    run_blocks(query_z.shape[1] // (2 * QB), query_block, steps)


def put_deltas(delta_ref, first_block, grad, mixed):
    for b in range(grad.shape[0] // QB):
        for p in range(grad.shape[1] // LANES):
            place = (slice(b * QB, (b + 1) * QB), slice(p * LANES, (p + 1) * LANES))
            product = (grad[place].astype(f32) * mixed[place].astype(f32)).T
            for h in range(2):
                delta_ref[first_block + b, p : p + 1, h * QB : (h + 1) * QB] = jnp.sum(
                    product[h * HEAD_DIM : (h + 1) * HEAD_DIM], axis=0, keepdims=True
                )


def attention_back(
    window, which, bounds, key_ref, key_t, value_ref, query_z, grad_z, delta_ref, lse_ref,
    dquery_ref, dkey_scr, dvalue_scr, dq_scr, steps=(),
):
    keys = key_ref.shape[0]
    pairs = query_z.shape[0]
    step = KEY_STEP if key_t is None else LANES

    def query_block(i):
        rows = rows_of(i, QB)
        pair_rows = rows_of(i, 2 * QB)
        low = bounds[2 * which : 2 * which + 1, rows]
        high = bounds[2 * which + 1 : 2 * which + 2, rows]
        first_key, blocks = window(i)
        dq_scr[...] = jnp.zeros_like(dq_scr)
        deltas = [delta_ref[i, p : p + 1, :] for p in range(pairs)]

        def key_step(j):
            start, nominal = key_block(first_key, j, keys, step)
            bias = block_bias(low, high, start, nominal)
            block = pl.ds(start, KB)
            held = {}

            def first(p):
                lanes = slice(p * LANES, (p + 1) * LANES)
                held["s", p] = nt(key_ref[block, lanes], query_z[p, pair_rows, :])
                held["d", p] = nt(value_ref[block, lanes], grad_z[p, pair_rows, :])

            def second(p):
                prob = jnp.exp(held.pop(("s", p)) + bias - lse_ref[i, p : p + 1, :])
                held["ds", p] = (prob * (held.pop(("d", p)) - deltas[p])).astype(bf16)
                held["p", p] = prob.astype(bf16)

            def third(p):
                lanes = slice(p * LANES, (p + 1) * LANES)
                dscore = held["ds", p]
                dvalue_scr[block, lanes] += nn(held["p", p], grad_z[p, pair_rows, :])
                dkey_scr[block, lanes] += nn(dscore, query_z[p, pair_rows, :])
                if key_t is None:
                    both = tn(key_ref[block, lanes], dscore)
                    dq_scr[p, 0:HEAD_DIM, :] += both[0:HEAD_DIM, :QB]
                    dq_scr[p, HEAD_DIM:, :] += both[HEAD_DIM:, QB:]
                    return
                for h in range(2):
                    heads = slice(h * HEAD_DIM, (h + 1) * HEAD_DIM)
                    key = key_t[
                        p * LANES + h * HEAD_DIM : p * LANES + (h + 1) * HEAD_DIM, block
                    ]
                    dq_scr[p, heads, :] += nn(key, dscore[:, h * QB : (h + 1) * QB])

            for stage in (first, second, third):
                for p in range(pairs):
                    stage(p)

        each_chunk(blocks, key_step)
        for p in range(pairs):
            dquery_ref[rows, p * LANES : (p + 1) * LANES] = (
                (dq_scr[p] * HEAD_DIM**-0.5).T.astype(bf16)
            )

    run_blocks(query_z.shape[1] // (2 * QB), query_block, steps)


def norm_parts(values):
    average = jnp.mean(values, axis=-1, keepdims=True)
    centred = values - average
    spread = jnp.mean(centred * centred, axis=-1, keepdims=True)
    inverse = lax.rsqrt(spread + norm_eps)
    return centred * inverse, inverse


def norm_back(gradient, normed, inverse, gain):
    scaled = gradient * gain
    first_mean = jnp.mean(scaled, axis=-1, keepdims=True)
    second_mean = jnp.mean(scaled * normed, axis=-1, keepdims=True)
    return inverse * (scaled - first_mean - normed * second_mean)


def fold_rows(values):
    return jnp.sum(values.reshape(values.shape[0] // 8, 8, values.shape[1]), axis=0)


def load_norms(norm_ref):
    group = norm_ref.shape[0] // 4
    blocks = [jnp.sum(norm_ref[group * i : group * (i + 1)].astype(f32), axis=0) for i in range(4)]
    rows = jnp.concatenate(blocks, axis=1)
    return [rows[i : i + 1, :] for i in range(6)]


def weight(ref, index):
    blocks = ref.shape[0]
    return ref[:, 16 * index : 16 * (index + 1), :].reshape(16 * blocks, ref.shape[2])


def put_gradient(ref, index, value):
    blocks = ref.shape[0]
    ref[:, 16 * index : 16 * (index + 1), :] = value.astype(bf16).reshape(blocks, 16, ref.shape[2])


def load_norm_rows(dst, norm_ref):
    for i, vector in enumerate(load_norms(norm_ref)):
        dst[i : i + 1, :] = vector


def sigmoid(values):
    return 0.5 * jnp.tanh(0.5 * values) + 0.5


class Mover:
    def __init__(self, sems):
        self.sems = sems
        self.count = 0
        self.open = []

    def start(self, src, dst):
        copy = pltpu.make_async_copy(src, dst, self.sems.at[self.count])
        self.count += 1
        copy.start()
        self.open.append(copy)
        return copy

    def wait(self, *copies):
        for copy in copies:
            copy.wait()
            self.open = [other for other in self.open if other is not copy]

    def finish(self):
        self.wait(*list(self.open))


def find_bounds(lengths, src_segments, bounds_ref, spans_ref):
    sentences = lengths.shape[1]
    length = bounds_ref.shape[1]
    row = lax.broadcasted_iota(jnp.int32, (sentences, sentences), 0)
    col = lax.broadcasted_iota(jnp.int32, (sentences, sentences), 1)
    sizes = jnp.broadcast_to(lengths[...].astype(f32), (sentences, sentences))

    def total(mask, values):
        return jnp.sum(jnp.where(mask, values, 0.0), axis=1, keepdims=True)

    own = total(col == row, sizes)
    starts = total(col < row, sizes)
    ends = starts + own
    sources = src_segments.shape[1]
    number = lax.broadcasted_iota(jnp.int32, (sentences, sources), 0)
    count = total(jnp.broadcast_to(src_segments[...], (sentences, sources)) == number, 1.0)
    places = lax.broadcasted_iota(jnp.int32, (sentences, length), 1).astype(f32)

    def gather(edges, values):
        return jnp.sum(jnp.where(edges <= places, values, 0.0), axis=0, keepdims=True).astype(jnp.int32)

    bounds_ref[0:1, :] = gather(ends, own)
    bounds_ref[1:2, :] = lax.broadcasted_iota(jnp.int32, (1, length), 1) + 1
    bounds_ref[2:3, :] = gather(ends, count)
    bounds_ref[3:4, :] = gather(starts, count)
    bounds_ref[4:8, :] = jnp.zeros((4, length), jnp.int32)
    blocks = length // QB
    for i in range(blocks):
        spans_ref[i : i + 1, :] = bounds_ref[2:3, i * QB : (i + 1) * QB]
        spans_ref[blocks + i : blocks + i + 1, :] = bounds_ref[3:4, i * QB : (i + 1) * QB]


def self_forward(tgt, attn, bounds, q, k, v, mix, lse, n1, s1, query_z, value_t, score_scr, out_scr, move, outs, steps):
    chunks = tgt.shape[0] // RC
    scale = jnp.array(HEAD_DIM**-0.5, bf16)

    def project(c):
        rows = rows_of(c, RC)
        x = tgt[rows, :]
        q[rows, :] = nn(x, weight(attn, 0)).astype(bf16) * scale
        k[rows, :] = nn(x, weight(attn, 1)).astype(bf16)
        v[rows, :] = nn(x, weight(attn, 2)).astype(bf16)

    each_chunk(chunks, project, 2)
    for i, ref in enumerate((q, k, v)):
        move.start(ref, outs[i])
    spread_heads(query_z, q)
    value_t[...] = v[...].T
    attention(near_window, 0, bounds, k, value_t, None, query_z, mix, lse, score_scr, out_scr, steps)
    move.start(mix, outs[3])
    move.start(lse, outs[4])

    def middle(c):
        rows = rows_of(c, RC)
        normed, inverse = norm_parts(tgt[rows, :].astype(f32) + nn(mix[rows, :], weight(attn, 3)))
        n1[rows, :] = normed
        s1[rows, :] = inverse

    each_chunk(chunks, middle, 2)
    move.start(n1, outs[5])
    move.start(s1, outs[6])


def middle_kernel(
    spans, bounds_h, full, memory_h, cot_h, n1_h, s1_h,
    out_h, d1_h, mgrad_h, gffn_h, gcross_h, gnorm_ref,
    bounds, norm_b, attn, ffn, memory, cot, n1, s1, cq, ck, cv, cmix, clse, query_z, grad_z, score_scr, small_scr,
    act_scr, dpre_scr, h2_scr, d3_scr, d2_scr, d2b_scr, grad_scr, dq_scr, dk_scr, dv_scr, out_scr, mgrad, gffn, gcross,
    sums, norm, delta, sems,
):
    width = n1.shape[1]
    chunks = n1.shape[0] // RC
    scale = jnp.array(HEAD_DIM**-0.5, bf16)
    move = Mover(sems)
    rows_cross = attn.shape[1]
    norm_rows = pl.ds(full.shape[1] - 16, 16)
    load_small = [move.start(full.at[:, norm_rows, pl.ds(0, width // 4)], norm_b), move.start(bounds_h, bounds)]
    load_cross = move.start(full.at[:, pl.ds(rows_cross, rows_cross)], attn)
    load_memory = move.start(memory_h, memory)
    load_n1 = move.start(n1_h, n1)
    load_ffn = move.start(full.at[:, pl.ds(2 * rows_cross, ffn.shape[1])], ffn)
    load_rest = [move.start(cot_h, cot), move.start(s1_h, s1)]
    sums[...] = jnp.zeros_like(sums)
    move.wait(*load_small)
    load_norm_rows(norm, norm_b)
    move.wait(load_cross, load_memory)

    def h1_of(rows):
        return n1[rows, :] * norm[0:1, :] + norm[1:2, :]

    def project(c):
        rows = rows_of(c, RC)
        mem = memory[rows, :]
        ck[rows, :] = nn(mem, weight(attn, 1)).astype(bf16)
        cv[rows, :] = nn(mem, weight(attn, 2)).astype(bf16)

    def project_queries(c):
        rows = rows_of(c, RC)
        cq[rows, :] = nn(h1_of(rows).astype(bf16), weight(attn, 0)).astype(bf16) * scale

    each_chunk(chunks, project, 2)
    move.wait(load_n1)
    each_chunk(chunks, project_queries, 2)
    spread_heads(query_z, cq)
    window = bound_window(spans, n1.shape[0] // QB)
    attention(window, 1, bounds, ck, None, cv, query_z, cmix, clse, score_scr, small_scr)
    move.wait(load_ffn, *load_rest)
    blocks = ffn.shape[0]
    parts = act_scr.shape[1] // width
    share = blocks // parts

    def outer(b):
        return ffn[share * b : share * (b + 1), 16 * parts :, :].reshape(width, width)

    def body(c):
        rows = [pl.ds(pl.multiple_of((c * WAYS + w) * RC, RC), RC) for w in range(WAYS)]
        ways = range(WAYS)
        state = [{} for _ in ways]

        def enter(w):
            st = state[w]
            st["n2"], st["s2"] = norm_parts(h1_of(rows[w]) + nn(cmix[rows[w], :], weight(attn, 3)))
            st["third"] = st["n2"] * norm[2:3, :] + norm[3:4, :]
            st["h2b"] = st["third"].astype(bf16)
            h2_scr[rows[w], :] = st["h2b"]

        def pre(w, b):
            state[w]["pre", b] = nn(state[w]["h2b"], weight(ffn, b))

        def act(w, b):
            st = state[w]
            sig = sigmoid(st["pre", b])
            swish = st.pop(("pre", b)) * sig
            st["act", b] = swish.astype(bf16)
            act_scr[rows[w], width * b : width * (b + 1)] = st["act", b]
            st["slope", b] = sig + swish * (1.0 - sig)

        def out(w, b):
            st = state[w]
            st["third"] = st["third"] + nn(st.pop(("act", b)), outer(b))

        def turn(w):
            st = state[w]
            n3, s3 = norm_parts(st.pop("third"))
            out_scr[rows[w], :] = (n3 * norm[4:5, :] + norm[5:6, :]).astype(bf16)
            up = cot[rows[w], :].astype(f32)
            sums[4] += fold_rows(up * n3)
            sums[5] += fold_rows(up)
            st["dh2"] = norm_back(up, n3, s3, norm[4:5, :])
            st["d3b"] = st["dh2"].astype(bf16)
            d3_scr[rows[w], :] = st["d3b"]

        def dact(w, b):
            state[w]["dact", b] = nt(state[w]["d3b"], outer(b))

        def dpre(w, b):
            st = state[w]
            st["dpre", b] = (st.pop(("dact", b)) * st.pop(("slope", b))).astype(bf16)
            dpre_scr[rows[w], width * b : width * (b + 1)] = st["dpre", b]

        def back(w, b):
            st = state[w]
            st["dh2"] = st["dh2"] + nt(st.pop(("dpre", b)), weight(ffn, b))

        def leave(w):
            st = state[w]
            dh2 = st["dh2"]
            sums[2] += fold_rows(dh2 * st["n2"])
            sums[3] += fold_rows(dh2)
            d2 = norm_back(dh2, st["n2"], st["s2"], norm[2:3, :])
            d2_scr[rows[w], :] = d2
            d2b = d2.astype(bf16)
            d2b_scr[rows[w], :] = d2b
            grad = nt(d2b, weight(attn, 3)).astype(bf16)
            grad_scr[rows[w], :] = grad
            put_deltas(delta, (c * WAYS + w) * (RC // QB), grad, cmix[rows[w], :])

        def skewed(w, first, second, third):
            for t in range(parts + 2):
                if t < parts:
                    first(w, t)
                if 0 <= t - 1 < parts:
                    second(w, t - 1)
                if 0 <= t - 2 < parts:
                    third(w, t - 2)

        for w in ways:
            enter(w)
            skewed(w, pre, act, out)
        for w in ways:
            turn(w)
            skewed(w, dact, dpre, back)
        for w in ways:
            leave(w)

    each_chunk(chunks // WAYS, body)
    move.start(out_scr, out_h)
    for b in range(parts):
        cols = slice(width * b, width * (b + 1))
        gffn[share * b : share * (b + 1), 16 * parts :, :] = (
            tn(act_scr[:, cols], d3_scr[...]).astype(bf16).reshape(share, width // share, width)
        )
        put_gradient(gffn, b, tn(h2_scr[...], dpre_scr[:, cols]))
    move.start(gffn, gffn_h)

    def put_cross(i, value):
        put_gradient(gcross, i, value)
        part = pl.ds(16 * i, 16)
        move.start(gcross.at[:, part], gcross_h.at[:, part])

    put_cross(3, tn(cmix[...], d2b_scr[...]))
    spread_heads(grad_z, grad_scr)
    dk_scr[...] = jnp.zeros_like(dk_scr)
    dv_scr[...] = jnp.zeros_like(dv_scr)
    attention_back(
        window, 1, bounds, ck, None, cv, query_z, grad_z, delta, clse, dq_scr, dk_scr, dv_scr, small_scr,
    )

    def leave(c):
        rows = rows_of(c, RC)
        dkb = dk_scr[rows, :].astype(bf16)
        dvb = dv_scr[rows, :].astype(bf16)
        ck[rows, :] = dkb
        cv[rows, :] = dvb
        mgrad[rows, :] = (nt(dkb, weight(attn, 1)) + nt(dvb, weight(attn, 2))).astype(bf16)
        normed = n1[rows, :]
        h2_scr[rows, :] = h1_of(rows).astype(bf16)
        dh1 = d2_scr[rows, :] + nt(dq_scr[rows, :], weight(attn, 0))
        sums[0] += fold_rows(dh1 * normed)
        sums[1] += fold_rows(dh1)
        d2_scr[rows, :] = norm_back(dh1, normed, s1[rows, :], norm[0:1, :])

    each_chunk(chunks, leave, 2)
    move.start(d2_scr, d1_h)
    move.start(mgrad, mgrad_h)
    for i in range(6):
        gnorm_ref[i : i + 1, :] = jnp.sum(sums[i], axis=0, keepdims=True)
    gnorm_ref[6:8, :] = jnp.zeros((2, width), f32)
    put_cross(0, tn(h2_scr[...], dq_scr[...]))
    put_cross(1, tn(memory[...], ck[...]))
    put_cross(2, tn(memory[...], cv[...]))
    move.finish()


def self_backward(
    tgt, attn, bounds, q, k, v, mix, lse, d1, tgrad, gself,
    query_z, grad_z, key_t, grad_scr, dq_scr, dk_scr, dv_scr, small_scr, d1_scr, delta, steps, begin, late,
):
    chunks = tgt.shape[0] // RC

    def enter(c):
        rows = rows_of(c, RC)
        d1b = d1[rows, :].astype(bf16)
        d1_scr[rows, :] = d1b
        grad = nt(d1b, weight(attn, 3)).astype(bf16)
        grad_scr[rows, :] = grad
        put_deltas(delta, c * (RC // QB), grad, mix[rows, :])

    each_chunk(chunks, enter, 2)
    begin[0]()
    put_gradient(gself, 3, tn(mix[...], d1_scr[...]))
    begin[1]()
    spread_heads(query_z, q)
    spread_heads(grad_z, grad_scr)
    key_t[...] = k[...].T
    dk_scr[...] = jnp.zeros_like(dk_scr)
    dv_scr[...] = jnp.zeros_like(dv_scr)
    attention_back(
        near_window, 0, bounds, k, key_t, v, query_z, grad_z, delta, lse, dq_scr, dk_scr, dv_scr, small_scr, steps,
    )
    for i, scr in enumerate((dq_scr, dk_scr, dv_scr)):
        put_gradient(gself, i, tn(tgt[...], scr[...].astype(bf16)))
    late()

    def leave(c):
        rows = rows_of(c, RC)
        tgrad[rows, :] = (
            d1[rows, :]
            + nt(dq_scr[rows, :], weight(attn, 0))
            + nt(dk_scr[rows, :].astype(bf16), weight(attn, 1))
            + nt(dv_scr[rows, :].astype(bf16), weight(attn, 2))
        ).astype(bf16)

    each_chunk(chunks, leave, 2)


def shape(dims, dtype):
    return jax.ShapeDtypeStruct(dims, dtype)


VMEM_SPEC = pl.BlockSpec(memory_space=pltpu.VMEM)
HBM_SPEC = pl.BlockSpec(memory_space=pltpu.HBM)
SMEM_SPEC = pl.BlockSpec(memory_space=pltpu.SMEM)


def vmem(*buffers):
    return [pltpu.VMEM(dims, dtype) for dims, dtype in buffers]


def dma(*dims):
    return pltpu.SemaphoreType.DMA(dims)


def adam_direction(master, gradient, moments):
    first_moment = beta_first * moments[0] + (1.0 - beta_first) * gradient
    second_moment = beta_second * moments[1] + (1.0 - beta_second) * gradient * gradient
    first_fix = 1.0 - beta_first**STEP
    second_fix = 1.0 - beta_second**STEP
    direction = (
        first_moment / first_fix / (jnp.sqrt(second_moment / second_fix) + adam_eps)
        + decay_rate * master
    )
    return (direction, first_moment, second_moment)


MESH = pl.DeviceIdType.MESH


class Place:
    def __init__(self):
        self.gx = lax.axis_index("gx")
        self.gy = lax.axis_index("gy")
        self.x = lax.rem(self.gx, 2)
        self.y = self.gx // 2
        self.z = self.gy // 2
        self.c = lax.rem(self.gy, 2)
        self.here = self.gx * 8 + self.gy

    def target(self, x, y, z, c):
        return (y * 2 + x, z * 2 + c)

    def index(self, x, y, z, c):
        return (y * 2 + x) * 8 + z * 2 + c

    def others(self):
        found = []
        for step in range(1, 32):
            device = lax.rem(self.here + step, 32)
            found.append((device // 8, lax.rem(device, 8)))
        return found


def greet(targets):
    barrier = pltpu.get_barrier_semaphore()
    for target in targets:
        pl.semaphore_signal(barrier, inc=1, device_id=target, device_id_type=MESH)
    pl.semaphore_wait(barrier, len(targets))


def remote(src, dst, send_sem, recv_sem, target):
    return pltpu.make_async_remote_copy(
        src_ref=src, dst_ref=dst, send_sem=send_sem, recv_sem=recv_sem, device_id=target, device_id_type=MESH
    )


def forward_sizes(length, width):
    pairs = width // LANES
    row = (length, width)
    lse = (length // QB, pairs, 2 * QB)
    kept = [(row, bf16)] * 4 + [(lse, f32), (row, f32), ((length, 1), f32)]
    scratch = [
        ((pairs, 2 * length, LANES), bf16), ((width, length), bf16),
        ((pairs, LONGEST + 2 * KB, 2 * QB), f32), ((pairs, LANES, QB), f32),
    ]
    return kept, scratch


class Gathering:
    parts = ((0, 32), (32, 32), (64, 96), (160, 112))

    def __init__(self, me, mine, near, full, zsend, xsend, ysend, csend, recv, crecv):
        self.me, self.mine, self.near, self.full = me, mine, near, full
        self.zsend, self.xsend, self.ysend, self.csend, self.recv, self.crecv = zsend, xsend, ysend, csend, recv, crecv
        x, y, z, c = me.x, me.y, me.z, me.c
        self.ox, self.oy, self.oc = 1 - x, 1 - y, 1 - c
        self.x_next = me.target(self.ox, y, z, c)
        self.y_next = me.target(x, self.oy, z, c)
        self.sibling = me.target(x, y, z, self.oc)
        self.up = me.target(x, y, lax.rem(z + 1, 4), c)
        self.down = me.target(x, y, lax.rem(z + 3, 4), c)

    def held(self, part):
        return self.near if part < 2 else self.full

    def copy(self, column, zz, part, target, sem, own=False):
        rows = pl.ds(*self.parts[part])
        c = self.me.c
        dst = self.held(part).at[column, zz, c, rows]
        return remote(self.mine.at[rows] if own else dst, dst, sem, self.recv.at[column, zz, part], target)

    def arrive(self, column, zz, part):
        self.copy(column, zz, part, self.sibling, self.xsend.at[part]).wait_recv()

    def to_x(self, column, zz, part, own=False):
        self.copy(column, zz, part, self.x_next, self.xsend.at[part], own).start()

    def to_y(self, column, zz, part, own=False):
        self.copy(column, zz, part, self.y_next, self.ysend.at[part], own).start()

    def column(self, x, y):
        return y * 2 + x

    def along(self, zz, part, upward, own=False):
        me = self.me
        target = self.up if upward else self.down
        sem = self.zsend.at[zz, part, 0 if upward else 1]

        if part < 2:
            return

        @pl.when((me.z < 3) if upward else (me.z > 0))
        def _():
            self.copy(me.gx, zz, part, target, sem, own).start()

    def straight(self, d, part):
        me = self.me
        target = me.target(me.x, me.y, lax.rem(me.z + d, 4), me.c)
        return self.copy(me.gx, me.z, part, target, self.zsend.at[d, part, 0], True)

    def own_straight(self, parts):
        for d in (1, 3, 2):
            for part in parts:
                self.straight(d, part).start()

    def own_z(self, parts):
        for part in parts:
            self.along(self.me.z, part, True, True)
            self.along(self.me.z, part, False, True)

    def own_sides(self, parts):
        for part in parts:
            self.to_x(self.me.gx, self.me.z, part, True)
            self.to_y(self.me.gx, self.me.z, part, True)

    def at_distance(self, d, action):
        z = self.me.z
        if d == 0:
            action(z, None)
            return

        @pl.when(z >= d)
        def _():
            action(z - d, True)

        @pl.when(z + d <= 3)
        def _():
            action(z + d, False)

    def inline(self, d, parts):
        me = self.me

        def action(zz, upward):
            for part in parts:
                self.arrive(me.gx, zz, part)
                self.along(zz, part, upward)
                self.to_x(me.gx, zz, part)
                self.to_y(me.gx, zz, part)

        self.at_distance(d, action)

    def side(self, d, parts):
        me = self.me

        def action(zz, _):
            for part in parts:
                if part % 2 == 0:
                    column = self.column(self.ox, me.y)
                    self.arrive(column, zz, part)
                    self.to_y(column, zz, part)
                else:
                    column = self.column(me.x, self.oy)
                    self.arrive(column, zz, part)
                    self.to_x(column, zz, part)

        self.at_distance(d, action)

    def last_columns(self, part):
        last = (self.me.x, self.oy) if part % 2 == 0 else (self.ox, self.me.y)
        return (self.column(*last), self.column(self.ox, self.oy))

    def far(self, d, parts):
        def action(zz, _):
            for part in parts:
                for column in self.last_columns(part):
                    self.arrive(column, zz, part)

        self.at_distance(d, action)

    def core(self, column, part):
        rows = pl.ds(*self.parts[part])
        block = self.held(part).at[column, :, self.me.c, rows]
        return remote(block, block, self.csend.at[column, part], self.crecv.at[column, part], self.sibling)

    def core_inline(self, parts):
        for part in parts:
            self.core(self.me.gx, part).start()

    def core_side(self, parts):
        me = self.me
        for part in parts:
            self.core(self.column(self.ox, me.y) if part % 2 == 0 else self.column(me.x, self.oy), part).start()

    def core_far(self, parts):
        for part in parts:
            for column in self.last_columns(part):
                self.core(column, part).start()

    def cores(self, parts):
        for part in parts:
            for column in range(4):
                self.core(column, part).wait_recv()

    def sent(self, parts):
        me = self.me
        for part in parts:
            if part < 2:
                for d in (1, 2, 3):
                    self.straight(d, part).wait_send()
            for zz in range(4 if part >= 2 else 0):

                @pl.when((me.z < 3) & (zz <= me.z))
                def _():
                    self.copy(me.gx, zz, part, self.up, self.zsend.at[zz, part, 0]).wait_send()

                @pl.when((me.z > 0) & (zz >= me.z))
                def _():
                    self.copy(me.gx, zz, part, self.down, self.zsend.at[zz, part, 1]).wait_send()

            rows = pl.ds(*self.parts[part])
            four, eight = self.held(part).at[0, :, 0, rows], self.held(part).at[pl.ds(0, 2), :, 0, rows]
            sems = (self.xsend.at[part], self.ysend.at[part])
            few, many = sems if part % 2 == 0 else sems[::-1]
            remote(four, four, few, self.recv.at[0, 0, part], self.sibling).wait_send()
            remote(eight, eight, many, self.recv.at[0, 0, part], self.sibling).wait_send()

    def cores_sent(self, parts):
        for part in parts:
            for column in range(4):
                self.core(column, part).wait_send()

    def stages(self, parts):
        return [
            lambda: self.inline(1, parts),
            lambda: (self.side(0, parts), self.inline(2, parts)),
            lambda: (self.side(1, parts), self.inline(3, parts), self.core_inline(parts)),
            lambda: (self.side(2, parts), self.far(0, parts)),
            lambda: (self.side(3, parts), self.core_side(parts), self.far(1, parts)),
            lambda: (self.far(2, parts), self.far(3, parts), self.core_far(parts)),
        ]


def first_kernel(
    attn_h, inner_h, outer_h, norm_h, lengths_h, src_h, tgt_h,
    full, bounds_out, spans_out, q_h, k_h, v_h, mix_h, lse_h, n1_h, s1_h,
    attn_f, inner_f, outer_f, norm_f, lengths, src, mine, bounds, spans, tgt, attn,
    q, k, v, mix, lse, n1, s1, query_z, value_t, score_scr, small_scr,
    sems, zsend, xsend, ysend, csend, recv, crecv,
):
    me = Place()
    move = Mover(sems)
    loads = [
        move.start(a, b)
        for a, b in (
            (attn_h, attn_f), (inner_h, inner_f), (outer_h, outer_f), (norm_h, norm_f), (lengths_h, lengths), (src_h, src),
        )
    ]
    load_tgt = move.start(tgt_h, tgt)
    gathering = Gathering(me, mine, attn, full, zsend, xsend, ysend, csend, recv, crecv)
    barrier = pltpu.get_barrier_semaphore()

    def greet(target):
        pl.semaphore_signal(barrier, inc=1, device_id=target, device_id_type=MESH)

    peers = [gathering.x_next, gathering.y_next, gathering.sibling]
    peers += [me.target(me.x, me.y, lax.rem(me.z + d, 4), me.c) for d in (1, 2, 3)]
    for target in peers:
        greet(target)
    move.wait(loads[0])
    for j in range(8):
        mine[16 * j : 16 * j + 16, :] = attn_f[j].astype(bf16)
    attn[me.gx, me.z, me.c] = mine[0:64, :]
    pl.semaphore_wait(barrier, len(peers))
    early, late = (0, 1), (2, 3)
    gathering.own_straight(early)
    gathering.own_sides(early)
    move.wait(*loads[1:])
    for b in range(4):
        mine[128 + 16 * b : 144 + 16 * b, :] = inner_f[:, 512 * b : 512 * b + 512].astype(bf16)
    mine[192:256, :] = outer_f[...].astype(bf16)
    lanes = jnp.concatenate([norm_f[...], jnp.zeros((6, 112), f32)], axis=1)
    lanes = jnp.concatenate([lanes, jnp.zeros((10, 128), f32)], axis=0)
    lanes = pltpu.roll(lanes, me.gy * 16, 1).astype(bf16)
    mine[256:272, :] = jnp.concatenate([lanes, jnp.zeros((16, 384), bf16)], axis=1)
    gathering.own_z(late)
    gathering.own_sides(late)
    keep = move.start(mine.at[pl.ds(64, 208)], full.at[me.gx, me.z, me.c, pl.ds(64, 208)])
    find_bounds(lengths, src, bounds, spans)
    move.start(bounds, bounds_out)
    move.start(spans, spans_out)
    sooner, later = gathering.stages(early), gathering.stages(late)
    for stage in (*sooner[:3], later[0], sooner[3], later[1], sooner[4], sooner[5]):
        stage()
    move.wait(keep)
    later[2]()
    gathering.cores(early)
    move.start(attn, full.at[:, :, :, pl.ds(0, 64)])
    move.wait(load_tgt)
    self_forward(
        tgt, attn.reshape(32, 64, 512), bounds, q, k, v, mix, lse, n1, s1, query_z, value_t, score_scr, small_scr,
        move, (q_h, k_h, v_h, mix_h, lse_h, n1_h, s1_h),
        (None, later[3], None, later[4], None, later[5]),
    )
    gathering.sent(early + late)
    gathering.cores_sent(early)
    gathering.cores(late)
    gathering.cores_sent(late)
    move.finish()


def gather_and_start(params, lengths, src_segments, tgt):
    length, width = tgt.shape
    kept, scratch = forward_sizes(length, width)
    row = (length, width)
    bounds, spans = ((8, length), jnp.int32), ((2 * length // QB, QB), jnp.int32)
    full = ((4, 4, 2, 272, 512), bf16)
    loads = [(p.shape, f32) for p in params] + [(lengths.shape, jnp.int32), (src_segments.shape, jnp.int32)]
    return pl.pallas_call(
        first_kernel,
        out_shape=tuple(shape(*item) for item in [full, bounds, spans] + kept),
        in_specs=[HBM_SPEC] * 7,
        out_specs=(HBM_SPEC,) * 10,
        scratch_shapes=vmem(
            *loads, ((272, 512), bf16), bounds, spans, (row, bf16), ((4, 4, 2, 64, 512), bf16), *kept, *scratch,
        )
        + [dma(24), dma(4, 4, 2), dma(4), dma(4), dma(4, 4), dma(4, 4, 4), dma(4, 4)],
        compiler_params=pltpu.CompilerParams(collective_id=0, has_side_effects=True, vmem_limit_bytes=GRANT),
    )(*params, lengths, src_segments, tgt)


def start_kernel(
    full, lengths, src, tgt, bounds_out, spans_out, q_h, k_h, v_h, mix_h, lse_h, n1_h, s1_h,
    bounds, spans, attn, q, k, v, mix, lse, n1, s1, query_z, value_t, score_scr, small_scr, sems,
):
    move = Mover(sems)
    load = move.start(full.at[:, pl.ds(0, attn.shape[1])], attn)
    find_bounds(lengths, src, bounds, spans)
    move.start(bounds, bounds_out)
    move.start(spans, spans_out)
    move.wait(load)
    self_forward(
        tgt, attn, bounds, q, k, v, mix, lse, n1, s1, query_z, value_t, score_scr, small_scr,
        move, (q_h, k_h, v_h, mix_h, lse_h, n1_h, s1_h), (),
    )
    move.finish()


def start_only(full, lengths, src_segments, tgt):
    length, width = tgt.shape
    kept, scratch = forward_sizes(length, width)
    bounds, spans = ((8, length), jnp.int32), ((2 * length // QB, QB), jnp.int32)
    return pl.pallas_call(
        start_kernel,
        out_shape=tuple(shape(*item) for item in [bounds, spans] + kept),
        in_specs=[HBM_SPEC] + [VMEM_SPEC] * 3,
        out_specs=(HBM_SPEC,) * 9,
        scratch_shapes=vmem(bounds, spans, ((full.shape[0], 64, width), bf16), *kept, *scratch) + [dma(16)],
        compiler_params=pltpu.CompilerParams(vmem_limit_bytes=GRANT),
    )(full, lengths, src_segments, tgt)


def middle(spans, bounds, full, memory, cotangent, n1, s1):
    length, width = n1.shape
    keys = memory.shape[0]
    blocks = full.shape[0]
    ffn_rows = full.shape[1] - 144
    hidden = ffn_rows * blocks // 2 * full.shape[2] // width
    pairs = width // LANES
    row, mem_row = (length, width), (keys, width)
    zeroed = ((pairs, 2 * length, LANES), bf16)
    gffn, gcross = ((blocks, ffn_rows, width), bf16), ((blocks, 64, width), bf16)
    outs = [(row, bf16), (row, f32), (mem_row, bf16), gffn, gcross, ((8, width), f32)]
    scratch = vmem(
        (bounds.shape, jnp.int32), ((blocks, 16, width // 4), bf16), gcross, gffn, (mem_row, bf16), (row, bf16), (row, f32),
        ((length, 1), f32), (row, bf16), (mem_row, bf16), (mem_row, bf16), (row, bf16),
        ((length // QB, pairs, 2 * QB), f32), zeroed, zeroed, ((pairs, keys + KB, 2 * QB), f32),
        ((pairs, LANES, QB), f32), ((length, hidden), bf16), ((length, hidden), bf16), (row, bf16), (row, bf16),
        (row, f32), (row, bf16), (row, bf16), (row, bf16), (mem_row, f32), (mem_row, f32), (row, bf16), (mem_row, bf16),
        gffn, gcross, ((6, 8, width), f32), ((8, width), f32),
        ((length // QB, pairs, 2 * QB), f32),
    )
    return pl.pallas_call(
        middle_kernel,
        out_shape=tuple(shape(*item) for item in outs),
        in_specs=[SMEM_SPEC] + [HBM_SPEC] * 6,
        out_specs=(HBM_SPEC,) * 5 + (VMEM_SPEC,),
        scratch_shapes=scratch + [dma(16)],
        compiler_params=pltpu.CompilerParams(vmem_limit_bytes=GRANT),
    )(spans, bounds, full, memory, cotangent, n1, s1)


OUTER_ROWS = slice(96, 160)


def attn_rows(j):
    return 192 + 16 * j if j < 4 else 64 + 16 * (j - 4) if j < 6 else 160 + 16 * (j - 6)


def add_rows(dst, *sources):
    total = sources[0][...].astype(f32)
    for source in sources[1:]:
        total = total + source[...].astype(f32)
    dst[...] = total.astype(dst.dtype)


class Summing:
    order = (2, 1, 3, 0)

    def __init__(self, me, sources, rows, pieces, first_a, first_b, second_a, second_b, third, result, sems):
        self.me, self.sources, self.rows, self.pieces = me, sources, rows, pieces
        self.first_a, self.first_b, self.second_a, self.second_b, self.third = first_a, first_b, second_a, second_b, third
        self.result = result
        (self.lsem, self.csend, self.crecv, self.send1, self.recv1, self.send2, self.recv2, self.send3, self.recv3) = sems
        x, y, z, c = me.x, me.y, me.z, me.c
        self.ox, self.oy, self.oc = 1 - x, 1 - y, 1 - c
        self.x_next = me.target(self.ox, y, z, c)
        self.y_next = me.target(x, self.oy, z, c)
        self.sibling = me.target(x, y, z, self.oc)
        self.zs = [lax.rem(z + d, 4) for d in range(4)]
        self.half = first_a.shape[2]
        self.top, self.bottom = pl.ds(0, self.half), pl.ds(self.half, self.half)
        self.pending, self.cores, self.own = [], {}, {}
        self.firsts, self.seconds, self.thirds = {}, {}, {}

    def send(self, *args):
        copy = remote(*args)
        copy.start()
        self.pending.append(copy)
        return copy

    def load(self):
        for d in self.order:
            for k, (source, kept, _) in enumerate(self.sources):
                if kept is not None:
                    copy = pltpu.make_async_copy(source.at[:, self.zs[d], self.me.c], kept.at[d], self.lsem.at[d, k])
                    copy.start()
                    self.own[d, k] = copy

    def core(self):
        for d in self.order:
            for k, (source, _, got) in enumerate(self.sources):
                self.cores[d, k] = self.send(
                    source.at[:, self.zs[d], self.oc], got.at[d], self.csend.at[d, k], self.crecv.at[d, k], self.sibling
                )

    def stage1(self, d):
        me = self.me
        for k in range(len(self.sources)):
            if (d, k) in self.own:
                self.own[d, k].wait()
            self.cores[d, k].wait_recv()

        def add(i):
            piece = self.pieces.at[d, i // 2, lax.rem(i, 2)]
            for start, count, k, first in self.rows:
                source, kept, got = self.sources[k]
                held = source.at[i, self.zs[d], me.c] if kept is None else kept.at[d, i]
                part = pl.ds(first, count)
                add_rows(piece.at[pl.ds(start, count)], held.at[part], got.at[d, i, part])

        each_chunk(4, add)
        self.firsts[d] = (
            self.send(
                self.pieces.at[d, self.oy, :, self.top], self.first_a.at[d], self.send1.at[d, 0], self.recv1.at[d, 0],
                self.y_next,
            ),
            self.send(
                self.pieces.at[d, :, self.ox, self.bottom], self.first_b.at[d], self.send1.at[d, 1],
                self.recv1.at[d, 1], self.x_next,
            ),
        )

    def stage2(self, d):
        me = self.me
        self.firsts[d][0].wait_recv()
        part = self.pieces.at[d, me.y, self.ox, self.top]
        add_rows(part, part, self.first_a.at[d, self.ox])
        one = self.send(part, self.second_a.at[d], self.send2.at[d, 0], self.recv2.at[d, 0], self.x_next)
        self.firsts[d][1].wait_recv()
        part = self.pieces.at[d, self.oy, me.x, self.bottom]
        add_rows(part, part, self.first_b.at[d, self.oy])
        two = self.send(part, self.second_b.at[d], self.send2.at[d, 1], self.recv2.at[d, 1], self.y_next)
        self.seconds[d] = (one, two)

    def stage3(self, d):
        me = self.me
        for copy in self.seconds[d]:
            copy.wait_recv()
        for rows, first, second, at in (
            (self.top, self.first_a, self.second_a, me.x), (self.bottom, self.first_b, self.second_b, me.y),
        ):
            part = self.pieces.at[d, me.y, me.x, rows]
            add_rows(part if d else self.result.at[rows], part, first.at[d, at], second.at[d])
        if d:
            self.thirds[d] = self.send(
                self.pieces.at[d, me.y, me.x], self.third.at[d - 1], self.send3.at[d - 1], self.recv3.at[d - 1],
                me.target(me.x, me.y, self.zs[d], me.c),
            )

    def end(self):
        for d in (1, 2, 3):
            self.thirds[d].wait_recv()
        add_rows(self.result, self.result, self.third.at[0], self.third.at[1], self.third.at[2])


def last_kernel(
    full, bounds_h, tgt_h, q_h, k_h, v_h, mix_h, lse_h, d1_h, gffn, gcross, gnorm_h,
    attn_ph, inner_ph, outer_ph, norm_ph, attn_mh, in_mh, out_mh, norm_mh,
    tgrad_h, g_h, gn_ref, totals_ref,
    g_ref, attn_p, inner_p, outer_p, norm_p, attn_m, in_m, out_m, norm_m,
    bounds, tgt, attn, q, k, v, mix, lse, d1, tgrad, gself, query_z, grad_z, key_t, grad_scr, dq_scr, dk_scr, dv_scr,
    small_scr, d1_scr, delta, own_ffn, own_cross, got_ffn, got_cross, pieces, first_a, first_b, second_a, second_b, third,
    got_self, pieces2, first_a2, first_b2, second_a2, second_b2, third2, vectors, squares, tiles,
    msems, psems, *sems,
):
    me = Place()
    move = Mover(msems)
    others = me.others()
    barrier = pltpu.get_barrier_semaphore()
    for target in others:
        pl.semaphore_signal(barrier, inc=1, device_id=target, device_id_type=MESH)
    load_first = [move.start(a, b) for a, b in ((gnorm_h, vectors.at[0]), (d1_h, d1), (full.at[:, pl.ds(0, 64)], attn))]
    load_mix = move.start(mix_h, mix)
    load_rest = [
        move.start(a, b)
        for a, b in ((q_h, q), (k_h, k), (v_h, v), (lse_h, lse), (bounds_h, bounds), (tgt_h, tgt))
    ]
    sems1, sems2, (nsend, nrecv, tsend, trecv) = sems[0:9], sems[9:18], sems[18:22]
    big = Summing(
        me, [(gffn, own_ffn, got_ffn), (gcross, own_cross, got_cross)],
        [(0, 64, 0, 0), (64, 32, 1, 0), (96, 64, 0, 64), (160, 32, 1, 32)],
        pieces, first_a, first_b, second_a, second_b, third, g_ref.at[pl.ds(0, 192)], sems1,
    )
    rest = Summing(
        me, [(gself, None, got_self)], [(0, 64, 0, 0)],
        pieces2, first_a2, first_b2, second_a2, second_b2, third2, g_ref.at[pl.ds(192, 64)], sems2,
    )
    big.load()
    pl.semaphore_wait(barrier, len(others))
    big.core()
    load_last = [
        move.start(a, b)
        for a, b in (
            (attn_ph, attn_p), (inner_ph, inner_p), (outer_ph, outer_p), (norm_ph, norm_p),
            (attn_mh, attn_m), (in_mh, in_m), (out_mh, out_m), (norm_mh, norm_m),
        )
    ]
    move.wait(*load_first, load_mix)
    norm_copies = [big.send(vectors.at[0], vectors.at[1], nsend.at[0], nrecv.at[0], big.sibling)]

    def norm_step(stage, target):
        norm_copies[-1].wait_recv()
        vectors[2 * stage] = vectors[2 * stage - 2] + vectors[2 * stage - 1]
        norm_copies.append(
            big.send(vectors.at[2 * stage], vectors.at[2 * stage + 1], nsend.at[stage], nrecv.at[stage], target)
        )

    def norm_last():
        norm_copies[-1].wait_recv()
        vectors[6] = vectors[4] + vectors[5]
        for d in range(1, 4):
            target = me.target(me.x, me.y, big.zs[d], me.c)
            norm_copies.append(big.send(vectors.at[6], vectors.at[6 + d], nsend.at[2 + d], nrecv.at[2 + d], target))

    far, up, down, here = big.order
    steps = [
        None,
        lambda: norm_step(1, big.x_next),
        None,
        lambda: (big.stage2(far), big.stage1(down)),
        None,
        lambda: (big.stage2(up), big.stage3(far), big.stage1(here), norm_step(2, big.y_next)),
        None,
        lambda: (big.stage2(down), big.stage3(up)),
    ]

    begin = (lambda: big.stage1(far), lambda: big.stage1(up))

    def late():
        rest.core()
        big.stage2(here)
        rest.stage1(far)
        rest.stage1(up)
        big.stage3(down)
        norm_last()

    move.wait(*load_rest)
    self_backward(
        tgt, attn, bounds, q, k, v, mix, lse, d1, tgrad, gself.reshape(32, 64, 512),
        query_z, grad_z, key_t, grad_scr, dq_scr, dk_scr, dv_scr, small_scr, d1_scr, delta, steps, begin, late,
    )
    move.start(tgrad, tgrad_h)
    rest.stage1(down)
    rest.stage1(here)
    big.stage3(here)
    rest.stage2(far)
    rest.stage2(up)
    rest.stage3(far)
    rest.stage2(down)
    rest.stage3(up)
    rest.stage2(here)
    rest.stage3(down)
    rest.stage3(here)
    big.end()
    for copy in norm_copies[3:]:
        copy.wait_recv()
    vectors[10] = (vectors[6] + vectors[8]) + (vectors[7] + vectors[9])
    lanes = vectors[10, :, pl.ds(pl.multiple_of(me.gx * 128, 128), 128)]
    gn_ref[...] = pltpu.roll(lanes, lax.rem(128 - me.gy * 16, 128), 1)

    def put(t, pairs):
        for i in range(2):
            squares[16 * i + t : 16 * i + t + 1, :] = sum(
                jnp.sum(pair[i] * pair[i], axis=0, keepdims=True) for pair in pairs
            )

    move.wait(*load_last)

    def direction(*args):
        return adam_direction(*args)[0]

    def put_attn(j):
        grad = g_ref[attn_rows(j) : attn_rows(j) + 16, :]
        put(j, [(attn_p[j], direction(attn_p[j], grad, (attn_m[0, j], attn_m[1, j])))])

    for j in range(4, 8):
        put_attn(j)
    pairs = []
    for b in range(4):
        cols = slice(512 * b, 512 * b + 512)
        grad = g_ref[16 * b : 16 * b + 16, :]
        pairs.append((inner_p[:, cols], direction(inner_p[:, cols], grad, (in_m[0, :, cols], in_m[1, :, cols]))))
    put(8, pairs)
    put(9, [(outer_p[...], direction(outer_p[...], g_ref[OUTER_ROWS, :], (out_m[0], out_m[1])))])
    master = norm_p[...]
    update = direction(master, gn_ref[0:6, 0:16], (norm_m[:, 0, :], norm_m[:, 1, :]))
    rest_lanes = jnp.zeros((6, 512 - 16), f32)
    master, update = (jnp.concatenate([item, rest_lanes], axis=1) for item in (master, update))
    for i in range(6):
        put(10 + i, [(master[i : i + 1], update[i : i + 1])])
    rest.end()
    move.start(g_ref, g_h)
    for j in range(4):
        put_attn(j)
    folded = (squares[:, 0:128] + squares[:, 128:256]) + (squares[:, 256:384] + squares[:, 384:512])
    row = jnp.sum(folded.T, axis=0, keepdims=True)
    row = jnp.concatenate([row, jnp.zeros((1, 96), f32)], axis=1)
    tiles[me.here] = jnp.concatenate([row, jnp.zeros((7, 128), f32)], axis=0)
    for target in others:
        remote(tiles.at[me.here], tiles.at[me.here], tsend, trecv, target).start()
    for copy in big.pending + rest.pending:
        copy.wait_send()
    received = tiles.at[pl.ds(0, 31)]
    every = remote(received, received, tsend, trecv, big.sibling)
    every.wait_recv()
    every.wait_send()
    totals_ref[...] = jnp.sum(tiles[...], axis=0)
    move.finish()


def backward_scratch(length, width):
    pairs = width // LANES
    row = (length, width)
    zeroed = ((pairs, 2 * length, LANES), bf16)
    return [
        zeroed, zeroed, ((width, length), bf16), (row, bf16), (row, bf16), (row, f32), (row, f32),
        ((pairs, LANES, QB), f32), (row, bf16), ((length // QB, pairs, 2 * QB), f32),
    ]


def finish_and_reduce(full, bounds, tgt, saved, d1, grads, norm_grad, params, moments):
    length, width = tgt.shape
    row = (length, width)
    lse = (length // QB, width // LANES, 2 * QB)

    def sums(half):
        return [
            ((4, 2, 2, 2 * half, 512), bf16), ((4, 2, half, 512), bf16), ((4, 2, half, 512), bf16),
            ((4, half, 512), bf16), ((4, half, 512), bf16), ((3, 2 * half, 512), bf16),
        ]

    scratch = vmem(
        ((256, 512), f32), *((item.shape, f32) for item in (*params, *moments)),
        (bounds.shape, jnp.int32), (row, bf16), ((32, 64, 512), bf16), *[(row, bf16)] * 4, (lse, f32), (row, f32),
        (row, bf16), ((4, 4, 2, 64, 512), bf16), *backward_scratch(length, width),
        ((4, 4, 128, 512), bf16), ((4, 4, 64, 512), bf16), ((4, 4, 128, 512), bf16), ((4, 4, 64, 512), bf16), *sums(96),
        ((4, 4, 64, 512), bf16), *sums(32), ((11, 8, 512), f32), ((32, 512), f32), ((32, 8, 128), f32),
    )
    round_sems = [dma(4, 2), dma(4, 2), dma(4, 2), dma(4, 2), dma(4, 2), dma(4, 2), dma(4, 2), dma(3), dma(3)]
    split = [grad.reshape(4, 4, 2, grad.shape[1], 512) for grad in grads]
    return pl.pallas_call(
        last_kernel,
        out_shape=(shape(row, bf16), shape((256, 512), f32), shape((8, 128), f32), shape((8, 128), f32)),
        in_specs=[HBM_SPEC] * 20,
        out_specs=(HBM_SPEC, HBM_SPEC, VMEM_SPEC, VMEM_SPEC),
        scratch_shapes=scratch + [dma(24), dma(1)] + round_sems + round_sems + [dma(6), dma(6)] + [pltpu.SemaphoreType.DMA] * 2,
        compiler_params=pltpu.CompilerParams(collective_id=1, has_side_effects=True, vmem_limit_bytes=GRANT),
    )(full, bounds, tgt, *saved, d1, *split, norm_grad, *params, *moments)


def finish_kernel(
    full, bounds, tgt, q, k, v, mix, lse, d1, tgrad, gself,
    attn, query_z, grad_z, key_t, grad_scr, dq_scr, dk_scr, dv_scr, small_scr, d1_scr, delta, sems,
):
    move = Mover(sems)
    move.wait(move.start(full.at[:, pl.ds(0, attn.shape[1])], attn))
    self_backward(
        tgt, attn, bounds, q, k, v, mix, lse, d1, tgrad, gself,
        query_z, grad_z, key_t, grad_scr, dq_scr, dk_scr, dv_scr, small_scr, d1_scr, delta, (), (lambda: None,) * 2, lambda: None,
    )


def finish_only(full, bounds, tgt, saved, d1):
    length, width = tgt.shape
    gself = ((full.shape[0], 64, width), bf16)
    return pl.pallas_call(
        finish_kernel,
        out_shape=(shape((length, width), bf16), shape(*gself)),
        in_specs=[HBM_SPEC] + [VMEM_SPEC] * 8,
        out_specs=(VMEM_SPEC, VMEM_SPEC),
        scratch_shapes=vmem(gself, *backward_scratch(length, width)) + [dma(2)],
        compiler_params=pltpu.CompilerParams(vmem_limit_bytes=GRANT),
    )(full, bounds, tgt, *saved, d1)


def update_kernel(*refs):
    ins, outs = refs[:12], refs[12:30]
    held, made, sems = refs[30:42], refs[42:59], refs[59]
    move = Mover(sems)
    order = (3, 2, 1, 7, 11, 6, 10, 5, 9, 4, 8, 0)
    loads = {i: move.start(ins[i], held[i]) for i in order}
    g_ref, gn_ref, totals_ref, attn, inner, outer, norm, attn_m, in_m, out_m, norm_m = held[1:]
    norms_ref = made[16]

    def results(t):
        return [(made[i], outs[1 + i]) for i in (t, 4 + 2 * t, 5 + 2 * t, 12 + t)]

    def step(t, master, gradient, moments, ratio, refs, place):
        direction, first_moment, second_moment = adam_direction(master, gradient, moments)
        value = master - ratio * direction
        for (ref, _), item in zip(refs, (value, first_moment, second_moment, value.astype(bf16))):
            ref[place] = item

    def leave(refs):
        for ref, out in refs:
            move.start(ref, out)

    move.wait(loads[3], loads[2], loads[7], loads[11])
    roots = jnp.sqrt(totals_ref[0:1, 0:32])
    norms_ref[0:1, :] = roots[:, 0:16]
    norms_ref[1:2, :] = roots[:, 16:32]
    move.start(norms_ref, outs[17])
    ratio = learn_rate * (roots[:, 0:16] / roots[:, 16:32])
    vectors = results(3)
    for i in range(6):
        one = slice(i, i + 1)
        moments = (norm_m[i, 0:1], norm_m[i, 1:2])
        step(10 + i, norm[one], gn_ref[one, 0:16], moments, ratio[:, 10 + i : 11 + i], vectors, one)
    leave(vectors)
    move.wait(loads[1], loads[6], loads[10])
    moments = (out_m[0], out_m[1])
    step(2, outer[...], g_ref[OUTER_ROWS, :], moments, ratio[:, 9:10], results(2), ...)
    leave(results(2))
    move.wait(loads[5], loads[9])
    for b in range(4):
        cols = slice(512 * b, 512 * b + 512)
        moments = (in_m[0, :, cols], in_m[1, :, cols])
        step(1, inner[:, cols], g_ref[16 * b : 16 * b + 16, :], moments, ratio[:, 8:9], results(1), (slice(None), cols))
    leave(results(1))
    move.wait(loads[4], loads[8], loads[0])
    move.start(held[0], outs[0])
    for j in range(8):
        grad = g_ref[attn_rows(j) : attn_rows(j) + 16, :]
        step(0, attn[j], grad, (attn_m[0, j], attn_m[1, j]), ratio[:, j : j + 1], results(0), j)
    leave(results(0))
    move.finish()


def update_params(summed, params, moments):
    args = (*summed, *params, *moments)
    outs = [shape(p.shape, f32) for p in params]
    outs += [shape(p.shape, f32) for p in params for _ in range(2)]
    outs += [shape(p.shape, bf16) for p in params] + [shape((2, 16), f32)]
    return pl.pallas_call(
        update_kernel,
        out_shape=(shape(summed[0].shape, bf16), *outs),
        in_specs=[HBM_SPEC] * len(args),
        out_specs=(HBM_SPEC,) * (1 + len(outs)),
        scratch_shapes=vmem(*((item.shape, item.dtype) for item in (*args, *outs))) + [dma(32)],
        compiler_params=pltpu.CompilerParams(vmem_limit_bytes=GRANT),
    )(*args)


def tensor_squares(attn_part, inner_part, outer_part, norm_part):
    return jnp.concatenate(
        [
            jnp.sum(attn_part * attn_part, axis=(1, 2)),
            jnp.sum(inner_part * inner_part)[None],
            jnp.sum(outer_part * outer_part)[None],
            jnp.sum(norm_part * norm_part, axis=1),
        ]
    )


def blocked(matrix, width):
    blocks = matrix.shape[0] // 16
    cols = matrix.shape[1] // width
    return matrix.reshape(blocks, 16, cols, width).transpose(0, 2, 1, 3).reshape(blocks, cols * 16, width)


def unblocked(blocks, width):
    count = blocks.shape[0]
    cols = blocks.shape[1] // 16
    return blocks.reshape(count, cols, 16, width).transpose(0, 2, 1, 3).reshape(count * 16, cols * width)


def gather_any(attn_w, ffn_in, ffn_out, norm_params):
    width = attn_w.shape[2]
    attn = lax.all_gather(attn_w.astype(bf16), AXES, axis=1, tiled=True)
    inner = lax.all_gather(ffn_in.astype(bf16), AXES, axis=0, tiled=True)
    outer = lax.all_gather(ffn_out.astype(bf16), AXES, axis=0, tiled=True)
    norm = lax.all_gather(norm_params.astype(bf16), AXES, axis=1, tiled=True)
    blocks = width // 16
    attn = attn.reshape(8, blocks, 16, width).transpose(1, 0, 2, 3).reshape(blocks, 8 * 16, width)
    lanes = jnp.pad(norm, ((0, 10), (0, 0))).reshape(16, 4, 1, width // 4).transpose(1, 2, 0, 3)
    lanes = jnp.pad(lanes, ((0, 0), (0, blocks // 4 - 1), (0, 0), (0, width - width // 4))).reshape(blocks, 16, width)
    return jnp.concatenate([attn, blocked(inner, width), outer.reshape(blocks, -1, width), lanes], axis=1)


def reduce_any(grads, norm_grad, params, moments):
    grad_ffn, grad_cross, grad_self = grads
    width = grad_ffn.shape[2]
    blocks = width // 16
    attn_w, ffn_in, ffn_out, norm_params = params
    attn_m, in_m, out_m, norm_m = moments
    stack = jnp.concatenate([grad_self, grad_cross], axis=1)
    stack = stack.reshape(blocks, 8, 16, width).transpose(1, 0, 2, 3).reshape(8, width, width)
    rows = ffn_in.shape[1] // width * 16
    inner = unblocked(grad_ffn[:, :rows], width)
    outer = grad_ffn[:, rows:].reshape(-1, width)
    shard_attn = lax.psum_scatter(stack, AXES, scatter_dimension=1, tiled=True).astype(f32)
    shard_inner = lax.psum_scatter(inner, AXES, scatter_dimension=0, tiled=True).astype(f32)
    shard_outer = lax.psum_scatter(outer, AXES, scatter_dimension=0, tiled=True).astype(f32)
    shard_norm = lax.psum_scatter(norm_grad, AXES, scatter_dimension=1, tiled=True)
    attn_dir, attn_first, attn_second = adam_direction(attn_w, shard_attn, attn_m)
    inner_dir, inner_first, inner_second = adam_direction(ffn_in, shard_inner, in_m)
    outer_dir, outer_first, outer_second = adam_direction(ffn_out, shard_outer, out_m)
    norm_dir, norm_first, norm_second = adam_direction(norm_params, shard_norm, norm_m)
    weight_total, update_total = lax.psum(
        (tensor_squares(*params), tensor_squares(attn_dir, inner_dir, outer_dir, norm_dir)), AXES
    )
    ratio = jnp.sqrt(weight_total) / jnp.sqrt(update_total)
    attn_new = attn_w - learn_rate * ratio[0:8][:, None, None] * attn_dir
    in_new = ffn_in - learn_rate * ratio[8] * inner_dir
    out_new = ffn_out - learn_rate * ratio[9] * outer_dir
    norm_new = norm_params - learn_rate * ratio[10:16][:, None] * norm_dir
    norms = jnp.stack([jnp.sqrt(weight_total), jnp.sqrt(update_total)])
    return (
        attn_new, in_new, out_new, norm_new,
        attn_first, attn_second, inner_first, inner_second, outer_first, outer_second, norm_first, norm_second,
        attn_new.astype(bf16), in_new.astype(bf16), out_new.astype(bf16), norm_new.astype(bf16), norms,
    )


def on_device(
    close, tgt, memory, cotangent, tgt_lengths, src_segments, attn_w, ffn_in, ffn_out, norm_params,
    attn_moments, in_moments, out_moments, norm_moments,
):
    params = (attn_w, ffn_in, ffn_out, norm_params)
    moments = (attn_moments, in_moments, out_moments, norm_moments)
    if close and tgt.shape[0] == 1:
        full, bounds, spans, *state = gather_and_start(params, tgt_lengths, src_segments, tgt[0])
        full = full.reshape(32, *full.shape[3:])
        saved, (n1, s1) = state[:5], state[5:]
        layer_out, d1, mem_grad, grad_ffn, grad_cross, norm_grad = middle(
            spans, bounds, full, memory[0], cotangent[0], n1, s1
        )
        moments = (*moments[:3], norm_moments.transpose(1, 0, 2))
        summed = finish_and_reduce(
            full, bounds, tgt[0], saved, d1, (grad_ffn, grad_cross), norm_grad, params, moments
        )
        tgt_grad, *updated = update_params(summed, params, moments)
        return (layer_out[None], tgt_grad[None], mem_grad[None], *updated)
    full = gather_any(*params)
    parts = []
    for r in range(tgt.shape[0]):
        bounds, spans, *state = start_only(full, tgt_lengths[r : r + 1], src_segments[r : r + 1], tgt[r])
        saved, (n1, s1) = state[:5], state[5:]
        layer_out, d1, mem_grad, grad_ffn, grad_cross, norm_grad = middle(
            spans, bounds, full, memory[r], cotangent[r], n1, s1
        )
        tgt_grad, grad_self = finish_only(full, bounds, tgt[r], saved, d1)
        parts.append((layer_out, tgt_grad, mem_grad, grad_ffn, grad_cross, grad_self, norm_grad[0:6]))
    outs = [jnp.stack([part[i] for part in parts]) for i in range(3)]
    sums = [sum(part[i].astype(f32) for part in parts) for i in range(3, 7)]
    grads = [grad.astype(bf16) for grad in sums[:3]]
    return (*outs, *reduce_any(grads, sums[3], params, moments))


def fits(mesh):
    return mesh.shape["gx"] == 4 and mesh.shape["gy"] == 8


def solution(mesh):
    rows = P(AXES, None, None)
    matrix = P(AXES, None)
    stack = P(None, AXES, None)
    vectors = P(None, AXES)
    return jax.shard_map(
        functools.partial(on_device, fits(mesh)),
        mesh=mesh,
        in_specs=(
            rows, rows, rows, matrix, matrix, stack, matrix, matrix, vectors,
            P(None, None, AXES, None), stack, stack, P(None, None, AXES),
        ),
        out_specs=(
            rows, rows, rows, stack, matrix, matrix, vectors, stack, stack, matrix, matrix, matrix, matrix,
            vectors, vectors, stack, matrix, matrix, vectors, P(),
        ),
        check_vma=False,
    )
```
